32 devices in a mesh: dp: 2 (over core), ctx: 4 (over z), head: 4 (over y, x).
Axes of the slice: x: 2, y: 2, z: 4, core: 2. Of those that a mesh axis runs over, the one named last changes fastest.
Arguments:
- queries: bfloat16 [2, 4096, 2048], P('dp', 'ctx', 'head'), may hold values from -6 to 6
- keys_raw: bfloat16 [2, 4096, 2048], P('dp', 'ctx', 'head'), may hold values from -0.625 to 0.625
- values: bfloat16 [2, 4096, 2048], P('dp', 'ctx', 'head'), may hold values from -6 to 6
- gates: float32 [2, 16, 4096], P('dp', 'head', 'ctx'), as said below
- lengths: int32 [2, 16], P('dp'), may hold values from 1 to 2048, 4096 in all within a row
- key_gain: float32 [16, 128], P('head'), may hold values from 0.1 to 1.9
- cotangent: bfloat16 [2, 4096, 2048], P('dp', 'ctx', 'head'), may hold values from -6 to 6
Outputs:
- attended: bfloat16 [2, 4096, 2048], P('dp', 'ctx', 'head')
- grad_queries: bfloat16 [2, 4096, 2048], P('dp', 'ctx', 'head')
- grad_keys: bfloat16 [2, 4096, 2048], P('dp', 'ctx', 'head')
- grad_values: bfloat16 [2, 4096, 2048], P('dp', 'ctx', 'head')
- grad_gates: float32 [2, 16, 4096], P('dp', 'head', 'ctx')
- grad_gain: float32 [16, 128], P('head', 'dp')
The draws below stay inside these ranges and needn't reach their ends.
Inputs may be any that keep to these rules, and one draw needn't show every extreme that they name: Each row of lengths gives its documents in packing order and sums to 4096. `gates`: every entry is negative.
All inputs are finite; a program needn't handle non-finite values.
Results may differ from the reference program's by a relative error of at most 0.009.
Values sent between devices are 32-bit elements; how exact they have to be, the bound alone decides.
No kernel may reach another device: no remote copies, remote signals or barrier semaphores. Data moves between devices by JAX's collectives and lax.ppermute only.
A program may use at most 128 MiB of HBM per device.

```python
import math
import jax
import jax.numpy as jnp
import numpy as np
from jax import lax

LOCAL_HEADS = 16
DH = 128
TOK_DEV = 1024
BLOCK = 512
DOCS = 16
SEQUENCE_LENGTH = 4096
BATCH_SEQUENCES = 2
DOC_MOST = 2048


def draw_gates(key, part):
    parallel_lanes = jax.random.split(key, 7)
    shards = SEQUENCE_LENGTH // TOK_DEV
    fast_share = 0.5
    is_fast = jax.random.uniform(parallel_lanes[0], (BATCH_SEQUENCES, LOCAL_HEADS, 1, 1)) < fast_share
    fast_rate = jnp.exp(jax.random.uniform(parallel_lanes[1], (BATCH_SEQUENCES, LOCAL_HEADS, 1, 1), minval=jnp.log(1.0 / 50.0), maxval=jnp.log(1.0 / 30.0)))
    slow_rate = jnp.exp(jax.random.uniform(parallel_lanes[2], (BATCH_SEQUENCES, LOCAL_HEADS, 1, 1), minval=jnp.log(0.05), maxval=jnp.log(0.3))) / DOC_MOST
    base_rate = jnp.where(is_fast, fast_rate, slow_rate)
    shard_factor = jnp.exp(jax.random.uniform(parallel_lanes[3], (BATCH_SEQUENCES, LOCAL_HEADS, shards, 1), minval=-0.7, maxval=0.7))
    jitter = jnp.exp(jax.random.uniform(parallel_lanes[4], (BATCH_SEQUENCES, LOCAL_HEADS, shards, TOK_DEV), minval=-0.7, maxval=0.7))
    gentle_gate = -(base_rate * shard_factor * jitter).reshape(BATCH_SEQUENCES, LOCAL_HEADS, SEQUENCE_LENGTH)
    spike_gate = jax.random.uniform(parallel_lanes[5], (BATCH_SEQUENCES, LOCAL_HEADS, SEQUENCE_LENGTH)) < 4.0 / SEQUENCE_LENGTH
    spike_gate_value = jnp.log(jax.random.uniform(parallel_lanes[6], (BATCH_SEQUENCES, LOCAL_HEADS, SEQUENCE_LENGTH), minval=0.5, maxval=0.8))
    return jnp.where(spike_gate, spike_gate_value, gentle_gate).astype(jnp.float32)


def block_levels(rng, extent, pieces, smallest, top_value):
    def one(axis_at, shards_of):
        draws = jax.random.uniform(jax.random.fold_in(jax.random.fold_in(rng, 6), axis_at), (shards_of,), jnp.float32, smallest / len(pieces), top_value / len(pieces))
        return jnp.repeat(jnp.exp(draws), extent[axis_at] // shards_of).reshape((-1,) + (1,) * (len(extent) - axis_at - 1))

    level = one(*pieces[0])
    for cut in pieces[1:]:
        level = level * one(*cut)
    return level


def length_profile(count, total, reach, skew):
    weights = [(1 << 20) // math.isqrt(grade ** skew) + 1 for grade in range(2, count + 1)]
    spare, given = total - reach - (count - 1), [1] * (count - 1)
    while spare > 0:
        movable = [i for i in range(count - 1) if given[i] < reach]
        whole, left = sum([weights[i] for i in movable]), spare
        for i in movable:
            addition = min(reach - given[i], max(1, left * weights[i] // whole), spare)
            given[i] = given[i] + addition
            spare = spare - addition
    return np.array([reach] + given)


def ragged_sizes(key, number_of, total, most, slope):
    if number_of == 2:
        one = jax.random.randint(key, (), max(1, total - most), min(most, total - 1) + 1)
        return jnp.stack([one, total - one])
    sizes = jnp.asarray(length_profile(number_of, total, most, slope), jnp.int32)
    twos = (number_of - 1) // 2
    giver, sink = sizes[1:1 + 2 * twos:2], sizes[2:2 + 2 * twos:2]
    slack = jnp.minimum(giver - 1, most - sink)
    passed = jax.random.randint(jax.random.fold_in(key, 1), (twos,), 0, 1 << 20) % (slack + 1)
    sizes = sizes.at[1:1 + 2 * twos:2].set(giver - passed).at[2:2 + 2 * twos:2].set(sink + passed)
    return sizes[jax.random.permutation(jax.random.fold_in(key, 2), number_of)]


def centred(stream_key, shape, scale, limit, cuts=(), held_as=jnp.bfloat16):
    loudness = block_levels(stream_key, shape, cuts, -0.22, 0.18) if cuts else 1.0
    result = jax.random.normal(stream_key, shape, jnp.float32) * scale * loudness
    return jnp.minimum(jnp.maximum(result, -limit), limit).astype(held_as)


def setup_inputs(seed: int = 0) -> dict:
    keys = jax.random.split(jax.random.key(seed), 8)
    queries = centred(keys[0], (BATCH_SEQUENCES, SEQUENCE_LENGTH, LOCAL_HEADS * DH), 1.0, 6.0, ((0, 2), (1, 4), (2, 4)))
    keys_raw = centred(keys[1], (BATCH_SEQUENCES, SEQUENCE_LENGTH, LOCAL_HEADS * DH), 0.1, 0.625, ((0, 2), (1, 4), (2, 4)))
    values = centred(keys[2], (BATCH_SEQUENCES, SEQUENCE_LENGTH, LOCAL_HEADS * DH), 1.0, 6.0, ((0, 2), (1, 4), (2, 4)))
    gates = draw_gates(jax.random.fold_in(keys[7], 71), 0)
    lengths = jax.vmap(lambda own: ragged_sizes(own, DOCS, SEQUENCE_LENGTH, DOC_MOST, 2))(jax.random.split(keys[4], BATCH_SEQUENCES)).reshape((BATCH_SEQUENCES, DOCS)).astype(jnp.int32)
    key_gain = jnp.clip(1.0 + 0.18 * jax.random.normal(keys[5], (LOCAL_HEADS, DH), jnp.float32), 0.1, 1.9)
    cotangent = centred(keys[6], (BATCH_SEQUENCES, SEQUENCE_LENGTH, LOCAL_HEADS * DH), 1.0, 6.0, ((0, 2), (1, 4), (2, 4)))
    return dict(queries=queries, keys_raw=keys_raw, values=values, gates=gates, lengths=lengths, key_gain=key_gain, cotangent=cotangent)


PRECISE = lax.Precision.HIGHEST

def start_flags(doc_lengths, first_pos, num_rows):
    starts = jnp.cumsum(doc_lengths, dtype=jnp.int32) - doc_lengths
    positions = first_pos + jnp.arange(num_rows, dtype=jnp.int32)
    matches = jnp.any(positions[:, None] == starts[None, :], axis=1)
    return matches.astype(jnp.float32)

def make_step(key_gain, head_width):
    q_scale = head_width ** (-0.5)

    def block_step(carried, inputs):
        q_block, k_block, v_block, gate_block, flag_block = inputs
        k_bf = (k_block.astype(jnp.float32) * key_gain[None]).astype(jnp.bfloat16)
        q_float = q_block.astype(jnp.float32) * q_scale
        k_float = lax.optimization_barrier(k_bf).astype(jnp.float32)
        v_float = v_block.astype(jnp.float32)
        segment = jnp.cumsum(flag_block)
        positions = jnp.arange(flag_block.shape[0])
        same_doc = (segment[:, None] == segment[None, :]) & (positions[:, None] >= positions[None, :])
        cum_decay = jnp.cumsum(gate_block, axis=1)
        exponent = cum_decay[:, :, None] - cum_decay[:, None, :]
        decays = jnp.where(same_doc[None], jnp.exp(jnp.where(same_doc[None], exponent, 0.0)), 0.0)
        scores = jnp.einsum('thd,shd->hts', q_block, k_bf, preferred_element_type=jnp.float32)
        weights = (scores * q_scale * decays).astype(jnp.bfloat16)
        within = jnp.einsum('hts,she->the', weights, v_block, preferred_element_type=jnp.float32)
        opened = (segment == 0).astype(cum_decay.dtype)
        carry_in = jnp.exp(cum_decay) * opened[None, :]
        across = jnp.einsum('thd,hde->the', q_float, carried, precision=PRECISE) * carry_in.T[:, :, None]
        tail_mask = (segment == segment[-1]).astype(cum_decay.dtype)
        to_end = jnp.exp(cum_decay[:, -1:] - cum_decay) * tail_mask[None, :]
        written = jnp.einsum('shd,she->hde', k_float * to_end.T[:, :, None], v_float, precision=PRECISE)
        end_state = carried * carry_in[:, -1][:, None, None] + written
        return (end_state, within + across)
    return block_step

def run_blocks(q_rows, k_rows, v_rows, gate_rows, flags, key_gain, start_state):
    num_rows = q_rows.shape[0]
    head_count = key_gain.shape[0]
    head_width = key_gain.shape[1]
    num_blocks = num_rows // BLOCK

    def to_blocks(tensor):
        return tensor.reshape(num_blocks, BLOCK, head_count, head_width)
    gate_blocks = gate_rows.reshape(head_count, num_blocks, BLOCK).transpose(1, 0, 2)
    flag_blocks = flags.reshape(num_blocks, BLOCK)
    end_state, outputs = lax.scan(jax.checkpoint(make_step(key_gain, head_width)), start_state, (to_blocks(q_rows), to_blocks(k_rows), to_blocks(v_rows), gate_blocks, flag_blocks))
    return (outputs.reshape(num_rows, head_count * head_width), end_state)

def reference(queries, keys_raw, values, gates, lengths, key_gain, cotangent):
    attended, grad_q, grad_k, grad_v, grad_a = ([], [], [], [], [])
    grad_gain = jnp.zeros((LOCAL_HEADS, DH), jnp.float32)
    for batch_row in range(BATCH_SEQUENCES):
        flags = start_flags(lengths[batch_row], 0, SEQUENCE_LENGTH)
        zero_state = jnp.zeros((LOCAL_HEADS, DH, DH), jnp.float32)

        def forward(q_rows, k_rows, v_rows, gate_rows, gain_rows):
            return run_blocks(q_rows, k_rows, v_rows, gate_rows, flags, gain_rows, zero_state)[0]
        primal, pullback = jax.vjp(forward, queries[batch_row], keys_raw[batch_row], values[batch_row], gates[batch_row], key_gain)
        grads = pullback(cotangent[batch_row].astype(jnp.float32))
        attended.append(primal.astype(jnp.bfloat16))
        grad_q.append(grads[0])
        grad_k.append(grads[1])
        grad_v.append(grads[2])
        grad_a.append(grads[3])
        grad_gain = grad_gain + grads[4]
    return (jnp.stack(attended), jnp.stack(grad_q), jnp.stack(grad_k), jnp.stack(grad_v), jnp.stack(grad_a), grad_gain)
```

```python
import functools

import jax
import jax.numpy as jnp
from jax import lax
from jax.experimental import pallas as pl
from jax.experimental.pallas import tpu as pltpu
from jax.sharding import PartitionSpec as P

CHUNK = 128
PRECISE = lax.Precision.HIGHEST
F32 = jnp.float32
BF16 = jnp.bfloat16


def dot_nn(a, b, precision=None):
    return lax.dot_general(
        a, b, (((1,), (0,)), ((), ())), precision=precision, preferred_element_type=F32
    )


def dot_nt(a, b):
    return lax.dot_general(a, b, (((1,), (1,)), ((), ())), preferred_element_type=F32)


def dot_tn(a, b):
    return lax.dot_general(a, b, (((0,), (0,)), ((), ())), preferred_element_type=F32)


def iota(shape, dim):
    return lax.broadcasted_iota(jnp.int32, shape, dim)


def upper(strict):
    rows, columns = iota((CHUNK, CHUNK), 0), iota((CHUNK, CHUNK), 1)
    return ((rows < columns) if strict else (rows <= columns)).astype(F32)


def lower(strict):
    rows, columns = iota((CHUNK, CHUNK), 0), iota((CHUNK, CHUNK), 1)
    return ((rows > columns) if strict else (rows >= columns)).astype(F32)


def decay_tables(lengths_ref, ctx_ref, gates_ref, spread, cum_ref, chunk_fac_ref, shard_fac_ref):
    rows = cum_ref.shape[0]
    num_chunks = rows // 8
    tokens = num_chunks * CHUNK
    for chunk in range(num_chunks):
        part = gates_ref[0, :, chunk * CHUNK : (chunk + 1) * CHUNK]
        spread[chunk * 8 : chunk * 8 + 4, :] = part
        spread[chunk * 8 + 4 : chunk * 8 + 8, :] = part
    gates = spread[...]
    prefix = dot_nn(gates, upper(False), PRECISE)
    suffix = dot_nn(gates, lower(True), PRECISE)
    totals = jnp.broadcast_to(prefix[:, CHUNK - 1 : CHUNK], (rows, CHUNK))
    row_a, row_b = iota((rows, rows), 0), iota((rows, rows), 1)
    same = (row_a % 8) == (row_b % 8)
    before = dot_nn((same & (row_b // 8 < row_a // 8)).astype(F32), totals, PRECISE)
    after = dot_nn((same & (row_b // 8 > row_a // 8)).astype(F32), totals, PRECISE)

    first = ctx_ref[0] * tokens
    chunk_first = first + (iota((rows, CHUNK), 0) // 8) * CHUNK
    positions = chunk_first + iota((rows, CHUNK), 1)
    segment = jnp.zeros((rows, CHUNK), jnp.int32)
    segment_before = jnp.zeros((rows, CHUNK), jnp.int32)
    segment_last = jnp.zeros((rows, CHUNK), jnp.int32)
    shard_before = jnp.int32(0)
    shard_last = jnp.int32(0)
    start = jnp.int32(0)
    for doc in range(lengths_ref.shape[1]):
        segment += (positions >= start).astype(jnp.int32)
        segment_before += (chunk_first > start).astype(jnp.int32)
        segment_last += (chunk_first + (CHUNK - 1) >= start).astype(jnp.int32)
        shard_before += (first > start).astype(jnp.int32)
        shard_last += (first + (tokens - 1) >= start).astype(jnp.int32)
        start += lengths_ref[0, doc]
    is_start = iota((rows, CHUNK), 0) % 8 < 4
    cum_ref[...] = jnp.where(is_start, prefix, segment.astype(F32))
    exponent = jnp.minimum(jnp.where(is_start, prefix, suffix), 0.0)
    keep = segment == jnp.where(is_start, segment_before, segment_last)
    chunk_fac_ref[...] = jnp.where(keep, jnp.exp(exponent), 0.0)
    exponent = jnp.minimum(jnp.where(is_start, prefix + before, suffix + after), 0.0)
    keep = segment == jnp.where(is_start, shard_before, shard_last)
    shard_fac_ref[...] = jnp.where(keep, jnp.exp(exponent), 0.0)


def ends_kernel(
    head_width, lengths_ref, ctx_ref, gates_ref, q_ref, k_ref, v_ref, cot_ref,
    cum_ref, chunk_fac_ref, shard_fac_ref, end_ref, grad_ref, spread,
):
    step = pl.program_id(0)
    heads = end_ref.shape[0]
    block = q_ref.shape[1]
    chunks = block // CHUNK

    @pl.when(step == 0)
    def _():
        decay_tables(
            lengths_ref, ctx_ref, gates_ref, spread, cum_ref, chunk_fac_ref, shard_fac_ref
        )
        end_ref[...] = jnp.zeros_like(end_ref)
        grad_ref[...] = jnp.zeros_like(grad_ref)

    columns = []
    for chunk in range(chunks):
        at = pl.multiple_of((step * chunks + chunk) * 8, 8)
        columns.append(jnp.transpose(shard_fac_ref[pl.ds(at, 8), :]))
    factors = jnp.concatenate(columns, axis=0)
    for head in range(heads):
        lanes = slice(head * head_width, (head + 1) * head_width)
        k_part = (k_ref[0, :, lanes].astype(F32) * factors[:, 4 + head : 5 + head]).astype(BF16)
        q_part = (
            q_ref[0, :, lanes].astype(F32)
            * (factors[:, head : head + 1] * head_width ** (-0.5))
        ).astype(BF16)
        end_ref[head] += dot_tn(k_part, v_ref[0, :, lanes])
        grad_ref[head] += dot_tn(q_part, cot_ref[0, :, lanes])


def local_kernel(
    head_width, q_ref, k_ref, v_ref, cot_ref, gain_ref, cum_ref, fac_ref,
    out_ref, dq_ref, dk_ref, dv_ref, dgate_ref, dgain_ref, leaving, state,
):
    heads = state.shape[0]
    num_chunks = leaving.shape[0]
    scale = head_width ** (-0.5)

    def lanes_of(head):
        return slice(head * head_width, (head + 1) * head_width)

    state[...] = jnp.zeros_like(state)

    def backward(index, carry):
        chunk = num_chunks - 1 - index
        rows = pl.ds(pl.multiple_of(chunk * CHUNK, CHUNK), CHUNK)
        fac = fac_ref[pl.ds(pl.multiple_of(chunk * 8, 8), 8), :]
        columns = jnp.transpose(fac)
        for head in range(heads):
            lanes = lanes_of(head)
            leaving[chunk, head] = state[head].astype(BF16)
            q_part = (
                q_ref[0, rows, lanes].astype(F32) * (columns[:, head : head + 1] * scale)
            ).astype(BF16)
            added = dot_tn(q_part, cot_ref[0, rows, lanes])
            state[head] = state[head] * fac[head : head + 1, CHUNK - 1 : CHUNK] + added
        return carry

    lax.fori_loop(0, num_chunks, backward, 0)
    state[...] = jnp.zeros_like(state)
    dgain_ref[...] = jnp.zeros_like(dgain_ref)

    def forward(chunk, carry):
        rows = pl.ds(pl.multiple_of(chunk * CHUNK, CHUNK), CHUNK)
        fac = fac_ref[pl.ds(pl.multiple_of(chunk * 8, 8), 8), :]
        cum = cum_ref[pl.ds(pl.multiple_of(chunk * 8, 8), 8), :]
        fac_columns = jnp.transpose(fac)
        cum_columns = jnp.transpose(cum)
        same = (cum_columns[:, 4:5] == cum[4:5, :]) & (
            iota((CHUNK, CHUNK), 0) >= iota((CHUNK, CHUNK), 1)
        )
        lane = iota((CHUNK, 8), 1)
        sums = jnp.zeros((CHUNK, 8), F32)
        column_sums, constants = [], []
        for head in range(heads):
            lanes = lanes_of(head)
            q, v, cot = q_ref[0, rows, lanes], v_ref[0, rows, lanes], cot_ref[0, rows, lanes]
            k_raw = k_ref[0, rows, lanes].astype(F32)
            gain = gain_ref[head : head + 1, :]
            k = (k_raw * gain).astype(BF16)
            from_start = fac_columns[:, head : head + 1] * scale
            to_end = fac_columns[:, 4 + head : 5 + head]
            exponent = jnp.minimum(cum_columns[:, head : head + 1] - cum[head : head + 1, :], 0.0)
            decays = jnp.where(same, jnp.exp(exponent) * scale, 0.0)
            grad_weights = dot_nt(cot, v)
            weights = dot_nt(q, k) * decays
            paired = weights * grad_weights
            weights = weights.astype(BF16)
            grad_scores = (grad_weights * decays).astype(BF16)
            held = state[head]
            entering = held.astype(BF16)
            later = leaving[chunk, head]
            across = dot_nn(q, entering) * from_start
            out_ref[0, rows, lanes] = (dot_nn(weights, v) + across).astype(BF16)
            dq_ref[0, rows, lanes] = (
                dot_nn(grad_scores, k) + dot_nt(cot, entering) * from_start
            ).astype(BF16)
            written = dot_nn(k, later) * to_end
            dv_ref[0, rows, lanes] = (dot_tn(weights, cot) + written).astype(BF16)
            grad_k = dot_tn(grad_scores, q) + dot_nt(v, later) * to_end
            dk_ref[0, rows, lanes] = (grad_k * gain).astype(BF16)
            dgain_ref[head : head + 1, :] += jnp.sum(grad_k * k_raw, axis=0, keepdims=True)
            queried = jnp.sum(across * cot.astype(F32) + paired, axis=1, keepdims=True)
            kept = jnp.sum(written * v.astype(F32), axis=1, keepdims=True)
            sums = jnp.where(lane == head, queried, jnp.where(lane == 4 + head, kept, sums))
            column_sums.append(jnp.sum(paired, axis=0, keepdims=True))
            decay = fac[head : head + 1, CHUNK - 1 : CHUNK]
            constants.append(
                jnp.sum(held * later.astype(F32), axis=(0, 1), keepdims=True) * decay
            )
            state[head] = held * decay + dot_tn((k.astype(F32) * to_end).astype(BF16), v)
        sum_rows = jnp.transpose(sums)
        by_query = sum_rows[0:4] - jnp.concatenate(column_sums, axis=0)
        dgate_ref[0, :, rows] = (
            dot_nn(by_query, lower(False), PRECISE)
            + dot_nn(sum_rows[4:8], upper(True), PRECISE)
            + jnp.concatenate(constants, axis=0)
        )
        return carry

    lax.fori_loop(0, num_chunks, forward, 0)


def merge_kernel(
    head_width, q_ref, k_ref, v_ref, cot_ref, gain_ref, fac_ref, state_ref, later_ref,
    out_in, dq_in, dk_in, dv_in, dgate_in,
    out_ref, dq_ref, dk_ref, dv_ref, dgate_ref, entering, leaving, sums_scr,
):
    step = pl.program_id(0)
    heads = entering.shape[0]
    block = q_ref.shape[1]
    chunks = block // CHUNK
    rows_all = fac_ref.shape[0]
    num_chunks = rows_all // 8
    scale = head_width ** (-0.5)

    @pl.when(step == 0)
    def _():
        gain_columns = jnp.transpose(jnp.concatenate([gain_ref[...], gain_ref[...]], axis=0))
        for head in range(heads):
            entering[head] = (state_ref[head] * scale).astype(BF16)
            leaving[head] = (later_ref[head] * gain_columns[:, head : head + 1]).astype(BF16)

    for chunk in range(chunks):
        at = pl.multiple_of((step * chunks + chunk) * 8, 8)
        columns = jnp.transpose(fac_ref[pl.ds(at, 8), :])
        rows = slice(chunk * CHUNK, (chunk + 1) * CHUNK)
        lane = iota((CHUNK, 8), 1)
        sums = jnp.zeros((CHUNK, 8), F32)
        for head in range(heads):
            lanes = slice(head * head_width, (head + 1) * head_width)
            q, k = q_ref[0, rows, lanes], k_ref[0, rows, lanes]
            v, cot = v_ref[0, rows, lanes], cot_ref[0, rows, lanes]
            from_start, to_end = columns[:, head : head + 1], columns[:, 4 + head : 5 + head]
            across = dot_nn(q, entering[head]) * from_start
            out_ref[0, rows, lanes] = (out_in[0, rows, lanes].astype(F32) + across).astype(BF16)
            dq_ref[0, rows, lanes] = (
                dq_in[0, rows, lanes].astype(F32) + dot_nt(cot, entering[head]) * from_start
            ).astype(BF16)
            written = dot_nn(k, leaving[head]) * to_end
            dv_ref[0, rows, lanes] = (dv_in[0, rows, lanes].astype(F32) + written).astype(BF16)
            dk_ref[0, rows, lanes] = (
                dk_in[0, rows, lanes].astype(F32) + dot_nt(v, leaving[head]) * to_end
            ).astype(BF16)
            queried = jnp.sum(across * cot.astype(F32), axis=1, keepdims=True)
            kept = jnp.sum(written * v.astype(F32), axis=1, keepdims=True)
            sums = jnp.where(lane == head, queried, jnp.where(lane == 4 + head, kept, sums))
        sums_scr[pl.ds(at, 8), :] = jnp.transpose(sums)

    @pl.when(step == pl.num_programs(0) - 1)
    def _():
        sums = sums_scr[...]
        by_query = dot_nn(sums, lower(False), PRECISE)
        by_key = dot_nn(sums, upper(True), PRECISE)
        last = fac_ref[(num_chunks - 1) * 8 : num_chunks * 8, CHUNK - 1 : CHUNK]
        constants = []
        for head in range(heads):
            product = jnp.sum(state_ref[head] * later_ref[head], axis=(0, 1), keepdims=True)
            constants.append(product * last[head : head + 1])
        base = jnp.concatenate(constants, axis=0)
        for chunk in range(num_chunks):
            lanes = slice(chunk * CHUNK, (chunk + 1) * CHUNK)
            dgate_ref[0, :, lanes] = (
                dgate_in[0, :, lanes]
                + by_query[chunk * 8 : chunk * 8 + 4]
                + by_key[chunk * 8 + 4 : chunk * 8 + 8]
                + base
            )
            if chunk < num_chunks - 1:
                base = base + jnp.sum(
                    sums[chunk * 8 + 4 : chunk * 8 + 8], axis=1, keepdims=True
                )
        tail = jnp.zeros((heads, 1), F32)
        for chunk in range(num_chunks - 2, -1, -1):
            lanes = slice(chunk * CHUNK, (chunk + 1) * CHUNK)
            tail = tail + jnp.sum(
                sums[(chunk + 1) * 8 : (chunk + 1) * 8 + 4], axis=1, keepdims=True
            )
            dgate_ref[0, :, lanes] += tail


def shards(queries, keys_raw, values, gates, lengths, key_gain, cotangent):
    tokens = queries.shape[1]
    width = queries.shape[2]
    heads, head_width = key_gain.shape
    num_chunks = tokens // CHUNK
    rows = num_chunks * 8
    block = min(256, tokens)
    steps = tokens // block
    ctx = lax.axis_index("ctx")
    count = lax.axis_size("ctx")
    streams = (queries, keys_raw, values, cotangent)
    stream_spec = pl.BlockSpec((1, block, width), lambda i: (0, i, 0))
    wide = jax.ShapeDtypeStruct(queries.shape, BF16)

    def whole(array):
        zeros = (0,) * len(array.shape)
        return pl.BlockSpec(array.shape, lambda *_: zeros)

    smem = pl.BlockSpec(memory_space=pltpu.SMEM)
    vmem = pl.BlockSpec(memory_space=pltpu.VMEM)
    table = jax.ShapeDtypeStruct((rows, CHUNK), F32)
    states = jax.ShapeDtypeStruct((heads, head_width, head_width), F32)
    product = 2 * tokens * width * head_width

    cum, chunk_fac, shard_fac, end_raw, local_grad = pl.pallas_call(
        functools.partial(ends_kernel, head_width),
        grid=(steps,),
        in_specs=[smem, smem, whole(gates)] + [stream_spec] * 4,
        out_specs=[whole(table)] * 3 + [whole(states)] * 2,
        out_shape=[table] * 3 + [states] * 2,
        scratch_shapes=[pltpu.VMEM((rows, CHUNK), F32)],
        compiler_params=pltpu.CompilerParams(vmem_limit_bytes=32 << 20),
        cost_estimate=pl.CostEstimate(
            flops=2 * product, bytes_accessed=8 * tokens * width, transcendentals=0
        ),
        name="shard_ends",
    )(lengths, jnp.reshape(ctx, (1,)).astype(jnp.int32), gates, *streams)

    out, dq, dk, dv, dgate, dgain = pl.pallas_call(
        functools.partial(local_kernel, head_width),
        in_specs=[vmem] * 7,
        out_specs=[vmem] * 6,
        out_shape=[wide] * 4
        + [
            jax.ShapeDtypeStruct(gates.shape, F32),
            jax.ShapeDtypeStruct((heads, head_width), F32),
        ],
        scratch_shapes=[
            pltpu.VMEM((num_chunks, heads, head_width, head_width), BF16),
            pltpu.VMEM((heads, head_width, head_width), F32),
        ],
        compiler_params=pltpu.CompilerParams(vmem_limit_bytes=32 << 20),
        cost_estimate=pl.CostEstimate(
            flops=12 * product, bytes_accessed=16 * tokens * width, transcendentals=0
        ),
        name="local_part",
    )(*streams, key_gain, cum, chunk_fac)

    local_end = end_raw * key_gain[:, :, None]
    decay = shard_fac[rows - 8 : rows - 8 + heads, CHUNK - 1][:, None, None]
    state_in = jnp.zeros_like(local_end)
    grad_in = jnp.zeros_like(local_end)
    arrived = None
    for hop in range(count - 1):
        sent = jnp.where(ctx == hop, local_end, local_grad)
        if arrived is not None:
            sent = sent + decay * arrived
        arrived = lax.ppermute(
            sent, "ctx", [(hop, hop + 1), (count - 1 - hop, count - 2 - hop)]
        )
        state_in = jnp.where(ctx == hop + 1, arrived, state_in)
        grad_in = jnp.where(ctx == count - 2 - hop, arrived, grad_in)

    gain_term = dgain + jnp.sum(grad_in * end_raw, axis=2)
    half = head_width // lax.axis_size("dp")
    dp = lax.axis_index("dp")
    away = jnp.where(dp == 0, gain_term[:, half:], gain_term[:, :half])
    kept = jnp.where(dp == 0, gain_term[:, :half], gain_term[:, half:])
    grad_gain = kept + lax.ppermute(away, "dp", [(0, 1), (1, 0)])
    reach = 1
    while reach < count:
        grad_gain = grad_gain + lax.ppermute(
            grad_gain, "ctx", [(i, i ^ reach) for i in range(count)]
        )
        reach *= 2

    merged = pl.pallas_call(
        functools.partial(merge_kernel, head_width),
        grid=(steps,),
        in_specs=[stream_spec] * 4
        + [whole(key_gain), whole(table), whole(states), whole(states)]
        + [stream_spec] * 4
        + [whole(gates)],
        out_specs=[stream_spec] * 4 + [whole(gates)],
        out_shape=[wide] * 4 + [jax.ShapeDtypeStruct(gates.shape, F32)],
        scratch_shapes=[
            pltpu.VMEM((heads, head_width, head_width), BF16),
            pltpu.VMEM((heads, head_width, head_width), BF16),
            pltpu.VMEM((rows, CHUNK), F32),
        ],
        compiler_params=pltpu.CompilerParams(vmem_limit_bytes=32 << 20),
        cost_estimate=pl.CostEstimate(
            flops=4 * product, bytes_accessed=24 * tokens * width, transcendentals=0
        ),
        name="merge_incoming",
    )(*streams, key_gain, shard_fac, state_in, grad_in, out, dq, dk, dv, dgate)
    return (*merged, grad_gain)


def solution(mesh):
    wide = P("dp", "ctx", "head")
    narrow = P("dp", "head", "ctx")
    return jax.shard_map(
        shards,
        mesh=mesh,
        in_specs=(wide, wide, wide, narrow, P("dp", None), P("head", None), wide),
        out_specs=(wide, wide, wide, wide, narrow, P("head", "dp")),
        check_vma=False,
    )
```

```python
import functools
import math

import jax
import jax.numpy as jnp
from jax import lax
from jax.experimental import pallas as pl
from jax.experimental.pallas import tpu as pltpu
from jax.sharding import PartitionSpec as P

CHUNK = 128
PARTS = 2
PRECISE = lax.Precision.HIGHEST
F32 = jnp.float32
BF16 = jnp.bfloat16
LOG2E = math.log2(math.e)


def dot_nn(a, b, precision=None):
    return lax.dot_general(
        a, b, (((1,), (0,)), ((), ())), precision=precision, preferred_element_type=F32
    )


def dot_nt(a, b):
    return lax.dot_general(a, b, (((1,), (1,)), ((), ())), preferred_element_type=F32)


def dot_tn(a, b):
    return lax.dot_general(a, b, (((0,), (0,)), ((), ())), preferred_element_type=F32)


def iota(shape, dim):
    return lax.broadcasted_iota(jnp.int32, shape, dim)


def total_of(array):
    return jnp.sum(jnp.sum(array, axis=0, keepdims=True), axis=1, keepdims=True)


def later_sums(column):
    kept = iota((CHUNK, CHUNK), 0) >= iota((CHUNK, CHUNK), 1)
    return jnp.sum(jnp.where(kept, column, 0.0), axis=0, keepdims=True)


def decay_tables(lengths_ref, ctx_ref, gates_ref, spread, cum_ref, chunk_fac_ref, shard_fac_ref):
    rows = cum_ref.shape[0]
    num_chunks = rows // 8
    tokens = num_chunks * CHUNK
    for chunk in range(num_chunks):
        part = gates_ref[0, :, chunk * CHUNK : (chunk + 1) * CHUNK]
        spread[chunk * 8 : chunk * 8 + 4, :] = part
        spread[chunk * 8 + 4 : chunk * 8 + 8, :] = part
    gates = spread[...] * LOG2E
    lane_a, lane_b = iota((CHUNK, CHUNK), 0), iota((CHUNK, CHUNK), 1)
    prefix = dot_nn(gates, (lane_a <= lane_b).astype(F32), PRECISE)
    suffix = dot_nn(gates, (lane_a > lane_b).astype(F32), PRECISE)
    totals = jnp.broadcast_to(prefix[:, CHUNK - 1 : CHUNK], (rows, CHUNK))
    row_a, row_b = iota((rows, rows), 0), iota((rows, rows), 1)
    same = (row_a % 8) == (row_b % 8)
    outside = ((row_a % 8 < 4) & (row_b // 8 < row_a // 8)) | (
        (row_a % 8 >= 4) & (row_b // 8 > row_a // 8)
    )
    others = dot_nn((same & outside).astype(F32), totals, PRECISE)

    first = ctx_ref[0] * tokens
    chunk_first = first + (iota((rows, CHUNK), 0) // 8) * CHUNK
    positions = chunk_first + iota((rows, CHUNK), 1)
    from_start = iota((rows, CHUNK), 0) % 8 < 4
    chunk_anchor = jnp.where(from_start, chunk_first - 1, chunk_first + (CHUNK - 1))
    segment = jnp.zeros((rows, CHUNK), F32)
    chunk_segment = jnp.zeros((rows, CHUNK), F32)
    shard_before = jnp.float32(0)
    shard_last = jnp.float32(0)
    start = jnp.int32(0)
    for doc in range(lengths_ref.shape[1]):
        segment += jnp.where(positions >= start, 1.0, 0.0)
        chunk_segment += jnp.where(chunk_anchor >= start, 1.0, 0.0)
        shard_before += jnp.where(first > start, 1.0, 0.0)
        shard_last += jnp.where(first + (tokens - 1) >= start, 1.0, 0.0)
        start += lengths_ref[0, doc]
    cum_ref[...] = jnp.where(from_start, prefix, segment)
    exponent = jnp.where(from_start, prefix, suffix)
    chunk_fac_ref[...] = jnp.where(
        segment == chunk_segment, jnp.exp2(jnp.minimum(exponent, 0.0)), 0.0
    )
    keep = segment == jnp.where(from_start, shard_before, shard_last)
    shard_fac_ref[...] = jnp.where(keep, jnp.exp2(jnp.minimum(exponent + others, 0.0)), 0.0)


def ends_kernel(head_width, part, half_ctx, *refs):
    if part == 0:
        (lengths_ref, ctx_ref, gates_ref, q_ref, k_ref, v_ref, cot_ref,
         near_ref, far_ref, decay_ref, cum_ref, chunk_fac_ref, shard_fac_ref,
         end_scr, grad_scr, spread) = refs
    else:
        (ctx_ref, shard_fac_ref, q_ref, k_ref, v_ref, cot_ref,
         near_ref, far_ref, decay_ref, end_scr, grad_scr) = refs
    step = pl.program_id(0)
    heads = near_ref.shape[0]
    block = q_ref.shape[1]
    chunks = block // CHUNK
    rows = shard_fac_ref.shape[0]

    @pl.when(step == 0)
    def _():
        if part == 0:
            decay_tables(
                lengths_ref, ctx_ref, gates_ref, spread, cum_ref, chunk_fac_ref, shard_fac_ref
            )
        for head in range(heads):
            row = rows - 8 + part * heads + head
            decay_ref[head] = jnp.broadcast_to(
                shard_fac_ref[row : row + 1, CHUNK - 1 : CHUNK], (1, head_width)
            )
        end_scr[...] = jnp.zeros_like(end_scr)
        grad_scr[...] = jnp.zeros_like(grad_scr)

    columns = []
    for chunk in range(chunks):
        at = pl.multiple_of((step * chunks + chunk) * 8, 8)
        columns.append(jnp.transpose(shard_fac_ref[pl.ds(at, 8), :]))
    factors = jnp.concatenate(columns, axis=0)
    for head in range(heads):
        lanes = slice(head * head_width, (head + 1) * head_width)
        row = part * heads + head
        k_part = (k_ref[0, :, lanes].astype(F32) * factors[:, 4 + row : 5 + row]).astype(BF16)
        q_part = (
            q_ref[0, :, lanes].astype(F32) * (factors[:, row : row + 1] * head_width ** (-0.5))
        ).astype(BF16)
        end_scr[head] += dot_tn(k_part, v_ref[0, :, lanes])
        grad_scr[head] += dot_tn(q_part, cot_ref[0, :, lanes])

    @pl.when(step == pl.num_programs(0) - 1)
    def _():
        low = ctx_ref[0] < half_ctx
        end, grad = end_scr[...], grad_scr[...]
        near_ref[...] = jnp.where(low, end, grad)
        far_ref[...] = jnp.where(low, grad, end)


def local_kernel(
    head_width, part, q_ref, k_ref, v_ref, cot_ref, gain_ref, cum_ref, fac_ref,
    out_ref, dq_ref, dk_ref, dv_ref, dgate_ref, dgain_ref, leaving, state,
):
    heads = state.shape[0]
    num_chunks = leaving.shape[0]
    scale = head_width ** (-0.5)
    unroll = 2 if num_chunks % 2 == 0 else 1

    def lanes_of(head):
        return slice((part * heads + head) * head_width, (part * heads + head + 1) * head_width)

    def own_lanes(head):
        return slice(head * head_width, (head + 1) * head_width)

    def backward(chunk):
        rows = pl.ds(pl.multiple_of(chunk * CHUNK, CHUNK), CHUNK)
        fac = fac_ref[pl.ds(pl.multiple_of(chunk * 8, 8), 8), :]
        columns = jnp.transpose(fac) * scale
        for head in range(heads):
            row = part * heads + head
            lanes = lanes_of(head)
            held = state[head]
            leaving[chunk, head] = held.astype(BF16)
            q_part = (q_ref[0, rows, lanes].astype(F32) * columns[:, row : row + 1]).astype(BF16)
            added = dot_tn(q_part, cot_ref[0, rows, lanes])
            state[head] = held * fac[row : row + 1, CHUNK - 1 : CHUNK] + added

    def forward(chunk):
        rows = pl.ds(pl.multiple_of(chunk * CHUNK, CHUNK), CHUNK)
        fac = fac_ref[pl.ds(pl.multiple_of(chunk * 8, 8), 8), :]
        cum = cum_ref[pl.ds(pl.multiple_of(chunk * 8, 8), 8), :]
        fac_columns = jnp.transpose(fac)
        cum_columns = jnp.transpose(cum)
        same = (cum_columns[:, 4:5] == cum[4:5, :]) & (
            iota((CHUNK, CHUNK), 0) >= iota((CHUNK, CHUNK), 1)
        )
        limit = jnp.where(same, math.log2(scale), -1e30)
        cum_columns = cum_columns + math.log2(scale)
        for head in range(heads):
            row = part * heads + head
            lanes, own = lanes_of(head), own_lanes(head)
            q, v, cot = q_ref[0, rows, lanes], v_ref[0, rows, lanes], cot_ref[0, rows, lanes]
            k_raw = k_ref[0, rows, lanes].astype(F32)
            gain = gain_ref[row : row + 1, :]
            k_wide = k_raw * gain
            k = k_wide.astype(BF16)
            from_start = fac_columns[:, row : row + 1] * scale
            to_end = fac_columns[:, 4 + row : 5 + row]
            decays = jnp.exp2(
                jnp.minimum(cum_columns[:, row : row + 1] - cum[row : row + 1, :], limit)
            )
            held = state[head]
            entering = held.astype(BF16)
            later = leaving[chunk, head]
            by_cot = dot_nt(cot, jnp.concatenate([v, entering], axis=0))
            weights = (dot_nt(q, k) * decays).astype(BF16)
            grad_scores = (by_cot[:, :CHUNK] * decays).astype(BF16)
            q_decayed = (q.astype(F32) * from_start).astype(BF16)
            k_decayed = (k_wide * to_end).astype(BF16)
            out = dot_nn(
                jnp.concatenate([weights, q_decayed], axis=1),
                jnp.concatenate([v, entering], axis=0),
            )
            out_ref[0, rows, own] = out.astype(BF16)
            dq_ref[0, rows, own] = (
                dot_nn(grad_scores, k) + by_cot[:, CHUNK:] * from_start
            ).astype(BF16)
            dv = dot_nn(
                jnp.concatenate([jnp.transpose(weights), k_decayed], axis=1),
                jnp.concatenate([cot, later], axis=0),
            )
            dv_ref[0, rows, own] = dv.astype(BF16)
            grad_k = dot_tn(grad_scores, q) + dot_nt(v, later) * to_end
            dk_ref[0, rows, own] = (grad_k * gain).astype(BF16)
            dgain_ref[head : head + 1, :] += jnp.sum(grad_k * k_raw, axis=0, keepdims=True)
            new_state = held * fac[row : row + 1, CHUNK - 1 : CHUNK] + dot_tn(k_decayed, v)
            state[head] = new_state
            balance = jnp.sum(
                out * cot.astype(F32) - dv * v.astype(F32), axis=1, keepdims=True
            )
            dgate_ref[0, head : head + 1, rows] = later_sums(balance) + total_of(
                new_state * later.astype(F32)
            )

    state[...] = jnp.zeros_like(state)

    def backward_group(index, carry):
        for offset in range(unroll):
            backward(num_chunks - 1 - (index * unroll + offset))
        return carry

    lax.fori_loop(0, num_chunks // unroll, backward_group, 0)
    state[...] = jnp.zeros_like(state)
    dgain_ref[...] = jnp.zeros_like(dgain_ref)

    def forward_group(index, carry):
        for offset in range(unroll):
            forward(index * unroll + offset)
        return carry

    lax.fori_loop(0, num_chunks // unroll, forward_group, 0)


def merge_kernel(head_width, part, half_ctx, *refs):
    (ctx_ref, q_ref, k_ref, v_ref, cot_ref, gain_ref, fac_ref, first_ref, second_ref, last_ref,
     out_in, dq_in, dk_in, dv_in, dgate_in) = refs[:15]
    refs = refs[15:]
    if part > 0:
        before_ref, refs = refs[0], refs[5:]
    out_ref, dq_ref, dk_ref, dv_ref, dgate_ref, entering, leaving, sums_scr, tot_scr = refs
    step = pl.program_id(0)
    heads = first_ref.shape[0]
    block = q_ref.shape[1]
    chunks = block // CHUNK
    num_chunks = fac_ref.shape[0] // 8
    scale = head_width ** (-0.5)

    def arrived(head):
        low = ctx_ref[0] < half_ctx
        first, second = first_ref[head], second_ref[head] + last_ref[head]
        return jnp.where(low, first, second), jnp.where(low, second, first)

    @pl.when(step == 0)
    def _():
        gain_columns = jnp.transpose(jnp.concatenate([gain_ref[...], gain_ref[...]], axis=0))
        entering[...] = jnp.zeros_like(entering)
        leaving[...] = jnp.zeros_like(leaving)
        for head in range(heads):
            row = part * heads + head
            own = slice(head * head_width, (head + 1) * head_width)
            gain = gain_columns[:, row : row + 1]
            state, later = arrived(head)
            entering[own, own] = (state * (gain * scale)).astype(BF16)
            leaving[own, own] = (later * gain).astype(BF16)

    for chunk in range(chunks):
        number = step * chunks + chunk
        columns = jnp.transpose(fac_ref[pl.ds(pl.multiple_of(number * 8, 8), 8), :])
        rows = slice(chunk * CHUNK, (chunk + 1) * CHUNK)
        across_all = dot_nn(q_ref[0, rows, :], entering[...])
        dq_all = dot_nt(cot_ref[0, rows, :], entering[...])
        written_all = dot_nn(k_ref[0, rows, :], leaving[...])
        dk_all = dot_nt(v_ref[0, rows, :], leaving[...])
        for head in range(heads):
            row = part * heads + head
            lanes = slice(head * head_width, (head + 1) * head_width)
            from_start, to_end = columns[:, row : row + 1], columns[:, 4 + row : 5 + row]
            across = across_all[:, lanes] * from_start
            written = written_all[:, lanes] * to_end
            out_ref[0, rows, lanes] = (out_in[0, rows, lanes].astype(F32) + across).astype(BF16)
            dq_ref[0, rows, lanes] = (
                dq_in[0, rows, lanes].astype(F32) + dq_all[:, lanes] * from_start
            ).astype(BF16)
            dv_ref[0, rows, lanes] = (dv_in[0, rows, lanes].astype(F32) + written).astype(BF16)
            dk_ref[0, rows, lanes] = (
                dk_in[0, rows, lanes].astype(F32) + dk_all[:, lanes] * to_end
            ).astype(BF16)
            kept = written * v_ref[0, rows, lanes].astype(F32)
            balance = jnp.sum(
                across * cot_ref[0, rows, lanes].astype(F32) - kept, axis=1, keepdims=True
            )
            sums_scr[number, head : head + 1, :] = later_sums(balance)
            tot_scr[number, head : head + 1, :] = jnp.sum(kept, axis=0, keepdims=True)

    @pl.when(step == pl.num_programs(0) - 1)
    def _():
        last = fac_ref[(num_chunks - 1) * 8 : num_chunks * 8, CHUNK - 1 : CHUNK]
        kept = tot_scr[0]
        for chunk in range(1, num_chunks):
            kept = kept + tot_scr[chunk]
        base = jnp.sum(kept, axis=1, keepdims=True)
        constants = []
        for head in range(heads):
            row = part * heads + head
            state, later = arrived(head)
            gain_columns = jnp.transpose(
                jnp.concatenate([gain_ref[...], gain_ref[...]], axis=0)
            )
            product = total_of(state * later * gain_columns[:, row : row + 1])
            constants.append(product * last[row : row + 1])
        base = base[:heads] + jnp.concatenate(constants, axis=0)
        if part > 0:
            dgate_ref[0, : part * heads, :] = before_ref[0]
        own = slice(part * heads, (part + 1) * heads)
        for chunk in range(num_chunks - 1, -1, -1):
            lanes = slice(chunk * CHUNK, (chunk + 1) * CHUNK)
            sums = sums_scr[chunk, :heads, :]
            dgate_ref[0, own, lanes] = dgate_in[0, :, lanes] + sums + base
            base = base + sums[:, 0:1]


def shards(queries, keys_raw, values, gates, lengths, key_gain, cotangent):
    tokens, width = queries.shape[1:]
    all_heads, head_width = key_gain.shape
    heads = all_heads // PARTS
    part_width = width // PARTS
    num_chunks = tokens // CHUNK
    rows = num_chunks * 8
    block = min(512, tokens)
    steps = tokens // block
    ctx = lax.axis_index("ctx")
    count = lax.axis_size("ctx")
    middle = count // 2 - 1
    streams = (queries, keys_raw, values, cotangent)
    ctx_scalar = jnp.reshape(ctx, (1,)).astype(jnp.int32)

    def stream_spec(part):
        return pl.BlockSpec((1, block, part_width), lambda i: (0, i, part))

    def whole(array):
        zeros = (0,) * len(array.shape)
        return pl.BlockSpec(array.shape, lambda *_: zeros)

    def shape_of(*shape, dtype=F32):
        return jax.ShapeDtypeStruct(shape, dtype)

    smem = pl.BlockSpec(memory_space=pltpu.SMEM)
    vmem = pl.BlockSpec(memory_space=pltpu.VMEM)
    table = shape_of(rows, CHUNK)
    states = shape_of(heads, head_width, head_width)
    decays = shape_of(heads, 1, head_width)
    part_gates = shape_of(1, heads, tokens)
    product = 2 * tokens * part_width * head_width

    def ends(part, *tables):
        specs = [smem, smem, whole(gates)] if part == 0 else [smem, whole(table)]
        outs = [states, states, decays] + ([table] * 3 if part == 0 else [])
        scratch = [pltpu.VMEM(states.shape, F32)] * 2
        if part == 0:
            scratch.append(pltpu.VMEM((rows, CHUNK), F32))
        return pl.pallas_call(
            functools.partial(ends_kernel, head_width, part, count // 2),
            grid=(steps,),
            in_specs=specs + [stream_spec(part)] * 4,
            out_specs=[whole(out) for out in outs],
            out_shape=outs,
            scratch_shapes=scratch,
            compiler_params=pltpu.CompilerParams(vmem_limit_bytes=56 << 20),
            cost_estimate=pl.CostEstimate(
                flops=2 * product, bytes_accessed=8 * tokens * part_width, transcendentals=0
            ),
            name=f"shard_ends_{part}",
        )(*tables, *streams)

    def local(part, arrays, gain, cum, fac):
        wide = shape_of(1, tokens, part_width, dtype=BF16)
        return pl.pallas_call(
            functools.partial(local_kernel, head_width, part),
            in_specs=[vmem] * 7,
            out_specs=[vmem] * 6,
            out_shape=[wide] * 4 + [part_gates, shape_of(heads, head_width)],
            scratch_shapes=[
                pltpu.VMEM((num_chunks, heads, head_width, head_width), BF16),
                pltpu.VMEM((heads, head_width, head_width), F32),
            ],
            compiler_params=pltpu.CompilerParams(vmem_limit_bytes=24 << 20),
            cost_estimate=pl.CostEstimate(
                flops=12 * product, bytes_accessed=16 * tokens * part_width, transcendentals=0
            ),
            name=f"local_{part}",
        )(*arrays, gain, cum, fac)

    def merge(part, arrivals, locals_, done):
        own_spec = pl.BlockSpec((1, block, part_width), lambda i: (0, i, 0))
        full_gates = shape_of(1, (part + 1) * heads, tokens)
        extra, extra_specs, aliases = [], [], {}
        if part > 0:
            extra = [done[4]] + list(done[:4])
            extra_specs = [whole(done[4])] + [pl.BlockSpec(memory_space=pl.ANY)] * 4
            aliases = {16 + i: i for i in range(4)}
        return pl.pallas_call(
            functools.partial(merge_kernel, head_width, part, count // 2),
            grid=(steps,),
            in_specs=[smem]
            + [stream_spec(part)] * 4
            + [whole(key_gain), whole(table)]
            + [whole(states)] * 3
            + [own_spec] * 4
            + [whole(part_gates)]
            + extra_specs,
            out_specs=[stream_spec(part)] * 4 + [whole(full_gates)],
            out_shape=[shape_of(1, tokens, width, dtype=BF16)] * 4 + [full_gates],
            scratch_shapes=[
                pltpu.VMEM((part_width, part_width), BF16),
                pltpu.VMEM((part_width, part_width), BF16),
                pltpu.VMEM((num_chunks, 8, CHUNK), F32),
                pltpu.VMEM((num_chunks, 8, CHUNK), F32),
            ],
            input_output_aliases=aliases,
            compiler_params=pltpu.CompilerParams(vmem_limit_bytes=24 << 20),
            cost_estimate=pl.CostEstimate(
                flops=4 * product, bytes_accessed=24 * tokens * part_width, transcendentals=0
            ),
            name=f"merge_{part}",
        )(ctx_scalar, *streams, key_gain, shard_fac, *arrivals, *locals_, *extra)

    near, far, decay = [None] * PARTS, [None] * PARTS, [None] * PARTS
    near[0], far[0], decay[0], cum, chunk_fac, shard_fac = ends(0, lengths, ctx_scalar, gates)
    sent = [[] for _ in range(PARTS)]
    arrived = [[] for _ in range(PARTS)]
    local_parts = [None] * PARTS

    def send(part, hop):
        payload = near[part] if hop <= middle else far[part]
        if hop > 0:
            payload = payload + decay[part] * arrived[part][-1]
        sent[part].append(payload)
        arrived[part].append(
            lax.ppermute(
                payload, "ctx", [(hop, hop + 1), (count - 1 - hop, count - 2 - hop)]
            )
        )

    for part in range(PARTS):
        if part > 0:
            near[part], far[part], decay[part] = ends(part, ctx_scalar, shard_fac)
        send(part, 0)
    for hop in range(count - 1):
        if hop < PARTS:
            local_cum = cum
            if hop > 0:
                local_cum, _ = lax.optimization_barrier((cum, arrived[0][hop - 1]))
            local_parts[hop] = list(local(hop, streams, key_gain, local_cum, chunk_fac))
            if hop + 1 < count - 1:
                local_parts[hop][5], arrived[0][-1] = lax.optimization_barrier(
                    (local_parts[hop][5], arrived[0][-1])
                )
        if hop + 1 < count - 1:
            for part in range(PARTS):
                send(part, hop + 1)

    terms = []
    for part in range(PARTS):
        crossed = jnp.sum(sent[part][middle] * arrived[part][middle], axis=2)
        term = local_parts[part][5] + jnp.where(ctx == middle, crossed, 0.0)
        if middle > 0:
            term = term + jnp.sum(sum(arrived[part][:middle]) * far[part], axis=2)
        terms.append(term)
    gain_term = jnp.concatenate(terms, axis=0)
    half = head_width // lax.axis_size("dp")
    dp = lax.axis_index("dp")
    away = jnp.where(dp == 0, gain_term[:, half:], gain_term[:, :half])
    kept = jnp.where(dp == 0, gain_term[:, :half], gain_term[:, half:])
    grad_gain = kept + lax.ppermute(away, "dp", [(0, 1), (1, 0)])
    reach = 1
    while reach < count:
        grad_gain = grad_gain + lax.ppermute(
            grad_gain, "ctx", [(i, i ^ reach) for i in range(count)]
        )
        reach *= 2

    done = None
    for part in range(PARTS):
        zeros = jnp.zeros(states.shape, F32)
        first = sum(arrived[part][:middle], zeros) if middle != 1 else arrived[part][0]
        second = sum(arrived[part][middle:-1], zeros) if middle != 1 else arrived[part][1]
        done = merge(part, (first, second, arrived[part][-1]), local_parts[part][:5], done)
    return (*done, grad_gain)


def solution(mesh):
    wide = P("dp", "ctx", "head")
    narrow = P("dp", "head", "ctx")
    return jax.shard_map(
        shards,
        mesh=mesh,
        in_specs=(wide, wide, wide, narrow, P("dp", None), P("head", None), wide),
        out_specs=(wide, wide, wide, wide, narrow, P("head", "dp")),
        check_vma=False,
    )
```

```python
import functools
import math

import jax
import jax.numpy as jnp
from jax import lax
from jax.experimental import pallas as pl
from jax.experimental.pallas import tpu as pltpu
from jax.sharding import PartitionSpec as P

CHUNK = 128
PARTS = 2
UNROLL = 4
PRECISE = lax.Precision.HIGHEST
F32 = jnp.float32
BF16 = jnp.bfloat16
LOG2E = math.log2(math.e)


def dot_nn(a, b, precision=None):
    return lax.dot_general(
        a, b, (((1,), (0,)), ((), ())), precision=precision, preferred_element_type=F32
    )


def dot_nt(a, b):
    return lax.dot_general(a, b, (((1,), (1,)), ((), ())), preferred_element_type=F32)


def dot_tn(a, b):
    return lax.dot_general(a, b, (((0,), (0,)), ((), ())), preferred_element_type=F32)


def iota(shape, dim):
    return lax.broadcasted_iota(jnp.int32, shape, dim)


def total_of(array):
    return jnp.sum(jnp.sum(array, axis=0, keepdims=True), axis=1, keepdims=True)


def later_sums(column):
    kept = iota((CHUNK, CHUNK), 0) >= iota((CHUNK, CHUNK), 1)
    return jnp.sum(jnp.where(kept, column, 0.0), axis=0, keepdims=True)


def decay_tables(lengths_ref, ctx_ref, gates_ref, spread, cum_ref, chunk_fac_ref, shard_fac_ref):
    rows = cum_ref.shape[0]
    num_chunks = rows // 8
    tokens = num_chunks * CHUNK
    for chunk in range(num_chunks):
        part = gates_ref[0, :, chunk * CHUNK : (chunk + 1) * CHUNK]
        spread[chunk * 8 : chunk * 8 + 4, :] = part
        spread[chunk * 8 + 4 : chunk * 8 + 8, :] = part
    gates = spread[...] * LOG2E
    lane_a, lane_b = iota((CHUNK, CHUNK), 0), iota((CHUNK, CHUNK), 1)
    prefix = dot_nn(gates, (lane_a <= lane_b).astype(F32), PRECISE)
    suffix = dot_nn(gates, (lane_a > lane_b).astype(F32), PRECISE)
    totals = jnp.broadcast_to(prefix[:, CHUNK - 1 : CHUNK], (rows, CHUNK))
    row_a, row_b = iota((rows, rows), 0), iota((rows, rows), 1)
    same = (row_a % 8) == (row_b % 8)
    outside = ((row_a % 8 < 4) & (row_b // 8 < row_a // 8)) | (
        (row_a % 8 >= 4) & (row_b // 8 > row_a // 8)
    )
    others = dot_nn((same & outside).astype(F32), totals, PRECISE)

    first = ctx_ref[0] * tokens
    chunk_first = first + (iota((rows, CHUNK), 0) // 8) * CHUNK
    positions = chunk_first + iota((rows, CHUNK), 1)
    from_start = iota((rows, CHUNK), 0) % 8 < 4
    chunk_anchor = jnp.where(from_start, chunk_first - 1, chunk_first + (CHUNK - 1))
    segment = jnp.zeros((rows, CHUNK), F32)
    chunk_segment = jnp.zeros((rows, CHUNK), F32)
    shard_before = jnp.float32(0)
    shard_last = jnp.float32(0)
    start = jnp.int32(0)
    for doc in range(lengths_ref.shape[1]):
        segment += jnp.where(positions >= start, 1.0, 0.0)
        chunk_segment += jnp.where(chunk_anchor >= start, 1.0, 0.0)
        shard_before += jnp.where(first > start, 1.0, 0.0)
        shard_last += jnp.where(first + (tokens - 1) >= start, 1.0, 0.0)
        start += lengths_ref[0, doc]
    cum_ref[...] = jnp.where(from_start, prefix, segment)
    exponent = jnp.where(from_start, prefix, suffix)
    chunk_fac_ref[...] = jnp.where(
        segment == chunk_segment, jnp.exp2(jnp.minimum(exponent, 0.0)), 0.0
    )
    keep = segment == jnp.where(from_start, shard_before, shard_last)
    shard_fac_ref[...] = jnp.where(keep, jnp.exp2(jnp.minimum(exponent + others, 0.0)), 0.0)


def ends_kernel(head_width, part, half_ctx, *refs):
    if part == 0:
        (lengths_ref, ctx_ref, gates_ref, q_ref, k_ref, v_ref, cot_ref,
         near_ref, far_ref, decay_ref, cum_ref, chunk_fac_ref, shard_fac_ref,
         end_scr, grad_scr, spread) = refs
    else:
        (ctx_ref, shard_fac_ref, q_ref, k_ref, v_ref, cot_ref,
         near_ref, far_ref, decay_ref, end_scr, grad_scr) = refs
    step = pl.program_id(0)
    heads = near_ref.shape[0]
    block = q_ref.shape[1]
    chunks = block // CHUNK
    rows = shard_fac_ref.shape[0]

    @pl.when(step == 0)
    def _():
        if part == 0:
            decay_tables(
                lengths_ref, ctx_ref, gates_ref, spread, cum_ref, chunk_fac_ref, shard_fac_ref
            )
        for head in range(heads):
            row = rows - 8 + part * heads + head
            decay_ref[head] = jnp.broadcast_to(
                shard_fac_ref[row : row + 1, CHUNK - 1 : CHUNK], (1, head_width)
            )
        end_scr[...] = jnp.zeros_like(end_scr)
        grad_scr[...] = jnp.zeros_like(grad_scr)

    factors = []
    for chunk in range(chunks):
        at = pl.multiple_of((step * chunks + chunk) * 8, 8)
        factors.append(shard_fac_ref[pl.ds(at, 8), :])

    def turned(ref, lanes, row, scale):
        pieces = []
        for chunk in range(chunks):
            rows_here = slice(chunk * CHUNK, (chunk + 1) * CHUNK)
            piece = jnp.transpose(ref[0, rows_here, lanes]).astype(F32)
            pieces.append((piece * (factors[chunk][row : row + 1, :] * scale)).astype(BF16))
        return jnp.concatenate(pieces, axis=1)

    for head in range(heads):
        lanes = slice(head * head_width, (head + 1) * head_width)
        row = part * heads + head
        end_scr[head] += dot_nn(turned(k_ref, lanes, 4 + row, 1.0), v_ref[0, :, lanes])
        grad_scr[head] += dot_nn(
            turned(q_ref, lanes, row, head_width ** (-0.5)), cot_ref[0, :, lanes]
        )

    @pl.when(step == pl.num_programs(0) - 1)
    def _():
        low = ctx_ref[0] < half_ctx
        end, grad = end_scr[...], grad_scr[...]
        near_ref[...] = jnp.where(low, end, grad)
        far_ref[...] = jnp.where(low, grad, end)


def local_kernel(
    head_width, part, q_ref, k_ref, v_ref, cot_ref, gain_ref, cum_ref, fac_ref,
    out_ref, dq_ref, dk_ref, dv_ref, dgate_ref, dgain_ref, leaving, state,
):
    heads = state.shape[0]
    num_chunks = leaving.shape[0]
    scale = head_width ** (-0.5)
    unroll = math.gcd(num_chunks, UNROLL)

    def lanes_of(head):
        return slice((part * heads + head) * head_width, (part * heads + head + 1) * head_width)

    def own_lanes(head):
        return slice(head * head_width, (head + 1) * head_width)

    def rows_of(chunk):
        return pl.ds(pl.multiple_of(chunk * CHUNK, CHUNK), CHUNK)

    def table(ref, chunk):
        return ref[pl.ds(pl.multiple_of(chunk * 8, 8), 8), :]

    pairs = [(at, head) for at in range(unroll) for head in range(heads)]

    def backward(chunks):
        facs = [table(fac_ref, chunk) for chunk in chunks]
        added = {}
        for at, head in pairs:
            row = part * heads + head
            rows, lanes = rows_of(chunks[at]), lanes_of(head)
            turned = jnp.transpose(q_ref[0, rows, lanes]).astype(F32)
            turned = (turned * (facs[at][row : row + 1, :] * scale)).astype(BF16)
            added[at, head] = dot_nn(turned, cot_ref[0, rows, lanes])
        for head in range(heads):
            row = part * heads + head
            held = state[head]
            for at in range(unroll):
                leaving[chunks[at], head] = held.astype(BF16)
                held = held * facs[at][row : row + 1, CHUNK - 1 : CHUNK] + added[at, head]
            state[head] = held

    def forward(chunks):
        facs = [table(fac_ref, chunk) for chunk in chunks]
        cums = [table(cum_ref, chunk) for chunk in chunks]
        fac_columns = [jnp.transpose(fac) for fac in facs]
        cum_columns = [jnp.transpose(cum) for cum in cums]
        causal = iota((CHUNK, CHUNK), 0) >= iota((CHUNK, CHUNK), 1)
        limits = [
            jnp.where((columns[:, 4:5] == cum[4:5, :]) & causal, math.log2(scale), -1e30)
            for columns, cum in zip(cum_columns, cums)
        ]
        cum_columns = [columns + math.log2(scale) for columns in cum_columns]
        q, k, v, cot, k_raw, k_decayed, q_decayed, later = ({} for _ in range(8))
        from_start, to_end, added, held, entering = ({} for _ in range(5))
        for key in pairs:
            at, head = key
            row = part * heads + head
            rows, lanes = rows_of(chunks[at]), lanes_of(head)
            q[key], v[key], cot[key] = q_ref[0, rows, lanes], v_ref[0, rows, lanes], cot_ref[0, rows, lanes]
            later[key] = leaving[chunks[at], head]
            k_raw[key] = k_ref[0, rows, lanes].astype(F32)
            k_wide = k_raw[key] * gain_ref[row : row + 1, :]
            k[key] = k_wide.astype(BF16)
            from_start[key] = fac_columns[at][:, row : row + 1] * scale
            to_end[key] = fac_columns[at][:, 4 + row : 5 + row]
            k_decayed[key] = (k_wide * to_end[key]).astype(BF16)
            q_decayed[key] = (q[key].astype(F32) * from_start[key]).astype(BF16)
            added[key] = dot_tn(k_decayed[key], v[key])
        for head in range(heads):
            row = part * heads + head
            now = state[head]
            for at in range(unroll):
                held[at, head] = now
                entering[at, head] = now.astype(BF16)
                now = now * facs[at][row : row + 1, CHUNK - 1 : CHUNK] + added[at, head]
            held[unroll, head] = now
            state[head] = now
        by_cot, scores, written = {}, {}, {}
        for key in pairs:
            by_cot[key] = dot_nt(cot[key], jnp.concatenate([v[key], entering[key]], axis=0))
            scores[key] = dot_nt(q[key], k[key])
            written[key] = dot_nt(v[key], later[key])
        weights, grad_scores = {}, {}
        for key in pairs:
            at, head = key
            row = part * heads + head
            decays = jnp.exp2(
                jnp.minimum(cum_columns[at][:, row : row + 1] - cums[at][row : row + 1, :], limits[at])
            )
            weights[key] = (scores[key] * decays).astype(BF16)
            grad_scores[key] = (by_cot[key][:, :CHUNK] * decays).astype(BF16)
        out, dq, dk, dv = {}, {}, {}, {}
        for key in pairs:
            out[key] = dot_nn(
                jnp.concatenate([weights[key], q_decayed[key]], axis=1),
                jnp.concatenate([v[key], entering[key]], axis=0),
            )
            dv[key] = dot_nn(
                jnp.concatenate([jnp.transpose(weights[key]), k_decayed[key]], axis=1),
                jnp.concatenate([cot[key], later[key]], axis=0),
            )
            dq[key] = dot_nn(grad_scores[key], k[key]) + by_cot[key][:, CHUNK:] * from_start[key]
            dk[key] = dot_tn(grad_scores[key], q[key]) + written[key] * to_end[key]
        gate_rows, gain_rows = {}, {}
        for key in pairs:
            at, head = key
            balance = jnp.sum(
                out[key] * cot[key].astype(F32) - dv[key] * v[key].astype(F32),
                axis=1, keepdims=True,
            )
            gate_rows[key] = later_sums(balance) + total_of(
                held[at + 1, head] * later[key].astype(F32)
            )
            gain_rows[key] = jnp.sum(dk[key] * k_raw[key], axis=0, keepdims=True)
        for key in pairs:
            at, head = key
            row = part * heads + head
            rows, own = rows_of(chunks[at]), own_lanes(head)
            out_ref[0, rows, own] = out[key].astype(BF16)
            dq_ref[0, rows, own] = dq[key].astype(BF16)
            dv_ref[0, rows, own] = dv[key].astype(BF16)
            dk_ref[0, rows, own] = (dk[key] * gain_ref[row : row + 1, :]).astype(BF16)
            dgate_ref[0, head : head + 1, rows] = gate_rows[key]
        for head in range(heads):
            dgain_ref[head : head + 1, :] += sum(gain_rows[at, head] for at in range(unroll))

    state[...] = jnp.zeros_like(state)

    def backward_group(index, carry):
        backward([num_chunks - 1 - (index * unroll + at) for at in range(unroll)])
        return carry

    lax.fori_loop(0, num_chunks // unroll, backward_group, 0)
    state[...] = jnp.zeros_like(state)
    dgain_ref[...] = jnp.zeros_like(dgain_ref)

    def forward_group(index, carry):
        forward([index * unroll + at for at in range(unroll)])
        return carry

    lax.fori_loop(0, num_chunks // unroll, forward_group, 0)


def merge_kernel(head_width, part, half_ctx, *refs):
    (ctx_ref, q_ref, k_ref, v_ref, cot_ref, gain_ref, fac_ref, first_ref, second_ref, last_ref,
     out_in, dq_in, dk_in, dv_in, dgate_in) = refs[:15]
    refs = refs[15:]
    if part > 0:
        before_ref, refs = refs[0], refs[5:]
    out_ref, dq_ref, dk_ref, dv_ref, dgate_ref, entering, leaving, sums_scr, tot_scr = refs
    step = pl.program_id(0)
    heads = first_ref.shape[0]
    block = q_ref.shape[1]
    chunks = block // CHUNK
    num_chunks = fac_ref.shape[0] // 8
    scale = head_width ** (-0.5)

    def arrived(head):
        low = ctx_ref[0] < half_ctx
        first, second = first_ref[head], second_ref[head] + last_ref[head]
        return jnp.where(low, first, second), jnp.where(low, second, first)

    @pl.when(step == 0)
    def _():
        gain_columns = jnp.transpose(jnp.concatenate([gain_ref[...], gain_ref[...]], axis=0))
        entering[...] = jnp.zeros_like(entering)
        leaving[...] = jnp.zeros_like(leaving)
        for head in range(heads):
            row = part * heads + head
            own = slice(head * head_width, (head + 1) * head_width)
            gain = gain_columns[:, row : row + 1]
            state, later = arrived(head)
            entering[own, own] = (state * (gain * scale)).astype(BF16)
            leaving[own, own] = (later * gain).astype(BF16)

    products, results = [], {}
    for chunk in range(chunks):
        rows = slice(chunk * CHUNK, (chunk + 1) * CHUNK)
        products.append(
            (
                dot_nn(q_ref[0, rows, :], entering[...]),
                dot_nt(cot_ref[0, rows, :], entering[...]),
                dot_nn(k_ref[0, rows, :], leaving[...]),
                dot_nt(v_ref[0, rows, :], leaving[...]),
            )
        )
    for chunk in range(chunks):
        number = step * chunks + chunk
        columns = jnp.transpose(fac_ref[pl.ds(pl.multiple_of(number * 8, 8), 8), :])
        rows = slice(chunk * CHUNK, (chunk + 1) * CHUNK)
        for head in range(heads):
            row = part * heads + head
            lanes = slice(head * head_width, (head + 1) * head_width)
            from_start, to_end = columns[:, row : row + 1], columns[:, 4 + row : 5 + row]
            across_all, dq_all, written_all, dk_all = products[chunk]
            across = across_all[:, lanes] * from_start
            written = written_all[:, lanes] * to_end
            kept = written * v_ref[0, rows, lanes].astype(F32)
            balance = jnp.sum(
                across * cot_ref[0, rows, lanes].astype(F32) - kept, axis=1, keepdims=True
            )
            results[chunk, head] = (
                (out_in[0, rows, lanes].astype(F32) + across).astype(BF16),
                (dq_in[0, rows, lanes].astype(F32) + dq_all[:, lanes] * from_start).astype(BF16),
                (dk_in[0, rows, lanes].astype(F32) + dk_all[:, lanes] * to_end).astype(BF16),
                (dv_in[0, rows, lanes].astype(F32) + written).astype(BF16),
                later_sums(balance),
                jnp.sum(kept, axis=0, keepdims=True),
            )
    for chunk in range(chunks):
        number = step * chunks + chunk
        rows = slice(chunk * CHUNK, (chunk + 1) * CHUNK)
        for head in range(heads):
            lanes = slice(head * head_width, (head + 1) * head_width)
            out, dq, dk, dv, sums, kept = results[chunk, head]
            out_ref[0, rows, lanes] = out
            dq_ref[0, rows, lanes] = dq
            dk_ref[0, rows, lanes] = dk
            dv_ref[0, rows, lanes] = dv
            sums_scr[number, head : head + 1, :] = sums
            tot_scr[number, head : head + 1, :] = kept

    @pl.when(step == pl.num_programs(0) - 1)
    def _():
        last = fac_ref[(num_chunks - 1) * 8 : num_chunks * 8, CHUNK - 1 : CHUNK]
        kept = tot_scr[0]
        for chunk in range(1, num_chunks):
            kept = kept + tot_scr[chunk]
        base = jnp.sum(kept, axis=1, keepdims=True)
        constants = []
        for head in range(heads):
            row = part * heads + head
            state, later = arrived(head)
            gain_columns = jnp.transpose(
                jnp.concatenate([gain_ref[...], gain_ref[...]], axis=0)
            )
            product = total_of(state * later * gain_columns[:, row : row + 1])
            constants.append(product * last[row : row + 1])
        base = base[:heads] + jnp.concatenate(constants, axis=0)
        if part > 0:
            dgate_ref[0, : part * heads, :] = before_ref[0]
        own = slice(part * heads, (part + 1) * heads)
        for chunk in range(num_chunks - 1, -1, -1):
            lanes = slice(chunk * CHUNK, (chunk + 1) * CHUNK)
            sums = sums_scr[chunk, :heads, :]
            dgate_ref[0, own, lanes] = dgate_in[0, :, lanes] + sums + base
            base = base + sums[:, 0:1]


def shards(queries, keys_raw, values, gates, lengths, key_gain, cotangent):
    tokens, width = queries.shape[1:]
    all_heads, head_width = key_gain.shape
    heads = all_heads // PARTS
    part_width = width // PARTS
    num_chunks = tokens // CHUNK
    rows = num_chunks * 8
    block = min(256, tokens)
    steps = tokens // block
    ctx = lax.axis_index("ctx")
    count = lax.axis_size("ctx")
    middle = count // 2 - 1
    streams = (queries, keys_raw, values, cotangent)
    ctx_scalar = jnp.reshape(ctx, (1,)).astype(jnp.int32)

    def stream_spec(part):
        return pl.BlockSpec((1, block, part_width), lambda i: (0, i, part))

    def whole(array):
        zeros = (0,) * len(array.shape)
        return pl.BlockSpec(array.shape, lambda *_: zeros)

    def shape_of(*shape, dtype=F32):
        return jax.ShapeDtypeStruct(shape, dtype)

    smem = pl.BlockSpec(memory_space=pltpu.SMEM)
    vmem = pl.BlockSpec(memory_space=pltpu.VMEM)
    table = shape_of(rows, CHUNK)
    states = shape_of(heads, head_width, head_width)
    decays = shape_of(heads, 1, head_width)
    part_gates = shape_of(1, heads, tokens)
    product = 2 * tokens * part_width * head_width

    def ends(part, *tables):
        specs = [smem, smem, whole(gates)] if part == 0 else [smem, whole(table)]
        outs = [states, states, decays] + ([table] * 3 if part == 0 else [])
        scratch = [pltpu.VMEM(states.shape, F32)] * 2
        if part == 0:
            scratch.append(pltpu.VMEM((rows, CHUNK), F32))
        return pl.pallas_call(
            functools.partial(ends_kernel, head_width, part, count // 2),
            grid=(steps,),
            in_specs=specs + [stream_spec(part)] * 4,
            out_specs=[whole(out) for out in outs],
            out_shape=outs,
            scratch_shapes=scratch,
            compiler_params=pltpu.CompilerParams(vmem_limit_bytes=56 << 20),
            cost_estimate=pl.CostEstimate(
                flops=2 * product, bytes_accessed=8 * tokens * part_width, transcendentals=0
            ),
            name=f"shard_ends_{part}",
        )(*tables, *streams)

    def local(part, arrays, gain, cum, fac):
        wide = shape_of(1, tokens, part_width, dtype=BF16)
        return pl.pallas_call(
            functools.partial(local_kernel, head_width, part),
            in_specs=[vmem] * 7,
            out_specs=[vmem] * 6,
            out_shape=[wide] * 4 + [part_gates, shape_of(heads, head_width)],
            scratch_shapes=[
                pltpu.VMEM((num_chunks, heads, head_width, head_width), BF16),
                pltpu.VMEM((heads, head_width, head_width), F32),
            ],
            compiler_params=pltpu.CompilerParams(vmem_limit_bytes=24 << 20),
            cost_estimate=pl.CostEstimate(
                flops=12 * product, bytes_accessed=16 * tokens * part_width, transcendentals=0
            ),
            name=f"local_{part}",
        )(*arrays, gain, cum, fac)

    def merge(part, arrivals, locals_, done):
        own_spec = pl.BlockSpec((1, block, part_width), lambda i: (0, i, 0))
        full_gates = shape_of(1, (part + 1) * heads, tokens)
        extra, extra_specs, aliases = [], [], {}
        if part > 0:
            extra = [done[4]] + list(done[:4])
            extra_specs = [whole(done[4])] + [pl.BlockSpec(memory_space=pl.ANY)] * 4
            aliases = {16 + i: i for i in range(4)}
        return pl.pallas_call(
            functools.partial(merge_kernel, head_width, part, count // 2),
            grid=(steps,),
            in_specs=[smem]
            + [stream_spec(part)] * 4
            + [whole(key_gain), whole(table)]
            + [whole(states)] * 3
            + [own_spec] * 4
            + [whole(part_gates)]
            + extra_specs,
            out_specs=[stream_spec(part)] * 4 + [whole(full_gates)],
            out_shape=[shape_of(1, tokens, width, dtype=BF16)] * 4 + [full_gates],
            scratch_shapes=[
                pltpu.VMEM((part_width, part_width), BF16),
                pltpu.VMEM((part_width, part_width), BF16),
                pltpu.VMEM((num_chunks, 8, CHUNK), F32),
                pltpu.VMEM((num_chunks, 8, CHUNK), F32),
            ],
            input_output_aliases=aliases,
            compiler_params=pltpu.CompilerParams(vmem_limit_bytes=24 << 20),
            cost_estimate=pl.CostEstimate(
                flops=4 * product, bytes_accessed=24 * tokens * part_width, transcendentals=0
            ),
            name=f"merge_{part}",
        )(ctx_scalar, *streams, key_gain, shard_fac, *arrivals, *locals_, *extra)

    near, far, decay = [None] * PARTS, [None] * PARTS, [None] * PARTS
    near[0], far[0], decay[0], cum, chunk_fac, shard_fac = ends(0, lengths, ctx_scalar, gates)
    sent = [[] for _ in range(PARTS)]
    arrived = [[] for _ in range(PARTS)]
    local_parts = [None] * PARTS

    def send(part, hop):
        payload = near[part] if hop <= middle else far[part]
        if hop > 0:
            payload = payload + decay[part] * arrived[part][-1]
        sent[part].append(payload)
        arrived[part].append(
            lax.ppermute(
                payload, "ctx", [(hop, hop + 1), (count - 1 - hop, count - 2 - hop)]
            )
        )

    for part in range(PARTS):
        if part > 0:
            near[part], far[part], decay[part] = ends(part, ctx_scalar, shard_fac)
        send(part, 0)
    for hop in range(count - 1):
        if hop < PARTS:
            local_cum = cum
            if hop > 0:
                local_cum, _ = lax.optimization_barrier((cum, arrived[0][hop - 1]))
            local_parts[hop] = list(local(hop, streams, key_gain, local_cum, chunk_fac))
            if hop + 1 < count - 1:
                local_parts[hop][5], arrived[0][-1] = lax.optimization_barrier(
                    (local_parts[hop][5], arrived[0][-1])
                )
        if hop + 1 < count - 1:
            for part in range(PARTS):
                send(part, hop + 1)

    terms = []
    for part in range(PARTS):
        crossed = jnp.sum(sent[part][middle] * arrived[part][middle], axis=2)
        term = local_parts[part][5] + jnp.where(ctx == middle, crossed, 0.0)
        if middle > 0:
            term = term + jnp.sum(sum(arrived[part][:middle]) * far[part], axis=2)
        terms.append(term)
    gain_term = jnp.concatenate(terms, axis=0)
    half = head_width // lax.axis_size("dp")
    dp = lax.axis_index("dp")
    away = jnp.where(dp == 0, gain_term[:, half:], gain_term[:, :half])
    kept = jnp.where(dp == 0, gain_term[:, :half], gain_term[:, half:])
    grad_gain = kept + lax.ppermute(away, "dp", [(0, 1), (1, 0)])

    done, reach = None, 1
    for part in range(PARTS):
        others = jnp.zeros_like(grad_gain)
        if reach < count:
            others = lax.ppermute(grad_gain, "ctx", [(i, i ^ reach) for i in range(count)])
            reach *= 2
        zeros = jnp.zeros(states.shape, F32)
        first = sum(arrived[part][:middle], zeros) if middle != 1 else arrived[part][0]
        second = sum(arrived[part][middle:-1], zeros) if middle != 1 else arrived[part][1]
        done = list(merge(part, (first, second, arrived[part][-1]), local_parts[part][:5], done))
        if part < PARTS - 1:
            done[4], others = lax.optimization_barrier((done[4], others))
        grad_gain = grad_gain + others
    while reach < count:
        grad_gain = grad_gain + lax.ppermute(
            grad_gain, "ctx", [(i, i ^ reach) for i in range(count)]
        )
        reach *= 2
    return (*done, grad_gain)


def solution(mesh):
    wide = P("dp", "ctx", "head")
    narrow = P("dp", "head", "ctx")
    return jax.shard_map(
        shards,
        mesh=mesh,
        in_specs=(wide, wide, wide, narrow, P("dp", None), P("head", None), wide),
        out_specs=(wide, wide, wide, wide, narrow, P("head", "dp")),
        check_vma=False,
    )
```

```python
import functools
import math

import jax
import jax.numpy as jnp
from jax import lax
from jax.experimental import pallas as pl
from jax.experimental.pallas import tpu as pltpu
from jax.sharding import PartitionSpec as P

CHUNK = 128
PARTS = 2
UNROLL = 4
PRECISE = lax.Precision.HIGHEST
F32 = jnp.float32
BF16 = jnp.bfloat16
LOG2E = math.log2(math.e)


def dot_nn(a, b, precision=None):
    return lax.dot_general(
        a, b, (((1,), (0,)), ((), ())), precision=precision, preferred_element_type=F32
    )


def dot_nt(a, b):
    return lax.dot_general(a, b, (((1,), (1,)), ((), ())), preferred_element_type=F32)


def dot_tn(a, b):
    return lax.dot_general(a, b, (((0,), (0,)), ((), ())), preferred_element_type=F32)


def iota(shape, dim):
    return lax.broadcasted_iota(jnp.int32, shape, dim)


def total_of(array):
    return jnp.sum(jnp.sum(array, axis=0, keepdims=True), axis=1, keepdims=True)


def later_sums(column):
    kept = iota((CHUNK, CHUNK), 0) >= iota((CHUNK, CHUNK), 1)
    return jnp.sum(jnp.where(kept, column, 0.0), axis=0, keepdims=True)


def decay_tables(lengths_ref, ctx_ref, gates_ref, spread, cum_ref, chunk_fac_ref, shard_fac_ref):
    rows = cum_ref.shape[0]
    num_chunks = rows // 8
    tokens = num_chunks * CHUNK
    for chunk in range(num_chunks):
        part = gates_ref[0, :, chunk * CHUNK : (chunk + 1) * CHUNK]
        spread[chunk * 8 : chunk * 8 + 4, :] = part
        spread[chunk * 8 + 4 : chunk * 8 + 8, :] = part
    gates = spread[...] * LOG2E
    lane_a, lane_b = iota((CHUNK, CHUNK), 0), iota((CHUNK, CHUNK), 1)
    prefix = dot_nn(gates, (lane_a <= lane_b).astype(F32), PRECISE)
    suffix = dot_nn(gates, (lane_a > lane_b).astype(F32), PRECISE)
    totals = jnp.broadcast_to(prefix[:, CHUNK - 1 : CHUNK], (rows, CHUNK))
    row_a, row_b = iota((rows, rows), 0), iota((rows, rows), 1)
    same = (row_a % 8) == (row_b % 8)
    outside = ((row_a % 8 < 4) & (row_b // 8 < row_a // 8)) | (
        (row_a % 8 >= 4) & (row_b // 8 > row_a // 8)
    )
    others = dot_nn((same & outside).astype(F32), totals, PRECISE)

    first = ctx_ref[0] * tokens
    chunk_first = first + (iota((rows, CHUNK), 0) // 8) * CHUNK
    positions = chunk_first + iota((rows, CHUNK), 1)
    from_start = iota((rows, CHUNK), 0) % 8 < 4
    chunk_anchor = jnp.where(from_start, chunk_first - 1, chunk_first + (CHUNK - 1))
    segment = jnp.zeros((rows, CHUNK), F32)
    chunk_segment = jnp.zeros((rows, CHUNK), F32)
    shard_before = jnp.float32(0)
    shard_last = jnp.float32(0)
    start = jnp.int32(0)
    for doc in range(lengths_ref.shape[1]):
        segment += jnp.where(positions >= start, 1.0, 0.0)
        chunk_segment += jnp.where(chunk_anchor >= start, 1.0, 0.0)
        shard_before += jnp.where(first > start, 1.0, 0.0)
        shard_last += jnp.where(first + (tokens - 1) >= start, 1.0, 0.0)
        start += lengths_ref[0, doc]
    cum_ref[...] = jnp.where(from_start, prefix, segment)
    exponent = jnp.where(from_start, prefix, suffix)
    chunk_fac_ref[...] = jnp.where(
        segment == chunk_segment, jnp.exp2(jnp.minimum(exponent, 0.0)), 0.0
    )
    keep = segment == jnp.where(from_start, shard_before, shard_last)
    shard_fac_ref[...] = jnp.where(keep, jnp.exp2(jnp.minimum(exponent + others, 0.0)), 0.0)


def ends_kernel(head_width, half_ctx, *refs):
    lengths_ref, ctx_ref, gates_ref = refs[:3]
    sources, targets = refs[3:7], refs[7:11]
    near_refs, far_refs, decay_refs = (
        refs[11 + i * PARTS : 11 + (i + 1) * PARTS] for i in range(3)
    )
    cum_ref, chunk_fac_ref, shard_fac_ref, spread, sems = refs[11 + 3 * PARTS :]
    q_ref, k_ref, v_ref, cot_ref = targets
    heads = near_refs[0].shape[0]
    rows = shard_fac_ref.shape[0]
    steps = sems.shape[0]
    block = q_ref.shape[1] // steps
    chunks = block // CHUNK

    def copies(step):
        at = pl.ds(step * block, block)
        return [
            pltpu.make_async_copy(source.at[:, at, :], target.at[:, at, :], sems.at[step, i])
            for i, (source, target) in enumerate(zip(sources, targets))
        ]

    for step in range(steps):
        for i, copy in enumerate(copies(step)):
            copy.start(priority=i % 2)
    decay_tables(lengths_ref, ctx_ref, gates_ref, spread, cum_ref, chunk_fac_ref, shard_fac_ref)
    for part in range(PARTS):
        for head in range(heads):
            row = rows - 8 + part * heads + head
            decay_refs[part][head] = jnp.broadcast_to(
                shard_fac_ref[row : row + 1, CHUNK - 1 : CHUNK], (1, head_width)
            )

    def turned(ref, step, row, scale):
        pieces = []
        head = row % 4
        for chunk in range(step * chunks, (step + 1) * chunks):
            factor = shard_fac_ref[chunk * 8 + row : chunk * 8 + row + 1, :]
            piece = jnp.transpose(
                ref[
                    0,
                    chunk * CHUNK : (chunk + 1) * CHUNK,
                    head * head_width : (head + 1) * head_width,
                ]
            )
            pieces.append((piece.astype(F32) * (factor * scale)).astype(BF16))
        return jnp.concatenate(pieces, axis=1)

    ends, grads = {}, {}
    for step in range(steps):
        for copy in copies(step):
            copy.wait()
        at = slice(step * block, (step + 1) * block)
        for row in range(PARTS * heads):
            lanes = slice(row * head_width, (row + 1) * head_width)
            end = dot_nn(turned(k_ref, step, 4 + row, 1.0), v_ref[0, at, lanes])
            grad = dot_nn(turned(q_ref, step, row, head_width ** (-0.5)), cot_ref[0, at, lanes])
            ends[row] = ends[row] + end if step else end
            grads[row] = grads[row] + grad if step else grad
    low = ctx_ref[0] < half_ctx
    for part in range(PARTS):
        for head in range(heads):
            row = part * heads + head
            near_refs[part][head] = jnp.where(low, ends[row], grads[row])
            far_refs[part][head] = jnp.where(low, grads[row], ends[row])


def local_kernel(
    head_width, part, q_ref, k_ref, v_ref, cot_ref, gain_ref, cum_ref, fac_ref,
    out_ref, dq_ref, dk_ref, dv_ref, dgate_ref, dgain_ref, leaving, state,
):
    heads = state.shape[0]
    num_chunks = leaving.shape[0]
    scale = head_width ** (-0.5)
    unroll = math.gcd(num_chunks, UNROLL)

    def lanes_of(head):
        return slice((part * heads + head) * head_width, (part * heads + head + 1) * head_width)

    def own_lanes(head):
        return slice(head * head_width, (head + 1) * head_width)

    def rows_of(chunk):
        return pl.ds(pl.multiple_of(chunk * CHUNK, CHUNK), CHUNK)

    def table(ref, chunk):
        return ref[pl.ds(pl.multiple_of(chunk * 8, 8), 8), :]

    pairs = [(at, head) for at in range(unroll) for head in range(heads)]

    def backward(chunks):
        facs = [table(fac_ref, chunk) for chunk in chunks]
        added = {}
        for at, head in pairs:
            row = part * heads + head
            rows, lanes = rows_of(chunks[at]), lanes_of(head)
            turned = jnp.transpose(q_ref[0, rows, lanes]).astype(F32)
            turned = (turned * (facs[at][row : row + 1, :] * scale)).astype(BF16)
            added[at, head] = dot_nn(turned, cot_ref[0, rows, lanes])
        for head in range(heads):
            row = part * heads + head
            held = state[head]
            for at in range(unroll):
                leaving[chunks[at], head] = held.astype(BF16)
                held = held * facs[at][row : row + 1, CHUNK - 1 : CHUNK] + added[at, head]
            state[head] = held

    def forward(chunks):
        facs = [table(fac_ref, chunk) for chunk in chunks]
        cums = [table(cum_ref, chunk) for chunk in chunks]
        fac_columns = [jnp.transpose(fac) for fac in facs]
        cum_columns = [jnp.transpose(cum) for cum in cums]
        causal = iota((CHUNK, CHUNK), 0) >= iota((CHUNK, CHUNK), 1)
        limits = [
            jnp.where((columns[:, 4:5] == cum[4:5, :]) & causal, math.log2(scale), -1e30)
            for columns, cum in zip(cum_columns, cums)
        ]
        cum_columns = [columns + math.log2(scale) for columns in cum_columns]
        q, k, v, cot, k_raw, k_decayed, q_decayed, later = ({} for _ in range(8))
        from_start, to_end, added, held, entering = ({} for _ in range(5))
        for key in pairs:
            at, head = key
            row = part * heads + head
            rows, lanes = rows_of(chunks[at]), lanes_of(head)
            q[key], v[key], cot[key] = q_ref[0, rows, lanes], v_ref[0, rows, lanes], cot_ref[0, rows, lanes]
            later[key] = leaving[chunks[at], head]
            k_raw[key] = k_ref[0, rows, lanes].astype(F32)
            k_wide = k_raw[key] * gain_ref[row : row + 1, :]
            k[key] = k_wide.astype(BF16)
            from_start[key] = fac_columns[at][:, row : row + 1] * scale
            to_end[key] = fac_columns[at][:, 4 + row : 5 + row]
            k_decayed[key] = (k_wide * to_end[key]).astype(BF16)
            q_decayed[key] = (q[key].astype(F32) * from_start[key]).astype(BF16)
            added[key] = dot_tn(k_decayed[key], v[key])
        for head in range(heads):
            row = part * heads + head
            now = state[head]
            for at in range(unroll):
                held[at, head] = now
                entering[at, head] = now.astype(BF16)
                now = now * facs[at][row : row + 1, CHUNK - 1 : CHUNK] + added[at, head]
            held[unroll, head] = now
            state[head] = now
        by_cot, scores, written = {}, {}, {}
        for key in pairs:
            by_cot[key] = dot_nt(cot[key], jnp.concatenate([v[key], entering[key]], axis=0))
            scores[key] = dot_nt(q[key], k[key])
            written[key] = dot_nt(v[key], later[key])
        weights, grad_scores = {}, {}
        for key in pairs:
            at, head = key
            row = part * heads + head
            decays = jnp.exp2(
                jnp.minimum(cum_columns[at][:, row : row + 1] - cums[at][row : row + 1, :], limits[at])
            )
            weights[key] = (scores[key] * decays).astype(BF16)
            grad_scores[key] = (by_cot[key][:, :CHUNK] * decays).astype(BF16)
        out, dq, dk, dv = {}, {}, {}, {}
        for key in pairs:
            out[key] = dot_nn(
                jnp.concatenate([weights[key], q_decayed[key]], axis=1),
                jnp.concatenate([v[key], entering[key]], axis=0),
            )
            dv[key] = dot_nn(
                jnp.concatenate([jnp.transpose(weights[key]), k_decayed[key]], axis=1),
                jnp.concatenate([cot[key], later[key]], axis=0),
            )
            dq[key] = dot_nn(grad_scores[key], k[key]) + by_cot[key][:, CHUNK:] * from_start[key]
            dk[key] = dot_tn(grad_scores[key], q[key]) + written[key] * to_end[key]
        gate_rows, gain_rows = {}, {}
        for key in pairs:
            at, head = key
            balance = jnp.sum(
                out[key] * cot[key].astype(F32) - dv[key] * v[key].astype(F32),
                axis=1, keepdims=True,
            )
            gate_rows[key] = later_sums(balance) + total_of(
                held[at + 1, head] * later[key].astype(F32)
            )
            gain_rows[key] = jnp.sum(dk[key] * k_raw[key], axis=0, keepdims=True)
        for key in pairs:
            at, head = key
            row = part * heads + head
            rows, own = rows_of(chunks[at]), own_lanes(head)
            out_ref[0, rows, own] = out[key].astype(BF16)
            dq_ref[0, rows, own] = dq[key].astype(BF16)
            dv_ref[0, rows, own] = dv[key].astype(BF16)
            dk_ref[0, rows, own] = (dk[key] * gain_ref[row : row + 1, :]).astype(BF16)
            dgate_ref[0, head : head + 1, rows] = gate_rows[key]
        for head in range(heads):
            dgain_ref[head : head + 1, :] += sum(gain_rows[at, head] for at in range(unroll))

    state[...] = jnp.zeros_like(state)

    def backward_group(index, carry):
        backward([num_chunks - 1 - (index * unroll + at) for at in range(unroll)])
        return carry

    lax.fori_loop(0, num_chunks // unroll, backward_group, 0)
    state[...] = jnp.zeros_like(state)
    dgain_ref[...] = jnp.zeros_like(dgain_ref)

    def forward_group(index, carry):
        forward([index * unroll + at for at in range(unroll)])
        return carry

    lax.fori_loop(0, num_chunks // unroll, forward_group, 0)


def merge_kernel(head_width, part, half_ctx, *refs):
    (ctx_ref, q_ref, k_ref, v_ref, cot_ref, gain_ref, fac_ref, first_ref, second_ref, last_ref,
     out_in, dq_in, dk_in, dv_in, dgate_in) = refs[:15]
    refs = refs[15:]
    if part > 0:
        before_ref, refs = refs[0], refs[5:]
    out_ref, dq_ref, dk_ref, dv_ref, dgate_ref, entering, leaving, sums_scr, tot_scr = refs
    step = pl.program_id(0)
    heads = first_ref.shape[0]
    block = out_ref.shape[1]
    chunks = block // CHUNK
    num_chunks = fac_ref.shape[0] // 8
    scale = head_width ** (-0.5)

    def arrived(head):
        low = ctx_ref[0] < half_ctx
        first, second = first_ref[head], second_ref[head] + last_ref[head]
        return jnp.where(low, first, second), jnp.where(low, second, first)

    @pl.when(step == 0)
    def _():
        gain_columns = jnp.transpose(jnp.concatenate([gain_ref[...], gain_ref[...]], axis=0))
        entering[...] = jnp.zeros_like(entering)
        leaving[...] = jnp.zeros_like(leaving)
        for head in range(heads):
            row = part * heads + head
            own = slice(head * head_width, (head + 1) * head_width)
            gain = gain_columns[:, row : row + 1]
            state, later = arrived(head)
            entering[own, own] = (state * (gain * scale)).astype(BF16)
            leaving[own, own] = (later * gain).astype(BF16)

    products, results = [], {}
    group = slice(part * heads * head_width, (part + 1) * heads * head_width)

    def rows_of(chunk):
        return pl.ds(pl.multiple_of(step * block + chunk * CHUNK, CHUNK), CHUNK)

    for chunk in range(chunks):
        rows = rows_of(chunk)
        products.append(
            (
                dot_nn(q_ref[0, rows, group], entering[...]),
                dot_nt(cot_ref[0, rows, group], entering[...]),
                dot_nn(k_ref[0, rows, group], leaving[...]),
                dot_nt(v_ref[0, rows, group], leaving[...]),
            )
        )
    for chunk in range(chunks):
        number = step * chunks + chunk
        columns = jnp.transpose(fac_ref[pl.ds(pl.multiple_of(number * 8, 8), 8), :])
        rows = rows_of(chunk)
        for head in range(heads):
            row = part * heads + head
            lanes = slice(head * head_width, (head + 1) * head_width)
            wide = slice(row * head_width, (row + 1) * head_width)
            from_start, to_end = columns[:, row : row + 1], columns[:, 4 + row : 5 + row]
            across_all, dq_all, written_all, dk_all = products[chunk]
            across = across_all[:, lanes] * from_start
            written = written_all[:, lanes] * to_end
            kept = written * v_ref[0, rows, wide].astype(F32)
            balance = jnp.sum(
                across * cot_ref[0, rows, wide].astype(F32) - kept, axis=1, keepdims=True
            )
            results[chunk, head] = (
                (out_in[0, rows, lanes].astype(F32) + across).astype(BF16),
                (dq_in[0, rows, lanes].astype(F32) + dq_all[:, lanes] * from_start).astype(BF16),
                (dk_in[0, rows, lanes].astype(F32) + dk_all[:, lanes] * to_end).astype(BF16),
                (dv_in[0, rows, lanes].astype(F32) + written).astype(BF16),
                later_sums(balance),
                jnp.sum(kept, axis=0, keepdims=True),
            )
    for chunk in range(chunks):
        number = step * chunks + chunk
        rows = slice(chunk * CHUNK, (chunk + 1) * CHUNK)
        for head in range(heads):
            lanes = slice(head * head_width, (head + 1) * head_width)
            out, dq, dk, dv, sums, kept = results[chunk, head]
            out_ref[0, rows, lanes] = out
            dq_ref[0, rows, lanes] = dq
            dk_ref[0, rows, lanes] = dk
            dv_ref[0, rows, lanes] = dv
            sums_scr[number, head : head + 1, :] = sums
            tot_scr[number, head : head + 1, :] = kept

    @pl.when(step == pl.num_programs(0) - 1)
    def _():
        last = fac_ref[(num_chunks - 1) * 8 : num_chunks * 8, CHUNK - 1 : CHUNK]
        kept = tot_scr[0]
        for chunk in range(1, num_chunks):
            kept = kept + tot_scr[chunk]
        base = jnp.sum(kept, axis=1, keepdims=True)
        constants = []
        for head in range(heads):
            row = part * heads + head
            state, later = arrived(head)
            gain_columns = jnp.transpose(
                jnp.concatenate([gain_ref[...], gain_ref[...]], axis=0)
            )
            product = total_of(state * later * gain_columns[:, row : row + 1])
            constants.append(product * last[row : row + 1])
        base = base[:heads] + jnp.concatenate(constants, axis=0)
        if part > 0:
            dgate_ref[0, : part * heads, :] = before_ref[0]
        own = slice(part * heads, (part + 1) * heads)
        for chunk in range(num_chunks - 1, -1, -1):
            lanes = slice(chunk * CHUNK, (chunk + 1) * CHUNK)
            sums = sums_scr[chunk, :heads, :]
            dgate_ref[0, own, lanes] = dgate_in[0, :, lanes] + sums + base
            base = base + sums[:, 0:1]


def shards(queries, keys_raw, values, gates, lengths, key_gain, cotangent):
    tokens, width = queries.shape[1:]
    all_heads, head_width = key_gain.shape
    heads = all_heads // PARTS
    part_width = width // PARTS
    num_chunks = tokens // CHUNK
    rows = num_chunks * 8
    block = min(256, tokens)
    steps = tokens // block
    ctx = lax.axis_index("ctx")
    count = lax.axis_size("ctx")
    middle = count // 2 - 1
    ctx_scalar = jnp.reshape(ctx, (1,)).astype(jnp.int32)

    def stream_spec(part):
        return pl.BlockSpec((1, block, part_width), lambda i: (0, i, part))

    def whole(array):
        zeros = (0,) * len(array.shape)
        return pl.BlockSpec(array.shape, lambda *_: zeros)

    def shape_of(*shape, dtype=F32):
        return jax.ShapeDtypeStruct(shape, dtype)

    smem = pl.BlockSpec(memory_space=pltpu.SMEM)
    vmem = pl.BlockSpec(memory_space=pltpu.VMEM)
    table = shape_of(rows, CHUNK)
    states = shape_of(heads, head_width, head_width)
    decays = shape_of(heads, 1, head_width)
    part_gates = shape_of(1, heads, tokens)
    product = 2 * tokens * part_width * head_width

    def ends():
        held = shape_of(1, tokens, width, dtype=BF16)
        outs = [held] * 4 + [states] * (2 * PARTS) + [decays] * PARTS + [table] * 3
        return pl.pallas_call(
            functools.partial(ends_kernel, head_width, count // 2),
            in_specs=[smem, smem, vmem] + [pl.BlockSpec(memory_space=pltpu.HBM)] * 4,
            out_specs=[vmem] * len(outs),
            out_shape=outs,
            scratch_shapes=[
                pltpu.VMEM((rows, CHUNK), F32),
                pltpu.SemaphoreType.DMA((steps, 4)),
            ],
            compiler_params=pltpu.CompilerParams(vmem_limit_bytes=56 << 20),
            cost_estimate=pl.CostEstimate(
                flops=2 * product * PARTS, bytes_accessed=8 * tokens * width, transcendentals=0
            ),
            name="shard_ends",
        )(lengths, ctx_scalar, gates, queries, keys_raw, values, cotangent)

    def local(part, arrays, gain, cum, fac):
        wide = shape_of(1, tokens, part_width, dtype=BF16)
        return pl.pallas_call(
            functools.partial(local_kernel, head_width, part),
            in_specs=[vmem] * 7,
            out_specs=[vmem] * 6,
            out_shape=[wide] * 4 + [part_gates, shape_of(heads, head_width)],
            scratch_shapes=[
                pltpu.VMEM((num_chunks, heads, head_width, head_width), BF16),
                pltpu.VMEM((heads, head_width, head_width), F32),
            ],
            compiler_params=pltpu.CompilerParams(vmem_limit_bytes=24 << 20),
            cost_estimate=pl.CostEstimate(
                flops=12 * product, bytes_accessed=16 * tokens * part_width, transcendentals=0
            ),
            name=f"local_{part}",
        )(*arrays, gain, cum, fac)

    def merge(part, arrivals, locals_, done):
        full_gates = shape_of(1, (part + 1) * heads, tokens)
        extra, extra_specs, aliases = [], [], {}
        if part > 0:
            extra = [done[4]] + list(done[:4])
            extra_specs = [vmem] + [pl.BlockSpec(memory_space=pl.ANY)] * 4
            aliases = {16 + i: i for i in range(4)}
        return pl.pallas_call(
            functools.partial(merge_kernel, head_width, part, count // 2),
            grid=(steps,),
            in_specs=[smem] + [vmem] * 14 + extra_specs,
            out_specs=[stream_spec(part)] * 4 + [whole(full_gates)],
            out_shape=[shape_of(1, tokens, width, dtype=BF16)] * 4 + [full_gates],
            scratch_shapes=[
                pltpu.VMEM((part_width, part_width), BF16),
                pltpu.VMEM((part_width, part_width), BF16),
                pltpu.VMEM((num_chunks, 8, CHUNK), F32),
                pltpu.VMEM((num_chunks, 8, CHUNK), F32),
            ],
            input_output_aliases=aliases,
            compiler_params=pltpu.CompilerParams(vmem_limit_bytes=24 << 20),
            cost_estimate=pl.CostEstimate(
                flops=4 * product, bytes_accessed=24 * tokens * part_width, transcendentals=0
            ),
            name=f"merge_{part}",
        )(ctx_scalar, *streams, key_gain, shard_fac, *arrivals, *locals_, *extra)

    results = ends()
    streams, results = results[:4], results[4:]
    near, far, decay = (results[i * PARTS : (i + 1) * PARTS] for i in range(3))
    cum, chunk_fac, shard_fac = results[3 * PARTS :]
    sent = [[] for _ in range(PARTS)]
    arrived = [[] for _ in range(PARTS)]
    local_parts = [None] * PARTS

    def send(part, hop):
        payload = near[part] if hop <= middle else far[part]
        if hop > 0:
            payload = payload + decay[part] * arrived[part][-1]
        sent[part].append(payload)
        arrived[part].append(
            lax.ppermute(
                payload, "ctx", [(hop, hop + 1), (count - 1 - hop, count - 2 - hop)]
            )
        )

    for part in range(PARTS):
        send(part, 0)
    for hop in range(count - 1):
        if hop < PARTS:
            local_cum = cum
            if hop > 0:
                local_cum, _ = lax.optimization_barrier((cum, arrived[0][hop - 1]))
            local_parts[hop] = list(local(hop, streams, key_gain, local_cum, chunk_fac))
            if hop + 1 < count - 1:
                local_parts[hop][5], arrived[0][-1] = lax.optimization_barrier(
                    (local_parts[hop][5], arrived[0][-1])
                )
        if hop + 1 < count - 1:
            for part in range(PARTS):
                send(part, hop + 1)

    terms = []
    for part in range(PARTS):
        crossed = jnp.sum(sent[part][middle] * arrived[part][middle], axis=2)
        term = local_parts[part][5] + jnp.where(ctx == middle, crossed, 0.0)
        if middle > 0:
            term = term + jnp.sum(sum(arrived[part][:middle]) * far[part], axis=2)
        terms.append(term)
    gain_term = jnp.concatenate(terms, axis=0)
    half = head_width // lax.axis_size("dp")
    dp = lax.axis_index("dp")
    away = jnp.where(dp == 0, gain_term[:, half:], gain_term[:, :half])
    kept = jnp.where(dp == 0, gain_term[:, :half], gain_term[:, half:])
    grad_gain = kept + lax.ppermute(away, "dp", [(0, 1), (1, 0)])

    done, reach = None, 1
    for part in range(PARTS):
        others = jnp.zeros_like(grad_gain)
        if reach < count:
            others = lax.ppermute(grad_gain, "ctx", [(i, i ^ reach) for i in range(count)])
            reach *= 2
        zeros = jnp.zeros(states.shape, F32)
        first = sum(arrived[part][:middle], zeros) if middle != 1 else arrived[part][0]
        second = sum(arrived[part][middle:-1], zeros) if middle != 1 else arrived[part][1]
        done = list(merge(part, (first, second, arrived[part][-1]), local_parts[part][:5], done))
        if part < PARTS - 1:
            done[4], others = lax.optimization_barrier((done[4], others))
        grad_gain = grad_gain + others
    while reach < count:
        grad_gain = grad_gain + lax.ppermute(
            grad_gain, "ctx", [(i, i ^ reach) for i in range(count)]
        )
        reach *= 2
    return (*done, grad_gain)


def solution(mesh):
    wide = P("dp", "ctx", "head")
    narrow = P("dp", "head", "ctx")
    return jax.shard_map(
        shards,
        mesh=mesh,
        in_specs=(wide, wide, wide, narrow, P("dp", None), P("head", None), wide),
        out_specs=(wide, wide, wide, wide, narrow, P("head", "dp")),
        check_vma=False,
    )
```

```python
import functools
import math

import jax
import jax.numpy as jnp
from jax import lax
from jax.experimental import pallas as pl
from jax.experimental.pallas import tpu as pltpu
from jax.sharding import PartitionSpec as P

CHUNK = 128
PARTS = 2
UNROLL = 4
PRECISE = lax.Precision.HIGHEST
F32 = jnp.float32
BF16 = jnp.bfloat16
LOG2E = math.log2(math.e)


def dot_nn(a, b, precision=None):
    return lax.dot_general(
        a, b, (((1,), (0,)), ((), ())), precision=precision, preferred_element_type=F32
    )


def dot_nt(a, b):
    return lax.dot_general(a, b, (((1,), (1,)), ((), ())), preferred_element_type=F32)


def dot_tn(a, b):
    return lax.dot_general(a, b, (((0,), (0,)), ((), ())), preferred_element_type=F32)


def iota(shape, dim):
    return lax.broadcasted_iota(jnp.int32, shape, dim)


def total_of(array):
    return jnp.sum(jnp.sum(array, axis=0, keepdims=True), axis=1, keepdims=True)


def later_sums(column):
    kept = iota((CHUNK, CHUNK), 0) >= iota((CHUNK, CHUNK), 1)
    return jnp.sum(jnp.where(kept, column, 0.0), axis=0, keepdims=True)


def decay_tables(lengths_ref, ctx_ref, gates_ref, spread, cum_ref, chunk_fac_ref, shard_fac_ref):
    rows = cum_ref.shape[0]
    num_chunks = rows // 8
    tokens = num_chunks * CHUNK
    for chunk in range(num_chunks):
        part = gates_ref[0, :, chunk * CHUNK : (chunk + 1) * CHUNK]
        spread[chunk * 8 : chunk * 8 + 4, :] = part
        spread[chunk * 8 + 4 : chunk * 8 + 8, :] = part
    gates = spread[...] * LOG2E
    lane_a, lane_b = iota((CHUNK, CHUNK), 0), iota((CHUNK, CHUNK), 1)
    prefix = dot_nn(gates, (lane_a <= lane_b).astype(F32), PRECISE)
    suffix = dot_nn(gates, (lane_a > lane_b).astype(F32), PRECISE)
    totals = jnp.broadcast_to(prefix[:, CHUNK - 1 : CHUNK], (rows, CHUNK))
    row_a, row_b = iota((rows, rows), 0), iota((rows, rows), 1)
    same = (row_a % 8) == (row_b % 8)
    outside = ((row_a % 8 < 4) & (row_b // 8 < row_a // 8)) | (
        (row_a % 8 >= 4) & (row_b // 8 > row_a // 8)
    )
    others = dot_nn((same & outside).astype(F32), totals, PRECISE)

    first = ctx_ref[0] * tokens
    chunk_first = first + (iota((rows, CHUNK), 0) // 8) * CHUNK
    positions = chunk_first + iota((rows, CHUNK), 1)
    from_start = iota((rows, CHUNK), 0) % 8 < 4
    chunk_anchor = jnp.where(from_start, chunk_first - 1, chunk_first + (CHUNK - 1))
    segment = jnp.zeros((rows, CHUNK), F32)
    chunk_segment = jnp.zeros((rows, CHUNK), F32)
    shard_before = jnp.float32(0)
    shard_last = jnp.float32(0)
    start = jnp.int32(0)
    for doc in range(lengths_ref.shape[1]):
        segment += jnp.where(positions >= start, 1.0, 0.0)
        chunk_segment += jnp.where(chunk_anchor >= start, 1.0, 0.0)
        shard_before += jnp.where(first > start, 1.0, 0.0)
        shard_last += jnp.where(first + (tokens - 1) >= start, 1.0, 0.0)
        start += lengths_ref[0, doc]
    cum_ref[...] = jnp.where(from_start, prefix, segment)
    exponent = jnp.where(from_start, prefix, suffix)
    chunk_fac_ref[...] = jnp.where(
        segment == chunk_segment, jnp.exp2(jnp.minimum(exponent, 0.0)), 0.0
    )
    keep = segment == jnp.where(from_start, shard_before, shard_last)
    shard_fac_ref[...] = jnp.where(keep, jnp.exp2(jnp.minimum(exponent + others, 0.0)), 0.0)


def ends_kernel(head_width, half_ctx, *refs):
    lengths_ref, ctx_ref, gates_ref = refs[:3]
    sources, targets = refs[3:7], refs[7:11]
    near_refs, far_refs, decay_refs = (
        refs[11 + i * PARTS : 11 + (i + 1) * PARTS] for i in range(3)
    )
    cum_ref, chunk_fac_ref, shard_fac_ref, spread, sems = refs[11 + 3 * PARTS :]
    q_ref, k_ref, v_ref, cot_ref = targets
    heads = near_refs[0].shape[0]
    rows = shard_fac_ref.shape[0]
    steps = sems.shape[0]
    block = q_ref.shape[1] // steps
    chunks = block // CHUNK

    def copies(step):
        at = pl.ds(step * block, block)
        return [
            pltpu.make_async_copy(source.at[:, at, :], target.at[:, at, :], sems.at[step, i])
            for i, (source, target) in enumerate(zip(sources, targets))
        ]

    for step in range(steps):
        for i, copy in enumerate(copies(step)):
            copy.start(priority=i % 2)
    decay_tables(lengths_ref, ctx_ref, gates_ref, spread, cum_ref, chunk_fac_ref, shard_fac_ref)
    for part in range(PARTS):
        for head in range(heads):
            row = rows - 8 + part * heads + head
            decay_refs[part][head] = jnp.broadcast_to(
                shard_fac_ref[row : row + 1, CHUNK - 1 : CHUNK], (1, head_width)
            )

    def turned(ref, step, row, scale):
        pieces = []
        head = row % 4
        for chunk in range(step * chunks, (step + 1) * chunks):
            factor = shard_fac_ref[chunk * 8 + row : chunk * 8 + row + 1, :]
            piece = jnp.transpose(
                ref[
                    0,
                    chunk * CHUNK : (chunk + 1) * CHUNK,
                    head * head_width : (head + 1) * head_width,
                ]
            )
            pieces.append((piece.astype(F32) * (factor * scale)).astype(BF16))
        return jnp.concatenate(pieces, axis=1)

    ends, grads = {}, {}
    for step in range(steps):
        for copy in copies(step):
            copy.wait()
        at = slice(step * block, (step + 1) * block)
        for row in range(PARTS * heads):
            lanes = slice(row * head_width, (row + 1) * head_width)
            end = dot_nn(turned(k_ref, step, 4 + row, 1.0), v_ref[0, at, lanes])
            grad = dot_nn(turned(q_ref, step, row, head_width ** (-0.5)), cot_ref[0, at, lanes])
            ends[row] = ends[row] + end if step else end
            grads[row] = grads[row] + grad if step else grad
    low = ctx_ref[0] < half_ctx
    for part in range(PARTS):
        for head in range(heads):
            row = part * heads + head
            near_refs[part][head] = jnp.where(low, ends[row], grads[row])
            far_refs[part][head] = jnp.where(low, grads[row], ends[row])


def local_kernel(
    head_width, part, q_ref, k_ref, v_ref, cot_ref, gain_ref, cum_ref, fac_ref,
    out_ref, dq_ref, dk_ref, dv_ref, dgate_ref, dgain_ref, leaving, state,
):
    heads = state.shape[0]
    num_chunks = leaving.shape[0]
    scale = head_width ** (-0.5)
    unroll = math.gcd(num_chunks, UNROLL)

    def lanes_of(head):
        return slice((part * heads + head) * head_width, (part * heads + head + 1) * head_width)

    def own_lanes(head):
        return slice(head * head_width, (head + 1) * head_width)

    def rows_of(chunk):
        return pl.ds(pl.multiple_of(chunk * CHUNK, CHUNK), CHUNK)

    def table(ref, chunk):
        return ref[pl.ds(pl.multiple_of(chunk * 8, 8), 8), :]

    pairs = [(at, head) for at in range(unroll) for head in range(heads)]

    def backward(chunks):
        facs = [table(fac_ref, chunk) for chunk in chunks]
        added = {}
        for at, head in pairs:
            row = part * heads + head
            rows, lanes = rows_of(chunks[at]), lanes_of(head)
            turned = jnp.transpose(q_ref[0, rows, lanes]).astype(F32)
            turned = (turned * (facs[at][row : row + 1, :] * scale)).astype(BF16)
            added[at, head] = dot_nn(turned, cot_ref[0, rows, lanes])
        for head in range(heads):
            row = part * heads + head
            held = state[head]
            for at in range(unroll):
                leaving[chunks[at], head] = held.astype(BF16)
                held = held * facs[at][row : row + 1, CHUNK - 1 : CHUNK] + added[at, head]
            state[head] = held

    def forward(chunks):
        facs = [table(fac_ref, chunk) for chunk in chunks]
        cums = [table(cum_ref, chunk) for chunk in chunks]
        fac_columns = [jnp.transpose(fac) for fac in facs]
        cum_columns = [jnp.transpose(cum) for cum in cums]
        causal = iota((CHUNK, CHUNK), 0) >= iota((CHUNK, CHUNK), 1)
        limits = [
            jnp.where((columns[:, 4:5] == cum[4:5, :]) & causal, math.log2(scale), -1e30)
            for columns, cum in zip(cum_columns, cums)
        ]
        cum_columns = [columns + math.log2(scale) for columns in cum_columns]
        q, k, v, cot, k_raw, k_decayed, q_decayed, later = ({} for _ in range(8))
        from_start, to_end, added, held, entering = ({} for _ in range(5))
        for key in pairs:
            at, head = key
            row = part * heads + head
            rows, lanes = rows_of(chunks[at]), lanes_of(head)
            q[key], v[key], cot[key] = q_ref[0, rows, lanes], v_ref[0, rows, lanes], cot_ref[0, rows, lanes]
            later[key] = leaving[chunks[at], head]
            k_raw[key] = k_ref[0, rows, lanes].astype(F32)
            k_wide = k_raw[key] * gain_ref[row : row + 1, :]
            k[key] = k_wide.astype(BF16)
            from_start[key] = fac_columns[at][:, row : row + 1] * scale
            to_end[key] = fac_columns[at][:, 4 + row : 5 + row]
            k_decayed[key] = (k_wide * to_end[key]).astype(BF16)
            q_decayed[key] = (q[key].astype(F32) * from_start[key]).astype(BF16)
            added[key] = dot_tn(k_decayed[key], v[key])
        for head in range(heads):
            row = part * heads + head
            now = state[head]
            for at in range(unroll):
                held[at, head] = now
                entering[at, head] = now.astype(BF16)
                now = now * facs[at][row : row + 1, CHUNK - 1 : CHUNK] + added[at, head]
            held[unroll, head] = now
            state[head] = now
        by_cot, scores, written = {}, {}, {}
        for key in pairs:
            by_cot[key] = dot_nt(cot[key], jnp.concatenate([v[key], entering[key]], axis=0))
            scores[key] = dot_nt(q[key], k[key])
            written[key] = dot_nt(v[key], later[key])
        weights, grad_scores = {}, {}
        for key in pairs:
            at, head = key
            row = part * heads + head
            decays = jnp.exp2(
                jnp.minimum(cum_columns[at][:, row : row + 1] - cums[at][row : row + 1, :], limits[at])
            )
            weights[key] = (scores[key] * decays).astype(BF16)
            grad_scores[key] = (by_cot[key][:, :CHUNK] * decays).astype(BF16)
        out, dq, dk, dv = {}, {}, {}, {}
        for key in pairs:
            out[key] = dot_nn(
                jnp.concatenate([weights[key], q_decayed[key]], axis=1),
                jnp.concatenate([v[key], entering[key]], axis=0),
            )
            dv[key] = dot_nn(
                jnp.concatenate([jnp.transpose(weights[key]), k_decayed[key]], axis=1),
                jnp.concatenate([cot[key], later[key]], axis=0),
            )
            dq[key] = dot_nn(grad_scores[key], k[key]) + by_cot[key][:, CHUNK:] * from_start[key]
            dk[key] = dot_tn(grad_scores[key], q[key]) + written[key] * to_end[key]
        gate_rows, gain_rows = {}, {}
        for key in pairs:
            at, head = key
            balance = jnp.sum(
                out[key] * cot[key].astype(F32) - dv[key] * v[key].astype(F32),
                axis=1, keepdims=True,
            )
            gate_rows[key] = later_sums(balance) + total_of(
                held[at + 1, head] * later[key].astype(F32)
            )
            gain_rows[key] = jnp.sum(dk[key] * k_raw[key], axis=0, keepdims=True)
        for key in pairs:
            at, head = key
            row = part * heads + head
            rows, own = rows_of(chunks[at]), own_lanes(head)
            out_ref[0, rows, own] = out[key].astype(BF16)
            dq_ref[0, rows, own] = dq[key].astype(BF16)
            dv_ref[0, rows, own] = dv[key].astype(BF16)
            dk_ref[0, rows, own] = (dk[key] * gain_ref[row : row + 1, :]).astype(BF16)
            dgate_ref[0, head : head + 1, rows] = gate_rows[key]
        for head in range(heads):
            dgain_ref[head : head + 1, :] += sum(gain_rows[at, head] for at in range(unroll))

    state[...] = jnp.zeros_like(state)

    def backward_group(index, carry):
        backward([num_chunks - 1 - (index * unroll + at) for at in range(unroll)])
        return carry

    lax.fori_loop(0, num_chunks // unroll, backward_group, 0)
    state[...] = jnp.zeros_like(state)
    dgain_ref[...] = jnp.zeros_like(dgain_ref)

    def forward_group(index, carry):
        forward([index * unroll + at for at in range(unroll)])
        return carry

    lax.fori_loop(0, num_chunks // unroll, forward_group, 0)


def merge_kernel(head_width, part, half_ctx, *refs):
    (ctx_ref, q_ref, k_ref, v_ref, cot_ref, gain_ref, fac_ref, first_ref, second_ref, last_ref,
     out_in, dq_in, dk_in, dv_in, dgate_in) = refs[:15]
    refs = refs[15:]
    if part > 0:
        before_ref, refs = refs[0], refs[5:]
    targets, dgate_ref, staged, entering, leaving, sems = refs[:4], *refs[4:]
    heads = first_ref.shape[0]
    steps = sems.shape[0]
    num_chunks = fac_ref.shape[0] // 8
    chunks = num_chunks // steps
    block = chunks * CHUNK
    scale = head_width ** (-0.5)
    group = slice(part * heads * head_width, (part + 1) * heads * head_width)
    partials = (out_in, dq_in, dk_in, dv_in)

    def copies(step):
        at = pl.ds(step * block, block)
        return [
            pltpu.make_async_copy(
                staged.at[i, at, :], target.at[0, at, group], sems.at[step, i]
            )
            for i, target in enumerate(targets)
        ]

    def arrived(head):
        low = ctx_ref[0] < half_ctx
        first, second = first_ref[head], second_ref[head] + last_ref[head]
        return jnp.where(low, first, second), jnp.where(low, second, first)

    gain_columns = jnp.transpose(jnp.concatenate([gain_ref[...], gain_ref[...]], axis=0))
    entering[...] = jnp.zeros_like(entering)
    leaving[...] = jnp.zeros_like(leaving)
    last = fac_ref[(num_chunks - 1) * 8 : num_chunks * 8, CHUNK - 1 : CHUNK]
    constants = []
    for head in range(heads):
        row = part * heads + head
        own = slice(head * head_width, (head + 1) * head_width)
        gain = gain_columns[:, row : row + 1]
        state, later = arrived(head)
        state = state * gain
        entering[own, own] = (state * scale).astype(BF16)
        leaving[own, own] = (later * gain).astype(BF16)
        constants.append(total_of(state * later) * last[row : row + 1])

    gate_sums, kept_sums = {}, {}
    for step in range(steps):
        numbers = range(step * chunks, (step + 1) * chunks)
        products, results = {}, {}
        for number in numbers:
            rows = slice(number * CHUNK, (number + 1) * CHUNK)
            products[number] = (
                dot_nn(q_ref[0, rows, group], entering[...]),
                dot_nt(cot_ref[0, rows, group], entering[...]),
                dot_nt(v_ref[0, rows, group], leaving[...]),
                dot_nn(k_ref[0, rows, group], leaving[...]),
            )
        for number in numbers:
            columns = jnp.transpose(fac_ref[number * 8 : number * 8 + 8, :])
            rows = slice(number * CHUNK, (number + 1) * CHUNK)
            for head in range(heads):
                row = part * heads + head
                lanes = slice(head * head_width, (head + 1) * head_width)
                wide = slice(row * head_width, (row + 1) * head_width)
                from_start, to_end = columns[:, row : row + 1], columns[:, 4 + row : 5 + row]
                across, dq, dk, written = (
                    product[:, lanes] * factor
                    for product, factor in zip(
                        products[number], (from_start, from_start, to_end, to_end)
                    )
                )
                results[number, head] = [
                    (partial[0, rows, lanes].astype(F32) + added).astype(BF16)
                    for partial, added in zip(partials, (across, dq, dk, written))
                ]
                kept = written * v_ref[0, rows, wide].astype(F32)
                balance = jnp.sum(
                    across * cot_ref[0, rows, wide].astype(F32) - kept, axis=1, keepdims=True
                )
                gate_sums[number, head] = later_sums(balance)
                kept_sums[number, head] = jnp.sum(kept, axis=0, keepdims=True)
        for number in numbers:
            rows = slice(number * CHUNK, (number + 1) * CHUNK)
            for head in range(heads):
                lanes = slice(head * head_width, (head + 1) * head_width)
                for i in range(4):
                    staged[i, rows, lanes] = results[number, head][i]
        for i, copy in enumerate(copies(step)):
            copy.start(priority=i % 2)

    if part > 0:
        dgate_ref[0, : part * heads, :] = before_ref[0]
    for head in range(heads):
        row = part * heads + head
        kept = sum(kept_sums[number, head] for number in range(num_chunks))
        base = jnp.sum(kept, axis=1, keepdims=True) + constants[head]
        for number in range(num_chunks - 1, -1, -1):
            lanes = slice(number * CHUNK, (number + 1) * CHUNK)
            sums = gate_sums[number, head]
            dgate_ref[0, row : row + 1, lanes] = (
                dgate_in[0, head : head + 1, lanes] + sums + base
            )
            base = base + sums[:, 0:1]
    for step in range(steps):
        for copy in copies(step):
            copy.wait()


def shards(queries, keys_raw, values, gates, lengths, key_gain, cotangent):
    tokens, width = queries.shape[1:]
    all_heads, head_width = key_gain.shape
    heads = all_heads // PARTS
    part_width = width // PARTS
    num_chunks = tokens // CHUNK
    rows = num_chunks * 8
    block = min(256, tokens)
    steps = tokens // block
    ctx = lax.axis_index("ctx")
    count = lax.axis_size("ctx")
    middle = count // 2 - 1
    ctx_scalar = jnp.reshape(ctx, (1,)).astype(jnp.int32)

    def shape_of(*shape, dtype=F32):
        return jax.ShapeDtypeStruct(shape, dtype)

    smem = pl.BlockSpec(memory_space=pltpu.SMEM)
    vmem = pl.BlockSpec(memory_space=pltpu.VMEM)
    table = shape_of(rows, CHUNK)
    states = shape_of(heads, head_width, head_width)
    decays = shape_of(heads, 1, head_width)
    part_gates = shape_of(1, heads, tokens)
    product = 2 * tokens * part_width * head_width

    def ends():
        held = shape_of(1, tokens, width, dtype=BF16)
        outs = [held] * 4 + [states] * (2 * PARTS) + [decays] * PARTS + [table] * 3
        return pl.pallas_call(
            functools.partial(ends_kernel, head_width, count // 2),
            in_specs=[smem, smem, vmem] + [pl.BlockSpec(memory_space=pltpu.HBM)] * 4,
            out_specs=[vmem] * len(outs),
            out_shape=outs,
            scratch_shapes=[
                pltpu.VMEM((rows, CHUNK), F32),
                pltpu.SemaphoreType.DMA((steps, 4)),
            ],
            compiler_params=pltpu.CompilerParams(vmem_limit_bytes=49 << 20),
            cost_estimate=pl.CostEstimate(
                flops=2 * product * PARTS, bytes_accessed=8 * tokens * width, transcendentals=0
            ),
            name="shard_ends",
        )(lengths, ctx_scalar, gates, queries, keys_raw, values, cotangent)

    def local(part, arrays, gain, cum, fac):
        wide = shape_of(1, tokens, part_width, dtype=BF16)
        return pl.pallas_call(
            functools.partial(local_kernel, head_width, part),
            in_specs=[vmem] * 7,
            out_specs=[vmem] * 6,
            out_shape=[wide] * 4 + [part_gates, shape_of(heads, head_width)],
            scratch_shapes=[
                pltpu.VMEM((num_chunks, heads, head_width, head_width), BF16),
                pltpu.VMEM((heads, head_width, head_width), F32),
            ],
            compiler_params=pltpu.CompilerParams(vmem_limit_bytes=24 << 20),
            cost_estimate=pl.CostEstimate(
                flops=12 * product, bytes_accessed=16 * tokens * part_width, transcendentals=0
            ),
            name=f"local_{part}",
        )(*arrays, gain, cum, fac)

    def merge(part, arrivals, locals_, done):
        full_gates = shape_of(1, (part + 1) * heads, tokens)
        extra, extra_specs, aliases = [], [], {}
        if part > 0:
            extra = [done[4]] + list(done[:4])
            extra_specs = [vmem] + [pl.BlockSpec(memory_space=pl.ANY)] * 4
            aliases = {16 + i: i for i in range(4)}
        return pl.pallas_call(
            functools.partial(merge_kernel, head_width, part, count // 2),
            in_specs=[smem] + [vmem] * 14 + extra_specs,
            out_specs=[pl.BlockSpec(memory_space=pl.ANY)] * 4 + [vmem],
            out_shape=[shape_of(1, tokens, width, dtype=BF16)] * 4 + [full_gates],
            scratch_shapes=[
                pltpu.VMEM((4, tokens, part_width), BF16),
                pltpu.VMEM((part_width, part_width), BF16),
                pltpu.VMEM((part_width, part_width), BF16),
                pltpu.SemaphoreType.DMA((steps, 4)),
            ],
            input_output_aliases=aliases,
            compiler_params=pltpu.CompilerParams(vmem_limit_bytes=24 << 20),
            cost_estimate=pl.CostEstimate(
                flops=4 * product, bytes_accessed=24 * tokens * part_width, transcendentals=0
            ),
            name=f"merge_{part}",
        )(ctx_scalar, *streams, key_gain, shard_fac, *arrivals, *locals_, *extra)

    results = ends()
    streams, results = results[:4], results[4:]
    near, far, decay = (results[i * PARTS : (i + 1) * PARTS] for i in range(3))
    cum, chunk_fac, shard_fac = results[3 * PARTS :]
    sent = [[] for _ in range(PARTS)]
    arrived = [[] for _ in range(PARTS)]
    local_parts = [None] * PARTS

    def send(part, hop):
        payload = near[part] if hop <= middle else far[part]
        if hop > 0:
            payload = payload + decay[part] * arrived[part][-1]
        sent[part].append(payload)
        arrived[part].append(
            lax.ppermute(
                payload, "ctx", [(hop, hop + 1), (count - 1 - hop, count - 2 - hop)]
            )
        )

    for part in range(PARTS):
        send(part, 0)
    for hop in range(count - 1):
        if hop < PARTS:
            local_cum = cum
            if hop > 0:
                local_cum, _ = lax.optimization_barrier((cum, arrived[0][hop - 1]))
            local_parts[hop] = list(local(hop, streams, key_gain, local_cum, chunk_fac))
            if hop + 1 < count - 1:
                local_parts[hop][5], arrived[0][-1] = lax.optimization_barrier(
                    (local_parts[hop][5], arrived[0][-1])
                )
        if hop + 1 < count - 1:
            for part in range(PARTS):
                send(part, hop + 1)

    terms = []
    for part in range(PARTS):
        crossed = jnp.sum(sent[part][middle] * arrived[part][middle], axis=2)
        term = local_parts[part][5] + jnp.where(ctx == middle, crossed, 0.0)
        if middle > 0:
            term = term + jnp.sum(sum(arrived[part][:middle]) * far[part], axis=2)
        terms.append(term)
    gain_term = jnp.concatenate(terms, axis=0)
    half = head_width // lax.axis_size("dp")
    dp = lax.axis_index("dp")
    away = jnp.where(dp == 0, gain_term[:, half:], gain_term[:, :half])
    kept = jnp.where(dp == 0, gain_term[:, :half], gain_term[:, half:])
    grad_gain = kept + lax.ppermute(away, "dp", [(0, 1), (1, 0)])

    done, reach = None, 1
    for part in range(PARTS):
        others = jnp.zeros_like(grad_gain)
        if reach < count:
            others = lax.ppermute(grad_gain, "ctx", [(i, i ^ reach) for i in range(count)])
            reach *= 2
        zeros = jnp.zeros(states.shape, F32)
        first = sum(arrived[part][:middle], zeros) if middle != 1 else arrived[part][0]
        second = sum(arrived[part][middle:-1], zeros) if middle != 1 else arrived[part][1]
        done = list(merge(part, (first, second, arrived[part][-1]), local_parts[part][:5], done))
        if part < PARTS - 1:
            done[4], others = lax.optimization_barrier((done[4], others))
        grad_gain = grad_gain + others
    while reach < count:
        grad_gain = grad_gain + lax.ppermute(
            grad_gain, "ctx", [(i, i ^ reach) for i in range(count)]
        )
        reach *= 2
    return (*done, grad_gain)


def solution(mesh):
    wide = P("dp", "ctx", "head")
    narrow = P("dp", "head", "ctx")
    return jax.shard_map(
        shards,
        mesh=mesh,
        in_specs=(wide, wide, wide, narrow, P("dp", None), P("head", None), wide),
        out_specs=(wide, wide, wide, wide, narrow, P("head", "dp")),
        check_vma=False,
    )
```

```python
import functools
import math

import jax
import jax.numpy as jnp
from jax import lax
from jax.experimental import pallas as pl
from jax.experimental.pallas import tpu as pltpu
from jax.sharding import PartitionSpec as P

CHUNK = 128
PARTS = 2
UNROLL = 4
ENDS_GRANT = 53 << 20
GRANT = 53 << 20
PRECISE = lax.Precision.HIGHEST
F32 = jnp.float32
BF16 = jnp.bfloat16
LOG2E = math.log2(math.e)


def dot_nn(a, b, precision=None):
    return lax.dot_general(
        a, b, (((1,), (0,)), ((), ())), precision=precision, preferred_element_type=F32
    )


def dot_nt(a, b):
    return lax.dot_general(a, b, (((1,), (1,)), ((), ())), preferred_element_type=F32)


def dot_tn(a, b):
    return lax.dot_general(a, b, (((0,), (0,)), ((), ())), preferred_element_type=F32)


def iota(shape, dim):
    return lax.broadcasted_iota(jnp.int32, shape, dim)


def total_of(array):
    return jnp.sum(jnp.sum(array, axis=0, keepdims=True), axis=1, keepdims=True)


def later_sums(column):
    kept = iota((CHUNK, CHUNK), 0) >= iota((CHUNK, CHUNK), 1)
    return jnp.sum(jnp.where(kept, column, 0.0), axis=0, keepdims=True)


def decay_tables(docs, ctx_ref, small_ref, spread, cum_ref, chunk_fac_ref, shard_fac_ref):
    rows = cum_ref.shape[0]
    num_chunks = rows // 8
    tokens = num_chunks * CHUNK
    for chunk in range(num_chunks):
        part = small_ref[:, chunk * CHUNK : (chunk + 1) * CHUNK]
        spread[chunk * 8 : chunk * 8 + 4, :] = part
        spread[chunk * 8 + 4 : chunk * 8 + 8, :] = part
    gates = spread[...] * LOG2E
    lane_a, lane_b = iota((CHUNK, CHUNK), 0), iota((CHUNK, CHUNK), 1)
    prefix = dot_nn(gates, (lane_a <= lane_b).astype(F32), PRECISE)
    suffix = dot_nn(gates, (lane_a > lane_b).astype(F32), PRECISE)
    totals = jnp.broadcast_to(prefix[:, CHUNK - 1 : CHUNK], (rows, CHUNK))
    row_a, row_b = iota((rows, rows), 0), iota((rows, rows), 1)
    same = (row_a % 8) == (row_b % 8)
    outside = ((row_a % 8 < 4) & (row_b // 8 < row_a // 8)) | (
        (row_a % 8 >= 4) & (row_b // 8 > row_a // 8)
    )
    others = dot_nn((same & outside).astype(F32), totals, PRECISE)

    first = ctx_ref[0] * tokens
    chunk_first = first + (iota((rows, CHUNK), 0) // 8) * CHUNK
    from_start = iota((rows, CHUNK), 0) % 8 < 4
    chunk_anchor = jnp.where(from_start, chunk_first - 1, chunk_first + (CHUNK - 1)).astype(F32)
    shard_anchor = jnp.where(from_start, first - 1, first + (tokens - 1)).astype(F32)
    positions = (chunk_first + iota((rows, CHUNK), 1)).astype(F32)
    segment = jnp.zeros((rows, CHUNK), F32)
    chunk_segment = jnp.zeros((rows, CHUNK), F32)
    shard_segment = jnp.zeros((rows, CHUNK), F32)
    begin = small_ref.shape[1] - CHUNK
    for doc in range(docs):
        start = small_ref[0:1, begin + doc : begin + doc + 1]
        segment += jnp.where(positions >= start, 1.0, 0.0)
        chunk_segment += jnp.where(chunk_anchor >= start, 1.0, 0.0)
        shard_segment += jnp.where(shard_anchor >= start, 1.0, 0.0)
    cum_ref[...] = jnp.where(from_start, prefix, segment)
    exponent = jnp.where(from_start, prefix, suffix)
    chunk_fac_ref[...] = jnp.where(
        segment == chunk_segment, jnp.exp2(jnp.minimum(exponent, 0.0)), 0.0
    )
    keep = segment == shard_segment
    shard_fac_ref[...] = jnp.where(keep, jnp.exp2(jnp.minimum(exponent + others, 0.0)), 0.0)


def ends_kernel(head_width, docs, half_ctx, *refs):
    ctx_ref, small_ref = refs[:2]
    sources = refs[2:6]
    near_refs, far_refs, decay_refs = (
        refs[6 + i * PARTS : 6 + (i + 1) * PARTS] for i in range(3)
    )
    cum_ref, chunk_fac_ref, shard_fac_ref, gain_ref, held, spread, sems = refs[6 + 3 * PARTS :]
    q_ref, k_ref, v_ref, cot_ref = (held.at[pl.ds(i, 1)] for i in range(4))
    heads = near_refs[0].shape[0]
    rows = shard_fac_ref.shape[0]
    steps = sems.shape[0]
    block = held.shape[1] // steps
    chunks = block // CHUNK

    def copies(step):
        at = pl.ds(step * block, block)
        return [
            pltpu.make_async_copy(source.at[0, at, :], held.at[i, at, :], sems.at[step, i])
            for i, source in enumerate(sources)
        ]

    for step in range(steps):
        for i, copy in enumerate(copies(step)):
            copy.start(priority=i % 2)
    decay_tables(docs, ctx_ref, small_ref, spread, cum_ref, chunk_fac_ref, shard_fac_ref)
    tokens = held.shape[1]
    gain_ref[...] = small_ref[:, tokens : tokens + head_width]
    for part in range(PARTS):
        for head in range(heads):
            row = rows - 8 + part * heads + head
            decay_refs[part][head] = jnp.broadcast_to(
                shard_fac_ref[row : row + 1, CHUNK - 1 : CHUNK], (1, head_width)
            )

    def turned(ref, step, row, scale):
        pieces = []
        head = row % 4
        for chunk in range(step * chunks, (step + 1) * chunks):
            factor = shard_fac_ref[chunk * 8 + row : chunk * 8 + row + 1, :]
            piece = jnp.transpose(
                ref[
                    0,
                    chunk * CHUNK : (chunk + 1) * CHUNK,
                    head * head_width : (head + 1) * head_width,
                ]
            )
            pieces.append((piece.astype(F32) * (factor * scale)).astype(BF16))
        return jnp.concatenate(pieces, axis=1)

    ends, grads = {}, {}
    for step in range(steps):
        for copy in copies(step):
            copy.wait()
        at = slice(step * block, (step + 1) * block)
        for row in range(PARTS * heads):
            lanes = slice(row * head_width, (row + 1) * head_width)
            end = dot_nn(turned(k_ref, step, 4 + row, 1.0), v_ref[0, at, lanes])
            grad = dot_nn(turned(q_ref, step, row, head_width ** (-0.5)), cot_ref[0, at, lanes])
            ends[row] = ends[row] + end if step else end
            grads[row] = grads[row] + grad if step else grad
    low = ctx_ref[0] < half_ctx
    for part in range(PARTS):
        for head in range(heads):
            row = part * heads + head
            near_refs[part][head] = jnp.where(low, ends[row], grads[row])
            far_refs[part][head] = jnp.where(low, grads[row], ends[row])


def local_kernel(
    head_width, part, q_src, k_src, v_src, cot_src, gain_ref, cum_ref, fac_ref,
    target, dgate_ref, dgain_ref, held_in, staged, leaving, state, in_sems, out_sems,
):
    q_ref, k_ref, v_ref, cot_ref = (held_in.at[pl.ds(i, 1)] for i in range(4))
    out_ref, dq_ref, dk_ref, dv_ref = (staged.at[pl.ds(i, 1)] for i in range(4))
    heads = state.shape[0]
    num_chunks = leaving.shape[0]
    scale = head_width ** (-0.5)
    unroll = math.gcd(num_chunks, UNROLL)

    groups = num_chunks // unroll
    size = unroll * CHUNK
    wide = slice(part * heads * head_width, (part + 1) * heads * head_width)

    def copy_in(i, group):
        at = pl.ds(pl.multiple_of(group * size, size), size)
        source = (q_src, k_src, v_src, cot_src)[i]
        return pltpu.make_async_copy(
            source.at[0, at, wide], held_in.at[i, at, :], in_sems.at[i, group]
        )

    def copy_out(group):
        at = pl.ds(pl.multiple_of(group * size, size), size)
        return pltpu.make_async_copy(
            staged.at[:, at, :], target.at[:, at, :], out_sems.at[group]
        )

    for group in range(groups - 1, -1, -1):
        copy_in(0, group).start(priority=0)
        copy_in(3, group).start(priority=1)
    for group in range(groups):
        copy_in(1, group).start(priority=0)
        copy_in(2, group).start(priority=1)

    def lanes_of(head):
        return slice(head * head_width, (head + 1) * head_width)

    def rows_of(chunk):
        return pl.ds(pl.multiple_of(chunk * CHUNK, CHUNK), CHUNK)

    def table(ref, chunk):
        return ref[pl.ds(pl.multiple_of(chunk * 8, 8), 8), :]

    pairs = [(at, head) for at in range(unroll) for head in range(heads)]

    def backward(chunks):
        facs = [table(fac_ref, chunk) for chunk in chunks]
        added = {}
        for at, head in pairs:
            row = part * heads + head
            rows, lanes = rows_of(chunks[at]), lanes_of(head)
            turned = jnp.transpose(q_ref[0, rows, lanes]).astype(F32)
            turned = (turned * (facs[at][row : row + 1, :] * scale)).astype(BF16)
            added[at, head] = dot_nn(turned, cot_ref[0, rows, lanes])
        for head in range(heads):
            row = part * heads + head
            held = state[head]
            for at in range(unroll):
                leaving[chunks[at], head] = held.astype(BF16)
                held = held * facs[at][row : row + 1, CHUNK - 1 : CHUNK] + added[at, head]
            state[head] = held

    def forward(chunks):
        facs = [table(fac_ref, chunk) for chunk in chunks]
        cums = [table(cum_ref, chunk) for chunk in chunks]
        fac_columns = [jnp.transpose(fac) for fac in facs]
        cum_columns = [jnp.transpose(cum) for cum in cums]
        causal = iota((CHUNK, CHUNK), 0) >= iota((CHUNK, CHUNK), 1)
        limits = [
            jnp.where((columns[:, 4:5] == cum[4:5, :]) & causal, math.log2(scale), -1e30)
            for columns, cum in zip(cum_columns, cums)
        ]
        cum_columns = [columns + math.log2(scale) for columns in cum_columns]
        q, k, v, cot, k_raw, k_decayed, q_decayed, later = ({} for _ in range(8))
        from_start, to_end, added, held, entering = ({} for _ in range(5))
        for key in pairs:
            at, head = key
            row = part * heads + head
            rows, lanes = rows_of(chunks[at]), lanes_of(head)
            q[key], v[key], cot[key] = q_ref[0, rows, lanes], v_ref[0, rows, lanes], cot_ref[0, rows, lanes]
            later[key] = leaving[chunks[at], head]
            k_raw[key] = k_ref[0, rows, lanes].astype(F32)
            k_wide = k_raw[key] * gain_ref[row : row + 1, :]
            k[key] = k_wide.astype(BF16)
            from_start[key] = fac_columns[at][:, row : row + 1] * scale
            to_end[key] = fac_columns[at][:, 4 + row : 5 + row]
            k_decayed[key] = (k_wide * to_end[key]).astype(BF16)
            q_decayed[key] = (q[key].astype(F32) * from_start[key]).astype(BF16)
            added[key] = dot_tn(k_decayed[key], v[key])
        for head in range(heads):
            row = part * heads + head
            now = state[head]
            for at in range(unroll):
                held[at, head] = now
                entering[at, head] = now.astype(BF16)
                now = now * facs[at][row : row + 1, CHUNK - 1 : CHUNK] + added[at, head]
            held[unroll, head] = now
            state[head] = now
        by_cot, scores, written = {}, {}, {}
        for key in pairs:
            by_cot[key] = dot_nt(cot[key], jnp.concatenate([v[key], entering[key]], axis=0))
            scores[key] = dot_nt(q[key], k[key])
            written[key] = dot_nt(v[key], later[key])
        weights, grad_scores = {}, {}
        for key in pairs:
            at, head = key
            row = part * heads + head
            decays = jnp.exp2(
                jnp.minimum(cum_columns[at][:, row : row + 1] - cums[at][row : row + 1, :], limits[at])
            )
            weights[key] = (scores[key] * decays).astype(BF16)
            grad_scores[key] = (by_cot[key][:, :CHUNK] * decays).astype(BF16)
        out, dq, dk, dv = {}, {}, {}, {}
        for key in pairs:
            out[key] = dot_nn(
                jnp.concatenate([weights[key], q_decayed[key]], axis=1),
                jnp.concatenate([v[key], entering[key]], axis=0),
            )
            dv[key] = dot_nn(
                jnp.concatenate([jnp.transpose(weights[key]), k_decayed[key]], axis=1),
                jnp.concatenate([cot[key], later[key]], axis=0),
            )
            dq[key] = dot_nn(grad_scores[key], k[key]) + by_cot[key][:, CHUNK:] * from_start[key]
            dk[key] = dot_tn(grad_scores[key], q[key]) + written[key] * to_end[key]
        gate_rows, gain_rows = {}, {}
        for key in pairs:
            at, head = key
            balance = jnp.sum(
                out[key] * cot[key].astype(F32) - dv[key] * v[key].astype(F32),
                axis=1, keepdims=True,
            )
            gate_rows[key] = later_sums(balance) + total_of(
                held[at + 1, head] * later[key].astype(F32)
            )
            gain_rows[key] = jnp.sum(dk[key] * k_raw[key], axis=0, keepdims=True)
        for key in pairs:
            at, head = key
            row = part * heads + head
            rows, own = rows_of(chunks[at]), lanes_of(head)
            out_ref[0, rows, own] = out[key].astype(BF16)
            dq_ref[0, rows, own] = dq[key].astype(BF16)
            dv_ref[0, rows, own] = dv[key].astype(BF16)
            dk_ref[0, rows, own] = (dk[key] * gain_ref[row : row + 1, :]).astype(BF16)
            dgate_ref[0, head : head + 1, rows] = gate_rows[key]
        for head in range(heads):
            dgain_ref[head : head + 1, :] += sum(gain_rows[at, head] for at in range(unroll))

    state[...] = jnp.zeros_like(state)

    def backward_group(index, carry):
        copy_in(0, groups - 1 - index).wait()
        copy_in(3, groups - 1 - index).wait()
        backward([num_chunks - 1 - (index * unroll + at) for at in range(unroll)])
        return carry

    lax.fori_loop(0, groups, backward_group, 0)
    state[...] = jnp.zeros_like(state)
    dgain_ref[...] = jnp.zeros_like(dgain_ref)

    def forward_group(index, carry):
        copy_in(1, index).wait()
        copy_in(2, index).wait()
        forward([index * unroll + at for at in range(unroll)])
        copy_out(index).start()
        return carry

    lax.fori_loop(0, groups, forward_group, 0)
    for group in range(groups):
        copy_out(group).wait()


def merge_kernel(head_width, part, half_ctx, *refs):
    sources = refs[:5]
    ctx_ref, gain_ref, fac_ref, first_ref, second_ref, last_ref, dgate_in = refs[5:12]
    refs = refs[12:]
    if part > 0:
        before_ref, refs = refs[0], refs[5:]
    targets, dgate_ref, held, staged, entering, leaving, in_sems, sems = refs[:4], *refs[4:]
    heads = first_ref.shape[0]
    steps = sems.shape[0]
    num_chunks = fac_ref.shape[0] // 8
    chunks = num_chunks // steps
    block = chunks * CHUNK
    scale = head_width ** (-0.5)
    group = slice(part * heads * head_width, (part + 1) * heads * head_width)

    def copies_in(step):
        at = pl.ds(step * block, block)
        return [
            pltpu.make_async_copy(
                source.at[0, at, group], held.at[i, at, :], in_sems.at[step, i]
            )
            for i, source in enumerate(sources[:4])
        ] + [
            pltpu.make_async_copy(
                sources[4].at[:, at, :], staged.at[:, at, :], in_sems.at[step, 4]
            )
        ]

    def copies(step):
        at = pl.ds(step * block, block)
        return [
            pltpu.make_async_copy(
                staged.at[i, at, :], target.at[0, at, group], sems.at[step, i]
            )
            for i, target in enumerate(targets)
        ]

    def arrived(head):
        low = ctx_ref[0] < half_ctx
        first, second = first_ref[head], second_ref[head] + last_ref[head]
        return jnp.where(low, first, second), jnp.where(low, second, first)

    for step in range(steps):
        for i, copy in enumerate(copies_in(step)):
            copy.start(priority=i % 2)
    gain_columns = jnp.transpose(jnp.concatenate([gain_ref[...], gain_ref[...]], axis=0))
    entering[...] = jnp.zeros_like(entering)
    leaving[...] = jnp.zeros_like(leaving)
    last = fac_ref[(num_chunks - 1) * 8 : num_chunks * 8, CHUNK - 1 : CHUNK]
    constants = []
    for head in range(heads):
        row = part * heads + head
        own = slice(head * head_width, (head + 1) * head_width)
        gain = gain_columns[:, row : row + 1]
        state, later = arrived(head)
        state = state * gain
        entering[own, own] = (state * scale).astype(BF16)
        leaving[own, own] = (later * gain).astype(BF16)
        constants.append(total_of(state * later) * last[row : row + 1])

    gate_sums, kept_sums = {}, {}
    for step in range(steps):
        numbers = range(step * chunks, (step + 1) * chunks)
        products, results = {}, {}
        for copy in copies_in(step):
            copy.wait()
        for number in numbers:
            rows = slice(number * CHUNK, (number + 1) * CHUNK)
            products[number] = (
                dot_nn(held[0, rows, :], entering[...]),
                dot_nt(held[3, rows, :], entering[...]),
                dot_nt(held[2, rows, :], leaving[...]),
                dot_nn(held[1, rows, :], leaving[...]),
            )
        for number in numbers:
            columns = jnp.transpose(fac_ref[number * 8 : number * 8 + 8, :])
            rows = slice(number * CHUNK, (number + 1) * CHUNK)
            for head in range(heads):
                row = part * heads + head
                lanes = slice(head * head_width, (head + 1) * head_width)
                from_start, to_end = columns[:, row : row + 1], columns[:, 4 + row : 5 + row]
                across, dq, dk, written = (
                    product[:, lanes] * factor
                    for product, factor in zip(
                        products[number], (from_start, from_start, to_end, to_end)
                    )
                )
                results[number, head] = [
                    (staged[i, rows, lanes].astype(F32) + added).astype(BF16)
                    for i, added in enumerate((across, dq, dk, written))
                ]
                kept = written * held[2, rows, lanes].astype(F32)
                balance = jnp.sum(
                    across * held[3, rows, lanes].astype(F32) - kept, axis=1, keepdims=True
                )
                gate_sums[number, head] = later_sums(balance)
                kept_sums[number, head] = jnp.sum(kept, axis=0, keepdims=True)
        for number in numbers:
            rows = slice(number * CHUNK, (number + 1) * CHUNK)
            for head in range(heads):
                lanes = slice(head * head_width, (head + 1) * head_width)
                for i in range(4):
                    staged[i, rows, lanes] = results[number, head][i]
        for i, copy in enumerate(copies(step)):
            copy.start(priority=i % 2)

    if part > 0:
        dgate_ref[0, : part * heads, :] = before_ref[0]
    for head in range(heads):
        row = part * heads + head
        kept = sum(kept_sums[number, head] for number in range(num_chunks))
        base = jnp.sum(kept, axis=1, keepdims=True) + constants[head]
        for number in range(num_chunks - 1, -1, -1):
            lanes = slice(number * CHUNK, (number + 1) * CHUNK)
            sums = gate_sums[number, head]
            dgate_ref[0, row : row + 1, lanes] = (
                dgate_in[0, head : head + 1, lanes] + sums + base
            )
            base = base + sums[:, 0:1]
    for step in range(steps):
        for copy in copies(step):
            copy.wait()


def shards(queries, keys_raw, values, gates, lengths, key_gain, cotangent):
    tokens, width = queries.shape[1:]
    all_heads, head_width = key_gain.shape
    heads = all_heads // PARTS
    part_width = width // PARTS
    num_chunks = tokens // CHUNK
    rows = num_chunks * 8
    block = min(256, tokens)
    steps = tokens // block
    ctx = lax.axis_index("ctx")
    count = lax.axis_size("ctx")
    middle = count // 2 - 1
    docs = lengths.shape[1]
    earlier = jnp.arange(docs)[:, None] < jnp.arange(CHUNK)[None, :]
    starts = jnp.sum(jnp.where(earlier, lengths[0][:, None], 0), axis=0).astype(F32)
    small = jnp.concatenate(
        [gates[0], key_gain, jnp.broadcast_to(starts[None], (all_heads, CHUNK))], axis=1
    )
    ctx_scalar = jnp.reshape(ctx, (1,)).astype(jnp.int32)

    def shape_of(*shape, dtype=F32):
        return jax.ShapeDtypeStruct(shape, dtype)

    hbm = pl.BlockSpec(memory_space=pltpu.HBM)
    smem = pl.BlockSpec(memory_space=pltpu.SMEM)
    vmem = pl.BlockSpec(memory_space=pltpu.VMEM)
    table = shape_of(rows, CHUNK)
    states = shape_of(heads, head_width, head_width)
    decays = shape_of(heads, 1, head_width)
    part_gates = shape_of(1, heads, tokens)
    partials = shape_of(4, tokens, part_width, dtype=BF16)
    streams = (queries, keys_raw, values, cotangent)
    product = 2 * tokens * part_width * head_width

    def ends():
        outs = [states] * (2 * PARTS) + [decays] * PARTS + [table] * 3
        outs.append(shape_of(all_heads, head_width))
        return pl.pallas_call(
            functools.partial(ends_kernel, head_width, lengths.shape[1], count // 2),
            in_specs=[smem, vmem] + [hbm] * 4,
            out_specs=[vmem] * len(outs),
            out_shape=outs,
            scratch_shapes=[
                pltpu.VMEM((4, tokens, width), BF16),
                pltpu.VMEM((rows, CHUNK), F32),
                pltpu.SemaphoreType.DMA((steps, 4)),
            ],
            compiler_params=pltpu.CompilerParams(vmem_limit_bytes=ENDS_GRANT),
            cost_estimate=pl.CostEstimate(
                flops=2 * product * PARTS, bytes_accessed=8 * tokens * width, transcendentals=0
            ),
            name="shard_ends",
        )(ctx_scalar, small, *streams)

    def local(part, gain, cum, fac):
        groups = num_chunks // math.gcd(num_chunks, UNROLL)
        return pl.pallas_call(
            functools.partial(local_kernel, head_width, part),
            in_specs=[hbm] * 4 + [vmem] * 3,
            out_specs=[hbm] + [vmem] * 2,
            out_shape=[partials, part_gates, shape_of(heads, head_width)],
            scratch_shapes=[
                pltpu.VMEM((4, tokens, part_width), BF16),
                pltpu.VMEM((4, tokens, part_width), BF16),
                pltpu.VMEM((num_chunks, heads, head_width, head_width), BF16),
                pltpu.VMEM((heads, head_width, head_width), F32),
                pltpu.SemaphoreType.DMA((4, groups)),
                pltpu.SemaphoreType.DMA((groups,)),
            ],
            compiler_params=pltpu.CompilerParams(vmem_limit_bytes=GRANT),
            cost_estimate=pl.CostEstimate(
                flops=12 * product, bytes_accessed=16 * tokens * part_width, transcendentals=0
            ),
            name=f"local_{part}",
        )(*streams, gain, cum, fac)

    def merge(part, arrivals, local_part, done):
        full_gates = shape_of(1, (part + 1) * heads, tokens)
        extra, extra_specs, aliases = [], [], {}
        if part > 0:
            extra = [done[4]] + list(done[:4])
            extra_specs = [vmem] + [hbm] * 4
            aliases = {13 + i: i for i in range(4)}
        return pl.pallas_call(
            functools.partial(merge_kernel, head_width, part, count // 2),
            in_specs=[hbm] * 5 + [smem] + [vmem] * 6 + extra_specs,
            out_specs=[hbm] * 4 + [vmem],
            out_shape=[shape_of(1, tokens, width, dtype=BF16)] * 4 + [full_gates],
            scratch_shapes=[
                pltpu.VMEM((4, tokens, part_width), BF16),
                pltpu.VMEM((4, tokens, part_width), BF16),
                pltpu.VMEM((part_width, part_width), BF16),
                pltpu.VMEM((part_width, part_width), BF16),
                pltpu.SemaphoreType.DMA((steps, 5)),
                pltpu.SemaphoreType.DMA((steps, 4)),
            ],
            input_output_aliases=aliases,
            compiler_params=pltpu.CompilerParams(vmem_limit_bytes=GRANT),
            cost_estimate=pl.CostEstimate(
                flops=4 * product, bytes_accessed=24 * tokens * part_width, transcendentals=0
            ),
            name=f"merge_{part}",
        )(
            *streams, local_part[0], ctx_scalar, gain, shard_fac, *arrivals, local_part[1], *extra
        )

    results = ends()
    near, far, decay = (results[i * PARTS : (i + 1) * PARTS] for i in range(3))
    cum, chunk_fac, shard_fac, gain = results[3 * PARTS :]
    sent = [[] for _ in range(PARTS)]
    arrived = [[] for _ in range(PARTS)]
    local_parts = [None] * PARTS

    def send(part, hop):
        payload = near[part] if hop <= middle else far[part]
        if hop > 0:
            payload = payload + decay[part] * arrived[part][-1]
        sent[part].append(payload)
        arrived[part].append(
            lax.ppermute(
                payload, "ctx", [(hop, hop + 1), (count - 1 - hop, count - 2 - hop)]
            )
        )

    for part in range(PARTS):
        send(part, 0)
    for hop in range(count - 1):
        if hop < PARTS:
            local_cum = cum
            if hop > 0:
                local_cum, _ = lax.optimization_barrier((cum, arrived[0][hop - 1]))
            local_parts[hop] = list(local(hop, gain, local_cum, chunk_fac))
            if hop + 1 < count - 1:
                local_parts[hop][2], arrived[0][-1] = lax.optimization_barrier(
                    (local_parts[hop][2], arrived[0][-1])
                )
        if hop + 1 < count - 1:
            for part in range(PARTS):
                send(part, hop + 1)

    terms = []
    for part in range(PARTS):
        crossed = jnp.sum(sent[part][middle] * arrived[part][middle], axis=2)
        term = local_parts[part][2] + jnp.where(ctx == middle, crossed, 0.0)
        if middle > 0:
            term = term + jnp.sum(sum(arrived[part][:middle]) * far[part], axis=2)
        terms.append(term)
    gain_term = jnp.concatenate(terms, axis=0)
    half = head_width // lax.axis_size("dp")
    dp = lax.axis_index("dp")
    away = jnp.where(dp == 0, gain_term[:, half:], gain_term[:, :half])
    kept = jnp.where(dp == 0, gain_term[:, :half], gain_term[:, half:])
    grad_gain = kept + lax.ppermute(away, "dp", [(0, 1), (1, 0)])

    done, reach = None, 1
    for part in range(PARTS):
        others = jnp.zeros_like(grad_gain)
        if reach < count:
            others = lax.ppermute(grad_gain, "ctx", [(i, i ^ reach) for i in range(count)])
            reach *= 2
        zeros = jnp.zeros(states.shape, F32)
        first = sum(arrived[part][:middle], zeros) if middle != 1 else arrived[part][0]
        second = sum(arrived[part][middle:-1], zeros) if middle != 1 else arrived[part][1]
        done = list(merge(part, (first, second, arrived[part][-1]), local_parts[part], done))
        if part < PARTS - 1:
            done[4], others = lax.optimization_barrier((done[4], others))
        grad_gain = grad_gain + others
    while reach < count:
        grad_gain = grad_gain + lax.ppermute(
            grad_gain, "ctx", [(i, i ^ reach) for i in range(count)]
        )
        reach *= 2
    return (*done, grad_gain)


def solution(mesh):
    wide = P("dp", "ctx", "head")
    narrow = P("dp", "head", "ctx")
    return jax.shard_map(
        shards,
        mesh=mesh,
        in_specs=(wide, wide, wide, narrow, P("dp", None), P("head", None), wide),
        out_specs=(wide, wide, wide, wide, narrow, P("head", "dp")),
        check_vma=False,
    )
```

```python
import functools
import math

import jax
import jax.numpy as jnp
from jax import lax
from jax.experimental import pallas as pl
from jax.experimental.pallas import tpu as pltpu
from jax.sharding import PartitionSpec as P

CHUNK = 128
PARTS = 2
UNROLL = 4
PRECISE = lax.Precision.HIGHEST
F32 = jnp.float32
BF16 = jnp.bfloat16
LOG2E = math.log2(math.e)


def dot_nn(a, b, precision=None):
    return lax.dot_general(
        a, b, (((1,), (0,)), ((), ())), precision=precision, preferred_element_type=F32
    )


def dot_nt(a, b):
    return lax.dot_general(a, b, (((1,), (1,)), ((), ())), preferred_element_type=F32)


def dot_tn(a, b):
    return lax.dot_general(a, b, (((0,), (0,)), ((), ())), preferred_element_type=F32)


def iota(shape, dim):
    return lax.broadcasted_iota(jnp.int32, shape, dim)


def total_of(array):
    return jnp.sum(jnp.sum(array, axis=0, keepdims=True), axis=1, keepdims=True)


def later_sums(column):
    kept = iota((CHUNK, CHUNK), 0) >= iota((CHUNK, CHUNK), 1)
    return jnp.sum(jnp.where(kept, column, 0.0), axis=0, keepdims=True)


def decay_tables(docs, place_ref, small_ref, spread, cum_ref, chunk_fac_ref, shard_fac_ref):
    rows = cum_ref.shape[0]
    num_chunks = rows // 8
    tokens = num_chunks * CHUNK
    for chunk in range(num_chunks):
        part = small_ref[:, chunk * CHUNK : (chunk + 1) * CHUNK]
        spread[chunk * 8 : chunk * 8 + 4, :] = part
        spread[chunk * 8 + 4 : chunk * 8 + 8, :] = part
    gates = spread[...] * LOG2E
    lane_a, lane_b = iota((CHUNK, CHUNK), 0), iota((CHUNK, CHUNK), 1)
    prefix = dot_nn(gates, (lane_a <= lane_b).astype(F32), PRECISE)
    suffix = dot_nn(gates, (lane_a > lane_b).astype(F32), PRECISE)
    totals = jnp.broadcast_to(prefix[:, CHUNK - 1 : CHUNK], (rows, CHUNK))
    row_a, row_b = iota((rows, rows), 0), iota((rows, rows), 1)
    same = (row_a % 8) == (row_b % 8)
    outside = ((row_a % 8 < 4) & (row_b // 8 < row_a // 8)) | (
        (row_a % 8 >= 4) & (row_b // 8 > row_a // 8)
    )
    others = dot_nn((same & outside).astype(F32), totals, PRECISE)

    first = place_ref[0] * tokens
    chunk_first = first + (iota((rows, CHUNK), 0) // 8) * CHUNK
    from_start = iota((rows, CHUNK), 0) % 8 < 4
    chunk_anchor = jnp.where(from_start, chunk_first - 1, chunk_first + (CHUNK - 1)).astype(F32)
    shard_anchor = jnp.where(from_start, first - 1, first + (tokens - 1)).astype(F32)
    positions = (chunk_first + iota((rows, CHUNK), 1)).astype(F32)
    segment = jnp.zeros((rows, CHUNK), F32)
    chunk_segment = jnp.zeros((rows, CHUNK), F32)
    shard_segment = jnp.zeros((rows, CHUNK), F32)
    begin = small_ref.shape[1] - CHUNK
    start = jnp.zeros((1, 1), F32)
    for doc in range(docs):
        segment += jnp.where(positions >= start, 1.0, 0.0)
        chunk_segment += jnp.where(chunk_anchor >= start, 1.0, 0.0)
        shard_segment += jnp.where(shard_anchor >= start, 1.0, 0.0)
        start = start + small_ref[0:1, begin + doc : begin + doc + 1]
    cum_ref[...] = jnp.where(from_start, prefix, segment)
    exponent = jnp.where(from_start, prefix, suffix)
    chunk_fac_ref[...] = jnp.where(
        segment == chunk_segment, jnp.exp2(jnp.minimum(exponent, 0.0)), 0.0
    )
    keep = segment == shard_segment
    shard_fac_ref[...] = jnp.where(keep, jnp.exp2(jnp.minimum(exponent + others, 0.0)), 0.0)


def ends_kernel(head_width, docs, half_ctx, *refs):
    place_ref, small_ref = refs[:2]
    sources = refs[2:6]
    near_refs, far_refs, decay_refs = (
        refs[6 + i * PARTS : 6 + (i + 1) * PARTS] for i in range(3)
    )
    (cum_ref, chunk_fac_ref, shard_fac_ref, gain_ref, flag_ref, q_ref, k_ref, v_ref, cot_ref,
     spread, sems) = refs[6 + 3 * PARTS :]
    heads = near_refs[0].shape[0]
    rows = shard_fac_ref.shape[0]
    steps = sems.shape[0]
    tokens = q_ref.shape[1]
    block = tokens // steps
    chunks = block // CHUNK

    def copies(step):
        at = pl.ds(step * block, block)
        return [
            pltpu.make_async_copy(source.at[:, at, :], target.at[:, at, :], sems.at[step, i])
            for i, (source, target) in enumerate(zip(sources, (q_ref, k_ref, v_ref, cot_ref)))
        ]

    for step in range(steps):
        for i, copy in enumerate(copies(step)):
            copy.start(priority=i % 2)
    decay_tables(docs, place_ref, small_ref, spread, cum_ref, chunk_fac_ref, shard_fac_ref)
    gain_ref[...] = small_ref[:, tokens : tokens + head_width]
    for part in range(PARTS):
        for head in range(heads):
            row = rows - 8 + part * heads + head
            decay_refs[part][head] = jnp.broadcast_to(
                shard_fac_ref[row : row + 1, CHUNK - 1 : CHUNK], (1, head_width)
            )

    def turned(ref, step, row, scale):
        pieces = []
        head = row % 4
        for chunk in range(step * chunks, (step + 1) * chunks):
            factor = shard_fac_ref[chunk * 8 + row : chunk * 8 + row + 1, :]
            piece = jnp.transpose(
                ref[
                    0,
                    chunk * CHUNK : (chunk + 1) * CHUNK,
                    head * head_width : (head + 1) * head_width,
                ]
            )
            pieces.append((piece.astype(F32) * (factor * scale)).astype(BF16))
        return jnp.concatenate(pieces, axis=1)

    ends, grads = {}, {}
    for step in range(steps):
        for copy in copies(step):
            copy.wait()
        at = slice(step * block, (step + 1) * block)
        for row in range(PARTS * heads):
            lanes = slice(row * head_width, (row + 1) * head_width)
            end = dot_nn(turned(k_ref, step, 4 + row, 1.0), v_ref[0, at, lanes])
            grad = dot_nn(turned(q_ref, step, row, head_width ** (-0.5)), cot_ref[0, at, lanes])
            ends[row] = ends[row] + end if step else end
            grads[row] = grads[row] + grad if step else grad
    middle = jnp.where(place_ref[0] == half_ctx - 1, 1.0, 0.0)
    flag_ref[...] = jnp.where(
        iota(flag_ref.shape, 0) == 0, middle, place_ref[1].astype(F32)
    )
    low = place_ref[0] < half_ctx
    for part in range(PARTS):
        for head in range(heads):
            row = part * heads + head
            near_refs[part][head] = jnp.where(low, ends[row], grads[row])
            far_refs[part][head] = jnp.where(low, grads[row], ends[row])


def local_kernel(
    head_width, part, q_ref, k_ref, v_ref, cot_ref, gain_ref, cum_ref, fac_ref,
    target, dgate_ref, dgain_ref, leaving, state,
):
    out_ref, dq_ref, dk_ref, dv_ref = (target.at[pl.ds(i, 1)] for i in range(4))
    heads = state.shape[0]
    num_chunks = leaving.shape[0]
    scale = head_width ** (-0.5)
    unroll = math.gcd(num_chunks, UNROLL)

    groups = num_chunks // unroll
    def wide_lanes(head):
        row = part * heads + head
        return slice(row * head_width, (row + 1) * head_width)

    def lanes_of(head):
        return slice(head * head_width, (head + 1) * head_width)

    def rows_of(chunk):
        return pl.ds(pl.multiple_of(chunk * CHUNK, CHUNK), CHUNK)

    def table(ref, chunk):
        return ref[pl.ds(pl.multiple_of(chunk * 8, 8), 8), :]

    pairs = [(at, head) for at in range(unroll) for head in range(heads)]

    def backward(chunks):
        facs = [table(fac_ref, chunk) for chunk in chunks]
        added = {}
        for at, head in pairs:
            row = part * heads + head
            rows, lanes = rows_of(chunks[at]), wide_lanes(head)
            turned = jnp.transpose(q_ref[0, rows, lanes]).astype(F32)
            turned = (turned * (facs[at][row : row + 1, :] * scale)).astype(BF16)
            added[at, head] = dot_nn(turned, cot_ref[0, rows, lanes])
        for head in range(heads):
            row = part * heads + head
            held = state[head]
            for at in range(unroll):
                leaving[chunks[at], head] = held.astype(BF16)
                held = held * facs[at][row : row + 1, CHUNK - 1 : CHUNK] + added[at, head]
            state[head] = held

    def forward(chunks):
        facs = [table(fac_ref, chunk) for chunk in chunks]
        cums = [table(cum_ref, chunk) for chunk in chunks]
        fac_columns = [jnp.transpose(fac) for fac in facs]
        cum_columns = [jnp.transpose(cum) for cum in cums]
        causal = iota((CHUNK, CHUNK), 0) >= iota((CHUNK, CHUNK), 1)
        limits = [
            jnp.where((columns[:, 4:5] == cum[4:5, :]) & causal, math.log2(scale), -1e30)
            for columns, cum in zip(cum_columns, cums)
        ]
        cum_columns = [columns + math.log2(scale) for columns in cum_columns]
        q, k, v, cot, k_raw, k_decayed, q_decayed, later = ({} for _ in range(8))
        from_start, to_end, added, held, entering = ({} for _ in range(5))
        for key in pairs:
            at, head = key
            row = part * heads + head
            rows, lanes = rows_of(chunks[at]), lanes_of(head)
            q[key], cot[key] = q_ref[0, rows, wide_lanes(head)], cot_ref[0, rows, wide_lanes(head)]
            v[key] = v_ref[0, rows, wide_lanes(head)]
            later[key] = leaving[chunks[at], head]
            k_raw[key] = k_ref[0, rows, wide_lanes(head)].astype(F32)
            k_wide = k_raw[key] * gain_ref[row : row + 1, :]
            k[key] = k_wide.astype(BF16)
            from_start[key] = fac_columns[at][:, row : row + 1] * scale
            to_end[key] = fac_columns[at][:, 4 + row : 5 + row]
            k_decayed[key] = (k_wide * to_end[key]).astype(BF16)
            q_decayed[key] = (q[key].astype(F32) * from_start[key]).astype(BF16)
            added[key] = dot_tn(k_decayed[key], v[key])
        for head in range(heads):
            row = part * heads + head
            now = state[head]
            for at in range(unroll):
                held[at, head] = now
                entering[at, head] = now.astype(BF16)
                now = now * facs[at][row : row + 1, CHUNK - 1 : CHUNK] + added[at, head]
            held[unroll, head] = now
            state[head] = now
        by_cot, scores, written = {}, {}, {}
        for key in pairs:
            by_cot[key] = dot_nt(cot[key], jnp.concatenate([v[key], entering[key]], axis=0))
            scores[key] = dot_nt(q[key], k[key])
            written[key] = dot_nt(v[key], later[key])
        weights, grad_scores = {}, {}
        for key in pairs:
            at, head = key
            row = part * heads + head
            decays = jnp.exp2(
                jnp.minimum(cum_columns[at][:, row : row + 1] - cums[at][row : row + 1, :], limits[at])
            )
            weights[key] = (scores[key] * decays).astype(BF16)
            grad_scores[key] = (by_cot[key][:, :CHUNK] * decays).astype(BF16)
        out, dq, dk, dv = {}, {}, {}, {}
        for key in pairs:
            out[key] = dot_nn(
                jnp.concatenate([weights[key], q_decayed[key]], axis=1),
                jnp.concatenate([v[key], entering[key]], axis=0),
            )
            dv[key] = dot_nn(
                jnp.concatenate([jnp.transpose(weights[key]), k_decayed[key]], axis=1),
                jnp.concatenate([cot[key], later[key]], axis=0),
            )
            dq[key] = dot_nn(grad_scores[key], k[key]) + by_cot[key][:, CHUNK:] * from_start[key]
            dk[key] = dot_tn(grad_scores[key], q[key]) + written[key] * to_end[key]
        gate_rows, gain_rows = {}, {}
        for key in pairs:
            at, head = key
            balance = jnp.sum(
                out[key] * cot[key].astype(F32) - dv[key] * v[key].astype(F32),
                axis=1, keepdims=True,
            )
            gate_rows[key] = later_sums(balance) + total_of(
                held[at + 1, head] * later[key].astype(F32)
            )
            gain_rows[key] = jnp.sum(dk[key] * k_raw[key], axis=0, keepdims=True)
        for key in pairs:
            at, head = key
            row = part * heads + head
            rows, own = rows_of(chunks[at]), lanes_of(head)
            out_ref[0, rows, own] = out[key].astype(BF16)
            dq_ref[0, rows, own] = dq[key].astype(BF16)
            dv_ref[0, rows, own] = dv[key].astype(BF16)
            dk_ref[0, rows, own] = (dk[key] * gain_ref[row : row + 1, :]).astype(BF16)
            dgate_ref[0, head : head + 1, rows] = gate_rows[key]
        for head in range(heads):
            dgain_ref[head : head + 1, :] += sum(gain_rows[at, head] for at in range(unroll))

    state[...] = jnp.zeros_like(state)

    def backward_group(index, carry):
        backward([num_chunks - 1 - (index * unroll + at) for at in range(unroll)])
        return carry

    lax.fori_loop(0, groups, backward_group, 0)
    state[...] = jnp.zeros_like(state)
    dgain_ref[...] = jnp.zeros_like(dgain_ref)

    def forward_group(index, carry):
        forward([index * unroll + at for at in range(unroll)])
        return carry

    lax.fori_loop(0, groups, forward_group, 0)


def merge_kernel(head_width, part, half_ctx, *refs):
    q_ref, k_ref, v_ref, cot_ref, partial_ref = refs[:5]
    place_ref, gain_ref, fac_ref, first_ref, second_ref, last_ref, dgate_in = refs[5:12]
    refs = refs[12:]
    if part > 0:
        before_ref, refs = refs[0], refs[5:]
    targets, dgate_ref, staged, entering, leaving, sems = refs[:4], *refs[4:]
    heads = first_ref.shape[0]
    steps = sems.shape[0]
    num_chunks = fac_ref.shape[0] // 8
    chunks = num_chunks // steps
    block = chunks * CHUNK
    scale = head_width ** (-0.5)
    group = slice(part * heads * head_width, (part + 1) * heads * head_width)

    def copies(step):
        at = pl.ds(step * block, block)
        return [
            pltpu.make_async_copy(
                staged.at[i, at, :], target.at[0, at, group], sems.at[step, i]
            )
            for i, target in enumerate(targets)
        ]

    def arrived(head):
        low = place_ref[0] < half_ctx
        first, second = first_ref[head], second_ref[head] + last_ref[head]
        return jnp.where(low, first, second), jnp.where(low, second, first)

    gain_columns = jnp.transpose(jnp.concatenate([gain_ref[...], gain_ref[...]], axis=0))
    entering[...] = jnp.zeros_like(entering)
    leaving[...] = jnp.zeros_like(leaving)
    last = fac_ref[(num_chunks - 1) * 8 : num_chunks * 8, CHUNK - 1 : CHUNK]
    constants = []
    for head in range(heads):
        row = part * heads + head
        own = slice(head * head_width, (head + 1) * head_width)
        gain = gain_columns[:, row : row + 1]
        state, later = arrived(head)
        state = state * gain
        entering[own, own] = (state * scale).astype(BF16)
        leaving[own, own] = (later * gain).astype(BF16)
        constants.append(total_of(state * later) * last[row : row + 1])

    gate_sums, kept_sums = {}, {}
    for step in range(steps):
        numbers = range(step * chunks, (step + 1) * chunks)
        products, results = {}, {}
        for number in numbers:
            rows = slice(number * CHUNK, (number + 1) * CHUNK)
            products[number] = (
                dot_nn(q_ref[0, rows, group], entering[...]),
                dot_nt(cot_ref[0, rows, group], entering[...]),
                dot_nt(v_ref[0, rows, group], leaving[...]),
                dot_nn(k_ref[0, rows, group], leaving[...]),
            )
        for number in numbers:
            columns = jnp.transpose(fac_ref[number * 8 : number * 8 + 8, :])
            rows = slice(number * CHUNK, (number + 1) * CHUNK)
            for head in range(heads):
                row = part * heads + head
                lanes = slice(head * head_width, (head + 1) * head_width)
                wide = slice(row * head_width, (row + 1) * head_width)
                from_start, to_end = columns[:, row : row + 1], columns[:, 4 + row : 5 + row]
                across, dq, dk, written = (
                    product[:, lanes] * factor
                    for product, factor in zip(
                        products[number], (from_start, from_start, to_end, to_end)
                    )
                )
                results[number, head] = [
                    (partial_ref[i, rows, lanes].astype(F32) + added).astype(BF16)
                    for i, added in enumerate((across, dq, dk, written))
                ]
                kept = written * v_ref[0, rows, wide].astype(F32)
                balance = jnp.sum(
                    across * cot_ref[0, rows, wide].astype(F32) - kept, axis=1, keepdims=True
                )
                gate_sums[number, head] = later_sums(balance)
                kept_sums[number, head] = jnp.sum(kept, axis=0, keepdims=True)
        for number in numbers:
            rows = slice(number * CHUNK, (number + 1) * CHUNK)
            for head in range(heads):
                lanes = slice(head * head_width, (head + 1) * head_width)
                for i in range(4):
                    staged[i, rows, lanes] = results[number, head][i]
        for i, copy in enumerate(copies(step)):
            copy.start(priority=i % 2)

    if part > 0:
        dgate_ref[0, : part * heads, :] = before_ref[0]
    for head in range(heads):
        row = part * heads + head
        kept = sum(kept_sums[number, head] for number in range(num_chunks))
        base = jnp.sum(kept, axis=1, keepdims=True) + constants[head]
        for number in range(num_chunks - 1, -1, -1):
            lanes = slice(number * CHUNK, (number + 1) * CHUNK)
            sums = gate_sums[number, head]
            dgate_ref[0, row : row + 1, lanes] = (
                dgate_in[0, head : head + 1, lanes] + sums + base
            )
            base = base + sums[:, 0:1]
    for step in range(steps):
        for copy in copies(step):
            copy.wait()


def shards(queries, keys_raw, values, gates, lengths, key_gain, cotangent):
    tokens, width = queries.shape[1:]
    all_heads, head_width = key_gain.shape
    heads = all_heads // PARTS
    part_width = width // PARTS
    num_chunks = tokens // CHUNK
    rows = num_chunks * 8
    block = min(256, tokens)
    steps = tokens // block
    ctx = lax.axis_index("ctx")
    count = lax.axis_size("ctx")
    middle = count // 2 - 1
    docs = lengths.shape[1]
    sizes = jnp.pad(lengths.astype(F32), ((0, all_heads - 1), (0, CHUNK - docs)))
    small = jnp.concatenate([gates[0], key_gain, sizes], axis=1)
    place = jnp.stack([ctx, lax.axis_index("dp")]).astype(jnp.int32)

    def shape_of(*shape, dtype=F32):
        return jax.ShapeDtypeStruct(shape, dtype)

    hbm = pl.BlockSpec(memory_space=pltpu.HBM)
    smem = pl.BlockSpec(memory_space=pltpu.SMEM)
    vmem = pl.BlockSpec(memory_space=pltpu.VMEM)
    table = shape_of(rows, CHUNK)
    states = shape_of(heads, head_width, head_width)
    decays = shape_of(heads, 1, head_width)
    part_gates = shape_of(1, heads, tokens)
    partials = shape_of(4, tokens, part_width, dtype=BF16)
    streams = (queries, keys_raw, values, cotangent)
    product = 2 * tokens * part_width * head_width

    def ends():
        outs = [states] * (2 * PARTS) + [decays] * PARTS + [table] * 3
        outs += [shape_of(all_heads, head_width), shape_of(2, head_width)]
        outs += [shape_of(1, tokens, width, dtype=BF16)] * 4
        return pl.pallas_call(
            functools.partial(ends_kernel, head_width, lengths.shape[1], count // 2),
            in_specs=[smem, vmem] + [hbm] * 4,
            out_specs=[vmem] * len(outs),
            out_shape=outs,
            scratch_shapes=[
                pltpu.VMEM((rows, CHUNK), F32),
                pltpu.SemaphoreType.DMA((steps, 4)),
            ],
            compiler_params=pltpu.CompilerParams(vmem_limit_bytes=49 << 20),
            cost_estimate=pl.CostEstimate(
                flops=2 * product * PARTS, bytes_accessed=8 * tokens * width, transcendentals=0
            ),
            name="shard_ends",
        )(place, small, *streams)

    def local(part, gain, cum, fac):
        return pl.pallas_call(
            functools.partial(local_kernel, head_width, part),
            in_specs=[vmem] * 7,
            out_specs=[vmem] * 3,
            out_shape=[partials, part_gates, shape_of(heads, head_width)],
            scratch_shapes=[
                pltpu.VMEM((num_chunks, heads, head_width, head_width), BF16),
                pltpu.VMEM((heads, head_width, head_width), F32),
            ],
            compiler_params=pltpu.CompilerParams(vmem_limit_bytes=24 << 20),
            cost_estimate=pl.CostEstimate(
                flops=12 * product, bytes_accessed=16 * tokens * part_width, transcendentals=0
            ),
            name=f"local_{part}",
        )(*held, gain, cum, fac)

    def merge(part, arrivals, local_part, done):
        full_gates = shape_of(1, (part + 1) * heads, tokens)
        extra, extra_specs, aliases = [], [], {}
        if part > 0:
            extra = [done[4]] + list(done[:4])
            extra_specs = [vmem] + [hbm] * 4
            aliases = {13 + i: i for i in range(4)}
        return pl.pallas_call(
            functools.partial(merge_kernel, head_width, part, count // 2),
            in_specs=[vmem] * 5 + [smem] + [vmem] * 6 + extra_specs,
            out_specs=[hbm] * 4 + [vmem],
            out_shape=[shape_of(1, tokens, width, dtype=BF16)] * 4 + [full_gates],
            scratch_shapes=[
                pltpu.VMEM((4, tokens, part_width), BF16),
                pltpu.VMEM((part_width, part_width), BF16),
                pltpu.VMEM((part_width, part_width), BF16),
                pltpu.SemaphoreType.DMA((steps, 4)),
            ],
            input_output_aliases=aliases,
            compiler_params=pltpu.CompilerParams(vmem_limit_bytes=24 << 20),
            cost_estimate=pl.CostEstimate(
                flops=4 * product, bytes_accessed=24 * tokens * part_width, transcendentals=0
            ),
            name=f"merge_{part}",
        )(
            *held, local_part[0], place, gain, shard_fac, *arrivals, local_part[1], *extra
        )

    results = ends()
    near, far, decay = (results[i * PARTS : (i + 1) * PARTS] for i in range(3))
    cum, chunk_fac, shard_fac, gain, flags = results[3 * PARTS : 3 * PARTS + 5]
    held = results[3 * PARTS + 5 :]
    sent = [[] for _ in range(PARTS)]
    arrived = [[] for _ in range(PARTS)]
    local_parts = [None] * PARTS

    def send(part, hop):
        payload = near[part] if hop <= middle else far[part]
        if hop > 0:
            payload = payload + decay[part] * arrived[part][-1]
        sent[part].append(payload)
        arrived[part].append(
            lax.ppermute(
                payload, "ctx", [(hop, hop + 1), (count - 1 - hop, count - 2 - hop)]
            )
        )

    for part in range(PARTS):
        send(part, 0)
    for hop in range(count - 1):
        if hop < PARTS:
            local_cum = cum
            if hop > 0:
                local_cum, _ = lax.optimization_barrier((cum, arrived[0][hop - 1]))
            local_parts[hop] = list(local(hop, gain, local_cum, chunk_fac))
            if hop + 1 < count - 1:
                local_parts[hop][2], arrived[0][-1] = lax.optimization_barrier(
                    (local_parts[hop][2], arrived[0][-1])
                )
        if hop + 1 < count - 1:
            for part in range(PARTS):
                send(part, hop + 1)

    terms = []
    for part in range(PARTS):
        crossed = jnp.sum(sent[part][middle] * arrived[part][middle], axis=2)
        term = local_parts[part][2] + flags[0:1] * crossed
        if middle > 0:
            term = term + jnp.sum(sum(arrived[part][:middle]) * far[part], axis=2)
        terms.append(term)
    gain_term = jnp.concatenate(terms, axis=0)
    gathered = lax.all_gather(gain_term, ("dp", "ctx"))

    done = None
    for part in range(PARTS):
        zeros = jnp.zeros(states.shape, F32)
        first = sum(arrived[part][:middle], zeros) if middle != 1 else arrived[part][0]
        second = sum(arrived[part][middle:-1], zeros) if middle != 1 else arrived[part][1]
        done = list(merge(part, (first, second, arrived[part][-1]), local_parts[part], done))
    gathered, done[4] = lax.optimization_barrier((gathered, done[4]))
    total = jnp.sum(gathered, axis=0)
    half = head_width // lax.axis_size("dp")
    second_half = flags[1:2, :half]
    grad_gain = (1.0 - second_half) * total[:, :half] + second_half * total[:, half:]
    return (*done, grad_gain)


def solution(mesh):
    wide = P("dp", "ctx", "head")
    narrow = P("dp", "head", "ctx")
    return jax.shard_map(
        shards,
        mesh=mesh,
        in_specs=(wide, wide, wide, narrow, P("dp", None), P("head", None), wide),
        out_specs=(wide, wide, wide, wide, narrow, P("head", "dp")),
        check_vma=False,
    )
```

```python
import functools
import math

import jax
import jax.numpy as jnp
from jax import lax
from jax.experimental import pallas as pl
from jax.experimental.pallas import tpu as pltpu
from jax.sharding import PartitionSpec as P

CHUNK = 128
PARTS = 2
UNROLL = 4
PRECISE = lax.Precision.HIGHEST
F32 = jnp.float32
BF16 = jnp.bfloat16
LOG2E = math.log2(math.e)


def dot_nn(a, b, precision=None):
    return lax.dot_general(
        a, b, (((1,), (0,)), ((), ())), precision=precision, preferred_element_type=F32
    )


def dot_nt(a, b):
    return lax.dot_general(a, b, (((1,), (1,)), ((), ())), preferred_element_type=F32)


def dot_tn(a, b):
    return lax.dot_general(a, b, (((0,), (0,)), ((), ())), preferred_element_type=F32)


def iota(shape, dim):
    return lax.broadcasted_iota(jnp.int32, shape, dim)


def total_of(array):
    return jnp.sum(jnp.sum(array, axis=0, keepdims=True), axis=1, keepdims=True)


def later_sums(column):
    kept = iota((CHUNK, CHUNK), 0) >= iota((CHUNK, CHUNK), 1)
    return jnp.sum(jnp.where(kept, column, 0.0), axis=0, keepdims=True)


def decay_tables(docs, ctx, small_ref, spread, cum_ref, chunk_fac_ref, shard_fac_ref):
    rows = cum_ref.shape[0]
    num_chunks = rows // 8
    tokens = num_chunks * CHUNK
    for chunk in range(num_chunks):
        part = small_ref[:, chunk * CHUNK : (chunk + 1) * CHUNK]
        spread[chunk * 8 : chunk * 8 + 4, :] = part
        spread[chunk * 8 + 4 : chunk * 8 + 8, :] = part
    gates = spread[...] * LOG2E
    lane_a, lane_b = iota((CHUNK, CHUNK), 0), iota((CHUNK, CHUNK), 1)
    prefix = dot_nn(gates, (lane_a <= lane_b).astype(F32), PRECISE)
    suffix = dot_nn(gates, (lane_a > lane_b).astype(F32), PRECISE)
    totals = jnp.broadcast_to(prefix[:, CHUNK - 1 : CHUNK], (rows, CHUNK))
    row_a, row_b = iota((rows, rows), 0), iota((rows, rows), 1)
    same = (row_a % 8) == (row_b % 8)
    outside = ((row_a % 8 < 4) & (row_b // 8 < row_a // 8)) | (
        (row_a % 8 >= 4) & (row_b // 8 > row_a // 8)
    )
    others = dot_nn((same & outside).astype(F32), totals, PRECISE)

    first = ctx * tokens
    chunk_first = first + (iota((rows, CHUNK), 0) // 8) * CHUNK
    from_start = iota((rows, CHUNK), 0) % 8 < 4
    chunk_anchor = jnp.where(from_start, chunk_first - 1, chunk_first + (CHUNK - 1)).astype(F32)
    shard_anchor = jnp.where(from_start, first - 1, first + (tokens - 1)).astype(F32)
    positions = (chunk_first + iota((rows, CHUNK), 1)).astype(F32)
    segment = jnp.zeros((rows, CHUNK), F32)
    chunk_segment = jnp.zeros((rows, CHUNK), F32)
    shard_segment = jnp.zeros((rows, CHUNK), F32)
    begin = small_ref.shape[1] - CHUNK
    start = jnp.zeros((1, 1), F32)
    for doc in range(docs):
        segment += jnp.where(positions >= start, 1.0, 0.0)
        chunk_segment += jnp.where(chunk_anchor >= start, 1.0, 0.0)
        shard_segment += jnp.where(shard_anchor >= start, 1.0, 0.0)
        start = start + small_ref[0:1, begin + doc : begin + doc + 1]
    cum_ref[...] = jnp.where(from_start, prefix, segment)
    exponent = jnp.where(from_start, prefix, suffix)
    chunk_fac_ref[...] = jnp.where(
        segment == chunk_segment, jnp.exp2(jnp.minimum(exponent, 0.0)), 0.0
    )
    keep = segment == shard_segment
    shard_fac_ref[...] = jnp.where(keep, jnp.exp2(jnp.minimum(exponent + others, 0.0)), 0.0)


def ends_kernel(head_width, docs, half_ctx, *refs):
    small_ref, sources = refs[0], refs[1:5]
    ctx, dp = lax.axis_index("ctx"), lax.axis_index("dp")
    near_refs, far_refs, decay_refs = (
        refs[5 + i * PARTS : 5 + (i + 1) * PARTS] for i in range(3)
    )
    (cum_ref, chunk_fac_ref, shard_fac_ref, gain_ref, flag_ref, q_ref, k_ref, v_ref, cot_ref,
     spread, sems) = refs[5 + 3 * PARTS :]
    heads = near_refs[0].shape[0]
    rows = shard_fac_ref.shape[0]
    steps = sems.shape[0]
    tokens = q_ref.shape[1]
    block = tokens // steps
    chunks = block // CHUNK

    def copies(step):
        at = pl.ds(step * block, block)
        return [
            pltpu.make_async_copy(source.at[:, at, :], target.at[:, at, :], sems.at[step, i])
            for i, (source, target) in enumerate(zip(sources, (q_ref, k_ref, v_ref, cot_ref)))
        ]

    for step in range(steps):
        for i, copy in enumerate(copies(step)):
            copy.start(priority=i % 2)
    decay_tables(docs, ctx, small_ref, spread, cum_ref, chunk_fac_ref, shard_fac_ref)
    gain_ref[...] = small_ref[:, tokens : tokens + head_width]
    for part in range(PARTS):
        for head in range(heads):
            row = rows - 8 + part * heads + head
            decay_refs[part][head] = jnp.broadcast_to(
                shard_fac_ref[row : row + 1, CHUNK - 1 : CHUNK], (1, head_width)
            )

    def turned(ref, step, row, scale):
        pieces = []
        head = row % 4
        for chunk in range(step * chunks, (step + 1) * chunks):
            factor = shard_fac_ref[chunk * 8 + row : chunk * 8 + row + 1, :]
            piece = jnp.transpose(
                ref[
                    0,
                    chunk * CHUNK : (chunk + 1) * CHUNK,
                    head * head_width : (head + 1) * head_width,
                ]
            )
            pieces.append((piece.astype(F32) * (factor * scale)).astype(BF16))
        return jnp.concatenate(pieces, axis=1)

    ends, grads = {}, {}
    for step in range(steps):
        for copy in copies(step):
            copy.wait()
        at = slice(step * block, (step + 1) * block)
        for row in range(PARTS * heads):
            lanes = slice(row * head_width, (row + 1) * head_width)
            end = dot_nn(turned(k_ref, step, 4 + row, 1.0), v_ref[0, at, lanes])
            grad = dot_nn(turned(q_ref, step, row, head_width ** (-0.5)), cot_ref[0, at, lanes])
            ends[row] = ends[row] + end if step else end
            grads[row] = grads[row] + grad if step else grad
    middle = jnp.where(ctx == half_ctx - 1, 1.0, 0.0)
    low = ctx < half_ctx
    row = iota(flag_ref.shape, 0)
    flag_ref[...] = jnp.where(
        row == 0, middle, jnp.where(row == 1, dp.astype(F32), jnp.where(low, 1.0, 0.0))
    )
    for part in range(PARTS):
        for head in range(heads):
            row = part * heads + head
            near_refs[part][head] = jnp.where(low, ends[row], grads[row])
            far_refs[part][head] = jnp.where(low, grads[row], ends[row])


def local_kernel(
    head_width, part, q_ref, k_ref, v_ref, cot_ref, gain_ref, cum_ref, fac_ref,
    target, dgate_ref, dgain_ref, leaving, state,
):
    out_ref, dq_ref, dk_ref, dv_ref = (target.at[pl.ds(i, 1)] for i in range(4))
    heads = state.shape[0]
    num_chunks = leaving.shape[0]
    scale = head_width ** (-0.5)
    unroll = math.gcd(num_chunks, UNROLL)

    groups = num_chunks // unroll
    def wide_lanes(head):
        row = part * heads + head
        return slice(row * head_width, (row + 1) * head_width)

    def lanes_of(head):
        return slice(head * head_width, (head + 1) * head_width)

    def rows_of(chunk):
        return pl.ds(pl.multiple_of(chunk * CHUNK, CHUNK), CHUNK)

    def table(ref, chunk):
        return ref[pl.ds(pl.multiple_of(chunk * 8, 8), 8), :]

    pairs = [(at, head) for at in range(unroll) for head in range(heads)]

    def backward(chunks):
        facs = [table(fac_ref, chunk) for chunk in chunks]
        added = {}
        for at, head in pairs:
            row = part * heads + head
            rows, lanes = rows_of(chunks[at]), wide_lanes(head)
            turned = jnp.transpose(q_ref[0, rows, lanes]).astype(F32)
            turned = (turned * (facs[at][row : row + 1, :] * scale)).astype(BF16)
            added[at, head] = dot_nn(turned, cot_ref[0, rows, lanes])
        for head in range(heads):
            row = part * heads + head
            held = state[head]
            for at in range(unroll):
                leaving[chunks[at], head] = held.astype(BF16)
                held = held * facs[at][row : row + 1, CHUNK - 1 : CHUNK] + added[at, head]
            state[head] = held

    def forward(chunks):
        facs = [table(fac_ref, chunk) for chunk in chunks]
        cums = [table(cum_ref, chunk) for chunk in chunks]
        fac_columns = [jnp.transpose(fac) for fac in facs]
        cum_columns = [jnp.transpose(cum) for cum in cums]
        causal = iota((CHUNK, CHUNK), 0) >= iota((CHUNK, CHUNK), 1)
        limits = [
            jnp.where((columns[:, 4:5] == cum[4:5, :]) & causal, math.log2(scale), -1e30)
            for columns, cum in zip(cum_columns, cums)
        ]
        cum_columns = [columns + math.log2(scale) for columns in cum_columns]
        q, k, v, cot, k_raw, k_decayed, q_decayed, later = ({} for _ in range(8))
        from_start, to_end, added, held, entering = ({} for _ in range(5))
        for key in pairs:
            at, head = key
            row = part * heads + head
            rows, lanes = rows_of(chunks[at]), lanes_of(head)
            q[key], cot[key] = q_ref[0, rows, wide_lanes(head)], cot_ref[0, rows, wide_lanes(head)]
            v[key] = v_ref[0, rows, wide_lanes(head)]
            later[key] = leaving[chunks[at], head]
            k_raw[key] = k_ref[0, rows, wide_lanes(head)].astype(F32)
            k_wide = k_raw[key] * gain_ref[row : row + 1, :]
            k[key] = k_wide.astype(BF16)
            from_start[key] = fac_columns[at][:, row : row + 1] * scale
            to_end[key] = fac_columns[at][:, 4 + row : 5 + row]
            k_decayed[key] = (k_wide * to_end[key]).astype(BF16)
            q_decayed[key] = (q[key].astype(F32) * from_start[key]).astype(BF16)
            added[key] = dot_tn(k_decayed[key], v[key])
        for head in range(heads):
            row = part * heads + head
            now = state[head]
            for at in range(unroll):
                held[at, head] = now
                entering[at, head] = now.astype(BF16)
                now = now * facs[at][row : row + 1, CHUNK - 1 : CHUNK] + added[at, head]
            held[unroll, head] = now
            state[head] = now
        by_cot, scores, written = {}, {}, {}
        for key in pairs:
            by_cot[key] = dot_nt(cot[key], jnp.concatenate([v[key], entering[key]], axis=0))
            scores[key] = dot_nt(q[key], k[key])
            written[key] = dot_nt(v[key], later[key])
        weights, grad_scores = {}, {}
        for key in pairs:
            at, head = key
            row = part * heads + head
            decays = jnp.exp2(
                jnp.minimum(cum_columns[at][:, row : row + 1] - cums[at][row : row + 1, :], limits[at])
            )
            weights[key] = (scores[key] * decays).astype(BF16)
            grad_scores[key] = (by_cot[key][:, :CHUNK] * decays).astype(BF16)
        out, dq, dk, dv = {}, {}, {}, {}
        for key in pairs:
            out[key] = dot_nn(
                jnp.concatenate([weights[key], q_decayed[key]], axis=1),
                jnp.concatenate([v[key], entering[key]], axis=0),
            )
            dv[key] = dot_nn(
                jnp.concatenate([jnp.transpose(weights[key]), k_decayed[key]], axis=1),
                jnp.concatenate([cot[key], later[key]], axis=0),
            )
            dq[key] = dot_nn(grad_scores[key], k[key]) + by_cot[key][:, CHUNK:] * from_start[key]
            dk[key] = dot_tn(grad_scores[key], q[key]) + written[key] * to_end[key]
        gate_rows, gain_rows = {}, {}
        for key in pairs:
            at, head = key
            balance = jnp.sum(
                out[key] * cot[key].astype(F32) - dv[key] * v[key].astype(F32),
                axis=1, keepdims=True,
            )
            gate_rows[key] = later_sums(balance) + total_of(
                held[at + 1, head] * later[key].astype(F32)
            )
            gain_rows[key] = jnp.sum(dk[key] * k_raw[key], axis=0, keepdims=True)
        for key in pairs:
            at, head = key
            row = part * heads + head
            rows, own = rows_of(chunks[at]), lanes_of(head)
            out_ref[0, rows, own] = out[key].astype(BF16)
            dq_ref[0, rows, own] = dq[key].astype(BF16)
            dv_ref[0, rows, own] = dv[key].astype(BF16)
            dk_ref[0, rows, own] = (dk[key] * gain_ref[row : row + 1, :]).astype(BF16)
            dgate_ref[0, head : head + 1, rows] = gate_rows[key]
        for head in range(heads):
            dgain_ref[head : head + 1, :] += sum(gain_rows[at, head] for at in range(unroll))

    state[...] = jnp.zeros_like(state)

    def backward_group(index, carry):
        backward([num_chunks - 1 - (index * unroll + at) for at in range(unroll)])
        return carry

    lax.fori_loop(0, groups, backward_group, 0)
    state[...] = jnp.zeros_like(state)
    dgain_ref[...] = jnp.zeros_like(dgain_ref)

    def forward_group(index, carry):
        forward([index * unroll + at for at in range(unroll)])
        return carry

    lax.fori_loop(0, groups, forward_group, 0)


def merge_kernel(head_width, *refs):
    q_ref, k_ref, v_ref, cot_ref, gain_ref, flag_ref, fac_ref = refs[:7]
    partial_refs, gate_refs, first_refs, second_refs, last_refs = (
        refs[7 + i * PARTS : 7 + (i + 1) * PARTS] for i in range(5)
    )
    refs = refs[7 + 5 * PARTS :]
    targets, dgate_ref, staged, entering, leaving, sems = refs[:4], *refs[4:]
    heads = first_refs[0].shape[0]
    steps = sems.shape[0]
    num_chunks = fac_ref.shape[0] // 8
    chunks = num_chunks // steps
    block = chunks * CHUNK
    group_width = heads * head_width
    scale = head_width ** (-0.5)

    def copies(step):
        at = pl.ds(step * block, block)
        return [
            pltpu.make_async_copy(staged.at[i, at, :], target.at[0, at, :], sems.at[step, i])
            for i, target in enumerate(targets)
        ]

    gain_columns = jnp.transpose(jnp.concatenate([gain_ref[...], gain_ref[...]], axis=0))
    entering[...] = jnp.zeros_like(entering)
    leaving[...] = jnp.zeros_like(leaving)
    last_factors = fac_ref[(num_chunks - 1) * 8 : num_chunks * 8, CHUNK - 1 : CHUNK]
    low = jnp.broadcast_to(flag_ref[2:3, :], (head_width, head_width)) > 0.5
    constants = []
    for part in range(PARTS):
        for head in range(heads):
            row = part * heads + head
            own = slice(head * head_width, (head + 1) * head_width)
            gain = gain_columns[:, row : row + 1]
            first = first_refs[part][head]
            second = second_refs[part][head] + last_refs[part][head]
            state = jnp.where(low, first, second) * gain
            later = jnp.where(low, second, first)
            entering[part, own, own] = (state * scale).astype(BF16)
            leaving[part, own, own] = (later * gain).astype(BF16)
            constants.append(total_of(state * later) * last_factors[row : row + 1])

    gate_sums, kept_sums = {}, {}
    for step in range(steps):
        numbers = range(step * chunks, (step + 1) * chunks)
        products, results = {}, {}
        for number in numbers:
            rows = slice(number * CHUNK, (number + 1) * CHUNK)
            for part in range(PARTS):
                group = slice(part * group_width, (part + 1) * group_width)
                products[number, part] = (
                    dot_nn(q_ref[0, rows, group], entering[part]),
                    dot_nt(cot_ref[0, rows, group], entering[part]),
                    dot_nt(v_ref[0, rows, group], leaving[part]),
                    dot_nn(k_ref[0, rows, group], leaving[part]),
                )
        for number in numbers:
            columns = jnp.transpose(fac_ref[number * 8 : number * 8 + 8, :])
            rows = slice(number * CHUNK, (number + 1) * CHUNK)
            for row in range(PARTS * heads):
                part, head = divmod(row, heads)
                lanes = slice(head * head_width, (head + 1) * head_width)
                wide = slice(row * head_width, (row + 1) * head_width)
                from_start, to_end = columns[:, row : row + 1], columns[:, 4 + row : 5 + row]
                across, dq, dk, written = (
                    product[:, lanes] * factor
                    for product, factor in zip(
                        products[number, part], (from_start, from_start, to_end, to_end)
                    )
                )
                results[number, row] = [
                    (partial_refs[part][i, rows, lanes].astype(F32) + added).astype(BF16)
                    for i, added in enumerate((across, dq, dk, written))
                ]
                kept = written * v_ref[0, rows, wide].astype(F32)
                balance = jnp.sum(
                    across * cot_ref[0, rows, wide].astype(F32) - kept, axis=1, keepdims=True
                )
                gate_sums[number, row] = later_sums(balance)
                kept_sums[number, row] = jnp.sum(kept, axis=0, keepdims=True)
        for number in numbers:
            rows = slice(number * CHUNK, (number + 1) * CHUNK)
            for row in range(PARTS * heads):
                wide = slice(row * head_width, (row + 1) * head_width)
                for i in range(4):
                    staged[i, rows, wide] = results[number, row][i]
        for i, copy in enumerate(copies(step)):
            copy.start(priority=i % 2)

    for row in range(PARTS * heads):
        part, head = divmod(row, heads)
        kept = sum(kept_sums[number, row] for number in range(num_chunks))
        base = jnp.sum(kept, axis=1, keepdims=True) + constants[row]
        for number in range(num_chunks - 1, -1, -1):
            lanes = slice(number * CHUNK, (number + 1) * CHUNK)
            sums = gate_sums[number, row]
            dgate_ref[0, row : row + 1, lanes] = (
                gate_refs[part][0, head : head + 1, lanes] + sums + base
            )
            base = base + sums[:, 0:1]
    for step in range(steps):
        for copy in copies(step):
            copy.wait()


def summed(own, others):
    if len(others) == 1:
        return own + others[0]
    return (own + others[0]) + (others[1] + others[2])


def shards(queries, keys_raw, values, gates, lengths, key_gain, cotangent):
    tokens, width = queries.shape[1:]
    all_heads, head_width = key_gain.shape
    heads = all_heads // PARTS
    part_width = width // PARTS
    num_chunks = tokens // CHUNK
    rows = num_chunks * 8
    block = min(256, tokens)
    steps = tokens // block
    count = lax.axis_size("ctx")
    middle = count // 2 - 1
    docs = lengths.shape[1]
    sizes = jnp.pad(lengths, ((0, all_heads - 1), (0, CHUNK - docs))).astype(F32)
    small = jnp.concatenate([gates[0], key_gain, sizes], axis=1)

    def shape_of(*shape, dtype=F32):
        return jax.ShapeDtypeStruct(shape, dtype)

    hbm = pl.BlockSpec(memory_space=pltpu.HBM)
    vmem = pl.BlockSpec(memory_space=pltpu.VMEM)
    table = shape_of(rows, CHUNK)
    states = shape_of(heads, head_width, head_width)
    decays = shape_of(heads, 1, head_width)
    part_gates = shape_of(1, heads, tokens)
    partials = shape_of(4, tokens, part_width, dtype=BF16)
    streams = (queries, keys_raw, values, cotangent)
    product = 2 * tokens * part_width * head_width

    def ends():
        outs = [states] * (2 * PARTS) + [decays] * PARTS + [table] * 3
        outs += [shape_of(all_heads, head_width), shape_of(4, head_width)]
        outs += [shape_of(1, tokens, width, dtype=BF16)] * 4
        return pl.pallas_call(
            functools.partial(ends_kernel, head_width, lengths.shape[1], count // 2),
            in_specs=[vmem] + [hbm] * 4,
            out_specs=[vmem] * len(outs),
            out_shape=outs,
            scratch_shapes=[
                pltpu.VMEM((rows, CHUNK), F32),
                pltpu.SemaphoreType.DMA((steps, 4)),
            ],
            compiler_params=pltpu.CompilerParams(vmem_limit_bytes=49 << 20),
            cost_estimate=pl.CostEstimate(
                flops=2 * product * PARTS, bytes_accessed=8 * tokens * width, transcendentals=0
            ),
            name="shard_ends",
        )(small, *streams)

    def local(part, gain, cum, fac):
        return pl.pallas_call(
            functools.partial(local_kernel, head_width, part),
            in_specs=[vmem] * 7,
            out_specs=[vmem] * 3,
            out_shape=[partials, part_gates, shape_of(heads, head_width)],
            scratch_shapes=[
                pltpu.VMEM((num_chunks, heads, head_width, head_width), BF16),
                pltpu.VMEM((heads, head_width, head_width), F32),
            ],
            compiler_params=pltpu.CompilerParams(vmem_limit_bytes=24 << 20),
            cost_estimate=pl.CostEstimate(
                flops=12 * product, bytes_accessed=16 * tokens * part_width, transcendentals=0
            ),
            name=f"local_{part}",
        )(*held, gain, cum, fac)

    def merge(*arrays):
        return pl.pallas_call(
            functools.partial(merge_kernel, head_width),
            in_specs=[vmem] * len(arrays),
            out_specs=[hbm] * 4 + [vmem],
            out_shape=[shape_of(1, tokens, width, dtype=BF16)] * 4 + [shape_of(*gates.shape)],
            scratch_shapes=[
                pltpu.VMEM((4, tokens, width), BF16),
                pltpu.VMEM((PARTS, part_width, part_width), BF16),
                pltpu.VMEM((PARTS, part_width, part_width), BF16),
                pltpu.SemaphoreType.DMA((steps, 4)),
            ],
            compiler_params=pltpu.CompilerParams(vmem_limit_bytes=24 << 20),
            cost_estimate=pl.CostEstimate(
                flops=4 * product * PARTS, bytes_accessed=24 * tokens * width, transcendentals=0
            ),
            name="merge",
        )(*arrays)

    results = ends()
    near, far, decay = (results[i * PARTS : (i + 1) * PARTS] for i in range(3))
    cum, chunk_fac, shard_fac, gain, flags = results[3 * PARTS : 3 * PARTS + 5]
    held = results[3 * PARTS + 5 :]
    sent = [[] for _ in range(PARTS)]
    arrived = [[] for _ in range(PARTS)]
    local_parts = [None] * PARTS

    def send(part, hop):
        payload = near[part] if hop <= middle else far[part]
        if hop > 0:
            payload = payload + decay[part] * arrived[part][-1]
        sent[part].append(payload)
        arrived[part].append(
            lax.ppermute(
                payload, "ctx", [(hop, hop + 1), (count - 1 - hop, count - 2 - hop)]
            )
        )

    for part in range(PARTS):
        send(part, 0)
    for hop in range(count - 1):
        if hop < PARTS:
            local_cum = cum
            if hop > 0:
                local_cum, _ = lax.optimization_barrier((cum, arrived[0][hop - 1]))
            local_parts[hop] = list(local(hop, gain, local_cum, chunk_fac))
            if hop + 1 < count - 1:
                local_parts[hop][2], arrived[0][-1] = lax.optimization_barrier(
                    (local_parts[hop][2], arrived[0][-1])
                )
        if hop + 1 < count - 1:
            for part in range(PARTS):
                send(part, hop + 1)

    terms = []
    for part in range(PARTS):
        crossed = jnp.sum(sent[part][middle] * arrived[part][middle], axis=2)
        term = local_parts[part][2] + flags[0:1] * crossed
        if middle > 0:
            term = term + jnp.sum(sum(arrived[part][:middle]) * far[part], axis=2)
        terms.append(term)
    gain_term = jnp.concatenate(terms, axis=0)
    half = head_width // lax.axis_size("dp")
    second_half = flags[1:2, :half]
    lower_half, upper_half = gain_term[:, :half], gain_term[:, half:]
    away = (1.0 - second_half) * upper_half + second_half * lower_half
    kept = (1.0 - second_half) * lower_half + second_half * upper_half
    grad_gain = kept + lax.ppermute(away, "dp", [(0, 1), (1, 0)])

    def exchanged(array, reach):
        return lax.ppermute(array, "ctx", [(i, i ^ reach) for i in range(count)])

    pending, reach = [], 1
    while reach < count:
        if pending:
            grad_gain = summed(grad_gain, pending)
        pending = [exchanged(grad_gain, reach)]
        if reach * 2 < count:
            pending += [exchanged(grad_gain, reach * 2), exchanged(grad_gain, reach * 3)]
        reach *= 2 * min(len(pending), 2)

    zeros = jnp.zeros(states.shape, F32)
    if middle == 1:
        firsts, seconds = ([own[i] for own in arrived] for i in range(2))
    else:
        firsts = [sum(own[:middle], zeros) for own in arrived]
        seconds = [sum(own[middle:-1], zeros) for own in arrived]
    done = list(
        merge(
            *held, gain, flags, shard_fac,
            *[local_part[0] for local_part in local_parts],
            *[local_part[1] for local_part in local_parts],
            *firsts, *seconds, *[own[-1] for own in arrived],
        )
    )
    pending, done[4] = lax.optimization_barrier((pending, done[4]))
    return (*done, summed(grad_gain, pending))


def solution(mesh):
    wide = P("dp", "ctx", "head")
    narrow = P("dp", "head", "ctx")
    return jax.shard_map(
        shards,
        mesh=mesh,
        in_specs=(wide, wide, wide, narrow, P("dp", None), P("head", None), wide),
        out_specs=(wide, wide, wide, wide, narrow, P("head", "dp")),
        check_vma=False,
    )
```

```python
import functools
import math

import jax
import jax.numpy as jnp
from jax import lax
from jax.experimental import pallas as pl
from jax.experimental.pallas import tpu as pltpu
from jax.sharding import PartitionSpec as P

CHUNK = 128
PARTS = 2
UNROLL = 8
PRECISE = lax.Precision.HIGHEST
F32 = jnp.float32
BF16 = jnp.bfloat16
LOG2E = math.log2(math.e)


def dot_nn(a, b, precision=None):
    return lax.dot_general(
        a, b, (((1,), (0,)), ((), ())), precision=precision, preferred_element_type=F32
    )


def dot_nt(a, b):
    return lax.dot_general(a, b, (((1,), (1,)), ((), ())), preferred_element_type=F32)


def dot_tn(a, b):
    return lax.dot_general(a, b, (((0,), (0,)), ((), ())), preferred_element_type=F32)


def iota(shape, dim):
    return lax.broadcasted_iota(jnp.int32, shape, dim)


def total_of(array):
    return jnp.sum(jnp.sum(array, axis=0, keepdims=True), axis=1, keepdims=True)


def later_sums(column):
    kept = iota((CHUNK, CHUNK), 0) >= iota((CHUNK, CHUNK), 1)
    return jnp.sum(jnp.where(kept, column, 0.0), axis=0, keepdims=True)


def earlier_sums(column):
    kept = iota((CHUNK, CHUNK), 0) < iota((CHUNK, CHUNK), 1)
    return jnp.sum(jnp.where(kept, column, 0.0), axis=0, keepdims=True)


def decay_tables(docs, ctx, small_ref, spread, cum_ref, chunk_fac_ref, shard_fac_ref):
    rows = cum_ref.shape[0]
    num_chunks = rows // 8
    tokens = num_chunks * CHUNK
    for chunk in range(num_chunks):
        part = small_ref[:, chunk * CHUNK : (chunk + 1) * CHUNK]
        spread[chunk * 8 : chunk * 8 + 4, :] = part
        spread[chunk * 8 + 4 : chunk * 8 + 8, :] = part
    gates = spread[...] * LOG2E
    lane_a, lane_b = iota((CHUNK, CHUNK), 0), iota((CHUNK, CHUNK), 1)
    prefix = dot_nn(gates, (lane_a <= lane_b).astype(F32), PRECISE)
    suffix = dot_nn(gates, (lane_a > lane_b).astype(F32), PRECISE)
    totals = jnp.broadcast_to(prefix[:, CHUNK - 1 : CHUNK], (rows, CHUNK))
    row_a, row_b = iota((rows, rows), 0), iota((rows, rows), 1)
    same = (row_a % 8) == (row_b % 8)
    outside = ((row_a % 8 < 4) & (row_b // 8 < row_a // 8)) | (
        (row_a % 8 >= 4) & (row_b // 8 > row_a // 8)
    )
    others = dot_nn((same & outside).astype(F32), totals, PRECISE)

    first = ctx * tokens
    chunk_first = first + (iota((rows, CHUNK), 0) // 8) * CHUNK
    from_start = iota((rows, CHUNK), 0) % 8 < 4
    chunk_anchor = jnp.where(from_start, chunk_first - 1, chunk_first + (CHUNK - 1)).astype(F32)
    shard_anchor = jnp.where(from_start, first - 1, first + (tokens - 1)).astype(F32)
    positions = (chunk_first + iota((rows, CHUNK), 1)).astype(F32)
    segment = jnp.zeros((rows, CHUNK), F32)
    chunk_segment = jnp.zeros((rows, CHUNK), F32)
    shard_segment = jnp.zeros((rows, CHUNK), F32)
    begin = small_ref.shape[1] - CHUNK
    start = jnp.zeros((1, 1), F32)
    for doc in range(docs):
        segment += jnp.where(positions >= start, 1.0, 0.0)
        chunk_segment += jnp.where(chunk_anchor >= start, 1.0, 0.0)
        shard_segment += jnp.where(shard_anchor >= start, 1.0, 0.0)
        start = start + small_ref[0:1, begin + doc : begin + doc + 1]
    cum_ref[...] = jnp.where(from_start, prefix, segment)
    exponent = jnp.where(from_start, prefix, suffix)
    chunk_fac_ref[...] = jnp.where(
        segment == chunk_segment, jnp.exp2(jnp.minimum(exponent, 0.0)), 0.0
    )
    keep = segment == shard_segment
    shard_fac_ref[...] = jnp.where(keep, jnp.exp2(jnp.minimum(exponent + others, 0.0)), 0.0)


def ends_kernel(head_width, docs, half_ctx, *refs):
    small_ref, sources = refs[0], refs[1:5]
    ctx, dp = lax.axis_index("ctx"), lax.axis_index("dp")
    near_refs, far_refs, decay_refs = (
        refs[5 + i * PARTS : 5 + (i + 1) * PARTS] for i in range(3)
    )
    (cum_ref, chunk_fac_ref, shard_fac_ref, gain_ref, flag_ref, q_ref, k_ref, v_ref, cot_ref,
     spread, sems) = refs[5 + 3 * PARTS :]
    heads = near_refs[0].shape[0]
    rows = shard_fac_ref.shape[0]
    steps = sems.shape[0]
    tokens = q_ref.shape[1]
    block = tokens // steps
    chunks = block // CHUNK

    def copies(step):
        at = pl.ds(step * block, block)
        return [
            pltpu.make_async_copy(source.at[:, at, :], target.at[:, at, :], sems.at[step, i])
            for i, (source, target) in enumerate(zip(sources, (q_ref, k_ref, v_ref, cot_ref)))
        ]

    for step in range(steps):
        for i, copy in enumerate(copies(step)):
            copy.start(priority=i % 2)
    decay_tables(docs, ctx, small_ref, spread, cum_ref, chunk_fac_ref, shard_fac_ref)
    gain_ref[...] = small_ref[:, tokens : tokens + head_width]
    for part in range(PARTS):
        for head in range(heads):
            row = rows - 8 + part * heads + head
            decay_refs[part][head] = jnp.broadcast_to(
                shard_fac_ref[row : row + 1, CHUNK - 1 : CHUNK], (1, head_width)
            )

    def turned(ref, step, row, scale):
        pieces = []
        head = row % 4
        for chunk in range(step * chunks, (step + 1) * chunks):
            factor = shard_fac_ref[chunk * 8 + row : chunk * 8 + row + 1, :]
            piece = jnp.transpose(
                ref[
                    0,
                    chunk * CHUNK : (chunk + 1) * CHUNK,
                    head * head_width : (head + 1) * head_width,
                ]
            )
            pieces.append((piece.astype(F32) * (factor * scale)).astype(BF16))
        return jnp.concatenate(pieces, axis=1)

    ends, grads = {}, {}
    for step in range(steps):
        for copy in copies(step):
            copy.wait()
        at = slice(step * block, (step + 1) * block)
        for row in range(PARTS * heads):
            lanes = slice(row * head_width, (row + 1) * head_width)
            end = dot_nn(turned(k_ref, step, 4 + row, 1.0), v_ref[0, at, lanes])
            grad = dot_nn(turned(q_ref, step, row, head_width ** (-0.5)), cot_ref[0, at, lanes])
            ends[row] = ends[row] + end if step else end
            grads[row] = grads[row] + grad if step else grad
    middle = jnp.where(ctx == half_ctx - 1, 1.0, 0.0)
    low = ctx < half_ctx
    row = iota(flag_ref.shape, 0)
    flag_ref[...] = jnp.where(
        row == 0, middle, jnp.where(row == 1, dp.astype(F32), jnp.where(low, 1.0, 0.0))
    )
    for part in range(PARTS):
        for head in range(heads):
            row = part * heads + head
            near_refs[part][head] = jnp.where(low, ends[row], grads[row])
            far_refs[part][head] = jnp.where(low, grads[row], ends[row])


def local_kernel(
    head_width, part, q_ref, k_ref, v_ref, cot_ref, gain_ref, cum_ref, fac_ref,
    target, dgate_ref, dgain_ref, leaving, state,
):
    out_ref, dq_ref, dk_ref, dv_ref = (target.at[pl.ds(i, 1)] for i in range(4))
    heads = state.shape[0]
    num_chunks = leaving.shape[0]
    scale = head_width ** (-0.5)
    unroll = math.gcd(num_chunks, UNROLL)

    groups = num_chunks // unroll
    def wide_lanes(head):
        row = part * heads + head
        return slice(row * head_width, (row + 1) * head_width)

    def lanes_of(head):
        return slice(head * head_width, (head + 1) * head_width)

    def rows_of(chunk):
        return pl.ds(pl.multiple_of(chunk * CHUNK, CHUNK), CHUNK)

    def table(ref, chunk):
        return ref[pl.ds(pl.multiple_of(chunk * 8, 8), 8), :]

    pairs = [(at, head) for at in range(unroll) for head in range(heads)]

    def backward(chunks):
        facs = [table(fac_ref, chunk) for chunk in chunks]
        added = {}
        for at, head in pairs:
            row = part * heads + head
            rows, lanes = rows_of(chunks[at]), wide_lanes(head)
            turned = jnp.transpose(q_ref[0, rows, lanes]).astype(F32)
            turned = (turned * (facs[at][row : row + 1, :] * scale)).astype(BF16)
            added[at, head] = dot_nn(turned, cot_ref[0, rows, lanes])
        for head in range(heads):
            row = part * heads + head
            held = state[head]
            for at in range(unroll):
                leaving[chunks[at], head] = held.astype(BF16)
                held = held * facs[at][row : row + 1, CHUNK - 1 : CHUNK] + added[at, head]
            state[head] = held

    def forward(chunks):
        facs = [table(fac_ref, chunk) for chunk in chunks]
        cums = [table(cum_ref, chunk) for chunk in chunks]
        fac_columns = [jnp.transpose(fac) for fac in facs]
        cum_columns = [jnp.transpose(cum) for cum in cums]
        causal = iota((CHUNK, CHUNK), 0) >= iota((CHUNK, CHUNK), 1)
        limits = [
            jnp.where((columns[:, 4:5] == cum[4:5, :]) & causal, math.log2(scale), -1e30)
            for columns, cum in zip(cum_columns, cums)
        ]
        cum_columns = [columns + math.log2(scale) for columns in cum_columns]
        q, k, v, cot, k_raw, k_decayed, q_decayed, later = ({} for _ in range(8))
        from_start, to_end, added, held, entering = ({} for _ in range(5))
        for key in pairs:
            at, head = key
            row = part * heads + head
            rows, lanes = rows_of(chunks[at]), lanes_of(head)
            q[key], cot[key] = q_ref[0, rows, wide_lanes(head)], cot_ref[0, rows, wide_lanes(head)]
            v[key] = v_ref[0, rows, wide_lanes(head)]
            later[key] = leaving[chunks[at], head]
            k_raw[key] = k_ref[0, rows, wide_lanes(head)].astype(F32)
            k_wide = k_raw[key] * gain_ref[row : row + 1, :]
            k[key] = k_wide.astype(BF16)
            from_start[key] = fac_columns[at][:, row : row + 1] * scale
            to_end[key] = fac_columns[at][:, 4 + row : 5 + row]
            k_decayed[key] = (k_wide * to_end[key]).astype(BF16)
            q_decayed[key] = (q[key].astype(F32) * from_start[key]).astype(BF16)
            added[key] = dot_tn(k_decayed[key], v[key])
        for head in range(heads):
            row = part * heads + head
            now = state[head]
            for at in range(unroll):
                held[at, head] = now
                entering[at, head] = now.astype(BF16)
                now = now * facs[at][row : row + 1, CHUNK - 1 : CHUNK] + added[at, head]
            held[unroll, head] = now
            state[head] = now
        by_cot, scores, written = {}, {}, {}
        for key in pairs:
            by_cot[key] = dot_nt(cot[key], jnp.concatenate([v[key], entering[key]], axis=0))
            scores[key] = dot_nt(q[key], k[key])
            written[key] = dot_nt(v[key], later[key])
        weights, grad_scores = {}, {}
        for key in pairs:
            at, head = key
            row = part * heads + head
            decays = jnp.exp2(
                jnp.minimum(cum_columns[at][:, row : row + 1] - cums[at][row : row + 1, :], limits[at])
            )
            weights[key] = (scores[key] * decays).astype(BF16)
            grad_scores[key] = (by_cot[key][:, :CHUNK] * decays).astype(BF16)
        out, dq, dk, dv = {}, {}, {}, {}
        for key in pairs:
            out[key] = dot_nn(
                jnp.concatenate([weights[key], q_decayed[key]], axis=1),
                jnp.concatenate([v[key], entering[key]], axis=0),
            )
            dv[key] = dot_nn(
                jnp.concatenate([jnp.transpose(weights[key]), k_decayed[key]], axis=1),
                jnp.concatenate([cot[key], later[key]], axis=0),
            )
            dq[key] = dot_nn(grad_scores[key], k[key]) + by_cot[key][:, CHUNK:] * from_start[key]
            dk[key] = dot_tn(grad_scores[key], q[key]) + written[key] * to_end[key]
        gate_rows, gain_rows = {}, {}
        for key in pairs:
            at, head = key
            balance = jnp.sum(
                out[key] * cot[key].astype(F32) - dv[key] * v[key].astype(F32),
                axis=1, keepdims=True,
            )
            gate_rows[key] = later_sums(balance) + total_of(
                held[at + 1, head] * later[key].astype(F32)
            )
            gain_rows[key] = jnp.sum(dk[key] * k_raw[key], axis=0, keepdims=True)
        for key in pairs:
            at, head = key
            row = part * heads + head
            rows, own = rows_of(chunks[at]), lanes_of(head)
            out_ref[0, rows, own] = out[key].astype(BF16)
            dq_ref[0, rows, own] = dq[key].astype(BF16)
            dv_ref[0, rows, own] = dv[key].astype(BF16)
            dk_ref[0, rows, own] = (dk[key] * gain_ref[row : row + 1, :]).astype(BF16)
            dgate_ref[0, head : head + 1, rows] = gate_rows[key]
        for head in range(heads):
            dgain_ref[head : head + 1, :] += sum(gain_rows[at, head] for at in range(unroll))

    state[...] = jnp.zeros_like(state)

    def backward_group(index, carry):
        backward([num_chunks - 1 - (index * unroll + at) for at in range(unroll)])
        return carry

    lax.fori_loop(0, groups, backward_group, 0)
    state[...] = jnp.zeros_like(state)
    dgain_ref[...] = jnp.zeros_like(dgain_ref)

    def forward_group(index, carry):
        forward([index * unroll + at for at in range(unroll)])
        return carry

    lax.fori_loop(0, groups, forward_group, 0)


def merge_kernel(head_width, stage, half_ctx, *refs):
    streams = refs[:4]
    gain_ref, fac_ref, gate_src = refs[4:7]
    rows_all = fac_ref.shape[0]
    all_heads = gain_ref.shape[0]
    partial_refs, refs = refs[7 : 7 + all_heads], refs[7 + all_heads :]
    first_refs, refs = refs[:PARTS], refs[PARTS:]
    if stage == 1:
        second_refs, last_refs, refs = refs[:PARTS], refs[PARTS : 2 * PARTS], refs[2 * PARTS + 4 :]
    targets, dgate_ref, staged, matrix, sems = refs[:4], *refs[4:]
    heads = all_heads // PARTS
    steps = sems.shape[0]
    num_chunks = rows_all // 8
    chunks = num_chunks // steps
    block = chunks * CHUNK
    group_width = heads * head_width
    scale = head_width ** (-0.5)

    def run(query_side):
        a_ref, b_ref = (streams[0], streams[3]) if query_side else (streams[1], streams[2])
        outputs = (0, 1) if query_side else (3, 2)

        def copies(step):
            at = pl.ds(step * block, block)
            return [
                pltpu.make_async_copy(
                    staged.at[i, at, :], targets[output].at[0, at, :], sems.at[step, i]
                )
                for i, output in enumerate(outputs)
            ]

        gain_columns = jnp.transpose(jnp.concatenate([gain_ref[...], gain_ref[...]], axis=0))
        matrix[...] = jnp.zeros_like(matrix)
        constants = [jnp.zeros((1, 1), F32)] * all_heads
        for row in range(all_heads):
            part, head = divmod(row, heads)
            own = slice(head * head_width, (head + 1) * head_width)
            gain = gain_columns[:, row : row + 1]
            state = first_refs[part][head]
            if stage == 1:
                second = second_refs[part][head] + last_refs[part][head]
                decay = fac_ref[rows_all - 8 + row : rows_all - 7 + row, CHUNK - 1 : CHUNK]
                constants[row] = total_of(state * second * gain) * decay
                state = second
            gain = gain * scale if query_side else gain
            matrix[part, own, own] = (state * gain).astype(BF16)

        gate_sums, totals = {}, {}
        for step in range(steps):
            numbers = range(step * chunks, (step + 1) * chunks)
            products, results = {}, {}
            for number in numbers:
                rows = slice(number * CHUNK, (number + 1) * CHUNK)
                for part in range(PARTS):
                    group = slice(part * group_width, (part + 1) * group_width)
                    products[number, part] = (
                        dot_nn(a_ref[0, rows, group], matrix[part]),
                        dot_nt(b_ref[0, rows, group], matrix[part]),
                    )
            for number in numbers:
                columns = jnp.transpose(fac_ref[number * 8 : number * 8 + 8, :])
                rows = slice(number * CHUNK, (number + 1) * CHUNK)
                for row in range(all_heads):
                    part, head = divmod(row, heads)
                    lanes = slice(head * head_width, (head + 1) * head_width)
                    wide = slice(row * head_width, (row + 1) * head_width)
                    column = row if query_side else 4 + row
                    factor = columns[:, column : column + 1]
                    added = [product[:, lanes] * factor for product in products[number, part]]
                    results[number, row] = [
                        (partial_refs[row][output, rows, :].astype(F32) + term).astype(BF16)
                        for output, term in zip(outputs, added)
                    ]
                    share = jnp.sum(
                        added[0] * b_ref[0, rows, wide].astype(F32), axis=1, keepdims=True
                    )
                    if query_side:
                        gate_sums[number, row] = later_sums(share)
                    else:
                        gate_sums[number, row] = earlier_sums(share)
                    totals[number, row] = jnp.sum(share, axis=0, keepdims=True)
            for number in numbers:
                rows = slice(number * CHUNK, (number + 1) * CHUNK)
                for row in range(all_heads):
                    wide = slice(row * head_width, (row + 1) * head_width)
                    for i in range(2):
                        staged[i, rows, wide] = results[number, row][i]
            for i, copy in enumerate(copies(step)):
                copy.start(priority=i % 2)
        order = range(num_chunks - 1, -1, -1) if query_side else range(num_chunks)
        for row in range(all_heads):
            base = constants[row]
            for number in order:
                lanes = slice(number * CHUNK, (number + 1) * CHUNK)
                dgate_ref[0, row : row + 1, lanes] = (
                    gate_src[0, row : row + 1, lanes] + gate_sums[number, row] + base
                )
                base = base + totals[number, row]
        for step in range(steps):
            for copy in copies(step):
                copy.wait()

    low = lax.axis_index("ctx") < half_ctx

    @pl.when(low)
    def _():
        run(stage == 0)

    @pl.when(jnp.logical_not(low))
    def _():
        run(stage == 1)


def summed(own, others):
    if len(others) == 1:
        return own + others[0]
    return (own + others[0]) + (others[1] + others[2])


def shards(queries, keys_raw, values, gates, lengths, key_gain, cotangent):
    tokens, width = queries.shape[1:]
    all_heads, head_width = key_gain.shape
    heads = all_heads // PARTS
    part_width = width // PARTS
    num_chunks = tokens // CHUNK
    rows = num_chunks * 8
    block = min(256, tokens)
    steps = tokens // block
    count = lax.axis_size("ctx")
    middle = count // 2 - 1
    docs = lengths.shape[1]
    sizes = jnp.pad(lengths, ((0, all_heads - 1), (0, CHUNK - docs))).astype(F32)
    small = jnp.concatenate([gates[0], key_gain, sizes], axis=1)

    def shape_of(*shape, dtype=F32):
        return jax.ShapeDtypeStruct(shape, dtype)

    hbm = pl.BlockSpec(memory_space=pltpu.HBM)
    vmem = pl.BlockSpec(memory_space=pltpu.VMEM)
    table = shape_of(rows, CHUNK)
    states = shape_of(heads, head_width, head_width)
    decays = shape_of(heads, 1, head_width)
    partials = shape_of(4, tokens, head_width, dtype=BF16)
    streams = (queries, keys_raw, values, cotangent)
    product = 2 * tokens * part_width * head_width

    def ends():
        outs = [states] * (2 * PARTS) + [decays] * PARTS + [table] * 3
        outs += [shape_of(all_heads, head_width), shape_of(4, head_width)]
        outs += [shape_of(1, tokens, width, dtype=BF16)] * 4
        return pl.pallas_call(
            functools.partial(ends_kernel, head_width, lengths.shape[1], count // 2),
            in_specs=[vmem] + [hbm] * 4,
            out_specs=[vmem] * len(outs),
            out_shape=outs,
            scratch_shapes=[
                pltpu.VMEM((rows, CHUNK), F32),
                pltpu.SemaphoreType.DMA((steps, 4)),
            ],
            compiler_params=pltpu.CompilerParams(vmem_limit_bytes=49 << 20),
            cost_estimate=pl.CostEstimate(
                flops=2 * product * PARTS, bytes_accessed=8 * tokens * width, transcendentals=0
            ),
            name="shard_ends",
        )(small, *streams)

    def local(row, cum):
        return pl.pallas_call(
            functools.partial(local_kernel, head_width, row),
            in_specs=[vmem] * 7,
            out_specs=[vmem] * 3,
            out_shape=[partials, shape_of(1, 1, tokens), shape_of(1, head_width)],
            scratch_shapes=[
                pltpu.VMEM((num_chunks, 1, head_width, head_width), BF16),
                pltpu.VMEM((1, head_width, head_width), F32),
            ],
            compiler_params=pltpu.CompilerParams(vmem_limit_bytes=24 << 20),
            cost_estimate=pl.CostEstimate(
                flops=12 * product // heads, bytes_accessed=16 * tokens * head_width, transcendentals=0
            ),
            name=f"local_{row}",
        )(*held, gain, cum, chunk_fac)

    def merge(stage, gate_grads, states_in, done):
        inputs = [*held, gain, shard_fac, gate_grads]
        inputs += [local_part[0] for local_part in locals_] + states_in
        aliases = {len(inputs) + i: i for i in range(len(done))}
        return pl.pallas_call(
            functools.partial(merge_kernel, head_width, stage, count // 2),
            in_specs=[vmem] * len(inputs) + [hbm] * len(done),
            out_specs=[hbm] * 4 + [vmem],
            out_shape=[shape_of(1, tokens, width, dtype=BF16)] * 4 + [shape_of(*gates.shape)],
            scratch_shapes=[
                pltpu.VMEM((2, tokens, width), BF16),
                pltpu.VMEM((PARTS, part_width, part_width), BF16),
                pltpu.SemaphoreType.DMA((steps, 2)),
            ],
            input_output_aliases=aliases,
            compiler_params=pltpu.CompilerParams(vmem_limit_bytes=24 << 20),
            cost_estimate=pl.CostEstimate(
                flops=2 * product * PARTS, bytes_accessed=12 * tokens * width, transcendentals=0
            ),
            name=f"merge_{stage}",
        )(*inputs, *done)

    results = ends()
    near, far, decay = (results[i * PARTS : (i + 1) * PARTS] for i in range(3))
    cum, chunk_fac, shard_fac, gain, flags = results[3 * PARTS : 3 * PARTS + 5]
    held = results[3 * PARTS + 5 :]
    sent = [[] for _ in range(PARTS)]
    arrived = [[] for _ in range(PARTS)]

    def send(part, hop):
        payload = near[part] if hop <= middle else far[part]
        if hop > 0:
            payload = payload + decay[part] * arrived[part][-1]
        sent[part].append(payload)
        arrived[part].append(
            lax.ppermute(
                payload, "ctx", [(hop, hop + 1), (count - 1 - hop, count - 2 - hop)]
            )
        )

    locals_, per_hop = [], [2, 1, 1]
    for hop in range(count - 1):
        for part in range(PARTS):
            send(part, hop)
        for _ in range(per_hop[hop] if hop < 3 else 0):
            local_cum = cum
            if hop > 0:
                local_cum, *_ = lax.optimization_barrier((cum, *[own[hop] for own in sent]))
            locals_.append(list(local(len(locals_), local_cum)))
            if hop + 1 < count - 1:
                locals_[-1][2], arrived[0][-1] = lax.optimization_barrier(
                    (locals_[-1][2], arrived[0][-1])
                )

    terms = []
    for part in range(PARTS):
        crossed = jnp.sum(sent[part][middle] * arrived[part][middle], axis=2)
        term = flags[0:1] * crossed
        if middle > 0:
            term = term + jnp.sum(sum(arrived[part][:middle]) * far[part], axis=2)
        terms.append(term)
    gain_term = jnp.concatenate(terms, axis=0) + jnp.concatenate(
        [local_part[2] for local_part in locals_], axis=0
    )
    local_gates = jnp.concatenate([local_part[1] for local_part in locals_], axis=1)

    zeros = jnp.zeros(states.shape, F32)
    if middle == 1:
        firsts, seconds = ([own[i] for own in arrived] for i in range(2))
    else:
        firsts = [sum(own[:middle], zeros) for own in arrived]
        seconds = [sum(own[middle:-1], zeros) for own in arrived]
    lasts = [own[-1] for own in arrived]
    half_done = merge(0, local_gates, firsts, [])
    half = head_width // lax.axis_size("dp")
    second_half = flags[1:2, :half]
    lower_half, upper_half = gain_term[:, :half], gain_term[:, half:]
    away = (1.0 - second_half) * upper_half + second_half * lower_half
    kept = (1.0 - second_half) * lower_half + second_half * upper_half
    grad_gain = kept + lax.ppermute(away, "dp", [(0, 1), (1, 0)])

    def exchanged(array, reach):
        return lax.ppermute(array, "ctx", [(i, i ^ reach) for i in range(count)])

    pending, reach = [], 1
    while reach < count:
        if pending:
            grad_gain = summed(grad_gain, pending)
        pending = [exchanged(grad_gain, reach)]
        if reach * 2 < count:
            pending += [exchanged(grad_gain, reach * 2), exchanged(grad_gain, reach * 3)]
        reach *= 2 * min(len(pending), 2)

    done = list(merge(1, half_done[4], firsts + seconds + lasts, half_done[:4]))
    pending, done[4] = lax.optimization_barrier((pending, done[4]))
    return (*done, summed(grad_gain, pending))


def solution(mesh):
    wide = P("dp", "ctx", "head")
    narrow = P("dp", "head", "ctx")
    return jax.shard_map(
        shards,
        mesh=mesh,
        in_specs=(wide, wide, wide, narrow, P("dp", None), P("head", None), wide),
        out_specs=(wide, wide, wide, wide, narrow, P("head", "dp")),
        check_vma=False,
    )
```

```python
import functools
import math

import jax
import jax.numpy as jnp
from jax import lax
from jax.experimental import pallas as pl
from jax.experimental.pallas import tpu as pltpu
from jax.sharding import PartitionSpec as P

CHUNK = 128
PARTS = 2
UNROLL = 8
PRECISE = lax.Precision.HIGHEST
F32 = jnp.float32
BF16 = jnp.bfloat16
LOG2E = math.log2(math.e)


def dot_nn(a, b, precision=None):
    return lax.dot_general(
        a, b, (((1,), (0,)), ((), ())), precision=precision, preferred_element_type=F32
    )


def dot_nt(a, b):
    return lax.dot_general(a, b, (((1,), (1,)), ((), ())), preferred_element_type=F32)


def dot_tn(a, b):
    return lax.dot_general(a, b, (((0,), (0,)), ((), ())), preferred_element_type=F32)


def iota(shape, dim):
    return lax.broadcasted_iota(jnp.int32, shape, dim)


def total_of(array):
    return jnp.sum(jnp.sum(array, axis=0, keepdims=True), axis=1, keepdims=True)


def later_sums(column):
    kept = iota((CHUNK, CHUNK), 0) >= iota((CHUNK, CHUNK), 1)
    return jnp.sum(jnp.where(kept, column, 0.0), axis=0, keepdims=True)


def decay_tables(docs, ctx, small_ref, spread, cum_ref, chunk_fac_ref, shard_fac_ref):
    rows = cum_ref.shape[0]
    num_chunks = rows // 8
    tokens = num_chunks * CHUNK
    for chunk in range(num_chunks):
        part = small_ref[:, chunk * CHUNK : (chunk + 1) * CHUNK]
        spread[chunk * 8 : chunk * 8 + 4, :] = part
        spread[chunk * 8 + 4 : chunk * 8 + 8, :] = part
    gates = spread[...] * LOG2E
    lane_a, lane_b = iota((CHUNK, CHUNK), 0), iota((CHUNK, CHUNK), 1)
    prefix = dot_nn(gates, (lane_a <= lane_b).astype(F32), PRECISE)
    suffix = dot_nn(gates, (lane_a > lane_b).astype(F32), PRECISE)
    totals = jnp.broadcast_to(prefix[:, CHUNK - 1 : CHUNK], (rows, CHUNK))
    row_a, row_b = iota((rows, rows), 0), iota((rows, rows), 1)
    same = (row_a % 8) == (row_b % 8)
    outside = ((row_a % 8 < 4) & (row_b // 8 < row_a // 8)) | (
        (row_a % 8 >= 4) & (row_b // 8 > row_a // 8)
    )
    others = dot_nn((same & outside).astype(F32), totals, PRECISE)

    first = ctx * tokens
    chunk_first = first + (iota((rows, CHUNK), 0) // 8) * CHUNK
    from_start = iota((rows, CHUNK), 0) % 8 < 4
    chunk_anchor = jnp.where(from_start, chunk_first - 1, chunk_first + (CHUNK - 1)).astype(F32)
    shard_anchor = jnp.where(from_start, first - 1, first + (tokens - 1)).astype(F32)
    positions = (chunk_first + iota((rows, CHUNK), 1)).astype(F32)
    segment = jnp.zeros((rows, CHUNK), F32)
    chunk_segment = jnp.zeros((rows, CHUNK), F32)
    shard_segment = jnp.zeros((rows, CHUNK), F32)
    begin = small_ref.shape[1] - CHUNK
    start = jnp.zeros((1, 1), F32)
    for doc in range(docs):
        segment += jnp.where(positions >= start, 1.0, 0.0)
        chunk_segment += jnp.where(chunk_anchor >= start, 1.0, 0.0)
        shard_segment += jnp.where(shard_anchor >= start, 1.0, 0.0)
        start = start + small_ref[0:1, begin + doc : begin + doc + 1]
    cum_ref[...] = jnp.where(from_start, prefix, segment)
    exponent = jnp.where(from_start, prefix, suffix)
    chunk_fac_ref[...] = jnp.where(
        segment == chunk_segment, jnp.exp2(jnp.minimum(exponent, 0.0)), 0.0
    )
    keep = segment == shard_segment
    shard_fac_ref[...] = jnp.where(keep, jnp.exp2(jnp.minimum(exponent + others, 0.0)), 0.0)


def ends_kernel(head_width, docs, half_ctx, *refs):
    small_ref, sources = refs[0], refs[1:5]
    ctx, dp = lax.axis_index("ctx"), lax.axis_index("dp")
    near_refs, far_refs, decay_refs = (
        refs[5 + i * PARTS : 5 + (i + 1) * PARTS] for i in range(3)
    )
    (cum_ref, chunk_fac_ref, shard_fac_ref, gain_ref, flag_ref, q_ref, k_ref, v_ref, cot_ref,
     spread, sems) = refs[5 + 3 * PARTS :]
    heads = near_refs[0].shape[0]
    rows = shard_fac_ref.shape[0]
    steps = sems.shape[0]
    tokens = q_ref.shape[1]
    block = tokens // steps
    chunks = block // CHUNK

    def copies(step):
        at = pl.ds(step * block, block)
        return [
            pltpu.make_async_copy(source.at[:, at, :], target.at[:, at, :], sems.at[step, i])
            for i, (source, target) in enumerate(zip(sources, (q_ref, k_ref, v_ref, cot_ref)))
        ]

    for step in range(steps):
        for i, copy in enumerate(copies(step)):
            copy.start(priority=i % 2)
    decay_tables(docs, ctx, small_ref, spread, cum_ref, chunk_fac_ref, shard_fac_ref)
    gain_ref[...] = small_ref[:, tokens : tokens + head_width]
    for part in range(PARTS):
        for head in range(heads):
            row = rows - 8 + part * heads + head
            decay_refs[part][head] = jnp.broadcast_to(
                shard_fac_ref[row : row + 1, CHUNK - 1 : CHUNK], (1, head_width)
            )

    def turned(ref, step, row, scale):
        pieces = []
        head = row % 4
        for chunk in range(step * chunks, (step + 1) * chunks):
            factor = shard_fac_ref[chunk * 8 + row : chunk * 8 + row + 1, :]
            piece = jnp.transpose(
                ref[
                    0,
                    chunk * CHUNK : (chunk + 1) * CHUNK,
                    head * head_width : (head + 1) * head_width,
                ]
            )
            pieces.append((piece.astype(F32) * (factor * scale)).astype(BF16))
        return jnp.concatenate(pieces, axis=1)

    ends, grads = {}, {}
    for step in range(steps):
        for copy in copies(step):
            copy.wait()
        at = slice(step * block, (step + 1) * block)
        for row in range(PARTS * heads):
            lanes = slice(row * head_width, (row + 1) * head_width)
            end = dot_nn(turned(k_ref, step, 4 + row, 1.0), v_ref[0, at, lanes])
            grad = dot_nn(turned(q_ref, step, row, head_width ** (-0.5)), cot_ref[0, at, lanes])
            ends[row] = ends[row] + end if step else end
            grads[row] = grads[row] + grad if step else grad
    middle = jnp.where(ctx == half_ctx - 1, 1.0, 0.0)
    low = ctx < half_ctx
    row = iota(flag_ref.shape, 0)
    flag_ref[...] = jnp.where(
        row == 0, middle, jnp.where(row == 1, dp.astype(F32), jnp.where(low, 1.0, 0.0))
    )
    for part in range(PARTS):
        for head in range(heads):
            row = part * heads + head
            near_refs[part][head] = jnp.where(low, ends[row], grads[row])
            far_refs[part][head] = jnp.where(low, grads[row], ends[row])


def local_kernel(
    head_width, part, q_ref, k_ref, v_ref, cot_ref, gain_ref, cum_ref, fac_ref,
    target, dgate_ref, dgain_ref, leaving, state,
):
    out_ref, dq_ref, dk_ref, dv_ref = (target.at[pl.ds(i, 1)] for i in range(4))
    heads = state.shape[0]
    num_chunks = leaving.shape[0]
    scale = head_width ** (-0.5)
    unroll = math.gcd(num_chunks, UNROLL)

    groups = num_chunks // unroll
    def wide_lanes(head):
        row = part * heads + head
        return slice(row * head_width, (row + 1) * head_width)

    def lanes_of(head):
        return slice(head * head_width, (head + 1) * head_width)

    def rows_of(chunk):
        return pl.ds(pl.multiple_of(chunk * CHUNK, CHUNK), CHUNK)

    def table(ref, chunk):
        return ref[pl.ds(pl.multiple_of(chunk * 8, 8), 8), :]

    pairs = [(at, head) for at in range(unroll) for head in range(heads)]

    def backward(chunks):
        facs = [table(fac_ref, chunk) for chunk in chunks]
        added = {}
        for at, head in pairs:
            row = part * heads + head
            rows, lanes = rows_of(chunks[at]), wide_lanes(head)
            turned = jnp.transpose(q_ref[0, rows, lanes]).astype(F32)
            turned = (turned * (facs[at][row : row + 1, :] * scale)).astype(BF16)
            added[at, head] = dot_nn(turned, cot_ref[0, rows, lanes])
        for head in range(heads):
            row = part * heads + head
            held = state[head]
            for at in range(unroll):
                leaving[chunks[at], head] = held.astype(BF16)
                held = held * facs[at][row : row + 1, CHUNK - 1 : CHUNK] + added[at, head]
            state[head] = held

    def forward(chunks):
        facs = [table(fac_ref, chunk) for chunk in chunks]
        cums = [table(cum_ref, chunk) for chunk in chunks]
        fac_columns = [jnp.transpose(fac) for fac in facs]
        cum_columns = [jnp.transpose(cum) for cum in cums]
        causal = iota((CHUNK, CHUNK), 0) >= iota((CHUNK, CHUNK), 1)
        limits = [
            jnp.where((columns[:, 4:5] == cum[4:5, :]) & causal, math.log2(scale), -1e30)
            for columns, cum in zip(cum_columns, cums)
        ]
        cum_columns = [columns + math.log2(scale) for columns in cum_columns]
        q, k, v, cot, k_raw, k_decayed, q_decayed, later = ({} for _ in range(8))
        from_start, to_end, added, held, entering = ({} for _ in range(5))
        for key in pairs:
            at, head = key
            row = part * heads + head
            rows, lanes = rows_of(chunks[at]), lanes_of(head)
            q[key], cot[key] = q_ref[0, rows, wide_lanes(head)], cot_ref[0, rows, wide_lanes(head)]
            v[key] = v_ref[0, rows, wide_lanes(head)]
            later[key] = leaving[chunks[at], head]
            k_raw[key] = k_ref[0, rows, wide_lanes(head)].astype(F32)
            k_wide = k_raw[key] * gain_ref[row : row + 1, :]
            k[key] = k_wide.astype(BF16)
            from_start[key] = fac_columns[at][:, row : row + 1] * scale
            to_end[key] = fac_columns[at][:, 4 + row : 5 + row]
            k_decayed[key] = (k_wide * to_end[key]).astype(BF16)
            q_decayed[key] = (q[key].astype(F32) * from_start[key]).astype(BF16)
            added[key] = dot_tn(k_decayed[key], v[key])
        for head in range(heads):
            row = part * heads + head
            now = state[head]
            for at in range(unroll):
                held[at, head] = now
                entering[at, head] = now.astype(BF16)
                now = now * facs[at][row : row + 1, CHUNK - 1 : CHUNK] + added[at, head]
            held[unroll, head] = now
            state[head] = now
        by_cot, scores, written = {}, {}, {}
        for key in pairs:
            by_cot[key] = dot_nt(cot[key], jnp.concatenate([v[key], entering[key]], axis=0))
            scores[key] = dot_nt(q[key], k[key])
            written[key] = dot_nt(v[key], later[key])
        weights, grad_scores = {}, {}
        for key in pairs:
            at, head = key
            row = part * heads + head
            decays = jnp.exp2(
                jnp.minimum(cum_columns[at][:, row : row + 1] - cums[at][row : row + 1, :], limits[at])
            )
            weights[key] = (scores[key] * decays).astype(BF16)
            grad_scores[key] = (by_cot[key][:, :CHUNK] * decays).astype(BF16)
        out, dq, dk, dv = {}, {}, {}, {}
        for key in pairs:
            out[key] = dot_nn(
                jnp.concatenate([weights[key], q_decayed[key]], axis=1),
                jnp.concatenate([v[key], entering[key]], axis=0),
            )
            dv[key] = dot_nn(
                jnp.concatenate([jnp.transpose(weights[key]), k_decayed[key]], axis=1),
                jnp.concatenate([cot[key], later[key]], axis=0),
            )
            dq[key] = dot_nn(grad_scores[key], k[key]) + by_cot[key][:, CHUNK:] * from_start[key]
            dk[key] = dot_tn(grad_scores[key], q[key]) + written[key] * to_end[key]
        gate_rows, gain_rows = {}, {}
        for key in pairs:
            at, head = key
            balance = jnp.sum(
                out[key] * cot[key].astype(F32) - dv[key] * v[key].astype(F32),
                axis=1, keepdims=True,
            )
            gate_rows[key] = later_sums(balance) + total_of(
                held[at + 1, head] * later[key].astype(F32)
            )
            gain_rows[key] = jnp.sum(dk[key] * k_raw[key], axis=0, keepdims=True)
        for key in pairs:
            at, head = key
            row = part * heads + head
            rows, own = rows_of(chunks[at]), lanes_of(head)
            out_ref[0, rows, own] = out[key].astype(BF16)
            dq_ref[0, rows, own] = dq[key].astype(BF16)
            dv_ref[0, rows, own] = dv[key].astype(BF16)
            dk_ref[0, rows, own] = (dk[key] * gain_ref[row : row + 1, :]).astype(BF16)
            dgate_ref[0, head : head + 1, rows] = gate_rows[key]
        for head in range(heads):
            dgain_ref[head : head + 1, :] += sum(gain_rows[at, head] for at in range(unroll))

    state[...] = jnp.zeros_like(state)

    def backward_group(index, carry):
        backward([num_chunks - 1 - (index * unroll + at) for at in range(unroll)])
        return carry

    lax.fori_loop(0, groups, backward_group, 0)
    state[...] = jnp.zeros_like(state)
    dgain_ref[...] = jnp.zeros_like(dgain_ref)

    def forward_group(index, carry):
        forward([index * unroll + at for at in range(unroll)])
        return carry

    lax.fori_loop(0, groups, forward_group, 0)


def merge_kernel(head_width, *refs):
    q_ref, k_ref, v_ref, cot_ref, gain_ref, flag_ref, fac_ref = refs[:7]
    all_heads = gain_ref.shape[0]
    partial_refs, gate_refs = (
        refs[7 + i * all_heads : 7 + (i + 1) * all_heads] for i in range(2)
    )
    refs = refs[7 + 2 * all_heads :]
    first_refs, second_refs, last_refs = (refs[i * PARTS : (i + 1) * PARTS] for i in range(3))
    refs = refs[3 * PARTS :]
    targets, dgate_ref, staged, matrices, sems = refs[:4], *refs[4:]
    heads = first_refs[0].shape[0]
    steps = sems.shape[0]
    num_chunks = fac_ref.shape[0] // 8
    chunks = num_chunks // steps
    block = chunks * CHUNK
    group_width = heads * head_width
    scale = head_width ** (-0.5)

    def copies(step):
        at = pl.ds(step * block, block)
        return [
            pltpu.make_async_copy(staged.at[i, at, :], target.at[0, at, :], sems.at[step, i])
            for i, target in enumerate(targets)
        ]

    gain_columns = jnp.transpose(jnp.concatenate([gain_ref[...], gain_ref[...]], axis=0))
    matrices[...] = jnp.zeros_like(matrices)
    last_factors = fac_ref[(num_chunks - 1) * 8 : num_chunks * 8, CHUNK - 1 : CHUNK]
    low = jnp.broadcast_to(flag_ref[2:3, :], (head_width, head_width)) > 0.5
    constants = []
    for part in range(PARTS):
        for head in range(heads):
            row = part * heads + head
            own = slice(head * head_width, (head + 1) * head_width)
            gain = gain_columns[:, row : row + 1]
            first = first_refs[part][head]
            second = second_refs[part][head] + last_refs[part][head]
            state = jnp.where(low, first, second) * gain
            later = jnp.where(low, second, first)
            entering = (state * scale).astype(BF16)
            leaving = (later * gain).astype(BF16)
            for i, matrix in enumerate(
                (entering, jnp.transpose(entering), leaving, jnp.transpose(leaving))
            ):
                matrices[part, i, own, own] = matrix
            constants.append(total_of(state * later) * last_factors[row : row + 1])

    gate_sums, kept_sums, totals = {}, {}, {}
    for step in range(steps):
        numbers = range(step * chunks, (step + 1) * chunks)
        products, results = {}, {}
        at = slice(step * block, (step + 1) * block)
        for part in range(PARTS):
            group = slice(part * group_width, (part + 1) * group_width)
            q_out, cot_out, k_out, v_out = (
                dot_nn(ref[0, at, group], matrices[part, i])
                for i, ref in enumerate((q_ref, cot_ref, k_ref, v_ref))
            )
            for i, number in enumerate(numbers):
                rows = slice(i * CHUNK, (i + 1) * CHUNK)
                products[number, part] = [
                    product[rows] for product in (q_out, cot_out, v_out, k_out)
                ]
        for number in numbers:
            columns = jnp.transpose(fac_ref[number * 8 : number * 8 + 8, :])
            rows = slice(number * CHUNK, (number + 1) * CHUNK)
            for row in range(PARTS * heads):
                part, head = divmod(row, heads)
                lanes = slice(head * head_width, (head + 1) * head_width)
                wide = slice(row * head_width, (row + 1) * head_width)
                from_start, to_end = columns[:, row : row + 1], columns[:, 4 + row : 5 + row]
                across, dq, dk, written = (
                    product[:, lanes] * factor
                    for product, factor in zip(
                        products[number, part], (from_start, from_start, to_end, to_end)
                    )
                )
                results[number, row] = [
                    (partial_refs[row][i, rows, :].astype(F32) + added).astype(BF16)
                    for i, added in enumerate((across, dq, dk, written))
                ]
                kept = written * v_ref[0, rows, wide].astype(F32)
                balance = jnp.sum(
                    across * cot_ref[0, rows, wide].astype(F32) - kept, axis=1, keepdims=True
                )
                gate_sums[number, row] = later_sums(balance)
                totals[number, row] = jnp.sum(balance, axis=0, keepdims=True)
                kept_sums[number, row] = jnp.sum(kept, axis=0, keepdims=True)
        for number in numbers:
            rows = slice(number * CHUNK, (number + 1) * CHUNK)
            for row in range(PARTS * heads):
                wide = slice(row * head_width, (row + 1) * head_width)
                for i in range(4):
                    staged[i, rows, wide] = results[number, row][i]
        for i, copy in enumerate(copies(step)):
            copy.start(priority=i % 2)

    for row in range(PARTS * heads):
        kept = sum(kept_sums[number, row] for number in range(num_chunks))
        base = jnp.sum(kept, axis=1, keepdims=True) + constants[row]
        for number in range(num_chunks - 1, -1, -1):
            lanes = slice(number * CHUNK, (number + 1) * CHUNK)
            dgate_ref[0, row : row + 1, lanes] = (
                gate_refs[row][0, :, lanes] + gate_sums[number, row] + base
            )
            base = base + totals[number, row]
    for step in range(steps):
        for copy in copies(step):
            copy.wait()


def summed(own, others):
    if len(others) == 1:
        return own + others[0]
    return (own + others[0]) + (others[1] + others[2])


def shards(queries, keys_raw, values, gates, lengths, key_gain, cotangent):
    tokens, width = queries.shape[1:]
    all_heads, head_width = key_gain.shape
    heads = all_heads // PARTS
    part_width = width // PARTS
    num_chunks = tokens // CHUNK
    rows = num_chunks * 8
    block = min(256, tokens)
    steps = tokens // block
    count = lax.axis_size("ctx")
    middle = count // 2 - 1
    docs = lengths.shape[1]
    sizes = jnp.pad(lengths, ((0, all_heads - 1), (0, CHUNK - docs))).astype(F32)
    small = jnp.concatenate([gates[0], key_gain, sizes], axis=1)

    def shape_of(*shape, dtype=F32):
        return jax.ShapeDtypeStruct(shape, dtype)

    hbm = pl.BlockSpec(memory_space=pltpu.HBM)
    vmem = pl.BlockSpec(memory_space=pltpu.VMEM)
    table = shape_of(rows, CHUNK)
    states = shape_of(heads, head_width, head_width)
    decays = shape_of(heads, 1, head_width)
    partials = shape_of(4, tokens, head_width, dtype=BF16)
    streams = (queries, keys_raw, values, cotangent)
    product = 2 * tokens * part_width * head_width

    def ends():
        outs = [states] * (2 * PARTS) + [decays] * PARTS + [table] * 3
        outs += [shape_of(all_heads, head_width), shape_of(4, head_width)]
        outs += [shape_of(1, tokens, width, dtype=BF16)] * 4
        return pl.pallas_call(
            functools.partial(ends_kernel, head_width, lengths.shape[1], count // 2),
            in_specs=[vmem] + [hbm] * 4,
            out_specs=[vmem] * len(outs),
            out_shape=outs,
            scratch_shapes=[
                pltpu.VMEM((rows, CHUNK), F32),
                pltpu.SemaphoreType.DMA((steps, 4)),
            ],
            compiler_params=pltpu.CompilerParams(vmem_limit_bytes=49 << 20),
            cost_estimate=pl.CostEstimate(
                flops=2 * product * PARTS, bytes_accessed=8 * tokens * width, transcendentals=0
            ),
            name="shard_ends",
        )(small, *streams)

    def local(row, cum):
        return pl.pallas_call(
            functools.partial(local_kernel, head_width, row),
            in_specs=[vmem] * 7,
            out_specs=[vmem] * 3,
            out_shape=[partials, shape_of(1, 1, tokens), shape_of(1, head_width)],
            scratch_shapes=[
                pltpu.VMEM((num_chunks, 1, head_width, head_width), BF16),
                pltpu.VMEM((1, head_width, head_width), F32),
            ],
            compiler_params=pltpu.CompilerParams(vmem_limit_bytes=24 << 20),
            cost_estimate=pl.CostEstimate(
                flops=12 * product // heads, bytes_accessed=16 * tokens * head_width, transcendentals=0
            ),
            name=f"local_{row}",
        )(*held, gain, cum, chunk_fac)

    def merge(*arrays):
        return pl.pallas_call(
            functools.partial(merge_kernel, head_width),
            in_specs=[vmem] * len(arrays),
            out_specs=[hbm] * 4 + [vmem],
            out_shape=[shape_of(1, tokens, width, dtype=BF16)] * 4 + [shape_of(*gates.shape)],
            scratch_shapes=[
                pltpu.VMEM((4, tokens, width), BF16),
                pltpu.VMEM((PARTS, 4, part_width, part_width), BF16),
                pltpu.SemaphoreType.DMA((steps, 4)),
            ],
            compiler_params=pltpu.CompilerParams(vmem_limit_bytes=24 << 20),
            cost_estimate=pl.CostEstimate(
                flops=4 * product * PARTS, bytes_accessed=24 * tokens * width, transcendentals=0
            ),
            name="merge",
        )(*arrays)

    results = ends()
    near, far, decay = (results[i * PARTS : (i + 1) * PARTS] for i in range(3))
    cum, chunk_fac, shard_fac, gain, flags = results[3 * PARTS : 3 * PARTS + 5]
    held = results[3 * PARTS + 5 :]
    sent = [[] for _ in range(PARTS)]
    arrived = [[] for _ in range(PARTS)]

    def send(part, hop):
        payload = near[part] if hop <= middle else far[part]
        if hop > 0:
            if part > 0:
                arrived[part][-1], _ = lax.optimization_barrier(
                    (arrived[part][-1], sent[part - 1][hop])
                )
            payload = payload + decay[part] * arrived[part][-1]
        sent[part].append(payload)
        arrived[part].append(
            lax.ppermute(
                payload, "ctx", [(hop, hop + 1), (count - 1 - hop, count - 2 - hop)]
            )
        )

    locals_, per_hop = [], [3, 1, 0]
    for hop in range(count - 1):
        for part in range(PARTS):
            send(part, hop)
        for _ in range(per_hop[hop] if hop < 3 else 0):
            local_cum = cum
            if hop > 0:
                local_cum, *_ = lax.optimization_barrier((cum, *[own[hop] for own in sent]))
            locals_.append(list(local(len(locals_), local_cum)))
            if hop + 1 < count - 1:
                locals_[-1][2], arrived[0][-1] = lax.optimization_barrier(
                    (locals_[-1][2], arrived[0][-1])
                )

    terms = []
    for part in range(PARTS):
        crossed = jnp.sum(sent[part][middle] * arrived[part][middle], axis=2)
        term = flags[0:1] * crossed
        if middle > 0:
            term = term + jnp.sum(sum(arrived[part][:middle]) * far[part], axis=2)
        terms.append(term)
    gain_term = jnp.concatenate(terms, axis=0) + jnp.concatenate(
        [local_part[2] for local_part in locals_], axis=0
    )

    zeros = jnp.zeros(states.shape, F32)
    if middle == 1:
        firsts, seconds = ([own[i] for own in arrived] for i in range(2))
    else:
        firsts = [sum(own[:middle], zeros) for own in arrived]
        seconds = [sum(own[middle:-1], zeros) for own in arrived]
    lasts = [own[-1] for own in arrived]
    half = head_width // lax.axis_size("dp")
    second_half = flags[1:2, :half]
    lower_half, upper_half = gain_term[:, :half], gain_term[:, half:]
    away = (1.0 - second_half) * upper_half + second_half * lower_half
    kept = (1.0 - second_half) * lower_half + second_half * upper_half
    grad_gain = kept + lax.ppermute(away, "dp", [(0, 1), (1, 0)])

    def exchanged(array, reach):
        return lax.ppermute(array, "ctx", [(i, i ^ reach) for i in range(count)])

    pending, reach = [], 1
    while reach < count:
        if pending:
            grad_gain = summed(grad_gain, pending)
        pending = [exchanged(grad_gain, reach)]
        if reach * 2 < count:
            pending += [exchanged(grad_gain, reach * 2), exchanged(grad_gain, reach * 3)]
        reach *= 2 * min(len(pending), 2)

    done = list(
        merge(
            *held, gain, flags, shard_fac,
            *[local_part[0] for local_part in locals_],
            *[local_part[1] for local_part in locals_],
            *firsts, *seconds, *lasts,
        )
    )
    pending, done[4] = lax.optimization_barrier((pending, done[4]))
    return (*done, summed(grad_gain, pending))


def solution(mesh):
    wide = P("dp", "ctx", "head")
    narrow = P("dp", "head", "ctx")
    return jax.shard_map(
        shards,
        mesh=mesh,
        in_specs=(wide, wide, wide, narrow, P("dp", None), P("head", None), wide),
        out_specs=(wide, wide, wide, wide, narrow, P("head", "dp")),
        check_vma=False,
    )
```

```python
import functools
import math

import jax
import jax.numpy as jnp
from jax import lax
from jax.experimental import pallas as pl
from jax.experimental.pallas import tpu as pltpu
from jax.sharding import PartitionSpec as P

CHUNK = 128
PARTS = 2
UNROLL = 8
PRECISE = lax.Precision.HIGHEST
F32 = jnp.float32
BF16 = jnp.bfloat16
LOG2E = math.log2(math.e)


def dot_nn(a, b, precision=None):
    return lax.dot_general(
        a, b, (((1,), (0,)), ((), ())), precision=precision, preferred_element_type=F32
    )


def dot_nt(a, b):
    return lax.dot_general(a, b, (((1,), (1,)), ((), ())), preferred_element_type=F32)


def dot_tn(a, b):
    return lax.dot_general(a, b, (((0,), (0,)), ((), ())), preferred_element_type=F32)


def iota(shape, dim):
    return lax.broadcasted_iota(jnp.int32, shape, dim)


def total_of(array):
    return jnp.sum(jnp.sum(array, axis=0, keepdims=True), axis=1, keepdims=True)


def later_sums(column):
    kept = iota((CHUNK, CHUNK), 0) >= iota((CHUNK, CHUNK), 1)
    return jnp.sum(jnp.where(kept, column, 0.0), axis=0, keepdims=True)


def decay_tables(docs, ctx, small_ref, spread, cum_ref, chunk_fac_ref, shard_fac_ref):
    rows = cum_ref.shape[0]
    num_chunks = rows // 8
    tokens = num_chunks * CHUNK
    for chunk in range(num_chunks):
        part = small_ref[:, chunk * CHUNK : (chunk + 1) * CHUNK]
        spread[chunk * 8 : chunk * 8 + 4, :] = part
        spread[chunk * 8 + 4 : chunk * 8 + 8, :] = part
    gates = spread[...] * LOG2E
    lane_a, lane_b = iota((CHUNK, CHUNK), 0), iota((CHUNK, CHUNK), 1)
    prefix = dot_nn(gates, (lane_a <= lane_b).astype(F32), PRECISE)
    suffix = dot_nn(gates, (lane_a > lane_b).astype(F32), PRECISE)
    totals = jnp.broadcast_to(prefix[:, CHUNK - 1 : CHUNK], (rows, CHUNK))
    row_a, row_b = iota((rows, rows), 0), iota((rows, rows), 1)
    same = (row_a % 8) == (row_b % 8)
    outside = ((row_a % 8 < 4) & (row_b // 8 < row_a // 8)) | (
        (row_a % 8 >= 4) & (row_b // 8 > row_a // 8)
    )
    others = dot_nn((same & outside).astype(F32), totals, PRECISE)

    first = ctx * tokens
    chunk_first = first + (iota((rows, CHUNK), 0) // 8) * CHUNK
    from_start = iota((rows, CHUNK), 0) % 8 < 4
    chunk_anchor = jnp.where(from_start, chunk_first - 1, chunk_first + (CHUNK - 1)).astype(F32)
    shard_anchor = jnp.where(from_start, first - 1, first + (tokens - 1)).astype(F32)
    positions = (chunk_first + iota((rows, CHUNK), 1)).astype(F32)
    segment = jnp.zeros((rows, CHUNK), F32)
    chunk_segment = jnp.zeros((rows, CHUNK), F32)
    shard_segment = jnp.zeros((rows, CHUNK), F32)
    begin = small_ref.shape[1] - CHUNK
    start = jnp.zeros((1, 1), F32)
    for doc in range(docs):
        segment += jnp.where(positions >= start, 1.0, 0.0)
        chunk_segment += jnp.where(chunk_anchor >= start, 1.0, 0.0)
        shard_segment += jnp.where(shard_anchor >= start, 1.0, 0.0)
        start = start + small_ref[0:1, begin + doc : begin + doc + 1]
    cum_ref[...] = jnp.where(from_start, prefix, segment)
    exponent = jnp.where(from_start, prefix, suffix)
    chunk_fac_ref[...] = jnp.where(
        segment == chunk_segment, jnp.exp2(jnp.minimum(exponent, 0.0)), 0.0
    )
    keep = segment == shard_segment
    shard_fac_ref[...] = jnp.where(keep, jnp.exp2(jnp.minimum(exponent + others, 0.0)), 0.0)


def ends_kernel(head_width, docs, half_ctx, *refs):
    small_ref, sources = refs[0], refs[1:5]
    ctx, dp = lax.axis_index("ctx"), lax.axis_index("dp")
    near_refs, far_refs, decay_refs = (
        refs[5 + i * PARTS : 5 + (i + 1) * PARTS] for i in range(3)
    )
    (cum_ref, chunk_fac_ref, shard_fac_ref, gain_ref, flag_ref, q_ref, k_ref, v_ref, cot_ref,
     spread, sems) = refs[5 + 3 * PARTS :]
    heads = near_refs[0].shape[0]
    rows = shard_fac_ref.shape[0]
    steps = sems.shape[0]
    tokens = q_ref.shape[1]
    block = tokens // steps
    chunks = block // CHUNK

    def copies(step):
        at = pl.ds(step * block, block)
        return [
            pltpu.make_async_copy(source.at[:, at, :], target.at[:, at, :], sems.at[step, i])
            for i, (source, target) in enumerate(zip(sources, (q_ref, k_ref, v_ref, cot_ref)))
        ]

    for step in range(steps):
        for i, copy in enumerate(copies(step)):
            copy.start(priority=i % 2)
    decay_tables(docs, ctx, small_ref, spread, cum_ref, chunk_fac_ref, shard_fac_ref)
    gain_ref[...] = small_ref[:, tokens : tokens + head_width]
    for part in range(PARTS):
        for head in range(heads):
            row = rows - 8 + part * heads + head
            decay_refs[part][head] = jnp.broadcast_to(
                shard_fac_ref[row : row + 1, CHUNK - 1 : CHUNK], (1, head_width)
            )

    def turned(ref, step, row, scale):
        pieces = []
        head = row % 4
        for chunk in range(step * chunks, (step + 1) * chunks):
            factor = shard_fac_ref[chunk * 8 + row : chunk * 8 + row + 1, :]
            piece = jnp.transpose(
                ref[
                    0,
                    chunk * CHUNK : (chunk + 1) * CHUNK,
                    head * head_width : (head + 1) * head_width,
                ]
            )
            pieces.append((piece.astype(F32) * (factor * scale)).astype(BF16))
        return jnp.concatenate(pieces, axis=1)

    ends, grads = {}, {}
    for step in range(steps):
        for copy in copies(step):
            copy.wait()
        at = slice(step * block, (step + 1) * block)
        for row in range(PARTS * heads):
            lanes = slice(row * head_width, (row + 1) * head_width)
            end = dot_nn(turned(k_ref, step, 4 + row, 1.0), v_ref[0, at, lanes])
            grad = dot_nn(turned(q_ref, step, row, head_width ** (-0.5)), cot_ref[0, at, lanes])
            ends[row] = ends[row] + end if step else end
            grads[row] = grads[row] + grad if step else grad
    middle = jnp.where(ctx == half_ctx - 1, 1.0, 0.0)
    low = ctx < half_ctx
    row = iota(flag_ref.shape, 0)
    flag_ref[...] = jnp.where(
        row == 0, middle, jnp.where(row == 1, dp.astype(F32), jnp.where(low, 1.0, 0.0))
    )
    for part in range(PARTS):
        for head in range(heads):
            row = part * heads + head
            near_refs[part][head] = jnp.where(low, ends[row], grads[row])
            far_refs[part][head] = jnp.where(low, grads[row], ends[row])


def local_kernel(
    head_width, part, q_ref, k_ref, v_ref, cot_ref, gain_ref, cum_ref, fac_ref,
    target, dgate_ref, dgain_ref, leaving, state,
):
    out_ref, dq_ref, dk_ref, dv_ref = (target.at[pl.ds(i, 1)] for i in range(4))
    heads = state.shape[0]
    num_chunks = leaving.shape[0]
    scale = head_width ** (-0.5)
    unroll = math.gcd(num_chunks, UNROLL)

    groups = num_chunks // unroll
    def wide_lanes(head):
        row = part * heads + head
        return slice(row * head_width, (row + 1) * head_width)

    def lanes_of(head):
        return slice(head * head_width, (head + 1) * head_width)

    def rows_of(chunk):
        return pl.ds(pl.multiple_of(chunk * CHUNK, CHUNK), CHUNK)

    def table(ref, chunk):
        return ref[pl.ds(pl.multiple_of(chunk * 8, 8), 8), :]

    pairs = [(at, head) for at in range(unroll) for head in range(heads)]

    def backward(chunks):
        facs = [table(fac_ref, chunk) for chunk in chunks]
        added = {}
        for at, head in pairs:
            row = part * heads + head
            rows, lanes = rows_of(chunks[at]), wide_lanes(head)
            turned = jnp.transpose(q_ref[0, rows, lanes]).astype(F32)
            turned = (turned * (facs[at][row : row + 1, :] * scale)).astype(BF16)
            added[at, head] = dot_nn(turned, cot_ref[0, rows, lanes])
        for head in range(heads):
            row = part * heads + head
            held = state[head]
            for at in range(unroll):
                leaving[chunks[at], head] = held.astype(BF16)
                held = held * facs[at][row : row + 1, CHUNK - 1 : CHUNK] + added[at, head]
            state[head] = held

    def forward(chunks):
        facs = [table(fac_ref, chunk) for chunk in chunks]
        cums = [table(cum_ref, chunk) for chunk in chunks]
        fac_columns = [jnp.transpose(fac) for fac in facs]
        cum_columns = [jnp.transpose(cum) for cum in cums]
        causal = iota((CHUNK, CHUNK), 0) >= iota((CHUNK, CHUNK), 1)
        limits = [
            jnp.where((columns[:, 4:5] == cum[4:5, :]) & causal, math.log2(scale), -1e30)
            for columns, cum in zip(cum_columns, cums)
        ]
        cum_columns = [columns + math.log2(scale) for columns in cum_columns]
        q, k, v, cot, k_raw, k_decayed, q_decayed, later = ({} for _ in range(8))
        from_start, to_end, added, held, entering = ({} for _ in range(5))
        for key in pairs:
            at, head = key
            row = part * heads + head
            rows, lanes = rows_of(chunks[at]), lanes_of(head)
            q[key], cot[key] = q_ref[0, rows, wide_lanes(head)], cot_ref[0, rows, wide_lanes(head)]
            v[key] = v_ref[0, rows, wide_lanes(head)]
            later[key] = leaving[chunks[at], head]
            k_raw[key] = k_ref[0, rows, wide_lanes(head)].astype(F32)
            k_wide = k_raw[key] * gain_ref[row : row + 1, :]
            k[key] = k_wide.astype(BF16)
            from_start[key] = fac_columns[at][:, row : row + 1] * scale
            to_end[key] = fac_columns[at][:, 4 + row : 5 + row]
            k_decayed[key] = (k_wide * to_end[key]).astype(BF16)
            q_decayed[key] = (q[key].astype(F32) * from_start[key]).astype(BF16)
            added[key] = dot_tn(k_decayed[key], v[key])
        for head in range(heads):
            row = part * heads + head
            now = state[head]
            for at in range(unroll):
                held[at, head] = now
                entering[at, head] = now.astype(BF16)
                now = now * facs[at][row : row + 1, CHUNK - 1 : CHUNK] + added[at, head]
            held[unroll, head] = now
            state[head] = now
        by_cot, scores, written = {}, {}, {}
        for key in pairs:
            by_cot[key] = dot_nt(cot[key], jnp.concatenate([v[key], entering[key]], axis=0))
            scores[key] = dot_nt(q[key], k[key])
            written[key] = dot_nt(v[key], later[key])
        weights, grad_scores = {}, {}
        for key in pairs:
            at, head = key
            row = part * heads + head
            decays = jnp.exp2(
                jnp.minimum(cum_columns[at][:, row : row + 1] - cums[at][row : row + 1, :], limits[at])
            )
            weights[key] = (scores[key] * decays).astype(BF16)
            grad_scores[key] = (by_cot[key][:, :CHUNK] * decays).astype(BF16)
        out, dq, dk, dv = {}, {}, {}, {}
        for key in pairs:
            out[key] = dot_nn(
                jnp.concatenate([weights[key], q_decayed[key]], axis=1),
                jnp.concatenate([v[key], entering[key]], axis=0),
            )
            dv[key] = dot_nn(
                jnp.concatenate([jnp.transpose(weights[key]), k_decayed[key]], axis=1),
                jnp.concatenate([cot[key], later[key]], axis=0),
            )
            dq[key] = dot_nn(grad_scores[key], k[key]) + by_cot[key][:, CHUNK:] * from_start[key]
            dk[key] = dot_tn(grad_scores[key], q[key]) + written[key] * to_end[key]
        gate_rows, gain_rows = {}, {}
        for key in pairs:
            at, head = key
            balance = jnp.sum(
                out[key] * cot[key].astype(F32) - dv[key] * v[key].astype(F32),
                axis=1, keepdims=True,
            )
            gate_rows[key] = later_sums(balance) + total_of(
                held[at + 1, head] * later[key].astype(F32)
            )
            gain_rows[key] = jnp.sum(dk[key] * k_raw[key], axis=0, keepdims=True)
        for key in pairs:
            at, head = key
            row = part * heads + head
            rows, own = rows_of(chunks[at]), lanes_of(head)
            out_ref[0, rows, own] = out[key].astype(BF16)
            dq_ref[0, rows, own] = dq[key].astype(BF16)
            dv_ref[0, rows, own] = dv[key].astype(BF16)
            dk_ref[0, rows, own] = (dk[key] * gain_ref[row : row + 1, :]).astype(BF16)
            dgate_ref[0, head : head + 1, rows] = gate_rows[key]
        for head in range(heads):
            dgain_ref[head : head + 1, :] += sum(gain_rows[at, head] for at in range(unroll))

    state[...] = jnp.zeros_like(state)

    def backward_group(index, carry):
        backward([num_chunks - 1 - (index * unroll + at) for at in range(unroll)])
        return carry

    lax.fori_loop(0, groups, backward_group, 0)
    state[...] = jnp.zeros_like(state)
    dgain_ref[...] = jnp.zeros_like(dgain_ref)

    def forward_group(index, carry):
        forward([index * unroll + at for at in range(unroll)])
        return carry

    lax.fori_loop(0, groups, forward_group, 0)


def merge_kernel(head_width, part, *refs):
    q_ref, k_ref, v_ref, cot_ref, gain_ref, flag_ref, fac_ref = refs[:7]
    first_ref, second_ref, last_ref = refs[7:10]
    heads = first_ref.shape[0]
    partial_refs, gate_refs = refs[10 : 10 + heads], refs[10 + heads : 10 + 2 * heads]
    refs = refs[10 + 2 * heads :]
    if part > 0:
        before_ref, refs = refs[0], refs[5:]
    targets, dgate_ref, staged, entering, leaving, sems = refs[:4], *refs[4:]
    steps = sems.shape[0]
    num_chunks = fac_ref.shape[0] // 8
    chunks = num_chunks // steps
    block = chunks * CHUNK
    scale = head_width ** (-0.5)
    group = slice(part * heads * head_width, (part + 1) * heads * head_width)

    def copies(step):
        at = pl.ds(step * block, block)
        return [
            pltpu.make_async_copy(
                staged.at[i, at, :], target.at[0, at, group], sems.at[step, i]
            )
            for i, target in enumerate(targets)
        ]

    def arrived(head):
        low = jnp.broadcast_to(flag_ref[2:3, :], (head_width, head_width)) > 0.5
        first, second = first_ref[head], second_ref[head] + last_ref[head]
        return jnp.where(low, first, second), jnp.where(low, second, first)

    gain_columns = jnp.transpose(jnp.concatenate([gain_ref[...], gain_ref[...]], axis=0))
    entering[...] = jnp.zeros_like(entering)
    leaving[...] = jnp.zeros_like(leaving)
    last = fac_ref[(num_chunks - 1) * 8 : num_chunks * 8, CHUNK - 1 : CHUNK]
    constants = []
    for head in range(heads):
        row = part * heads + head
        own = slice(head * head_width, (head + 1) * head_width)
        gain = gain_columns[:, row : row + 1]
        state, later = arrived(head)
        state = state * gain
        entering[own, own] = (state * scale).astype(BF16)
        leaving[own, own] = (later * gain).astype(BF16)
        constants.append(total_of(state * later) * last[row : row + 1])

    gate_sums, kept_sums, totals = {}, {}, {}
    for step in range(steps):
        numbers = range(step * chunks, (step + 1) * chunks)
        products, results = {}, {}
        for number in numbers:
            rows = slice(number * CHUNK, (number + 1) * CHUNK)
            products[number] = (
                dot_nn(q_ref[0, rows, group], entering[...]),
                dot_nt(cot_ref[0, rows, group], entering[...]),
                dot_nt(v_ref[0, rows, group], leaving[...]),
                dot_nn(k_ref[0, rows, group], leaving[...]),
            )
        for number in numbers:
            columns = jnp.transpose(fac_ref[number * 8 : number * 8 + 8, :])
            rows = slice(number * CHUNK, (number + 1) * CHUNK)
            for head in range(heads):
                row = part * heads + head
                lanes = slice(head * head_width, (head + 1) * head_width)
                wide = slice(row * head_width, (row + 1) * head_width)
                from_start, to_end = columns[:, row : row + 1], columns[:, 4 + row : 5 + row]
                across, dq, dk, written = (
                    product[:, lanes] * factor
                    for product, factor in zip(
                        products[number], (from_start, from_start, to_end, to_end)
                    )
                )
                results[number, head] = [
                    (partial_refs[head][i, rows, :].astype(F32) + added).astype(BF16)
                    for i, added in enumerate((across, dq, dk, written))
                ]
                kept = written * v_ref[0, rows, wide].astype(F32)
                balance = jnp.sum(
                    across * cot_ref[0, rows, wide].astype(F32) - kept, axis=1, keepdims=True
                )
                gate_sums[number, head] = later_sums(balance)
                totals[number, head] = jnp.sum(balance, axis=0, keepdims=True)
                kept_sums[number, head] = jnp.sum(kept, axis=0, keepdims=True)
        for number in numbers:
            rows = slice(number * CHUNK, (number + 1) * CHUNK)
            for head in range(heads):
                lanes = slice(head * head_width, (head + 1) * head_width)
                for i in range(4):
                    staged[i, rows, lanes] = results[number, head][i]
        for i, copy in enumerate(copies(step)):
            copy.start(priority=i % 2)

    if part > 0:
        dgate_ref[0, : part * heads, :] = before_ref[0]
    for head in range(heads):
        row = part * heads + head
        kept = sum(kept_sums[number, head] for number in range(num_chunks))
        base = jnp.sum(kept, axis=1, keepdims=True) + constants[head]
        for number in range(num_chunks - 1, -1, -1):
            lanes = slice(number * CHUNK, (number + 1) * CHUNK)
            dgate_ref[0, row : row + 1, lanes] = (
                gate_refs[head][0, :, lanes] + gate_sums[number, head] + base
            )
            base = base + totals[number, head]
    for step in range(steps):
        for copy in copies(step):
            copy.wait()


def summed(own, others):
    if len(others) == 1:
        return own + others[0]
    return (own + others[0]) + (others[1] + others[2])


def shards(queries, keys_raw, values, gates, lengths, key_gain, cotangent):
    tokens, width = queries.shape[1:]
    all_heads, head_width = key_gain.shape
    heads = all_heads // PARTS
    part_width = width // PARTS
    num_chunks = tokens // CHUNK
    rows = num_chunks * 8
    block = min(256, tokens)
    steps = tokens // block
    count = lax.axis_size("ctx")
    middle = count // 2 - 1
    docs = lengths.shape[1]
    sizes = jnp.pad(lengths, ((0, all_heads - 1), (0, CHUNK - docs))).astype(F32)
    small = jnp.concatenate([gates[0], key_gain, sizes], axis=1)

    def shape_of(*shape, dtype=F32):
        return jax.ShapeDtypeStruct(shape, dtype)

    hbm = pl.BlockSpec(memory_space=pltpu.HBM)
    vmem = pl.BlockSpec(memory_space=pltpu.VMEM)
    table = shape_of(rows, CHUNK)
    states = shape_of(heads, head_width, head_width)
    decays = shape_of(heads, 1, head_width)
    partials = shape_of(4, tokens, head_width, dtype=BF16)
    streams = (queries, keys_raw, values, cotangent)
    product = 2 * tokens * part_width * head_width

    def ends():
        outs = [states] * (2 * PARTS) + [decays] * PARTS + [table] * 3
        outs += [shape_of(all_heads, head_width), shape_of(4, head_width)]
        outs += [shape_of(1, tokens, width, dtype=BF16)] * 4
        return pl.pallas_call(
            functools.partial(ends_kernel, head_width, lengths.shape[1], count // 2),
            in_specs=[vmem] + [hbm] * 4,
            out_specs=[vmem] * len(outs),
            out_shape=outs,
            scratch_shapes=[
                pltpu.VMEM((rows, CHUNK), F32),
                pltpu.SemaphoreType.DMA((steps, 4)),
            ],
            compiler_params=pltpu.CompilerParams(vmem_limit_bytes=49 << 20),
            cost_estimate=pl.CostEstimate(
                flops=2 * product * PARTS, bytes_accessed=8 * tokens * width, transcendentals=0
            ),
            name="shard_ends",
        )(small, *streams)

    def local(row, cum):
        return pl.pallas_call(
            functools.partial(local_kernel, head_width, row),
            in_specs=[vmem] * 7,
            out_specs=[vmem] * 3,
            out_shape=[partials, shape_of(1, 1, tokens), shape_of(1, head_width)],
            scratch_shapes=[
                pltpu.VMEM((num_chunks, 1, head_width, head_width), BF16),
                pltpu.VMEM((1, head_width, head_width), F32),
            ],
            compiler_params=pltpu.CompilerParams(vmem_limit_bytes=24 << 20),
            cost_estimate=pl.CostEstimate(
                flops=12 * product // heads, bytes_accessed=16 * tokens * head_width, transcendentals=0
            ),
            name=f"local_{row}",
        )(*held, gain, cum, chunk_fac)

    def merge(part, flag_rows, arrivals, done):
        own = locals_[part * heads : (part + 1) * heads]
        inputs = [*held, gain, flag_rows, shard_fac, *arrivals]
        inputs += [local_part[0] for local_part in own] + [local_part[1] for local_part in own]
        extra = [done[4], *done[:4]] if part > 0 else []
        aliases = {len(inputs) + 1 + i: i for i in range(4)} if part > 0 else {}
        full_gates = shape_of(1, (part + 1) * heads, tokens)
        return pl.pallas_call(
            functools.partial(merge_kernel, head_width, part),
            in_specs=[vmem] * len(inputs) + ([vmem] + [hbm] * 4 if part > 0 else []),
            out_specs=[hbm] * 4 + [vmem],
            out_shape=[shape_of(1, tokens, width, dtype=BF16)] * 4 + [full_gates],
            scratch_shapes=[
                pltpu.VMEM((4, tokens, part_width), BF16),
                pltpu.VMEM((part_width, part_width), BF16),
                pltpu.VMEM((part_width, part_width), BF16),
                pltpu.SemaphoreType.DMA((steps, 4)),
            ],
            input_output_aliases=aliases,
            compiler_params=pltpu.CompilerParams(vmem_limit_bytes=24 << 20),
            cost_estimate=pl.CostEstimate(
                flops=4 * product, bytes_accessed=24 * tokens * part_width, transcendentals=0
            ),
            name=f"merge_{part}",
        )(*inputs, *extra)

    results = ends()
    near, far, decay = (results[i * PARTS : (i + 1) * PARTS] for i in range(3))
    cum, chunk_fac, shard_fac, gain, flags = results[3 * PARTS : 3 * PARTS + 5]
    held = results[3 * PARTS + 5 :]
    sent = [[] for _ in range(PARTS)]
    arrived = [[] for _ in range(PARTS)]

    def send(part, hop, started):
        payload = near[part] if hop <= middle else far[part]
        if hop > 0:
            payload = payload + decay[part] * arrived[part][-1]
        if started:
            payload, *_ = lax.optimization_barrier((payload, *started))
        sent[part].append(payload)
        arrived[part].append(
            lax.ppermute(
                payload, "ctx", [(hop, hop + 1), (count - 1 - hop, count - 2 - hop)]
            )
        )

    locals_, per_stage = [], [2, 1, 1]
    for stage in range(count - 2 + PARTS):
        started = []
        for part in range(PARTS):
            if 0 <= stage - part < count - 1:
                send(part, stage - part, started)
                started.append(sent[part][-1])
        for _ in range(per_stage[stage] if stage < 3 else 0):
            local_cum = cum
            if stage > 0:
                local_cum, *_ = lax.optimization_barrier((cum, *started))
            locals_.append(list(local(len(locals_), local_cum)))
            behind = 0 if stage + 1 < count - 1 else PARTS - 1
            locals_[-1][2], arrived[behind][-1] = lax.optimization_barrier(
                (locals_[-1][2], arrived[behind][-1])
            )

    terms = []
    for part in range(PARTS):
        crossed = jnp.sum(sent[part][middle] * arrived[part][middle], axis=2)
        term = flags[0:1] * crossed
        if middle > 0:
            term = term + jnp.sum(sum(arrived[part][:middle]) * far[part], axis=2)
        terms.append(term)
    gain_term = jnp.concatenate(terms, axis=0) + jnp.concatenate(
        [local_part[2] for local_part in locals_], axis=0
    )

    zeros = jnp.zeros(states.shape, F32)
    if middle == 1:
        firsts, seconds = ([own[i] for own in arrived] for i in range(2))
    else:
        firsts = [sum(own[:middle], zeros) for own in arrived]
        seconds = [sum(own[middle:-1], zeros) for own in arrived]
    lasts = [own[-1] for own in arrived]
    half = head_width // lax.axis_size("dp")
    second_half = flags[1:2, :half]
    lower_half, upper_half = gain_term[:, :half], gain_term[:, half:]
    away = (1.0 - second_half) * upper_half + second_half * lower_half
    kept = (1.0 - second_half) * lower_half + second_half * upper_half
    grad_gain = kept + lax.ppermute(away, "dp", [(0, 1), (1, 0)])

    def exchanged(array, reach):
        return lax.ppermute(array, "ctx", [(i, i ^ reach) for i in range(count)])

    pending, reach = [], 1
    while reach < count:
        if pending:
            grad_gain = summed(grad_gain, pending)
        pending = [exchanged(grad_gain, reach)]
        if reach * 2 < count:
            pending += [exchanged(grad_gain, reach * 2), exchanged(grad_gain, reach * 3)]
        reach *= 2 * min(len(pending), 2)

    done = []
    for part in range(PARTS):
        flag_rows = flags
        if part < PARTS - 1:
            flag_rows, _ = lax.optimization_barrier((flags, sent[part + 1][-1]))
        done = list(merge(part, flag_rows, (firsts[part], seconds[part], lasts[part]), done))
    pending, done[4] = lax.optimization_barrier((pending, done[4]))
    return (*done, summed(grad_gain, pending))


def solution(mesh):
    wide = P("dp", "ctx", "head")
    narrow = P("dp", "head", "ctx")
    return jax.shard_map(
        shards,
        mesh=mesh,
        in_specs=(wide, wide, wide, narrow, P("dp", None), P("head", None), wide),
        out_specs=(wide, wide, wide, wide, narrow, P("head", "dp")),
        check_vma=False,
    )
```

```python
import functools
import math

import jax
import jax.numpy as jnp
from jax import lax
from jax.experimental import pallas as pl
from jax.experimental.pallas import tpu as pltpu
from jax.sharding import PartitionSpec as P

CHUNK = 128
PARTS = 2
UNROLL = 4
PRECISE = lax.Precision.HIGHEST
F32 = jnp.float32
BF16 = jnp.bfloat16
LOG2E = math.log2(math.e)


def dot_nn(a, b, precision=None):
    return lax.dot_general(
        a, b, (((1,), (0,)), ((), ())), precision=precision, preferred_element_type=F32
    )


def dot_nt(a, b):
    return lax.dot_general(a, b, (((1,), (1,)), ((), ())), preferred_element_type=F32)


def dot_tn(a, b):
    return lax.dot_general(a, b, (((0,), (0,)), ((), ())), preferred_element_type=F32)


def iota(shape, dim):
    return lax.broadcasted_iota(jnp.int32, shape, dim)


def total_of(array):
    return jnp.sum(jnp.sum(array, axis=0, keepdims=True), axis=1, keepdims=True)


def later_sums(column):
    kept = iota((CHUNK, CHUNK), 0) >= iota((CHUNK, CHUNK), 1)
    return jnp.sum(jnp.where(kept, column, 0.0), axis=0, keepdims=True)


def decay_tables(docs, ctx, small_ref, spread, cum_ref, chunk_fac_ref, shard_fac_ref):
    rows = cum_ref.shape[0]
    num_chunks = rows // 8
    tokens = num_chunks * CHUNK
    for chunk in range(num_chunks):
        part = small_ref[:, chunk * CHUNK : (chunk + 1) * CHUNK]
        spread[chunk * 8 : chunk * 8 + 4, :] = part
        spread[chunk * 8 + 4 : chunk * 8 + 8, :] = part
    gates = spread[...] * LOG2E
    lane_a, lane_b = iota((CHUNK, CHUNK), 0), iota((CHUNK, CHUNK), 1)
    prefix = dot_nn(gates, (lane_a <= lane_b).astype(F32), PRECISE)
    suffix = dot_nn(gates, (lane_a > lane_b).astype(F32), PRECISE)
    totals = jnp.broadcast_to(prefix[:, CHUNK - 1 : CHUNK], (rows, CHUNK))
    row_a, row_b = iota((rows, rows), 0), iota((rows, rows), 1)
    same = (row_a % 8) == (row_b % 8)
    outside = ((row_a % 8 < 4) & (row_b // 8 < row_a // 8)) | (
        (row_a % 8 >= 4) & (row_b // 8 > row_a // 8)
    )
    others = dot_nn((same & outside).astype(F32), totals, PRECISE)

    first = ctx * tokens
    chunk_first = first + (iota((rows, CHUNK), 0) // 8) * CHUNK
    from_start = iota((rows, CHUNK), 0) % 8 < 4
    chunk_anchor = jnp.where(from_start, chunk_first - 1, chunk_first + (CHUNK - 1)).astype(F32)
    shard_anchor = jnp.where(from_start, first - 1, first + (tokens - 1)).astype(F32)
    positions = (chunk_first + iota((rows, CHUNK), 1)).astype(F32)
    segment = jnp.zeros((rows, CHUNK), F32)
    chunk_segment = jnp.zeros((rows, CHUNK), F32)
    shard_segment = jnp.zeros((rows, CHUNK), F32)
    begin = small_ref.shape[1] - CHUNK
    start = jnp.zeros((1, 1), F32)
    for doc in range(docs):
        segment += jnp.where(positions >= start, 1.0, 0.0)
        chunk_segment += jnp.where(chunk_anchor >= start, 1.0, 0.0)
        shard_segment += jnp.where(shard_anchor >= start, 1.0, 0.0)
        start = start + small_ref[0:1, begin + doc : begin + doc + 1]
    cum_ref[...] = jnp.where(from_start, prefix, segment)
    exponent = jnp.where(from_start, prefix, suffix)
    chunk_fac_ref[...] = jnp.where(
        segment == chunk_segment, jnp.exp2(jnp.minimum(exponent, 0.0)), 0.0
    )
    keep = segment == shard_segment
    shard_fac_ref[...] = jnp.where(keep, jnp.exp2(jnp.minimum(exponent + others, 0.0)), 0.0)


def ends_kernel(head_width, docs, half_ctx, *refs):
    small_ref, sources = refs[0], refs[1:5]
    ctx, dp = lax.axis_index("ctx"), lax.axis_index("dp")
    near_refs, far_refs, decay_refs = (
        refs[5 + i * PARTS : 5 + (i + 1) * PARTS] for i in range(3)
    )
    (cum_ref, chunk_fac_ref, shard_fac_ref, gain_ref, flag_ref, q_ref, k_ref, v_ref, cot_ref,
     spread, sems) = refs[5 + 3 * PARTS :]
    heads = near_refs[0].shape[0]
    rows = shard_fac_ref.shape[0]
    steps = sems.shape[0]
    tokens = q_ref.shape[1]
    block = tokens // steps
    chunks = block // CHUNK

    def copies(step):
        at = pl.ds(step * block, block)
        return [
            pltpu.make_async_copy(source.at[:, at, :], target.at[:, at, :], sems.at[step, i])
            for i, (source, target) in enumerate(zip(sources, (q_ref, k_ref, v_ref, cot_ref)))
        ]

    for step in range(steps):
        for i, copy in enumerate(copies(step)):
            copy.start(priority=i % 2)
    decay_tables(docs, ctx, small_ref, spread, cum_ref, chunk_fac_ref, shard_fac_ref)
    gain_ref[...] = small_ref[:, tokens : tokens + head_width]
    for part in range(PARTS):
        for head in range(heads):
            row = rows - 8 + part * heads + head
            decay_refs[part][head] = jnp.broadcast_to(
                shard_fac_ref[row : row + 1, CHUNK - 1 : CHUNK], (1, head_width)
            )

    def turned(ref, step, row, scale):
        pieces = []
        head = row % 4
        for chunk in range(step * chunks, (step + 1) * chunks):
            factor = shard_fac_ref[chunk * 8 + row : chunk * 8 + row + 1, :]
            piece = jnp.transpose(
                ref[
                    0,
                    chunk * CHUNK : (chunk + 1) * CHUNK,
                    head * head_width : (head + 1) * head_width,
                ]
            )
            pieces.append((piece.astype(F32) * (factor * scale)).astype(BF16))
        return jnp.concatenate(pieces, axis=1)

    ends, grads = {}, {}
    for step in range(steps):
        for copy in copies(step):
            copy.wait()
        at = slice(step * block, (step + 1) * block)
        for row in range(PARTS * heads):
            lanes = slice(row * head_width, (row + 1) * head_width)
            end = dot_nn(turned(k_ref, step, 4 + row, 1.0), v_ref[0, at, lanes])
            grad = dot_nn(turned(q_ref, step, row, head_width ** (-0.5)), cot_ref[0, at, lanes])
            ends[row] = ends[row] + end if step else end
            grads[row] = grads[row] + grad if step else grad
    middle = jnp.where(ctx == half_ctx - 1, 1.0, 0.0)
    low = ctx < half_ctx
    row = iota(flag_ref.shape, 0)
    flag_ref[...] = jnp.where(
        row == 0, middle, jnp.where(row == 1, dp.astype(F32), jnp.where(low, 1.0, 0.0))
    )
    for part in range(PARTS):
        for head in range(heads):
            row = part * heads + head
            near_refs[part][head] = jnp.where(low, ends[row], grads[row])
            far_refs[part][head] = jnp.where(low, grads[row], ends[row])


def local_kernel(
    head_width, part, q_ref, k_ref, v_ref, cot_ref, gain_ref, cum_ref, fac_ref,
    target, dgate_ref, dgain_ref, leaving, state,
):
    out_ref, dq_ref, dk_ref, dv_ref = (target.at[pl.ds(i, 1)] for i in range(4))
    heads = state.shape[0]
    num_chunks = leaving.shape[0]
    scale = head_width ** (-0.5)
    unroll = math.gcd(num_chunks, UNROLL)

    groups = num_chunks // unroll
    def wide_lanes(head):
        row = part * heads + head
        return slice(row * head_width, (row + 1) * head_width)

    def lanes_of(head):
        return slice(head * head_width, (head + 1) * head_width)

    def rows_of(chunk):
        return pl.ds(pl.multiple_of(chunk * CHUNK, CHUNK), CHUNK)

    def table(ref, chunk):
        return ref[pl.ds(pl.multiple_of(chunk * 8, 8), 8), :]

    pairs = [(at, head) for at in range(unroll) for head in range(heads)]

    def backward(chunks):
        facs = [table(fac_ref, chunk) for chunk in chunks]
        added = {}
        for at, head in pairs:
            row = part * heads + head
            rows, lanes = rows_of(chunks[at]), wide_lanes(head)
            turned = jnp.transpose(q_ref[0, rows, lanes]).astype(F32)
            turned = (turned * (facs[at][row : row + 1, :] * scale)).astype(BF16)
            added[at, head] = dot_nn(turned, cot_ref[0, rows, lanes])
        for head in range(heads):
            row = part * heads + head
            held = state[head]
            for at in range(unroll):
                leaving[chunks[at], head] = held.astype(BF16)
                held = held * facs[at][row : row + 1, CHUNK - 1 : CHUNK] + added[at, head]
            state[head] = held

    def forward(chunks):
        facs = [table(fac_ref, chunk) for chunk in chunks]
        cums = [table(cum_ref, chunk) for chunk in chunks]
        fac_columns = [jnp.transpose(fac) for fac in facs]
        cum_columns = [jnp.transpose(cum) for cum in cums]
        causal = iota((CHUNK, CHUNK), 0) >= iota((CHUNK, CHUNK), 1)
        limits = [
            jnp.where((columns[:, 4:5] == cum[4:5, :]) & causal, math.log2(scale), -1e30)
            for columns, cum in zip(cum_columns, cums)
        ]
        cum_columns = [columns + math.log2(scale) for columns in cum_columns]
        q, k, v, cot, k_raw, k_decayed, q_decayed, later = ({} for _ in range(8))
        from_start, to_end, added, held, entering = ({} for _ in range(5))
        for key in pairs:
            at, head = key
            row = part * heads + head
            rows, lanes = rows_of(chunks[at]), lanes_of(head)
            q[key], cot[key] = q_ref[0, rows, wide_lanes(head)], cot_ref[0, rows, wide_lanes(head)]
            v[key] = v_ref[0, rows, wide_lanes(head)]
            later[key] = leaving[chunks[at], head]
            k_raw[key] = k_ref[0, rows, wide_lanes(head)].astype(F32)
            k_wide = k_raw[key] * gain_ref[row : row + 1, :]
            k[key] = k_wide.astype(BF16)
            from_start[key] = fac_columns[at][:, row : row + 1] * scale
            to_end[key] = fac_columns[at][:, 4 + row : 5 + row]
            k_decayed[key] = (k_wide * to_end[key]).astype(BF16)
            q_decayed[key] = (q[key].astype(F32) * from_start[key]).astype(BF16)
            added[key] = dot_tn(k_decayed[key], v[key])
        for head in range(heads):
            row = part * heads + head
            now = state[head]
            for at in range(unroll):
                held[at, head] = now
                entering[at, head] = now.astype(BF16)
                now = now * facs[at][row : row + 1, CHUNK - 1 : CHUNK] + added[at, head]
            held[unroll, head] = now
            state[head] = now
        by_cot, scores, written = {}, {}, {}
        for key in pairs:
            by_cot[key] = dot_nt(cot[key], jnp.concatenate([v[key], entering[key]], axis=0))
            scores[key] = dot_nt(q[key], k[key])
            written[key] = dot_nt(v[key], later[key])
        weights, grad_scores = {}, {}
        for key in pairs:
            at, head = key
            row = part * heads + head
            decays = jnp.exp2(
                jnp.minimum(cum_columns[at][:, row : row + 1] - cums[at][row : row + 1, :], limits[at])
            )
            weights[key] = (scores[key] * decays).astype(BF16)
            grad_scores[key] = (by_cot[key][:, :CHUNK] * decays).astype(BF16)
        out, dq, dk, dv = {}, {}, {}, {}
        for key in pairs:
            out[key] = dot_nn(
                jnp.concatenate([weights[key], q_decayed[key]], axis=1),
                jnp.concatenate([v[key], entering[key]], axis=0),
            )
            dv[key] = dot_nn(
                jnp.concatenate([jnp.transpose(weights[key]), k_decayed[key]], axis=1),
                jnp.concatenate([cot[key], later[key]], axis=0),
            )
            dq[key] = dot_nn(grad_scores[key], k[key]) + by_cot[key][:, CHUNK:] * from_start[key]
            dk[key] = dot_tn(grad_scores[key], q[key]) + written[key] * to_end[key]
        gate_rows, gain_rows = {}, {}
        for key in pairs:
            at, head = key
            balance = jnp.sum(
                out[key] * cot[key].astype(F32) - dv[key] * v[key].astype(F32),
                axis=1, keepdims=True,
            )
            gate_rows[key] = later_sums(balance) + total_of(
                held[at + 1, head] * later[key].astype(F32)
            )
            gain_rows[key] = jnp.sum(dk[key] * k_raw[key], axis=0, keepdims=True)
        for key in pairs:
            at, head = key
            row = part * heads + head
            rows, own = rows_of(chunks[at]), lanes_of(head)
            out_ref[0, rows, own] = out[key].astype(BF16)
            dq_ref[0, rows, own] = dq[key].astype(BF16)
            dv_ref[0, rows, own] = dv[key].astype(BF16)
            dk_ref[0, rows, own] = (dk[key] * gain_ref[row : row + 1, :]).astype(BF16)
            dgate_ref[0, head : head + 1, rows] = gate_rows[key]
        for head in range(heads):
            dgain_ref[head : head + 1, :] += sum(gain_rows[at, head] for at in range(unroll))

    state[...] = jnp.zeros_like(state)

    def backward_group(index, carry):
        backward([num_chunks - 1 - (index * unroll + at) for at in range(unroll)])
        return carry

    lax.fori_loop(0, groups, backward_group, 0)
    state[...] = jnp.zeros_like(state)
    dgain_ref[...] = jnp.zeros_like(dgain_ref)

    def forward_group(index, carry):
        forward([index * unroll + at for at in range(unroll)])
        return carry

    lax.fori_loop(0, groups, forward_group, 0)


def merge_kernel(head_width, *refs):
    q_ref, k_ref, v_ref, cot_ref, gain_ref, flag_ref, fac_ref = refs[:7]
    partial_refs, gate_refs, first_refs, second_refs, last_refs = (
        refs[7 + i * PARTS : 7 + (i + 1) * PARTS] for i in range(5)
    )
    refs = refs[7 + 5 * PARTS :]
    targets, dgate_ref, staged, entering, leaving, spread_ref, gate_scr, sems = refs[:4], *refs[4:]
    heads = first_refs[0].shape[0]
    steps = sems.shape[0]
    num_chunks = fac_ref.shape[0] // 8
    chunks = num_chunks // steps
    block = chunks * CHUNK
    group_width = heads * head_width
    scale = head_width ** (-0.5)

    def copies(step):
        at = pl.ds(step * block, block)
        return [
            pltpu.make_async_copy(staged.at[i, at, :], target.at[0, at, :], sems.at[step, i])
            for i, target in enumerate(targets)
        ]

    gain_columns = jnp.transpose(jnp.concatenate([gain_ref[...], gain_ref[...]], axis=0))
    entering[...] = jnp.zeros_like(entering)
    leaving[...] = jnp.zeros_like(leaving)
    last_factors = fac_ref[(num_chunks - 1) * 8 : num_chunks * 8, CHUNK - 1 : CHUNK]
    low = jnp.broadcast_to(flag_ref[2:3, :], (head_width, head_width)) > 0.5
    constants = []
    for part in range(PARTS):
        for head in range(heads):
            row = part * heads + head
            own = slice(head * head_width, (head + 1) * head_width)
            gain = gain_columns[:, row : row + 1]
            first = first_refs[part][head]
            second = second_refs[part][head] + last_refs[part][head]
            state = jnp.where(low, first, second) * gain
            later = jnp.where(low, second, first)
            entering[part, own, own] = (state * scale).astype(BF16)
            leaving[part, own, own] = (later * gain).astype(BF16)
            constants.append(total_of(state * later) * last_factors[row : row + 1])

    spread = (iota(spread_ref.shape, 1) // head_width == iota(spread_ref.shape, 0) % 8).astype(F32)
    spread_ref[...] = spread.astype(BF16)
    ones = jnp.ones((8, head_width), BF16)
    for step in range(steps):
        numbers = range(step * chunks, (step + 1) * chunks)
        products, results, factors = {}, {}, {}
        for number in numbers:
            rows = slice(number * CHUNK, (number + 1) * CHUNK)
            fac = fac_ref[number * 8 : number * 8 + 8, :]
            high = fac.astype(BF16).astype(F32)
            both = jnp.concatenate([high, fac - high], axis=0).astype(BF16)
            factors[number] = dot_tn(both, spread_ref[...])
            for part in range(PARTS):
                group = slice(part * group_width, (part + 1) * group_width)
                products[number, part] = (
                    dot_nn(q_ref[0, rows, group], entering[part]),
                    dot_nt(cot_ref[0, rows, group], entering[part]),
                    dot_nt(v_ref[0, rows, group], leaving[part]),
                    dot_nn(k_ref[0, rows, group], leaving[part]),
                )
        for number in numbers:
            rows = slice(number * CHUNK, (number + 1) * CHUNK)
            for row in range(PARTS * heads):
                part, head = divmod(row, heads)
                lanes = slice(head * head_width, (head + 1) * head_width)
                wide = slice(row * head_width, (row + 1) * head_width)
                from_start = factors[number][:, wide]
                to_end = factors[number][:, (4 + row) * head_width : (5 + row) * head_width]
                across, dq, dk, written = (
                    product[:, lanes] * factor
                    for product, factor in zip(
                        products[number, part], (from_start, from_start, to_end, to_end)
                    )
                )
                results[number, row] = [
                    (partial_refs[part][i, rows, lanes].astype(F32) + added).astype(BF16)
                    for i, added in enumerate((across, dq, dk, written))
                ]
                queried = (across * cot_ref[0, rows, wide].astype(F32)).astype(BF16)
                kept = (written * v_ref[0, rows, wide].astype(F32)).astype(BF16)
                shares = dot_nt(ones, jnp.concatenate([queried, kept], axis=0))
                at = number * 8 + row
                gate_scr[at : at + 1, :] = shares[0:1, :CHUNK]
                gate_scr[at + 4 : at + 5, :] = shares[0:1, CHUNK:]
        for number in numbers:
            rows = slice(number * CHUNK, (number + 1) * CHUNK)
            for row in range(PARTS * heads):
                wide = slice(row * head_width, (row + 1) * head_width)
                for i in range(4):
                    staged[i, rows, wide] = results[number, row][i]
        for i, copy in enumerate(copies(step)):
            copy.start(priority=i % 2)

    shares = gate_scr[...]
    lane_a, lane_b = iota((CHUNK, CHUNK), 0), iota((CHUNK, CHUNK), 1)
    from_here = dot_nn(shares, (lane_a >= lane_b).astype(F32), PRECISE)
    up_to_here = dot_nn(shares, (lane_a < lane_b).astype(F32), PRECISE)
    all_rows = shares.shape[0]
    totals = jnp.broadcast_to(from_here[:, 0:1], shares.shape)
    row_a, row_b = iota((all_rows, all_rows), 0), iota((all_rows, all_rows), 1)
    outside = ((row_a % 8 < 4) & (row_b // 8 > row_a // 8)) | (
        (row_a % 8 >= 4) & (row_b // 8 < row_a // 8)
    )
    outside = (outside & (row_a % 8 == row_b % 8)).astype(F32)
    sums = dot_nn(outside, totals, PRECISE) + jnp.where(
        iota(shares.shape, 0) % 8 < 4, from_here, up_to_here
    )
    for number in range(num_chunks):
        lanes = slice(number * CHUNK, (number + 1) * CHUNK)
        for row in range(PARTS * heads):
            part, head = divmod(row, heads)
            at = number * 8 + row
            dgate_ref[0, row : row + 1, lanes] = (
                gate_refs[part][0, head : head + 1, lanes]
                + sums[at : at + 1, :]
                + sums[at + 4 : at + 5, :]
                + constants[row]
            )
    for step in range(steps):
        for copy in copies(step):
            copy.wait()


def summed(own, others):
    if len(others) == 1:
        return own + others[0]
    return (own + others[0]) + (others[1] + others[2])


def shards(queries, keys_raw, values, gates, lengths, key_gain, cotangent):
    tokens, width = queries.shape[1:]
    all_heads, head_width = key_gain.shape
    heads = all_heads // PARTS
    part_width = width // PARTS
    num_chunks = tokens // CHUNK
    rows = num_chunks * 8
    block = min(256, tokens)
    steps = tokens // block
    count = lax.axis_size("ctx")
    middle = count // 2 - 1
    docs = lengths.shape[1]
    after = head_width + CHUNK
    small = (
        jnp.pad(gates[0], ((0, 0), (0, after)))
        + jnp.pad(key_gain, ((0, 0), (tokens, CHUNK)))
        + jnp.pad(lengths, ((0, all_heads - 1), (tokens + head_width, CHUNK - docs))).astype(F32)
    )

    def shape_of(*shape, dtype=F32):
        return jax.ShapeDtypeStruct(shape, dtype)

    hbm = pl.BlockSpec(memory_space=pltpu.HBM)
    vmem = pl.BlockSpec(memory_space=pltpu.VMEM)
    table = shape_of(rows, CHUNK)
    states = shape_of(heads, head_width, head_width)
    decays = shape_of(heads, 1, head_width)
    part_gates = shape_of(1, heads, tokens)
    partials = shape_of(4, tokens, part_width, dtype=BF16)
    streams = (queries, keys_raw, values, cotangent)
    product = 2 * tokens * part_width * head_width

    def ends():
        outs = [states] * (2 * PARTS) + [decays] * PARTS + [table] * 3
        outs += [shape_of(all_heads, head_width), shape_of(4, head_width)]
        outs += [shape_of(1, tokens, width, dtype=BF16)] * 4
        return pl.pallas_call(
            functools.partial(ends_kernel, head_width, lengths.shape[1], count // 2),
            in_specs=[vmem] + [hbm] * 4,
            out_specs=[vmem] * len(outs),
            out_shape=outs,
            scratch_shapes=[
                pltpu.VMEM((rows, CHUNK), F32),
                pltpu.SemaphoreType.DMA((steps, 4)),
            ],
            compiler_params=pltpu.CompilerParams(vmem_limit_bytes=49 << 20),
            cost_estimate=pl.CostEstimate(
                flops=2 * product * PARTS, bytes_accessed=8 * tokens * width, transcendentals=0
            ),
            name="shard_ends",
        )(small, *streams)

    def local(part, gain, cum, fac):
        return pl.pallas_call(
            functools.partial(local_kernel, head_width, part),
            in_specs=[vmem] * 7,
            out_specs=[vmem] * 3,
            out_shape=[partials, part_gates, shape_of(heads, head_width)],
            scratch_shapes=[
                pltpu.VMEM((num_chunks, heads, head_width, head_width), BF16),
                pltpu.VMEM((heads, head_width, head_width), F32),
            ],
            compiler_params=pltpu.CompilerParams(vmem_limit_bytes=24 << 20),
            cost_estimate=pl.CostEstimate(
                flops=12 * product, bytes_accessed=16 * tokens * part_width, transcendentals=0
            ),
            name=f"local_{part}",
        )(*held, gain, cum, fac)

    def merge(*arrays):
        return pl.pallas_call(
            functools.partial(merge_kernel, head_width),
            in_specs=[vmem] * len(arrays),
            out_specs=[hbm] * 4 + [vmem],
            out_shape=[shape_of(1, tokens, width, dtype=BF16)] * 4 + [shape_of(*gates.shape)],
            scratch_shapes=[
                pltpu.VMEM((4, tokens, width), BF16),
                pltpu.VMEM((PARTS, part_width, part_width), BF16),
                pltpu.VMEM((PARTS, part_width, part_width), BF16),
                pltpu.VMEM((16, 8 * head_width), BF16),
                pltpu.VMEM((rows, CHUNK), F32),
                pltpu.SemaphoreType.DMA((steps, 4)),
            ],
            compiler_params=pltpu.CompilerParams(vmem_limit_bytes=24 << 20),
            cost_estimate=pl.CostEstimate(
                flops=4 * product * PARTS, bytes_accessed=24 * tokens * width, transcendentals=0
            ),
            name="merge",
        )(*arrays)

    results = ends()
    near, far, decay = (results[i * PARTS : (i + 1) * PARTS] for i in range(3))
    cum, chunk_fac, shard_fac, gain, flags = results[3 * PARTS : 3 * PARTS + 5]
    held = results[3 * PARTS + 5 :]
    sent = [[] for _ in range(PARTS)]
    arrived = [[] for _ in range(PARTS)]
    local_parts = [None] * PARTS

    def send(part, hop):
        payload = near[part] if hop <= middle else far[part]
        if hop > 0:
            payload = payload + decay[part] * arrived[part][-1]
        sent[part].append(payload)
        arrived[part].append(
            lax.ppermute(
                payload, "ctx", [(hop, hop + 1), (count - 1 - hop, count - 2 - hop)]
            )
        )

    for part in range(PARTS):
        send(part, 0)
    for hop in range(count - 1):
        if hop < PARTS:
            local_cum = cum
            if hop > 0:
                local_cum, _ = lax.optimization_barrier((cum, arrived[0][hop - 1]))
            local_parts[hop] = list(local(hop, gain, local_cum, chunk_fac))
            if hop + 1 < count - 1:
                local_parts[hop][2], arrived[0][-1] = lax.optimization_barrier(
                    (local_parts[hop][2], arrived[0][-1])
                )
        if hop + 1 < count - 1:
            for part in range(PARTS):
                send(part, hop + 1)

    terms = []
    for part in range(PARTS):
        crossed = jnp.sum(sent[part][middle] * arrived[part][middle], axis=2)
        term = local_parts[part][2] + flags[0:1] * crossed
        if middle > 0:
            term = term + jnp.sum(sum(arrived[part][:middle]) * far[part], axis=2)
        terms.append(term)
    gain_term = jnp.concatenate(terms, axis=0)
    half = head_width // lax.axis_size("dp")
    second_half = flags[1:2, :half]
    lower_half, upper_half = gain_term[:, :half], gain_term[:, half:]
    away = (1.0 - second_half) * upper_half + second_half * lower_half
    kept = (1.0 - second_half) * lower_half + second_half * upper_half
    grad_gain = kept + lax.ppermute(away, "dp", [(0, 1), (1, 0)])

    def exchanged(array, reach):
        return lax.ppermute(array, "ctx", [(i, i ^ reach) for i in range(count)])

    pending, reach = [], 1
    while reach < count:
        if pending:
            grad_gain = summed(grad_gain, pending)
        pending = [exchanged(grad_gain, reach)]
        if reach * 2 < count:
            pending += [exchanged(grad_gain, reach * 2), exchanged(grad_gain, reach * 3)]
        reach *= 2 * min(len(pending), 2)

    zeros = jnp.zeros(states.shape, F32)
    if middle == 1:
        firsts, seconds = ([own[i] for own in arrived] for i in range(2))
    else:
        firsts = [sum(own[:middle], zeros) for own in arrived]
        seconds = [sum(own[middle:-1], zeros) for own in arrived]
    done = list(
        merge(
            *held, gain, flags, shard_fac,
            *[local_part[0] for local_part in local_parts],
            *[local_part[1] for local_part in local_parts],
            *firsts, *seconds, *[own[-1] for own in arrived],
        )
    )
    pending, done[4] = lax.optimization_barrier((pending, done[4]))
    return (*done, summed(grad_gain, pending))


def solution(mesh):
    wide = P("dp", "ctx", "head")
    narrow = P("dp", "head", "ctx")
    return jax.shard_map(
        shards,
        mesh=mesh,
        in_specs=(wide, wide, wide, narrow, P("dp", None), P("head", None), wide),
        out_specs=(wide, wide, wide, wide, narrow, P("head", "dp")),
        check_vma=False,
    )
```

```python
import functools
import math

import jax
import jax.numpy as jnp
from jax import lax
from jax.experimental import pallas as pl
from jax.experimental.pallas import tpu as pltpu
from jax.sharding import PartitionSpec as P

CHUNK = 128
PARTS = 2
UNROLL = 4
PRECISE = lax.Precision.HIGHEST
F32 = jnp.float32
BF16 = jnp.bfloat16
LOG2E = math.log2(math.e)


def dot_nn(a, b, precision=None):
    return lax.dot_general(
        a, b, (((1,), (0,)), ((), ())), precision=precision, preferred_element_type=F32
    )


def dot_nt(a, b):
    return lax.dot_general(a, b, (((1,), (1,)), ((), ())), preferred_element_type=F32)


def dot_tn(a, b):
    return lax.dot_general(a, b, (((0,), (0,)), ((), ())), preferred_element_type=F32)


def iota(shape, dim):
    return lax.broadcasted_iota(jnp.int32, shape, dim)


def total_of(array):
    return jnp.sum(jnp.sum(array, axis=0, keepdims=True), axis=1, keepdims=True)


def later_sums(column):
    kept = iota((CHUNK, CHUNK), 0) >= iota((CHUNK, CHUNK), 1)
    return jnp.sum(jnp.where(kept, column, 0.0), axis=0, keepdims=True)


def decay_tables(docs, ctx, small_ref, spread, cum_ref, chunk_fac_ref, shard_fac_ref):
    rows = cum_ref.shape[0]
    num_chunks = rows // 8
    tokens = num_chunks * CHUNK
    for chunk in range(num_chunks):
        part = small_ref[:, chunk * CHUNK : (chunk + 1) * CHUNK]
        spread[chunk * 8 : chunk * 8 + 4, :] = part
        spread[chunk * 8 + 4 : chunk * 8 + 8, :] = part
    gates = spread[...] * LOG2E
    lane_a, lane_b = iota((CHUNK, CHUNK), 0), iota((CHUNK, CHUNK), 1)
    prefix = dot_nn(gates, (lane_a <= lane_b).astype(F32), PRECISE)
    suffix = dot_nn(gates, (lane_a > lane_b).astype(F32), PRECISE)
    totals = jnp.broadcast_to(prefix[:, CHUNK - 1 : CHUNK], (rows, CHUNK))
    row_a, row_b = iota((rows, rows), 0), iota((rows, rows), 1)
    same = (row_a % 8) == (row_b % 8)
    outside = ((row_a % 8 < 4) & (row_b // 8 < row_a // 8)) | (
        (row_a % 8 >= 4) & (row_b // 8 > row_a // 8)
    )
    others = dot_nn((same & outside).astype(F32), totals, PRECISE)

    first = ctx * tokens
    chunk_first = first + (iota((rows, CHUNK), 0) // 8) * CHUNK
    from_start = iota((rows, CHUNK), 0) % 8 < 4
    chunk_anchor = jnp.where(from_start, chunk_first - 1, chunk_first + (CHUNK - 1)).astype(F32)
    shard_anchor = jnp.where(from_start, first - 1, first + (tokens - 1)).astype(F32)
    positions = (chunk_first + iota((rows, CHUNK), 1)).astype(F32)
    segment = jnp.zeros((rows, CHUNK), F32)
    chunk_segment = jnp.zeros((rows, CHUNK), F32)
    shard_segment = jnp.zeros((rows, CHUNK), F32)
    begin = small_ref.shape[1] - CHUNK
    start = jnp.zeros((1, 1), F32)
    for doc in range(docs):
        segment += jnp.where(positions >= start, 1.0, 0.0)
        chunk_segment += jnp.where(chunk_anchor >= start, 1.0, 0.0)
        shard_segment += jnp.where(shard_anchor >= start, 1.0, 0.0)
        start = start + small_ref[0:1, begin + doc : begin + doc + 1]
    cum_ref[...] = jnp.where(from_start, prefix, segment)
    exponent = jnp.where(from_start, prefix, suffix)
    chunk_fac_ref[...] = jnp.where(
        segment == chunk_segment, jnp.exp2(jnp.minimum(exponent, 0.0)), 0.0
    )
    keep = segment == shard_segment
    shard_fac_ref[...] = jnp.where(keep, jnp.exp2(jnp.minimum(exponent + others, 0.0)), 0.0)


def ends_kernel(head_width, docs, half_ctx, *refs):
    small_ref, sources = refs[0], refs[1:5]
    ctx, dp = lax.axis_index("ctx"), lax.axis_index("dp")
    near_refs, far_refs, decay_refs = (
        refs[5 + i * PARTS : 5 + (i + 1) * PARTS] for i in range(3)
    )
    (cum_ref, chunk_fac_ref, shard_fac_ref, gain_ref, flag_ref, q_ref, k_ref, v_ref, cot_ref,
     spread, sems) = refs[5 + 3 * PARTS :]
    heads = near_refs[0].shape[0]
    rows = shard_fac_ref.shape[0]
    steps = sems.shape[0]
    tokens = q_ref.shape[1]
    block = tokens // steps
    chunks = block // CHUNK

    def copies(step):
        at = pl.ds(step * block, block)
        return [
            pltpu.make_async_copy(source.at[:, at, :], target.at[:, at, :], sems.at[step, i])
            for i, (source, target) in enumerate(zip(sources, (q_ref, k_ref, v_ref, cot_ref)))
        ]

    for step in range(steps):
        for i, copy in enumerate(copies(step)):
            copy.start(priority=i % 2)
    decay_tables(docs, ctx, small_ref, spread, cum_ref, chunk_fac_ref, shard_fac_ref)
    gain_ref[...] = small_ref[:, tokens : tokens + head_width]
    for part in range(PARTS):
        for head in range(heads):
            row = rows - 8 + part * heads + head
            decay_refs[part][head] = jnp.broadcast_to(
                shard_fac_ref[row : row + 1, CHUNK - 1 : CHUNK], (1, head_width)
            )

    def turned(ref, step, row, scale):
        pieces = []
        head = row % 4
        for chunk in range(step * chunks, (step + 1) * chunks):
            factor = shard_fac_ref[chunk * 8 + row : chunk * 8 + row + 1, :]
            piece = jnp.transpose(
                ref[
                    0,
                    chunk * CHUNK : (chunk + 1) * CHUNK,
                    head * head_width : (head + 1) * head_width,
                ]
            )
            pieces.append((piece.astype(F32) * (factor * scale)).astype(BF16))
        return jnp.concatenate(pieces, axis=1)

    ends, grads = {}, {}
    for step in range(steps):
        for copy in copies(step):
            copy.wait()
        at = slice(step * block, (step + 1) * block)
        for row in range(PARTS * heads):
            lanes = slice(row * head_width, (row + 1) * head_width)
            end = dot_nn(turned(k_ref, step, 4 + row, 1.0), v_ref[0, at, lanes])
            grad = dot_nn(turned(q_ref, step, row, head_width ** (-0.5)), cot_ref[0, at, lanes])
            ends[row] = ends[row] + end if step else end
            grads[row] = grads[row] + grad if step else grad
    middle = jnp.where(ctx == half_ctx - 1, 1.0, 0.0)
    low = ctx < half_ctx
    row = iota(flag_ref.shape, 0)
    flag_ref[...] = jnp.where(
        row == 0, middle, jnp.where(row == 1, dp.astype(F32), jnp.where(low, 1.0, 0.0))
    )
    for part in range(PARTS):
        for head in range(heads):
            row = part * heads + head
            near_refs[part][head] = jnp.where(low, ends[row], grads[row])
            far_refs[part][head] = jnp.where(low, grads[row], ends[row])


def local_kernel(
    head_width, part, q_ref, k_ref, v_ref, cot_ref, gain_ref, cum_ref, fac_ref,
    target, dgate_ref, dgain_ref, leaving, state,
):
    out_ref, dq_ref, dk_ref, dv_ref = (target.at[pl.ds(i, 1)] for i in range(4))
    heads = state.shape[0]
    num_chunks = leaving.shape[0]
    scale = head_width ** (-0.5)
    unroll = math.gcd(num_chunks, UNROLL)

    groups = num_chunks // unroll
    def wide_lanes(head):
        row = part * heads + head
        return slice(row * head_width, (row + 1) * head_width)

    def lanes_of(head):
        return slice(head * head_width, (head + 1) * head_width)

    def rows_of(chunk):
        return pl.ds(pl.multiple_of(chunk * CHUNK, CHUNK), CHUNK)

    def table(ref, chunk):
        return ref[pl.ds(pl.multiple_of(chunk * 8, 8), 8), :]

    pairs = [(at, head) for at in range(unroll) for head in range(heads)]

    def backward(chunks):
        facs = [table(fac_ref, chunk) for chunk in chunks]
        added = {}
        for at, head in pairs:
            row = part * heads + head
            rows, lanes = rows_of(chunks[at]), wide_lanes(head)
            turned = jnp.transpose(q_ref[0, rows, lanes]).astype(F32)
            turned = (turned * (facs[at][row : row + 1, :] * scale)).astype(BF16)
            added[at, head] = dot_nn(turned, cot_ref[0, rows, lanes])
        for head in range(heads):
            row = part * heads + head
            held = state[head]
            for at in range(unroll):
                leaving[chunks[at], head] = held.astype(BF16)
                held = held * facs[at][row : row + 1, CHUNK - 1 : CHUNK] + added[at, head]
            state[head] = held

    def forward(chunks):
        facs = [table(fac_ref, chunk) for chunk in chunks]
        cums = [table(cum_ref, chunk) for chunk in chunks]
        fac_columns = [jnp.transpose(fac) for fac in facs]
        cum_columns = [jnp.transpose(cum) for cum in cums]
        causal = iota((CHUNK, CHUNK), 0) >= iota((CHUNK, CHUNK), 1)
        limits = [
            jnp.where((columns[:, 4:5] == cum[4:5, :]) & causal, math.log2(scale), -1e30)
            for columns, cum in zip(cum_columns, cums)
        ]
        cum_columns = [columns + math.log2(scale) for columns in cum_columns]
        q, k, v, cot, k_raw, k_decayed, q_decayed, later = ({} for _ in range(8))
        from_start, to_end, added, held, entering = ({} for _ in range(5))
        for key in pairs:
            at, head = key
            row = part * heads + head
            rows, lanes = rows_of(chunks[at]), lanes_of(head)
            q[key], cot[key] = q_ref[0, rows, wide_lanes(head)], cot_ref[0, rows, wide_lanes(head)]
            v[key] = v_ref[0, rows, wide_lanes(head)]
            later[key] = leaving[chunks[at], head]
            k_raw[key] = k_ref[0, rows, wide_lanes(head)].astype(F32)
            k_wide = k_raw[key] * gain_ref[row : row + 1, :]
            k[key] = k_wide.astype(BF16)
            from_start[key] = fac_columns[at][:, row : row + 1] * scale
            to_end[key] = fac_columns[at][:, 4 + row : 5 + row]
            k_decayed[key] = (k_wide * to_end[key]).astype(BF16)
            q_decayed[key] = (q[key].astype(F32) * from_start[key]).astype(BF16)
            added[key] = dot_tn(k_decayed[key], v[key])
        for head in range(heads):
            row = part * heads + head
            now = state[head]
            for at in range(unroll):
                held[at, head] = now
                entering[at, head] = now.astype(BF16)
                now = now * facs[at][row : row + 1, CHUNK - 1 : CHUNK] + added[at, head]
            held[unroll, head] = now
            state[head] = now
        by_cot, scores, written = {}, {}, {}
        for key in pairs:
            by_cot[key] = dot_nt(cot[key], jnp.concatenate([v[key], entering[key]], axis=0))
            scores[key] = dot_nt(q[key], k[key])
            written[key] = dot_nt(v[key], later[key])
        weights, grad_scores = {}, {}
        for key in pairs:
            at, head = key
            row = part * heads + head
            decays = jnp.exp2(
                jnp.minimum(cum_columns[at][:, row : row + 1] - cums[at][row : row + 1, :], limits[at])
            )
            weights[key] = (scores[key] * decays).astype(BF16)
            grad_scores[key] = (by_cot[key][:, :CHUNK] * decays).astype(BF16)
        out, dq, dk, dv = {}, {}, {}, {}
        for key in pairs:
            out[key] = dot_nn(
                jnp.concatenate([weights[key], q_decayed[key]], axis=1),
                jnp.concatenate([v[key], entering[key]], axis=0),
            )
            dv[key] = dot_nn(
                jnp.concatenate([jnp.transpose(weights[key]), k_decayed[key]], axis=1),
                jnp.concatenate([cot[key], later[key]], axis=0),
            )
            dq[key] = dot_nn(grad_scores[key], k[key]) + by_cot[key][:, CHUNK:] * from_start[key]
            dk[key] = dot_tn(grad_scores[key], q[key]) + written[key] * to_end[key]
        gate_rows, gain_rows = {}, {}
        for key in pairs:
            at, head = key
            balance = jnp.sum(
                out[key] * cot[key].astype(F32) - dv[key] * v[key].astype(F32),
                axis=1, keepdims=True,
            )
            gate_rows[key] = later_sums(balance) + total_of(
                held[at + 1, head] * later[key].astype(F32)
            )
            gain_rows[key] = jnp.sum(dk[key] * k_raw[key], axis=0, keepdims=True)
        for key in pairs:
            at, head = key
            row = part * heads + head
            rows, own = rows_of(chunks[at]), lanes_of(head)
            out_ref[0, rows, own] = out[key].astype(BF16)
            dq_ref[0, rows, own] = dq[key].astype(BF16)
            dv_ref[0, rows, own] = dv[key].astype(BF16)
            dk_ref[0, rows, own] = (dk[key] * gain_ref[row : row + 1, :]).astype(BF16)
            dgate_ref[0, head : head + 1, rows] = gate_rows[key]
        for head in range(heads):
            dgain_ref[head : head + 1, :] += sum(gain_rows[at, head] for at in range(unroll))

    state[...] = jnp.zeros_like(state)

    def backward_group(index, carry):
        backward([num_chunks - 1 - (index * unroll + at) for at in range(unroll)])
        return carry

    lax.fori_loop(0, groups, backward_group, 0)
    state[...] = jnp.zeros_like(state)
    dgain_ref[...] = jnp.zeros_like(dgain_ref)

    def forward_group(index, carry):
        forward([index * unroll + at for at in range(unroll)])
        return carry

    lax.fori_loop(0, groups, forward_group, 0)


def merge_kernel(head_width, *refs):
    q_ref, k_ref, v_ref, cot_ref, gain_ref, flag_ref, fac_ref = refs[:7]
    partial_refs, gate_refs, first_refs, second_refs, last_refs = (
        refs[7 + i * PARTS : 7 + (i + 1) * PARTS] for i in range(5)
    )
    refs = refs[7 + 5 * PARTS :]
    extra = len(refs) - 12
    gain_refs, refs = refs[:extra], refs[extra:]
    targets, dgate_ref, dgain_ref, staged, entering, leaving, spread_ref, gate_scr, sems = (
        refs[:4], *refs[4:]
    )
    dgain_ref[...] = summed(gain_refs[0][...], [ref[...] for ref in gain_refs[1:]])
    heads = first_refs[0].shape[0]
    steps = sems.shape[0]
    num_chunks = fac_ref.shape[0] // 8
    chunks = num_chunks // steps
    block = chunks * CHUNK
    group_width = heads * head_width
    scale = head_width ** (-0.5)

    def copies(step):
        at = pl.ds(step * block, block)
        return [
            pltpu.make_async_copy(staged.at[i, at, :], target.at[0, at, :], sems.at[step, i])
            for i, target in enumerate(targets)
        ]

    gain_columns = jnp.transpose(jnp.concatenate([gain_ref[...], gain_ref[...]], axis=0))
    entering[...] = jnp.zeros_like(entering)
    leaving[...] = jnp.zeros_like(leaving)
    last_factors = fac_ref[(num_chunks - 1) * 8 : num_chunks * 8, CHUNK - 1 : CHUNK]
    low = jnp.broadcast_to(flag_ref[2:3, :], (head_width, head_width)) > 0.5
    constants = []
    for part in range(PARTS):
        for head in range(heads):
            row = part * heads + head
            own = slice(head * head_width, (head + 1) * head_width)
            gain = gain_columns[:, row : row + 1]
            first = first_refs[part][head]
            second = second_refs[part][head] + last_refs[part][head]
            state = jnp.where(low, first, second) * gain
            later = jnp.where(low, second, first)
            entering[part, own, own] = (state * scale).astype(BF16)
            leaving[part, own, own] = (later * gain).astype(BF16)
            constants.append(total_of(state * later) * last_factors[row : row + 1])

    spread = (iota(spread_ref.shape, 1) // head_width == iota(spread_ref.shape, 0) % 8).astype(F32)
    spread_ref[...] = spread.astype(BF16)
    ones = jnp.ones((8, head_width), BF16)
    for step in range(steps):
        numbers = range(step * chunks, (step + 1) * chunks)
        products, results, factors = {}, {}, {}
        for number in numbers:
            rows = slice(number * CHUNK, (number + 1) * CHUNK)
            fac = fac_ref[number * 8 : number * 8 + 8, :]
            high = fac.astype(BF16).astype(F32)
            both = jnp.concatenate([high, fac - high], axis=0).astype(BF16)
            factors[number] = dot_tn(both, spread_ref[...])
            for part in range(PARTS):
                group = slice(part * group_width, (part + 1) * group_width)
                products[number, part] = (
                    dot_nn(q_ref[0, rows, group], entering[part]),
                    dot_nt(cot_ref[0, rows, group], entering[part]),
                    dot_nt(v_ref[0, rows, group], leaving[part]),
                    dot_nn(k_ref[0, rows, group], leaving[part]),
                )
        for number in numbers:
            rows = slice(number * CHUNK, (number + 1) * CHUNK)
            for row in range(PARTS * heads):
                part, head = divmod(row, heads)
                lanes = slice(head * head_width, (head + 1) * head_width)
                wide = slice(row * head_width, (row + 1) * head_width)
                from_start = factors[number][:, wide]
                to_end = factors[number][:, (4 + row) * head_width : (5 + row) * head_width]
                across, dq, dk, written = (
                    product[:, lanes] * factor
                    for product, factor in zip(
                        products[number, part], (from_start, from_start, to_end, to_end)
                    )
                )
                results[number, row] = [
                    (partial_refs[part][i, rows, lanes].astype(F32) + added).astype(BF16)
                    for i, added in enumerate((across, dq, dk, written))
                ]
                queried = (across * cot_ref[0, rows, wide].astype(F32)).astype(BF16)
                kept = (written * v_ref[0, rows, wide].astype(F32)).astype(BF16)
                shares = dot_nt(ones, jnp.concatenate([queried, kept], axis=0))
                at = number * 8 + row
                gate_scr[at : at + 1, :] = shares[0:1, :CHUNK]
                gate_scr[at + 4 : at + 5, :] = shares[0:1, CHUNK:]
        for number in numbers:
            rows = slice(number * CHUNK, (number + 1) * CHUNK)
            for row in range(PARTS * heads):
                wide = slice(row * head_width, (row + 1) * head_width)
                for i in range(4):
                    staged[i, rows, wide] = results[number, row][i]
        for i, copy in enumerate(copies(step)):
            copy.start(priority=i % 2)

    shares = gate_scr[...]
    lane_a, lane_b = iota((CHUNK, CHUNK), 0), iota((CHUNK, CHUNK), 1)
    from_here = dot_nn(shares, (lane_a >= lane_b).astype(F32), PRECISE)
    up_to_here = dot_nn(shares, (lane_a < lane_b).astype(F32), PRECISE)
    all_rows = shares.shape[0]
    totals = jnp.broadcast_to(from_here[:, 0:1], shares.shape)
    row_a, row_b = iota((all_rows, all_rows), 0), iota((all_rows, all_rows), 1)
    outside = ((row_a % 8 < 4) & (row_b // 8 > row_a // 8)) | (
        (row_a % 8 >= 4) & (row_b // 8 < row_a // 8)
    )
    outside = (outside & (row_a % 8 == row_b % 8)).astype(F32)
    sums = dot_nn(outside, totals, PRECISE) + jnp.where(
        iota(shares.shape, 0) % 8 < 4, from_here, up_to_here
    )
    for number in range(num_chunks):
        lanes = slice(number * CHUNK, (number + 1) * CHUNK)
        for row in range(PARTS * heads):
            part, head = divmod(row, heads)
            at = number * 8 + row
            dgate_ref[0, row : row + 1, lanes] = (
                gate_refs[part][0, head : head + 1, lanes]
                + sums[at : at + 1, :]
                + sums[at + 4 : at + 5, :]
                + constants[row]
            )
    for step in range(steps):
        for copy in copies(step):
            copy.wait()


def summed(own, others):
    if not others:
        return own
    if len(others) == 1:
        return own + others[0]
    return (own + others[0]) + (others[1] + others[2])


def shards(queries, keys_raw, values, gates, lengths, key_gain, cotangent):
    tokens, width = queries.shape[1:]
    all_heads, head_width = key_gain.shape
    heads = all_heads // PARTS
    part_width = width // PARTS
    num_chunks = tokens // CHUNK
    rows = num_chunks * 8
    block = min(128, tokens)
    steps = tokens // block
    count = lax.axis_size("ctx")
    middle = count // 2 - 1
    docs = lengths.shape[1]
    after = head_width + CHUNK
    small = (
        jnp.pad(gates[0], ((0, 0), (0, after)))
        + jnp.pad(key_gain, ((0, 0), (tokens, CHUNK)))
        + jnp.pad(lengths, ((0, all_heads - 1), (tokens + head_width, CHUNK - docs))).astype(F32)
    )

    def shape_of(*shape, dtype=F32):
        return jax.ShapeDtypeStruct(shape, dtype)

    hbm = pl.BlockSpec(memory_space=pltpu.HBM)
    vmem = pl.BlockSpec(memory_space=pltpu.VMEM)
    table = shape_of(rows, CHUNK)
    states = shape_of(heads, head_width, head_width)
    decays = shape_of(heads, 1, head_width)
    part_gates = shape_of(1, heads, tokens)
    partials = shape_of(4, tokens, part_width, dtype=BF16)
    streams = (queries, keys_raw, values, cotangent)
    product = 2 * tokens * part_width * head_width

    def ends():
        outs = [states] * (2 * PARTS) + [decays] * PARTS + [table] * 3
        outs += [shape_of(all_heads, head_width), shape_of(4, head_width)]
        outs += [shape_of(1, tokens, width, dtype=BF16)] * 4
        return pl.pallas_call(
            functools.partial(ends_kernel, head_width, lengths.shape[1], count // 2),
            in_specs=[vmem] + [hbm] * 4,
            out_specs=[vmem] * len(outs),
            out_shape=outs,
            scratch_shapes=[
                pltpu.VMEM((rows, CHUNK), F32),
                pltpu.SemaphoreType.DMA((steps, 4)),
            ],
            compiler_params=pltpu.CompilerParams(vmem_limit_bytes=49 << 20),
            cost_estimate=pl.CostEstimate(
                flops=2 * product * PARTS, bytes_accessed=8 * tokens * width, transcendentals=0
            ),
            name="shard_ends",
        )(small, *streams)

    def local(part, gain, cum, fac):
        return pl.pallas_call(
            functools.partial(local_kernel, head_width, part),
            in_specs=[vmem] * 7,
            out_specs=[vmem] * 3,
            out_shape=[partials, part_gates, shape_of(heads, head_width)],
            scratch_shapes=[
                pltpu.VMEM((num_chunks, heads, head_width, head_width), BF16),
                pltpu.VMEM((heads, head_width, head_width), F32),
            ],
            compiler_params=pltpu.CompilerParams(vmem_limit_bytes=24 << 20),
            cost_estimate=pl.CostEstimate(
                flops=12 * product, bytes_accessed=16 * tokens * part_width, transcendentals=0
            ),
            name=f"local_{part}",
        )(*held, gain, cum, fac)

    def merge(*arrays):
        return pl.pallas_call(
            functools.partial(merge_kernel, head_width),
            in_specs=[vmem] * len(arrays),
            out_specs=[hbm] * 4 + [vmem] * 2,
            out_shape=[shape_of(1, tokens, width, dtype=BF16)] * 4
            + [shape_of(*gates.shape), shape_of(*arrays[-1].shape)],
            scratch_shapes=[
                pltpu.VMEM((4, tokens, width), BF16),
                pltpu.VMEM((PARTS, part_width, part_width), BF16),
                pltpu.VMEM((PARTS, part_width, part_width), BF16),
                pltpu.VMEM((16, 8 * head_width), BF16),
                pltpu.VMEM((rows, CHUNK), F32),
                pltpu.SemaphoreType.DMA((steps, 4)),
            ],
            compiler_params=pltpu.CompilerParams(vmem_limit_bytes=24 << 20),
            cost_estimate=pl.CostEstimate(
                flops=4 * product * PARTS, bytes_accessed=24 * tokens * width, transcendentals=0
            ),
            name="merge",
        )(*arrays)

    results = ends()
    near, far, decay = (results[i * PARTS : (i + 1) * PARTS] for i in range(3))
    cum, chunk_fac, shard_fac, gain, flags = results[3 * PARTS : 3 * PARTS + 5]
    held = results[3 * PARTS + 5 :]
    sent = [[] for _ in range(PARTS)]
    arrived = [[] for _ in range(PARTS)]
    local_parts = [None] * PARTS

    def send(part, hop):
        payload = near[part] if hop <= middle else far[part]
        if hop > 0:
            payload = payload + decay[part] * arrived[part][-1]
        sent[part].append(payload)
        arrived[part].append(
            lax.ppermute(
                payload, "ctx", [(hop, hop + 1), (count - 1 - hop, count - 2 - hop)]
            )
        )

    for part in range(PARTS):
        send(part, 0)
    for hop in range(count - 1):
        if hop < PARTS:
            local_cum = cum
            if hop > 0:
                local_cum, _ = lax.optimization_barrier((cum, arrived[0][hop - 1]))
            local_parts[hop] = list(local(hop, gain, local_cum, chunk_fac))
            if hop + 1 < count - 1:
                local_parts[hop][2], arrived[0][-1] = lax.optimization_barrier(
                    (local_parts[hop][2], arrived[0][-1])
                )
        if hop + 1 < count - 1:
            for part in range(PARTS):
                send(part, hop + 1)

    terms = []
    for part in range(PARTS):
        crossed = jnp.sum(sent[part][middle] * arrived[part][middle], axis=2)
        term = local_parts[part][2] + flags[0:1] * crossed
        if middle > 0:
            term = term + jnp.sum(sum(arrived[part][:middle]) * far[part], axis=2)
        terms.append(term)
    gain_term = jnp.concatenate(terms, axis=0)
    half = head_width // lax.axis_size("dp")
    second_half = flags[1:2, :half]
    lower_half, upper_half = gain_term[:, :half], gain_term[:, half:]
    away = (1.0 - second_half) * upper_half + second_half * lower_half
    kept = (1.0 - second_half) * lower_half + second_half * upper_half
    grad_gain = kept + lax.ppermute(away, "dp", [(0, 1), (1, 0)])

    def exchanged(array, reach):
        return lax.ppermute(array, "ctx", [(i, i ^ reach) for i in range(count)])

    pending, reach = [], 1
    while reach < count:
        if pending:
            grad_gain = summed(grad_gain, pending)
        pending = [exchanged(grad_gain, reach)]
        if reach * 2 < count:
            pending += [exchanged(grad_gain, reach * 2), exchanged(grad_gain, reach * 3)]
        reach *= 2 * min(len(pending), 2)

    zeros = jnp.zeros(states.shape, F32)
    if middle == 1:
        firsts, seconds = ([own[i] for own in arrived] for i in range(2))
    else:
        firsts = [sum(own[:middle], zeros) for own in arrived]
        seconds = [sum(own[middle:-1], zeros) for own in arrived]
    done = list(
        merge(
            *held, gain, flags, shard_fac,
            *[local_part[0] for local_part in local_parts],
            *[local_part[1] for local_part in local_parts],
            *firsts, *seconds, *[own[-1] for own in arrived],
            grad_gain, *pending,
        )
    )
    return tuple(done)


def solution(mesh):
    wide = P("dp", "ctx", "head")
    narrow = P("dp", "head", "ctx")
    return jax.shard_map(
        shards,
        mesh=mesh,
        in_specs=(wide, wide, wide, narrow, P("dp", None), P("head", None), wide),
        out_specs=(wide, wide, wide, wide, narrow, P("head", "dp")),
        check_vma=False,
    )
```

```python
import functools
import math

import jax
import jax.numpy as jnp
from jax import lax
from jax.experimental import pallas as pl
from jax.experimental.pallas import tpu as pltpu
from jax.sharding import PartitionSpec as P

CHUNK = 128
PARTS = 2
UNROLL = 4
PRECISE = lax.Precision.HIGHEST
F32 = jnp.float32
BF16 = jnp.bfloat16
LOG2E = math.log2(math.e)


def dot_nn(a, b, precision=None):
    return lax.dot_general(
        a, b, (((1,), (0,)), ((), ())), precision=precision, preferred_element_type=F32
    )


def dot_nt(a, b):
    return lax.dot_general(a, b, (((1,), (1,)), ((), ())), preferred_element_type=F32)


def dot_tn(a, b):
    return lax.dot_general(a, b, (((0,), (0,)), ((), ())), preferred_element_type=F32)


def iota(shape, dim):
    return lax.broadcasted_iota(jnp.int32, shape, dim)


def total_of(array):
    return jnp.sum(jnp.sum(array, axis=0, keepdims=True), axis=1, keepdims=True)


def later_sums(column):
    kept = iota((CHUNK, CHUNK), 0) >= iota((CHUNK, CHUNK), 1)
    return jnp.sum(jnp.where(kept, column, 0.0), axis=0, keepdims=True)


def decay_tables(docs, ctx, small_ref, spread, cum_ref, chunk_fac_ref, shard_fac_ref):
    rows = cum_ref.shape[0]
    num_chunks = rows // 8
    tokens = num_chunks * CHUNK
    for chunk in range(num_chunks):
        part = small_ref[:, chunk * CHUNK : (chunk + 1) * CHUNK]
        spread[chunk * 8 : chunk * 8 + 4, :] = part
        spread[chunk * 8 + 4 : chunk * 8 + 8, :] = part
    gates = spread[...] * LOG2E
    lane_a, lane_b = iota((CHUNK, CHUNK), 0), iota((CHUNK, CHUNK), 1)
    prefix = dot_nn(gates, (lane_a <= lane_b).astype(F32), PRECISE)
    suffix = dot_nn(gates, (lane_a > lane_b).astype(F32), PRECISE)
    totals = jnp.broadcast_to(prefix[:, CHUNK - 1 : CHUNK], (rows, CHUNK))
    row_a, row_b = iota((rows, rows), 0), iota((rows, rows), 1)
    same = (row_a % 8) == (row_b % 8)
    outside = ((row_a % 8 < 4) & (row_b // 8 < row_a // 8)) | (
        (row_a % 8 >= 4) & (row_b // 8 > row_a // 8)
    )
    others = dot_nn((same & outside).astype(F32), totals, PRECISE)

    first = ctx * tokens
    chunk_first = first + (iota((rows, CHUNK), 0) // 8) * CHUNK
    from_start = iota((rows, CHUNK), 0) % 8 < 4
    chunk_anchor = jnp.where(from_start, chunk_first - 1, chunk_first + (CHUNK - 1)).astype(F32)
    shard_anchor = jnp.where(from_start, first - 1, first + (tokens - 1)).astype(F32)
    positions = (chunk_first + iota((rows, CHUNK), 1)).astype(F32)
    segment = jnp.zeros((rows, CHUNK), F32)
    chunk_segment = jnp.zeros((rows, CHUNK), F32)
    shard_segment = jnp.zeros((rows, CHUNK), F32)
    begin = small_ref.shape[1] - CHUNK
    start = jnp.zeros((1, 1), F32)
    for doc in range(docs):
        segment += jnp.where(positions >= start, 1.0, 0.0)
        chunk_segment += jnp.where(chunk_anchor >= start, 1.0, 0.0)
        shard_segment += jnp.where(shard_anchor >= start, 1.0, 0.0)
        start = start + small_ref[0:1, begin + doc : begin + doc + 1]
    cum_ref[...] = jnp.where(from_start, prefix, segment)
    exponent = jnp.where(from_start, prefix, suffix)
    chunk_fac_ref[...] = jnp.where(
        segment == chunk_segment, jnp.exp2(jnp.minimum(exponent, 0.0)), 0.0
    )
    keep = segment == shard_segment
    shard_fac_ref[...] = jnp.where(keep, jnp.exp2(jnp.minimum(exponent + others, 0.0)), 0.0)


def ends_kernel(head_width, docs, half_ctx, *refs):
    small_ref, sources = refs[0], refs[1:5]
    ctx, dp = lax.axis_index("ctx"), lax.axis_index("dp")
    near_refs, far_refs, decay_refs = (
        refs[5 + i * PARTS : 5 + (i + 1) * PARTS] for i in range(3)
    )
    (cum_ref, chunk_fac_ref, shard_fac_ref, gain_ref, flag_ref, q_ref, k_ref, v_ref, cot_ref,
     spread, sems) = refs[5 + 3 * PARTS :]
    heads = near_refs[0].shape[0]
    rows = shard_fac_ref.shape[0]
    steps = sems.shape[0]
    tokens = q_ref.shape[1]
    block = tokens // steps
    chunks = block // CHUNK

    def copies(step):
        at = pl.ds(step * block, block)
        return [
            pltpu.make_async_copy(source.at[:, at, :], target.at[:, at, :], sems.at[step, i])
            for i, (source, target) in enumerate(zip(sources, (q_ref, k_ref, v_ref, cot_ref)))
        ]

    for step in range(steps):
        for i, copy in enumerate(copies(step)):
            copy.start(priority=i % 2)
    decay_tables(docs, ctx, small_ref, spread, cum_ref, chunk_fac_ref, shard_fac_ref)
    gain_ref[...] = small_ref[:, tokens : tokens + head_width]
    for part in range(PARTS):
        for head in range(heads):
            row = rows - 8 + part * heads + head
            decay_refs[part][head] = jnp.broadcast_to(
                shard_fac_ref[row : row + 1, CHUNK - 1 : CHUNK], (1, head_width)
            )

    def turned(ref, step, row, scale):
        pieces = []
        head = row % 4
        for chunk in range(step * chunks, (step + 1) * chunks):
            factor = shard_fac_ref[chunk * 8 + row : chunk * 8 + row + 1, :]
            piece = jnp.transpose(
                ref[
                    0,
                    chunk * CHUNK : (chunk + 1) * CHUNK,
                    head * head_width : (head + 1) * head_width,
                ]
            )
            pieces.append((piece.astype(F32) * (factor * scale)).astype(BF16))
        return jnp.concatenate(pieces, axis=1)

    ends, grads = {}, {}
    for step in range(steps):
        for copy in copies(step):
            copy.wait()
        at = slice(step * block, (step + 1) * block)
        for row in range(PARTS * heads):
            lanes = slice(row * head_width, (row + 1) * head_width)
            end = dot_nn(turned(k_ref, step, 4 + row, 1.0), v_ref[0, at, lanes])
            grad = dot_nn(turned(q_ref, step, row, head_width ** (-0.5)), cot_ref[0, at, lanes])
            ends[row] = ends[row] + end if step else end
            grads[row] = grads[row] + grad if step else grad
    middle = jnp.where(ctx == half_ctx - 1, 1.0, 0.0)
    low = ctx < half_ctx
    row = iota(flag_ref.shape, 0)
    flag_ref[...] = jnp.where(
        row == 0, middle, jnp.where(row == 1, dp.astype(F32), jnp.where(low, 1.0, 0.0))
    )
    for part in range(PARTS):
        for head in range(heads):
            row = part * heads + head
            near_refs[part][head] = jnp.where(low, ends[row], grads[row])
            far_refs[part][head] = jnp.where(low, grads[row], ends[row])


def local_kernel(
    head_width, part, q_ref, k_ref, v_ref, cot_ref, gain_ref, cum_ref, fac_ref,
    target, dgate_ref, dgain_ref, leaving, state,
):
    out_ref, dq_ref, dk_ref, dv_ref = (target.at[pl.ds(i, 1)] for i in range(4))
    heads = state.shape[0]
    num_chunks = leaving.shape[0]
    scale = head_width ** (-0.5)
    unroll = math.gcd(num_chunks, UNROLL)

    groups = num_chunks // unroll
    def wide_lanes(head):
        row = part * heads + head
        return slice(row * head_width, (row + 1) * head_width)

    def lanes_of(head):
        return slice(head * head_width, (head + 1) * head_width)

    def rows_of(chunk):
        return pl.ds(pl.multiple_of(chunk * CHUNK, CHUNK), CHUNK)

    def table(ref, chunk):
        return ref[pl.ds(pl.multiple_of(chunk * 8, 8), 8), :]

    pairs = [(at, head) for at in range(unroll) for head in range(heads)]

    def backward(chunks):
        facs = [table(fac_ref, chunk) for chunk in chunks]
        added = {}
        for at, head in pairs:
            row = part * heads + head
            rows, lanes = rows_of(chunks[at]), wide_lanes(head)
            turned = jnp.transpose(q_ref[0, rows, lanes]).astype(F32)
            turned = (turned * (facs[at][row : row + 1, :] * scale)).astype(BF16)
            added[at, head] = dot_nn(turned, cot_ref[0, rows, lanes])
        for head in range(heads):
            row = part * heads + head
            held = state[head]
            for at in range(unroll):
                leaving[chunks[at], head] = held.astype(BF16)
                held = held * facs[at][row : row + 1, CHUNK - 1 : CHUNK] + added[at, head]
            state[head] = held

    def forward(chunks):
        facs = [table(fac_ref, chunk) for chunk in chunks]
        cums = [table(cum_ref, chunk) for chunk in chunks]
        fac_columns = [jnp.transpose(fac) for fac in facs]
        cum_columns = [jnp.transpose(cum) for cum in cums]
        causal = iota((CHUNK, CHUNK), 0) >= iota((CHUNK, CHUNK), 1)
        limits = [
            jnp.where((columns[:, 4:5] == cum[4:5, :]) & causal, math.log2(scale), -1e30)
            for columns, cum in zip(cum_columns, cums)
        ]
        cum_columns = [columns + math.log2(scale) for columns in cum_columns]
        q, k, v, cot, k_raw, k_decayed, q_decayed, later = ({} for _ in range(8))
        from_start, to_end, added, held, entering = ({} for _ in range(5))
        for key in pairs:
            at, head = key
            row = part * heads + head
            rows, lanes = rows_of(chunks[at]), lanes_of(head)
            q[key], cot[key] = q_ref[0, rows, wide_lanes(head)], cot_ref[0, rows, wide_lanes(head)]
            v[key] = v_ref[0, rows, wide_lanes(head)]
            later[key] = leaving[chunks[at], head]
            k_raw[key] = k_ref[0, rows, wide_lanes(head)].astype(F32)
            k_wide = k_raw[key] * gain_ref[row : row + 1, :]
            k[key] = k_wide.astype(BF16)
            from_start[key] = fac_columns[at][:, row : row + 1] * scale
            to_end[key] = fac_columns[at][:, 4 + row : 5 + row]
            k_decayed[key] = (k_wide * to_end[key]).astype(BF16)
            q_decayed[key] = (q[key].astype(F32) * from_start[key]).astype(BF16)
            added[key] = dot_tn(k_decayed[key], v[key])
        for head in range(heads):
            row = part * heads + head
            now = state[head]
            for at in range(unroll):
                held[at, head] = now
                entering[at, head] = now.astype(BF16)
                now = now * facs[at][row : row + 1, CHUNK - 1 : CHUNK] + added[at, head]
            held[unroll, head] = now
            state[head] = now
        by_cot, scores, written = {}, {}, {}
        for key in pairs:
            by_cot[key] = dot_nt(cot[key], jnp.concatenate([v[key], entering[key]], axis=0))
            scores[key] = dot_nt(q[key], k[key])
            written[key] = dot_nt(v[key], later[key])
        weights, grad_scores = {}, {}
        for key in pairs:
            at, head = key
            row = part * heads + head
            decays = jnp.exp2(
                jnp.minimum(cum_columns[at][:, row : row + 1] - cums[at][row : row + 1, :], limits[at])
            )
            weights[key] = (scores[key] * decays).astype(BF16)
            grad_scores[key] = (by_cot[key][:, :CHUNK] * decays).astype(BF16)
        out, dq, dk, dv = {}, {}, {}, {}
        for key in pairs:
            out[key] = dot_nn(
                jnp.concatenate([weights[key], q_decayed[key]], axis=1),
                jnp.concatenate([v[key], entering[key]], axis=0),
            )
            dv[key] = dot_nn(
                jnp.concatenate([jnp.transpose(weights[key]), k_decayed[key]], axis=1),
                jnp.concatenate([cot[key], later[key]], axis=0),
            )
            dq[key] = dot_nn(grad_scores[key], k[key]) + by_cot[key][:, CHUNK:] * from_start[key]
            dk[key] = dot_tn(grad_scores[key], q[key]) + written[key] * to_end[key]
        gate_rows, gain_rows = {}, {}
        for key in pairs:
            at, head = key
            balance = jnp.sum(
                out[key] * cot[key].astype(F32) - dv[key] * v[key].astype(F32),
                axis=1, keepdims=True,
            )
            gate_rows[key] = later_sums(balance) + total_of(
                held[at + 1, head] * later[key].astype(F32)
            )
            gain_rows[key] = jnp.sum(dk[key] * k_raw[key], axis=0, keepdims=True)
        for key in pairs:
            at, head = key
            row = part * heads + head
            rows, own = rows_of(chunks[at]), lanes_of(head)
            out_ref[0, rows, own] = out[key].astype(BF16)
            dq_ref[0, rows, own] = dq[key].astype(BF16)
            dv_ref[0, rows, own] = dv[key].astype(BF16)
            dk_ref[0, rows, own] = (dk[key] * gain_ref[row : row + 1, :]).astype(BF16)
            dgate_ref[0, head : head + 1, rows] = gate_rows[key]
        for head in range(heads):
            dgain_ref[head : head + 1, :] += sum(gain_rows[at, head] for at in range(unroll))

    state[...] = jnp.zeros_like(state)

    def backward_group(index, carry):
        backward([num_chunks - 1 - (index * unroll + at) for at in range(unroll)])
        return carry

    lax.fori_loop(0, groups, backward_group, 0)
    state[...] = jnp.zeros_like(state)
    dgain_ref[...] = jnp.zeros_like(dgain_ref)

    def forward_group(index, carry):
        forward([index * unroll + at for at in range(unroll)])
        return carry

    lax.fori_loop(0, groups, forward_group, 0)


def merge_kernel(head_width, *refs):
    q_ref, k_ref, v_ref, cot_ref, gain_ref, flag_ref, fac_ref = refs[:7]
    partial_refs, gate_refs, first_refs, second_refs, last_refs = (
        refs[7 + i * PARTS : 7 + (i + 1) * PARTS] for i in range(5)
    )
    refs = refs[7 + 5 * PARTS :]
    extra = len(refs) - 11
    gain_refs, refs = refs[:extra], refs[extra:]
    targets, dgate_ref, dgain_ref, staged, matrices, spread_ref, gate_scr, sems = (
        refs[:4], *refs[4:]
    )
    dgain_ref[...] = summed(gain_refs[0][...], [ref[...] for ref in gain_refs[1:]])
    heads = first_refs[0].shape[0]
    steps = sems.shape[0]
    num_chunks = fac_ref.shape[0] // 8
    chunks = num_chunks // steps
    block = chunks * CHUNK
    group_width = heads * head_width
    scale = head_width ** (-0.5)

    def copies(step):
        at = pl.ds(step * block, block)
        return [
            pltpu.make_async_copy(staged.at[i, at, :], target.at[0, at, :], sems.at[step, i])
            for i, target in enumerate(targets)
        ]

    gain_columns = jnp.transpose(jnp.concatenate([gain_ref[...], gain_ref[...]], axis=0))
    matrices[...] = jnp.zeros_like(matrices)
    last_factors = fac_ref[(num_chunks - 1) * 8 : num_chunks * 8, CHUNK - 1 : CHUNK]
    low = jnp.broadcast_to(flag_ref[2:3, :], (head_width, head_width)) > 0.5
    constants = []
    for part in range(PARTS):
        for head in range(heads):
            row = part * heads + head
            own = slice(head * head_width, (head + 1) * head_width)
            gain = gain_columns[:, row : row + 1]
            first = first_refs[part][head]
            second = second_refs[part][head] + last_refs[part][head]
            state = jnp.where(low, first, second) * gain
            later = jnp.where(low, second, first)
            entering, leaving = state * scale, later * gain
            for i, matrix in enumerate(
                (entering, jnp.transpose(entering), jnp.transpose(leaving), leaving)
            ):
                matrices[part, i, own, own] = matrix.astype(BF16)
            constants.append(total_of(state * later) * last_factors[row : row + 1])

    spread = (iota(spread_ref.shape, 1) // head_width == iota(spread_ref.shape, 0) % 8).astype(F32)
    spread_ref[...] = spread.astype(BF16)
    ones = jnp.ones((8, head_width), BF16)
    for step in range(steps):
        numbers = range(step * chunks, (step + 1) * chunks)
        products, results, factors = {}, {}, {}
        block_rows = slice(step * block, (step + 1) * block)
        for part in range(PARTS):
            group = slice(part * group_width, (part + 1) * group_width)
            block_products = [
                dot_nn(ref[0, block_rows, group], matrices[part, i])
                for i, ref in enumerate((q_ref, cot_ref, v_ref, k_ref))
            ]
            for i, number in enumerate(numbers):
                products[number, part] = [
                    product[i * CHUNK : (i + 1) * CHUNK] for product in block_products
                ]
        for number in numbers:
            fac = fac_ref[number * 8 : number * 8 + 8, :]
            high = fac.astype(BF16).astype(F32)
            both = jnp.concatenate([high, fac - high], axis=0).astype(BF16)
            factors[number] = dot_tn(both, spread_ref[...])
        for number in numbers:
            rows = slice(number * CHUNK, (number + 1) * CHUNK)
            for row in range(PARTS * heads):
                part, head = divmod(row, heads)
                lanes = slice(head * head_width, (head + 1) * head_width)
                wide = slice(row * head_width, (row + 1) * head_width)
                from_start = factors[number][:, wide]
                to_end = factors[number][:, (4 + row) * head_width : (5 + row) * head_width]
                across, dq, dk, written = (
                    product[:, lanes] * factor
                    for product, factor in zip(
                        products[number, part], (from_start, from_start, to_end, to_end)
                    )
                )
                results[number, row] = [
                    (partial_refs[part][i, rows, lanes].astype(F32) + added).astype(BF16)
                    for i, added in enumerate((across, dq, dk, written))
                ]
                queried = (across * cot_ref[0, rows, wide].astype(F32)).astype(BF16)
                kept = (written * v_ref[0, rows, wide].astype(F32)).astype(BF16)
                shares = dot_nt(ones, jnp.concatenate([queried, kept], axis=0))
                at = number * 8 + row
                gate_scr[at : at + 1, :] = shares[0:1, :CHUNK]
                gate_scr[at + 4 : at + 5, :] = shares[0:1, CHUNK:]
        for number in numbers:
            rows = slice(number * CHUNK, (number + 1) * CHUNK)
            for row in range(PARTS * heads):
                wide = slice(row * head_width, (row + 1) * head_width)
                for i in range(4):
                    staged[i, rows, wide] = results[number, row][i]
        for i, copy in enumerate(copies(step)):
            copy.start(priority=i % 2)

    shares = gate_scr[...]
    lane_a, lane_b = iota((CHUNK, CHUNK), 0), iota((CHUNK, CHUNK), 1)
    from_here = dot_nn(shares, (lane_a >= lane_b).astype(F32), PRECISE)
    up_to_here = dot_nn(shares, (lane_a < lane_b).astype(F32), PRECISE)
    all_rows = shares.shape[0]
    totals = jnp.broadcast_to(from_here[:, 0:1], shares.shape)
    row_a, row_b = iota((all_rows, all_rows), 0), iota((all_rows, all_rows), 1)
    outside = ((row_a % 8 < 4) & (row_b // 8 > row_a // 8)) | (
        (row_a % 8 >= 4) & (row_b // 8 < row_a // 8)
    )
    outside = (outside & (row_a % 8 == row_b % 8)).astype(F32)
    sums = dot_nn(outside, totals, PRECISE) + jnp.where(
        iota(shares.shape, 0) % 8 < 4, from_here, up_to_here
    )
    for number in range(num_chunks):
        lanes = slice(number * CHUNK, (number + 1) * CHUNK)
        for row in range(PARTS * heads):
            part, head = divmod(row, heads)
            at = number * 8 + row
            dgate_ref[0, row : row + 1, lanes] = (
                gate_refs[part][0, head : head + 1, lanes]
                + sums[at : at + 1, :]
                + sums[at + 4 : at + 5, :]
                + constants[row]
            )
    for step in range(steps):
        for copy in copies(step):
            copy.wait()


def summed(own, others):
    if not others:
        return own
    if len(others) == 1:
        return own + others[0]
    return (own + others[0]) + (others[1] + others[2])


def shards(queries, keys_raw, values, gates, lengths, key_gain, cotangent):
    tokens, width = queries.shape[1:]
    all_heads, head_width = key_gain.shape
    heads = all_heads // PARTS
    part_width = width // PARTS
    num_chunks = tokens // CHUNK
    rows = num_chunks * 8
    block = min(256, tokens)
    steps = tokens // block
    count = lax.axis_size("ctx")
    middle = count // 2 - 1
    docs = lengths.shape[1]
    after = head_width + CHUNK
    small = (
        jnp.pad(gates[0], ((0, 0), (0, after)))
        + jnp.pad(key_gain, ((0, 0), (tokens, CHUNK)))
        + jnp.pad(lengths, ((0, all_heads - 1), (tokens + head_width, CHUNK - docs))).astype(F32)
    )

    def shape_of(*shape, dtype=F32):
        return jax.ShapeDtypeStruct(shape, dtype)

    hbm = pl.BlockSpec(memory_space=pltpu.HBM)
    vmem = pl.BlockSpec(memory_space=pltpu.VMEM)
    table = shape_of(rows, CHUNK)
    states = shape_of(heads, head_width, head_width)
    decays = shape_of(heads, 1, head_width)
    part_gates = shape_of(1, heads, tokens)
    partials = shape_of(4, tokens, part_width, dtype=BF16)
    streams = (queries, keys_raw, values, cotangent)
    product = 2 * tokens * part_width * head_width

    def ends():
        outs = [states] * (2 * PARTS) + [decays] * PARTS + [table] * 3
        outs += [shape_of(all_heads, head_width), shape_of(4, head_width)]
        outs += [shape_of(1, tokens, width, dtype=BF16)] * 4
        return pl.pallas_call(
            functools.partial(ends_kernel, head_width, lengths.shape[1], count // 2),
            in_specs=[vmem] + [hbm] * 4,
            out_specs=[vmem] * len(outs),
            out_shape=outs,
            scratch_shapes=[
                pltpu.VMEM((rows, CHUNK), F32),
                pltpu.SemaphoreType.DMA((steps, 4)),
            ],
            compiler_params=pltpu.CompilerParams(vmem_limit_bytes=49 << 20),
            cost_estimate=pl.CostEstimate(
                flops=2 * product * PARTS, bytes_accessed=8 * tokens * width, transcendentals=0
            ),
            name="shard_ends",
        )(small, *streams)

    def local(part, gain, cum, fac):
        return pl.pallas_call(
            functools.partial(local_kernel, head_width, part),
            in_specs=[vmem] * 7,
            out_specs=[vmem] * 3,
            out_shape=[partials, part_gates, shape_of(heads, head_width)],
            scratch_shapes=[
                pltpu.VMEM((num_chunks, heads, head_width, head_width), BF16),
                pltpu.VMEM((heads, head_width, head_width), F32),
            ],
            compiler_params=pltpu.CompilerParams(vmem_limit_bytes=24 << 20),
            cost_estimate=pl.CostEstimate(
                flops=12 * product, bytes_accessed=16 * tokens * part_width, transcendentals=0
            ),
            name=f"local_{part}",
        )(*held, gain, cum, fac)

    def merge(*arrays):
        return pl.pallas_call(
            functools.partial(merge_kernel, head_width),
            in_specs=[vmem] * len(arrays),
            out_specs=[hbm] * 4 + [vmem] * 2,
            out_shape=[shape_of(1, tokens, width, dtype=BF16)] * 4
            + [shape_of(*gates.shape), shape_of(*arrays[-1].shape)],
            scratch_shapes=[
                pltpu.VMEM((4, tokens, width), BF16),
                pltpu.VMEM((PARTS, 4, part_width, part_width), BF16),
                pltpu.VMEM((16, 8 * head_width), BF16),
                pltpu.VMEM((rows, CHUNK), F32),
                pltpu.SemaphoreType.DMA((steps, 4)),
            ],
            compiler_params=pltpu.CompilerParams(vmem_limit_bytes=24 << 20),
            cost_estimate=pl.CostEstimate(
                flops=4 * product * PARTS, bytes_accessed=24 * tokens * width, transcendentals=0
            ),
            name="merge",
        )(*arrays)

    results = ends()
    near, far, decay = (results[i * PARTS : (i + 1) * PARTS] for i in range(3))
    cum, chunk_fac, shard_fac, gain, flags = results[3 * PARTS : 3 * PARTS + 5]
    held = results[3 * PARTS + 5 :]
    sent = [[] for _ in range(PARTS)]
    arrived = [[] for _ in range(PARTS)]
    local_parts = [None] * PARTS

    def send(part, hop):
        payload = near[part] if hop <= middle else far[part]
        if hop > 0:
            payload = payload + decay[part] * arrived[part][-1]
        sent[part].append(payload)
        arrived[part].append(
            lax.ppermute(
                payload, "ctx", [(hop, hop + 1), (count - 1 - hop, count - 2 - hop)]
            )
        )

    for part in range(PARTS):
        send(part, 0)
    for hop in range(count - 1):
        if hop < PARTS:
            local_cum = cum
            if hop > 0:
                local_cum, _ = lax.optimization_barrier((cum, arrived[0][hop - 1]))
            local_parts[hop] = list(local(hop, gain, local_cum, chunk_fac))
            if hop + 1 < count - 1:
                local_parts[hop][2], arrived[0][-1] = lax.optimization_barrier(
                    (local_parts[hop][2], arrived[0][-1])
                )
        if hop + 1 < count - 1:
            for part in range(PARTS):
                send(part, hop + 1)

    terms = []
    for part in range(PARTS):
        crossed = jnp.sum(sent[part][middle] * arrived[part][middle], axis=2)
        term = local_parts[part][2] + flags[0:1] * crossed
        if middle > 0:
            term = term + jnp.sum(sum(arrived[part][:middle]) * far[part], axis=2)
        terms.append(term)
    gain_term = jnp.concatenate(terms, axis=0)
    half = head_width // lax.axis_size("dp")
    second_half = flags[1:2, :half]
    lower_half, upper_half = gain_term[:, :half], gain_term[:, half:]
    away = (1.0 - second_half) * upper_half + second_half * lower_half
    kept = (1.0 - second_half) * lower_half + second_half * upper_half
    grad_gain = kept + lax.ppermute(away, "dp", [(0, 1), (1, 0)])

    def exchanged(array, reach):
        return lax.ppermute(array, "ctx", [(i, i ^ reach) for i in range(count)])

    pending, reach = [], 1
    while reach < count:
        if pending:
            grad_gain = summed(grad_gain, pending)
        pending = [exchanged(grad_gain, reach)]
        if reach * 2 < count:
            pending += [exchanged(grad_gain, reach * 2), exchanged(grad_gain, reach * 3)]
        reach *= 2 * min(len(pending), 2)

    zeros = jnp.zeros(states.shape, F32)
    if middle == 1:
        firsts, seconds = ([own[i] for own in arrived] for i in range(2))
    else:
        firsts = [sum(own[:middle], zeros) for own in arrived]
        seconds = [sum(own[middle:-1], zeros) for own in arrived]
    done = list(
        merge(
            *held, gain, flags, shard_fac,
            *[local_part[0] for local_part in local_parts],
            *[local_part[1] for local_part in local_parts],
            *firsts, *seconds, *[own[-1] for own in arrived],
            grad_gain, *pending,
        )
    )
    return tuple(done)


def solution(mesh):
    wide = P("dp", "ctx", "head")
    narrow = P("dp", "head", "ctx")
    return jax.shard_map(
        shards,
        mesh=mesh,
        in_specs=(wide, wide, wide, narrow, P("dp", None), P("head", None), wide),
        out_specs=(wide, wide, wide, wide, narrow, P("head", "dp")),
        check_vma=False,
    )
```

```python
import functools
import math

import jax
import jax.numpy as jnp
from jax import lax
from jax.experimental import pallas as pl
from jax.experimental.pallas import tpu as pltpu
from jax.sharding import PartitionSpec as P

CHUNK = 128
PARTS = 2
UNROLL = 4
PRECISE = lax.Precision.HIGHEST
F32 = jnp.float32
BF16 = jnp.bfloat16
LOG2E = math.log2(math.e)


def dot_nn(a, b, precision=None):
    return lax.dot_general(
        a, b, (((1,), (0,)), ((), ())), precision=precision, preferred_element_type=F32
    )


def dot_nt(a, b):
    return lax.dot_general(a, b, (((1,), (1,)), ((), ())), preferred_element_type=F32)


def dot_tn(a, b):
    return lax.dot_general(a, b, (((0,), (0,)), ((), ())), preferred_element_type=F32)


def iota(shape, dim):
    return lax.broadcasted_iota(jnp.int32, shape, dim)


def total_of(array):
    return jnp.sum(jnp.sum(array, axis=0, keepdims=True), axis=1, keepdims=True)


def later_sums(column):
    kept = iota((CHUNK, CHUNK), 0) >= iota((CHUNK, CHUNK), 1)
    return jnp.sum(jnp.where(kept, column, 0.0), axis=0, keepdims=True)


def decay_tables(docs, ctx, small_ref, spread, cum_ref, chunk_fac_ref, shard_fac_ref):
    rows = cum_ref.shape[0]
    num_chunks = rows // 8
    tokens = num_chunks * CHUNK
    for chunk in range(num_chunks):
        part = small_ref[:, chunk * CHUNK : (chunk + 1) * CHUNK]
        spread[chunk * 8 : chunk * 8 + 4, :] = part
        spread[chunk * 8 + 4 : chunk * 8 + 8, :] = part
    gates = spread[...] * LOG2E
    lane_a, lane_b = iota((CHUNK, CHUNK), 0), iota((CHUNK, CHUNK), 1)
    prefix = dot_nn(gates, (lane_a <= lane_b).astype(F32), PRECISE)
    suffix = dot_nn(gates, (lane_a > lane_b).astype(F32), PRECISE)
    totals = jnp.broadcast_to(prefix[:, CHUNK - 1 : CHUNK], (rows, CHUNK))
    row_a, row_b = iota((rows, rows), 0), iota((rows, rows), 1)
    same = (row_a % 8) == (row_b % 8)
    outside = ((row_a % 8 < 4) & (row_b // 8 < row_a // 8)) | (
        (row_a % 8 >= 4) & (row_b // 8 > row_a // 8)
    )
    others = dot_nn((same & outside).astype(F32), totals, PRECISE)

    first = ctx * tokens
    chunk_first = first + (iota((rows, CHUNK), 0) // 8) * CHUNK
    from_start = iota((rows, CHUNK), 0) % 8 < 4
    chunk_anchor = jnp.where(from_start, chunk_first - 1, chunk_first + (CHUNK - 1)).astype(F32)
    shard_anchor = jnp.where(from_start, first - 1, first + (tokens - 1)).astype(F32)
    positions = (chunk_first + iota((rows, CHUNK), 1)).astype(F32)
    segment = jnp.zeros((rows, CHUNK), F32)
    chunk_segment = jnp.zeros((rows, CHUNK), F32)
    shard_segment = jnp.zeros((rows, CHUNK), F32)
    begin = small_ref.shape[1] - CHUNK
    start = jnp.zeros((1, 1), F32)
    for doc in range(docs):
        segment += jnp.where(positions >= start, 1.0, 0.0)
        chunk_segment += jnp.where(chunk_anchor >= start, 1.0, 0.0)
        shard_segment += jnp.where(shard_anchor >= start, 1.0, 0.0)
        start = start + small_ref[0:1, begin + doc : begin + doc + 1]
    cum_ref[...] = jnp.where(from_start, prefix, segment)
    exponent = jnp.where(from_start, prefix, suffix)
    chunk_fac_ref[...] = jnp.where(
        segment == chunk_segment, jnp.exp2(jnp.minimum(exponent, 0.0)), 0.0
    )
    keep = segment == shard_segment
    shard_fac_ref[...] = jnp.where(keep, jnp.exp2(jnp.minimum(exponent + others, 0.0)), 0.0)


def ends_kernel(head_width, docs, half_ctx, *refs):
    small_ref, sources = refs[0], refs[1:5]
    ctx, dp = lax.axis_index("ctx"), lax.axis_index("dp")
    near_refs, far_refs, decay_refs = (
        refs[5 + i * PARTS : 5 + (i + 1) * PARTS] for i in range(3)
    )
    (cum_ref, chunk_fac_ref, shard_fac_ref, gain_ref, flag_ref, q_ref, k_ref, v_ref, cot_ref,
     spread, sems) = refs[5 + 3 * PARTS :]
    heads = near_refs[0].shape[0]
    rows = shard_fac_ref.shape[0]
    steps = sems.shape[0]
    tokens = q_ref.shape[1]
    block = tokens // steps
    chunks = block // CHUNK

    def copies(step):
        at = pl.ds(step * block, block)
        return [
            pltpu.make_async_copy(source.at[:, at, :], target.at[:, at, :], sems.at[step, i])
            for i, (source, target) in enumerate(zip(sources, (q_ref, k_ref, v_ref, cot_ref)))
        ]

    for step in range(steps):
        for i, copy in enumerate(copies(step)):
            copy.start(priority=i % 2)
    decay_tables(docs, ctx, small_ref, spread, cum_ref, chunk_fac_ref, shard_fac_ref)
    gain_ref[...] = small_ref[:, tokens : tokens + head_width]
    for part in range(PARTS):
        for head in range(heads):
            row = rows - 8 + part * heads + head
            decay_refs[part][head] = jnp.broadcast_to(
                shard_fac_ref[row : row + 1, CHUNK - 1 : CHUNK], (1, head_width)
            )

    def turned(ref, step, row, scale):
        pieces = []
        head = row % 4
        for chunk in range(step * chunks, (step + 1) * chunks):
            factor = shard_fac_ref[chunk * 8 + row : chunk * 8 + row + 1, :]
            piece = jnp.transpose(
                ref[
                    0,
                    chunk * CHUNK : (chunk + 1) * CHUNK,
                    head * head_width : (head + 1) * head_width,
                ]
            )
            pieces.append((piece.astype(F32) * (factor * scale)).astype(BF16))
        return jnp.concatenate(pieces, axis=1)

    ends, grads = {}, {}
    for step in range(steps):
        for copy in copies(step):
            copy.wait()
        at = slice(step * block, (step + 1) * block)
        for row in range(PARTS * heads):
            lanes = slice(row * head_width, (row + 1) * head_width)
            end = dot_nn(turned(k_ref, step, 4 + row, 1.0), v_ref[0, at, lanes])
            grad = dot_nn(turned(q_ref, step, row, head_width ** (-0.5)), cot_ref[0, at, lanes])
            ends[row] = ends[row] + end if step else end
            grads[row] = grads[row] + grad if step else grad
    middle = jnp.where(ctx == half_ctx - 1, 1.0, 0.0)
    low = ctx < half_ctx
    row = iota(flag_ref.shape, 0)
    flag_ref[...] = jnp.where(
        row == 0, middle, jnp.where(row == 1, dp.astype(F32), jnp.where(low, 1.0, 0.0))
    )
    for part in range(PARTS):
        for head in range(heads):
            row = part * heads + head
            near_refs[part][head] = jnp.where(low, ends[row], grads[row])
            far_refs[part][head] = jnp.where(low, grads[row], ends[row])


def local_kernel(
    head_width, part, q_ref, k_ref, v_ref, cot_ref, gain_ref, cum_ref, fac_ref,
    target, dgate_ref, dgain_ref, leaving, state,
):
    out_ref, dq_ref, dk_ref, dv_ref = (target.at[pl.ds(i, 1)] for i in range(4))
    heads = state.shape[0]
    num_chunks = leaving.shape[0]
    scale = head_width ** (-0.5)
    unroll = math.gcd(num_chunks, UNROLL)

    groups = num_chunks // unroll
    def wide_lanes(head):
        row = part * heads + head
        return slice(row * head_width, (row + 1) * head_width)

    def lanes_of(head):
        return slice(head * head_width, (head + 1) * head_width)

    def rows_of(chunk):
        return pl.ds(pl.multiple_of(chunk * CHUNK, CHUNK), CHUNK)

    def table(ref, chunk):
        return ref[pl.ds(pl.multiple_of(chunk * 8, 8), 8), :]

    pairs = [(at, head) for at in range(unroll) for head in range(heads)]

    def backward(chunks):
        facs = [table(fac_ref, chunk) for chunk in chunks]
        added = {}
        for at, head in pairs:
            row = part * heads + head
            rows, lanes = rows_of(chunks[at]), wide_lanes(head)
            turned = jnp.transpose(q_ref[0, rows, lanes]).astype(F32)
            turned = (turned * (facs[at][row : row + 1, :] * scale)).astype(BF16)
            added[at, head] = dot_nn(turned, cot_ref[0, rows, lanes])
        for head in range(heads):
            row = part * heads + head
            held = state[head]
            for at in range(unroll):
                leaving[chunks[at], head] = held.astype(BF16)
                held = held * facs[at][row : row + 1, CHUNK - 1 : CHUNK] + added[at, head]
            state[head] = held

    def forward(chunks):
        facs = [table(fac_ref, chunk) for chunk in chunks]
        cums = [table(cum_ref, chunk) for chunk in chunks]
        fac_columns = [jnp.transpose(fac) for fac in facs]
        cum_columns = [jnp.transpose(cum) for cum in cums]
        causal = iota((CHUNK, CHUNK), 0) >= iota((CHUNK, CHUNK), 1)
        limits = [
            jnp.where((columns[:, 4:5] == cum[4:5, :]) & causal, math.log2(scale), -1e30)
            for columns, cum in zip(cum_columns, cums)
        ]
        cum_columns = [columns + math.log2(scale) for columns in cum_columns]
        q, k, v, cot, k_raw, k_decayed, q_decayed, later = ({} for _ in range(8))
        from_start, to_end, added, held, entering = ({} for _ in range(5))
        for key in pairs:
            at, head = key
            row = part * heads + head
            rows, lanes = rows_of(chunks[at]), lanes_of(head)
            q[key], cot[key] = q_ref[0, rows, wide_lanes(head)], cot_ref[0, rows, wide_lanes(head)]
            v[key] = v_ref[0, rows, wide_lanes(head)]
            later[key] = leaving[chunks[at], head]
            k_raw[key] = k_ref[0, rows, wide_lanes(head)].astype(F32)
            k_wide = k_raw[key] * gain_ref[row : row + 1, :]
            k[key] = k_wide.astype(BF16)
            from_start[key] = fac_columns[at][:, row : row + 1] * scale
            to_end[key] = fac_columns[at][:, 4 + row : 5 + row]
            k_decayed[key] = (k_wide * to_end[key]).astype(BF16)
            q_decayed[key] = (q[key].astype(F32) * from_start[key]).astype(BF16)
            added[key] = dot_tn(k_decayed[key], v[key])
        for head in range(heads):
            row = part * heads + head
            now = state[head]
            for at in range(unroll):
                held[at, head] = now
                entering[at, head] = now.astype(BF16)
                now = now * facs[at][row : row + 1, CHUNK - 1 : CHUNK] + added[at, head]
            held[unroll, head] = now
            state[head] = now
        by_cot, scores, written = {}, {}, {}
        for key in pairs:
            by_cot[key] = dot_nt(cot[key], jnp.concatenate([v[key], entering[key]], axis=0))
            scores[key] = dot_nt(q[key], k[key])
            written[key] = dot_nt(v[key], later[key])
        weights, grad_scores = {}, {}
        for key in pairs:
            at, head = key
            row = part * heads + head
            decays = jnp.exp2(
                jnp.minimum(cum_columns[at][:, row : row + 1] - cums[at][row : row + 1, :], limits[at])
            )
            weights[key] = (scores[key] * decays).astype(BF16)
            grad_scores[key] = (by_cot[key][:, :CHUNK] * decays).astype(BF16)
        out, dq, dk, dv = {}, {}, {}, {}
        for key in pairs:
            out[key] = dot_nn(
                jnp.concatenate([weights[key], q_decayed[key]], axis=1),
                jnp.concatenate([v[key], entering[key]], axis=0),
            )
            dv[key] = dot_nn(
                jnp.concatenate([jnp.transpose(weights[key]), k_decayed[key]], axis=1),
                jnp.concatenate([cot[key], later[key]], axis=0),
            )
            dq[key] = dot_nn(grad_scores[key], k[key]) + by_cot[key][:, CHUNK:] * from_start[key]
            dk[key] = dot_tn(grad_scores[key], q[key]) + written[key] * to_end[key]
        gate_rows, gain_rows = {}, {}
        for key in pairs:
            at, head = key
            balance = jnp.sum(
                out[key] * cot[key].astype(F32) - dv[key] * v[key].astype(F32),
                axis=1, keepdims=True,
            )
            gate_rows[key] = later_sums(balance) + total_of(
                held[at + 1, head] * later[key].astype(F32)
            )
            gain_rows[key] = jnp.sum(dk[key] * k_raw[key], axis=0, keepdims=True)
        for key in pairs:
            at, head = key
            row = part * heads + head
            rows, own = rows_of(chunks[at]), lanes_of(head)
            out_ref[0, rows, own] = out[key].astype(BF16)
            dq_ref[0, rows, own] = dq[key].astype(BF16)
            dv_ref[0, rows, own] = dv[key].astype(BF16)
            dk_ref[0, rows, own] = (dk[key] * gain_ref[row : row + 1, :]).astype(BF16)
            dgate_ref[0, head : head + 1, rows] = gate_rows[key]
        for head in range(heads):
            dgain_ref[head : head + 1, :] += sum(gain_rows[at, head] for at in range(unroll))

    state[...] = jnp.zeros_like(state)

    def backward_group(index, carry):
        backward([num_chunks - 1 - (index * unroll + at) for at in range(unroll)])
        return carry

    lax.fori_loop(0, groups, backward_group, 0)
    state[...] = jnp.zeros_like(state)
    dgain_ref[...] = jnp.zeros_like(dgain_ref)

    def forward_group(index, carry):
        forward([index * unroll + at for at in range(unroll)])
        return carry

    lax.fori_loop(0, groups, forward_group, 0)


def merge_kernel(head_width, *refs):
    q_ref, k_ref, v_ref, cot_ref, gain_ref, flag_ref, fac_ref = refs[:7]
    partial_refs, gate_refs, first_refs, second_refs, last_refs = (
        refs[7 + i * PARTS : 7 + (i + 1) * PARTS] for i in range(5)
    )
    refs = refs[7 + 5 * PARTS :]
    extra = len(refs) - 12
    gain_refs, refs = refs[:extra], refs[extra:]
    targets, dgate_ref, dgain_ref, staged, entering, leaving, spread_ref, gate_scr, sems = (
        refs[:4], *refs[4:]
    )
    dgain_ref[...] = summed(gain_refs[0][...], [ref[...] for ref in gain_refs[1:]])
    heads = first_refs[0].shape[0]
    steps = sems.shape[0]
    num_chunks = fac_ref.shape[0] // 8
    chunks = num_chunks // steps
    block = chunks * CHUNK
    group_width = heads * head_width
    scale = head_width ** (-0.5)

    def copies(step):
        at = pl.ds(step * block, block)
        return [
            pltpu.make_async_copy(staged.at[i, at, :], target.at[0, at, :], sems.at[step, i])
            for i, target in enumerate(targets)
        ]

    gain_columns = jnp.transpose(jnp.concatenate([gain_ref[...], gain_ref[...]], axis=0))
    entering[...] = jnp.zeros_like(entering)
    leaving[...] = jnp.zeros_like(leaving)
    last_factors = fac_ref[(num_chunks - 1) * 8 : num_chunks * 8, CHUNK - 1 : CHUNK]
    low = jnp.broadcast_to(flag_ref[2:3, :], (head_width, head_width)) > 0.5
    constants = []
    for part in range(PARTS):
        for head in range(heads):
            row = part * heads + head
            own = slice(head * head_width, (head + 1) * head_width)
            gain = gain_columns[:, row : row + 1]
            first = first_refs[part][head]
            second = second_refs[part][head] + last_refs[part][head]
            state = jnp.where(low, first, second) * gain
            later = jnp.where(low, second, first)
            entering[part, own, own] = (state * scale).astype(BF16)
            leaving[part, own, own] = (later * gain).astype(BF16)
            constants.append(total_of(state * later) * last_factors[row : row + 1])

    spread = (iota(spread_ref.shape, 1) // head_width == iota(spread_ref.shape, 0) % 8).astype(F32)
    spread_ref[...] = spread.astype(BF16)
    ones = jnp.ones((8, head_width), BF16)
    for step in range(steps):
        numbers = range(step * chunks, (step + 1) * chunks)
        products, results, factors = {}, {}, {}
        for number in numbers:
            rows = slice(number * CHUNK, (number + 1) * CHUNK)
            fac = fac_ref[number * 8 : number * 8 + 8, :]
            high = fac.astype(BF16).astype(F32)
            both = jnp.concatenate([high, fac - high], axis=0).astype(BF16)
            factors[number] = dot_tn(both, spread_ref[...])
            for part in range(PARTS):
                group = slice(part * group_width, (part + 1) * group_width)
                products[number, part] = (
                    dot_nn(q_ref[0, rows, group], entering[part]),
                    dot_nt(cot_ref[0, rows, group], entering[part]),
                    dot_nt(v_ref[0, rows, group], leaving[part]),
                    dot_nn(k_ref[0, rows, group], leaving[part]),
                )
        for number in numbers:
            rows = slice(number * CHUNK, (number + 1) * CHUNK)
            for row in range(PARTS * heads):
                part, head = divmod(row, heads)
                lanes = slice(head * head_width, (head + 1) * head_width)
                wide = slice(row * head_width, (row + 1) * head_width)
                from_start = factors[number][:, wide]
                to_end = factors[number][:, (4 + row) * head_width : (5 + row) * head_width]
                across, dq, dk, written = (
                    product[:, lanes] * factor
                    for product, factor in zip(
                        products[number, part], (from_start, from_start, to_end, to_end)
                    )
                )
                results[number, row] = [
                    (partial_refs[part][i, rows, lanes].astype(F32) + added).astype(BF16)
                    for i, added in enumerate((across, dq, dk, written))
                ]
                queried = (across * cot_ref[0, rows, wide].astype(F32)).astype(BF16)
                kept = (written * v_ref[0, rows, wide].astype(F32)).astype(BF16)
                shares = dot_nt(ones, jnp.concatenate([queried, kept], axis=0))
                at = number * 8 + row
                gate_scr[at : at + 1, :] = shares[0:1, :CHUNK]
                gate_scr[at + 4 : at + 5, :] = shares[0:1, CHUNK:]
        for number in numbers:
            rows = slice(number * CHUNK, (number + 1) * CHUNK)
            for row in range(PARTS * heads):
                wide = slice(row * head_width, (row + 1) * head_width)
                for i in range(4):
                    staged[i, rows, wide] = results[number, row][i]
        for i, copy in enumerate(copies(step)):
            copy.start(priority=i % 2)

    shares = gate_scr[...]
    lane_a, lane_b = iota((CHUNK, CHUNK), 0), iota((CHUNK, CHUNK), 1)
    from_here = dot_nn(shares, (lane_a >= lane_b).astype(F32), PRECISE)
    up_to_here = dot_nn(shares, (lane_a < lane_b).astype(F32), PRECISE)
    all_rows = shares.shape[0]
    totals = jnp.broadcast_to(from_here[:, 0:1], shares.shape)
    row_a, row_b = iota((all_rows, all_rows), 0), iota((all_rows, all_rows), 1)
    outside = ((row_a % 8 < 4) & (row_b // 8 > row_a // 8)) | (
        (row_a % 8 >= 4) & (row_b // 8 < row_a // 8)
    )
    outside = (outside & (row_a % 8 == row_b % 8)).astype(F32)
    sums = dot_nn(outside, totals, PRECISE) + jnp.where(
        iota(shares.shape, 0) % 8 < 4, from_here, up_to_here
    )
    for number in range(num_chunks):
        lanes = slice(number * CHUNK, (number + 1) * CHUNK)
        for row in range(PARTS * heads):
            part, head = divmod(row, heads)
            at = number * 8 + row
            dgate_ref[0, row : row + 1, lanes] = (
                gate_refs[part][0, head : head + 1, lanes]
                + sums[at : at + 1, :]
                + sums[at + 4 : at + 5, :]
                + constants[row]
            )
    for step in range(steps):
        for copy in copies(step):
            copy.wait()


def summed(own, others):
    if not others:
        return own
    if len(others) == 1:
        return own + others[0]
    return (own + others[0]) + (others[1] + others[2])


def shards(queries, keys_raw, values, gates, lengths, key_gain, cotangent):
    tokens, width = queries.shape[1:]
    all_heads, head_width = key_gain.shape
    heads = all_heads // PARTS
    part_width = width // PARTS
    num_chunks = tokens // CHUNK
    rows = num_chunks * 8
    block = min(256, tokens)
    steps = tokens // block
    count = lax.axis_size("ctx")
    middle = count // 2 - 1
    docs = lengths.shape[1]
    after = head_width + CHUNK
    small = (
        jnp.pad(gates[0], ((0, 0), (0, after)))
        + jnp.pad(key_gain, ((0, 0), (tokens, CHUNK)))
        + jnp.pad(lengths, ((0, all_heads - 1), (tokens + head_width, CHUNK - docs))).astype(F32)
    )

    def shape_of(*shape, dtype=F32):
        return jax.ShapeDtypeStruct(shape, dtype)

    hbm = pl.BlockSpec(memory_space=pltpu.HBM)
    vmem = pl.BlockSpec(memory_space=pltpu.VMEM)
    table = shape_of(rows, CHUNK)
    states = shape_of(heads, head_width, head_width)
    decays = shape_of(heads, 1, head_width)
    part_gates = shape_of(1, heads, tokens)
    partials = shape_of(4, tokens, part_width, dtype=BF16)
    streams = (queries, keys_raw, values, cotangent)
    product = 2 * tokens * part_width * head_width

    def ends():
        outs = [states] * (2 * PARTS) + [decays] * PARTS + [table] * 3
        outs += [shape_of(all_heads, head_width), shape_of(4, head_width)]
        outs += [shape_of(1, tokens, width, dtype=BF16)] * 4
        return pl.pallas_call(
            functools.partial(ends_kernel, head_width, lengths.shape[1], count // 2),
            in_specs=[vmem] + [hbm] * 4,
            out_specs=[vmem] * len(outs),
            out_shape=outs,
            scratch_shapes=[
                pltpu.VMEM((rows, CHUNK), F32),
                pltpu.SemaphoreType.DMA((steps, 4)),
            ],
            compiler_params=pltpu.CompilerParams(vmem_limit_bytes=49 << 20),
            cost_estimate=pl.CostEstimate(
                flops=2 * product * PARTS, bytes_accessed=8 * tokens * width, transcendentals=0
            ),
            name="shard_ends",
        )(small, *streams)

    def local(part, gain, cum, fac):
        return pl.pallas_call(
            functools.partial(local_kernel, head_width, part),
            in_specs=[vmem] * 7,
            out_specs=[vmem] * 3,
            out_shape=[partials, part_gates, shape_of(heads, head_width)],
            scratch_shapes=[
                pltpu.VMEM((num_chunks, heads, head_width, head_width), BF16),
                pltpu.VMEM((heads, head_width, head_width), F32),
            ],
            compiler_params=pltpu.CompilerParams(vmem_limit_bytes=24 << 20),
            cost_estimate=pl.CostEstimate(
                flops=12 * product, bytes_accessed=16 * tokens * part_width, transcendentals=0
            ),
            name=f"local_{part}",
        )(*held, gain, cum, fac)

    def merge(*arrays):
        return pl.pallas_call(
            functools.partial(merge_kernel, head_width),
            in_specs=[vmem] * len(arrays),
            out_specs=[hbm] * 4 + [vmem] * 2,
            out_shape=[shape_of(1, tokens, width, dtype=BF16)] * 4
            + [shape_of(*gates.shape), shape_of(*arrays[-1].shape)],
            scratch_shapes=[
                pltpu.VMEM((4, tokens, width), BF16),
                pltpu.VMEM((PARTS, part_width, part_width), BF16),
                pltpu.VMEM((PARTS, part_width, part_width), BF16),
                pltpu.VMEM((16, 8 * head_width), BF16),
                pltpu.VMEM((rows, CHUNK), F32),
                pltpu.SemaphoreType.DMA((steps, 4)),
            ],
            compiler_params=pltpu.CompilerParams(vmem_limit_bytes=24 << 20),
            cost_estimate=pl.CostEstimate(
                flops=4 * product * PARTS, bytes_accessed=24 * tokens * width, transcendentals=0
            ),
            name="merge",
        )(*arrays)

    results = ends()
    near, far, decay = (results[i * PARTS : (i + 1) * PARTS] for i in range(3))
    cum, chunk_fac, shard_fac, gain, flags = results[3 * PARTS : 3 * PARTS + 5]
    held = results[3 * PARTS + 5 :]
    sent = [[] for _ in range(PARTS)]
    arrived = [[] for _ in range(PARTS)]
    local_parts = [None] * PARTS

    def send(part, hop):
        payload = near[part] if hop <= middle else far[part]
        if hop > 0:
            payload = payload + decay[part] * arrived[part][-1]
        sent[part].append(payload)
        arrived[part].append(
            lax.ppermute(
                payload, "ctx", [(hop, hop + 1), (count - 1 - hop, count - 2 - hop)]
            )
        )

    for part in range(PARTS):
        send(part, 0)
    for hop in range(count - 1):
        if hop < PARTS:
            local_cum = cum
            if hop > 0:
                local_cum, _ = lax.optimization_barrier((cum, arrived[0][hop - 1]))
            local_parts[hop] = list(local(hop, gain, local_cum, chunk_fac))
            if hop + 1 < count - 1:
                local_parts[hop][2], arrived[0][-1] = lax.optimization_barrier(
                    (local_parts[hop][2], arrived[0][-1])
                )
        if hop + 1 < count - 1:
            for part in range(PARTS):
                send(part, hop + 1)

    terms = []
    for part in range(PARTS):
        crossed = jnp.sum(sent[part][middle] * arrived[part][middle], axis=2)
        term = local_parts[part][2] + flags[0:1] * crossed
        if middle > 0:
            term = term + jnp.sum(sum(arrived[part][:middle]) * far[part], axis=2)
        terms.append(term)
    gain_term = jnp.concatenate(terms, axis=0)
    half = head_width // lax.axis_size("dp")
    second_half = flags[1:2, :half]
    lower_half, upper_half = gain_term[:, :half], gain_term[:, half:]
    away = (1.0 - second_half) * upper_half + second_half * lower_half
    kept = (1.0 - second_half) * lower_half + second_half * upper_half
    grad_gain = kept + lax.ppermute(away, "dp", [(0, 1), (1, 0)])

    def exchanged(array, reach):
        return lax.ppermute(array, "ctx", [(i, i ^ reach) for i in range(count)])

    pending, reach = [], 1
    while reach < count:
        if pending:
            grad_gain = summed(grad_gain, pending)
        pending = [exchanged(grad_gain, reach)]
        if reach * 2 < count:
            pending += [exchanged(grad_gain, reach * 2), exchanged(grad_gain, reach * 3)]
        reach *= 2 * min(len(pending), 2)

    zeros = jnp.zeros(states.shape, F32)
    if middle == 1:
        firsts, seconds = ([own[i] for own in arrived] for i in range(2))
    else:
        firsts = [sum(own[:middle], zeros) for own in arrived]
        seconds = [sum(own[middle:-1], zeros) for own in arrived]
    done = list(
        merge(
            *held, gain, flags, shard_fac,
            *[local_part[0] for local_part in local_parts],
            *[local_part[1] for local_part in local_parts],
            *firsts, *seconds, *[own[-1] for own in arrived],
            grad_gain, *pending,
        )
    )
    return tuple(done)


def solution(mesh):
    wide = P("dp", "ctx", "head")
    narrow = P("dp", "head", "ctx")
    return jax.shard_map(
        shards,
        mesh=mesh,
        in_specs=(wide, wide, wide, narrow, P("dp", None), P("head", None), wide),
        out_specs=(wide, wide, wide, wide, narrow, P("head", "dp")),
        check_vma=False,
    )
```

```python
import functools
import math

import jax
import jax.numpy as jnp
from jax import lax
from jax.experimental import pallas as pl
from jax.experimental.pallas import tpu as pltpu
from jax.sharding import PartitionSpec as P

CHUNK = 128
PARTS = 2
UNROLL = 4
PRECISE = lax.Precision.HIGHEST
F32 = jnp.float32
BF16 = jnp.bfloat16
LOG2E = math.log2(math.e)


def dot_nn(a, b, precision=None):
    return lax.dot_general(
        a, b, (((1,), (0,)), ((), ())), precision=precision, preferred_element_type=F32
    )


def dot_nt(a, b):
    return lax.dot_general(a, b, (((1,), (1,)), ((), ())), preferred_element_type=F32)


def dot_tn(a, b):
    return lax.dot_general(a, b, (((0,), (0,)), ((), ())), preferred_element_type=F32)


def iota(shape, dim):
    return lax.broadcasted_iota(jnp.int32, shape, dim)


def total_of(array):
    return jnp.sum(jnp.sum(array, axis=0, keepdims=True), axis=1, keepdims=True)


def later_sums(column):
    kept = iota((CHUNK, CHUNK), 0) >= iota((CHUNK, CHUNK), 1)
    return jnp.sum(jnp.where(kept, column, 0.0), axis=0, keepdims=True)


def decay_tables(docs, ctx, small_ref, spread, cum_ref, chunk_fac_ref, shard_fac_ref):
    rows = cum_ref.shape[0]
    num_chunks = rows // 8
    tokens = num_chunks * CHUNK
    for chunk in range(num_chunks):
        part = small_ref[:, chunk * CHUNK : (chunk + 1) * CHUNK]
        spread[chunk * 8 : chunk * 8 + 4, :] = part
        spread[chunk * 8 + 4 : chunk * 8 + 8, :] = part
    gates = spread[...] * LOG2E
    lane_a, lane_b = iota((CHUNK, CHUNK), 0), iota((CHUNK, CHUNK), 1)
    prefix = dot_nn(gates, (lane_a <= lane_b).astype(F32), PRECISE)
    suffix = dot_nn(gates, (lane_a > lane_b).astype(F32), PRECISE)
    totals = jnp.broadcast_to(prefix[:, CHUNK - 1 : CHUNK], (rows, CHUNK))
    row_a, row_b = iota((rows, rows), 0), iota((rows, rows), 1)
    same = (row_a % 8) == (row_b % 8)
    outside = ((row_a % 8 < 4) & (row_b // 8 < row_a // 8)) | (
        (row_a % 8 >= 4) & (row_b // 8 > row_a // 8)
    )
    others = dot_nn((same & outside).astype(F32), totals, PRECISE)

    first = ctx * tokens
    chunk_first = first + (iota((rows, CHUNK), 0) // 8) * CHUNK
    from_start = iota((rows, CHUNK), 0) % 8 < 4
    chunk_anchor = jnp.where(from_start, chunk_first - 1, chunk_first + (CHUNK - 1)).astype(F32)
    shard_anchor = jnp.where(from_start, first - 1, first + (tokens - 1)).astype(F32)
    positions = (chunk_first + iota((rows, CHUNK), 1)).astype(F32)
    segment = jnp.zeros((rows, CHUNK), F32)
    chunk_segment = jnp.zeros((rows, CHUNK), F32)
    shard_segment = jnp.zeros((rows, CHUNK), F32)
    begin = small_ref.shape[1] - CHUNK
    start = jnp.zeros((1, 1), F32)
    for doc in range(docs):
        segment += jnp.where(positions >= start, 1.0, 0.0)
        chunk_segment += jnp.where(chunk_anchor >= start, 1.0, 0.0)
        shard_segment += jnp.where(shard_anchor >= start, 1.0, 0.0)
        start = start + small_ref[0:1, begin + doc : begin + doc + 1]
    cum_ref[...] = jnp.where(from_start, prefix, segment)
    exponent = jnp.where(from_start, prefix, suffix)
    chunk_fac_ref[...] = jnp.where(
        segment == chunk_segment, jnp.exp2(jnp.minimum(exponent, 0.0)), 0.0
    )
    keep = segment == shard_segment
    shard_fac_ref[...] = jnp.where(keep, jnp.exp2(jnp.minimum(exponent + others, 0.0)), 0.0)


def ends_kernel(head_width, docs, half_ctx, *refs):
    small_ref, sources = refs[0], refs[1:5]
    ctx, dp = lax.axis_index("ctx"), lax.axis_index("dp")
    near_refs, far_refs, decay_refs = (
        refs[5 + i * PARTS : 5 + (i + 1) * PARTS] for i in range(3)
    )
    (cum_ref, chunk_fac_ref, shard_fac_ref, gain_ref, flag_ref, q_ref, k_ref, v_ref, cot_ref,
     spread, sems) = refs[5 + 3 * PARTS :]
    heads = near_refs[0].shape[0]
    rows = shard_fac_ref.shape[0]
    steps = sems.shape[0]
    tokens = q_ref.shape[1]
    block = tokens // steps
    chunks = block // CHUNK

    def copies(step):
        at = pl.ds(step * block, block)
        return [
            pltpu.make_async_copy(source.at[:, at, :], target.at[:, at, :], sems.at[step, i])
            for i, (source, target) in enumerate(zip(sources, (q_ref, k_ref, v_ref, cot_ref)))
        ]

    for step in range(steps):
        for i, copy in enumerate(copies(step)):
            copy.start(priority=i % 2)
    decay_tables(docs, ctx, small_ref, spread, cum_ref, chunk_fac_ref, shard_fac_ref)
    gain_ref[...] = small_ref[:, tokens : tokens + head_width]
    for part in range(PARTS):
        for head in range(heads):
            row = rows - 8 + part * heads + head
            decay_refs[part][head] = jnp.broadcast_to(
                shard_fac_ref[row : row + 1, CHUNK - 1 : CHUNK], (1, head_width)
            )

    def turned(ref, step, row, scale):
        pieces = []
        head = row % 4
        for chunk in range(step * chunks, (step + 1) * chunks):
            factor = shard_fac_ref[chunk * 8 + row : chunk * 8 + row + 1, :]
            piece = jnp.transpose(
                ref[
                    0,
                    chunk * CHUNK : (chunk + 1) * CHUNK,
                    head * head_width : (head + 1) * head_width,
                ]
            )
            pieces.append((piece.astype(F32) * (factor * scale)).astype(BF16))
        return jnp.concatenate(pieces, axis=1)

    ends, grads = {}, {}
    for step in range(steps):
        for copy in copies(step):
            copy.wait()
        at = slice(step * block, (step + 1) * block)
        for row in range(PARTS * heads):
            lanes = slice(row * head_width, (row + 1) * head_width)
            end = dot_nn(turned(k_ref, step, 4 + row, 1.0), v_ref[0, at, lanes])
            grad = dot_nn(turned(q_ref, step, row, head_width ** (-0.5)), cot_ref[0, at, lanes])
            ends[row] = ends[row] + end if step else end
            grads[row] = grads[row] + grad if step else grad
    middle = jnp.where(ctx == half_ctx - 1, 1.0, 0.0)
    low = ctx < half_ctx
    row = iota(flag_ref.shape, 0)
    flag_ref[...] = jnp.where(
        row == 0, middle, jnp.where(row == 1, dp.astype(F32), jnp.where(low, 1.0, 0.0))
    )
    for part in range(PARTS):
        for head in range(heads):
            row = part * heads + head
            near_refs[part][head] = jnp.where(low, ends[row], grads[row])
            far_refs[part][head] = jnp.where(low, grads[row], ends[row])


def local_kernel(
    head_width, part, q_ref, k_ref, v_ref, cot_ref, gain_ref, cum_ref, fac_ref,
    target, dgate_ref, dgain_ref, leaving, state,
):
    out_ref, dq_ref, dk_ref, dv_ref = (target.at[pl.ds(i, 1)] for i in range(4))
    heads = state.shape[0]
    num_chunks = leaving.shape[0]
    scale = head_width ** (-0.5)
    unroll = math.gcd(num_chunks, UNROLL)

    groups = num_chunks // unroll
    def wide_lanes(head):
        row = part * heads + head
        return slice(row * head_width, (row + 1) * head_width)

    def lanes_of(head):
        return slice(head * head_width, (head + 1) * head_width)

    def rows_of(chunk):
        return pl.ds(pl.multiple_of(chunk * CHUNK, CHUNK), CHUNK)

    def table(ref, chunk):
        return ref[pl.ds(pl.multiple_of(chunk * 8, 8), 8), :]

    pairs = [(at, head) for at in range(unroll) for head in range(heads)]

    def backward(chunks):
        facs = [table(fac_ref, chunk) for chunk in chunks]
        added = {}
        for at, head in pairs:
            row = part * heads + head
            rows, lanes = rows_of(chunks[at]), wide_lanes(head)
            turned = jnp.transpose(q_ref[0, rows, lanes]).astype(F32)
            turned = (turned * (facs[at][row : row + 1, :] * scale)).astype(BF16)
            added[at, head] = dot_nn(turned, cot_ref[0, rows, lanes])
        for head in range(heads):
            row = part * heads + head
            held = state[head]
            for at in range(unroll):
                leaving[chunks[at], head] = held.astype(BF16)
                held = held * facs[at][row : row + 1, CHUNK - 1 : CHUNK] + added[at, head]
            state[head] = held

    def forward(chunks):
        facs = [table(fac_ref, chunk) for chunk in chunks]
        cums = [table(cum_ref, chunk) for chunk in chunks]
        fac_columns = [jnp.transpose(fac) for fac in facs]
        cum_columns = [jnp.transpose(cum) for cum in cums]
        causal = iota((CHUNK, CHUNK), 0) >= iota((CHUNK, CHUNK), 1)
        limits = [
            jnp.where((columns[:, 4:5] == cum[4:5, :]) & causal, math.log2(scale), -1e30)
            for columns, cum in zip(cum_columns, cums)
        ]
        cum_columns = [columns + math.log2(scale) for columns in cum_columns]
        q, k, v, cot, k_raw, k_decayed, q_decayed, later = ({} for _ in range(8))
        from_start, to_end, added, held, entering = ({} for _ in range(5))
        for key in pairs:
            at, head = key
            row = part * heads + head
            rows, lanes = rows_of(chunks[at]), lanes_of(head)
            q[key], cot[key] = q_ref[0, rows, wide_lanes(head)], cot_ref[0, rows, wide_lanes(head)]
            v[key] = v_ref[0, rows, wide_lanes(head)]
            later[key] = leaving[chunks[at], head]
            k_raw[key] = k_ref[0, rows, wide_lanes(head)].astype(F32)
            k_wide = k_raw[key] * gain_ref[row : row + 1, :]
            k[key] = k_wide.astype(BF16)
            from_start[key] = fac_columns[at][:, row : row + 1] * scale
            to_end[key] = fac_columns[at][:, 4 + row : 5 + row]
            k_decayed[key] = (k_wide * to_end[key]).astype(BF16)
            q_decayed[key] = (q[key].astype(F32) * from_start[key]).astype(BF16)
            added[key] = dot_tn(k_decayed[key], v[key])
        for head in range(heads):
            row = part * heads + head
            now = state[head]
            for at in range(unroll):
                held[at, head] = now
                entering[at, head] = now.astype(BF16)
                now = now * facs[at][row : row + 1, CHUNK - 1 : CHUNK] + added[at, head]
            held[unroll, head] = now
            state[head] = now
        by_cot, scores, written = {}, {}, {}
        for key in pairs:
            by_cot[key] = dot_nt(cot[key], jnp.concatenate([v[key], entering[key]], axis=0))
            scores[key] = dot_nt(q[key], k[key])
            written[key] = dot_nt(v[key], later[key])
        weights, grad_scores = {}, {}
        for key in pairs:
            at, head = key
            row = part * heads + head
            decays = jnp.exp2(
                jnp.minimum(cum_columns[at][:, row : row + 1] - cums[at][row : row + 1, :], limits[at])
            )
            weights[key] = (scores[key] * decays).astype(BF16)
            grad_scores[key] = (by_cot[key][:, :CHUNK] * decays).astype(BF16)
        out, dq, dk, dv = {}, {}, {}, {}
        for key in pairs:
            out[key] = dot_nn(
                jnp.concatenate([weights[key], q_decayed[key]], axis=1),
                jnp.concatenate([v[key], entering[key]], axis=0),
            )
            dv[key] = dot_nn(
                jnp.concatenate([jnp.transpose(weights[key]), k_decayed[key]], axis=1),
                jnp.concatenate([cot[key], later[key]], axis=0),
            )
            dq[key] = dot_nn(grad_scores[key], k[key]) + by_cot[key][:, CHUNK:] * from_start[key]
            dk[key] = dot_tn(grad_scores[key], q[key]) + written[key] * to_end[key]
        gate_rows, gain_rows = {}, {}
        for key in pairs:
            at, head = key
            balance = jnp.sum(
                out[key] * cot[key].astype(F32) - dv[key] * v[key].astype(F32),
                axis=1, keepdims=True,
            )
            gate_rows[key] = later_sums(balance) + total_of(
                held[at + 1, head] * later[key].astype(F32)
            )
            gain_rows[key] = jnp.sum(dk[key] * k_raw[key], axis=0, keepdims=True)
        for key in pairs:
            at, head = key
            row = part * heads + head
            rows, own = rows_of(chunks[at]), lanes_of(head)
            out_ref[0, rows, own] = out[key].astype(BF16)
            dq_ref[0, rows, own] = dq[key].astype(BF16)
            dv_ref[0, rows, own] = dv[key].astype(BF16)
            dk_ref[0, rows, own] = (dk[key] * gain_ref[row : row + 1, :]).astype(BF16)
            dgate_ref[0, head : head + 1, rows] = gate_rows[key]
        for head in range(heads):
            dgain_ref[head : head + 1, :] += sum(gain_rows[at, head] for at in range(unroll))

    state[...] = jnp.zeros_like(state)

    def backward_group(index, carry):
        backward([num_chunks - 1 - (index * unroll + at) for at in range(unroll)])
        return carry

    lax.fori_loop(0, groups, backward_group, 0)
    state[...] = jnp.zeros_like(state)
    dgain_ref[...] = jnp.zeros_like(dgain_ref)

    def forward_group(index, carry):
        forward([index * unroll + at for at in range(unroll)])
        return carry

    lax.fori_loop(0, groups, forward_group, 0)


def merge_kernel(head_width, *refs):
    q_ref, k_ref, v_ref, cot_ref, gain_ref, flag_ref, fac_ref = refs[:7]
    partial_refs, gate_refs, first_refs, second_refs, last_refs = (
        refs[7 + i * PARTS : 7 + (i + 1) * PARTS] for i in range(5)
    )
    refs = refs[7 + 5 * PARTS :]
    extra = len(refs) - 12
    gain_refs, refs = refs[:extra], refs[extra:]
    targets, dgate_ref, dgain_ref, staged, entering, leaving, spread_ref, gate_scr, sems = (
        refs[:4], *refs[4:]
    )
    dgain_ref[...] = summed(gain_refs[0][...], [ref[...] for ref in gain_refs[1:]])
    heads = first_refs[0].shape[0]
    steps = sems.shape[0]
    num_chunks = fac_ref.shape[0] // 8
    chunks = num_chunks // steps
    block = chunks * CHUNK
    group_width = heads * head_width
    scale = head_width ** (-0.5)

    def copies(step):
        at = pl.ds(step * block, block)
        return [
            pltpu.make_async_copy(staged.at[i, at, :], target.at[0, at, :], sems.at[step, i])
            for i, target in enumerate(targets)
        ]

    gain_columns = jnp.transpose(jnp.concatenate([gain_ref[...], gain_ref[...]], axis=0))
    entering[...] = jnp.zeros_like(entering)
    leaving[...] = jnp.zeros_like(leaving)
    last_factors = fac_ref[(num_chunks - 1) * 8 : num_chunks * 8, CHUNK - 1 : CHUNK]
    low = jnp.broadcast_to(flag_ref[2:3, :], (head_width, head_width)) > 0.5
    constants = []
    for part in range(PARTS):
        for head in range(heads):
            row = part * heads + head
            own = slice(head * head_width, (head + 1) * head_width)
            gain = gain_columns[:, row : row + 1]
            first = first_refs[part][head]
            second = second_refs[part][head] + last_refs[part][head]
            state = jnp.where(low, first, second) * gain
            later = jnp.where(low, second, first)
            entering[part, own, own] = (state * scale).astype(BF16)
            leaving[part, own, own] = (later * gain).astype(BF16)
            constants.append(total_of(state * later) * last_factors[row : row + 1])

    spread = (iota(spread_ref.shape, 1) // head_width == iota(spread_ref.shape, 0) % 8).astype(F32)
    spread_ref[...] = spread.astype(BF16)
    ones = jnp.ones((8, head_width), BF16)
    for step in range(steps):
        numbers = range(step * chunks, (step + 1) * chunks)
        products, results, factors = {}, {}, {}
        for number in numbers:
            rows = slice(number * CHUNK, (number + 1) * CHUNK)
            fac = fac_ref[number * 8 : number * 8 + 8, :]
            high = fac.astype(BF16).astype(F32)
            both = jnp.concatenate([high, fac - high], axis=0).astype(BF16)
            factors[number] = dot_tn(both, spread_ref[...])
            for part in range(PARTS):
                group = slice(part * group_width, (part + 1) * group_width)
                products[number, part] = (
                    dot_nn(q_ref[0, rows, group], entering[part]),
                    dot_nt(cot_ref[0, rows, group], entering[part]),
                    dot_nt(v_ref[0, rows, group], leaving[part]),
                    dot_nn(k_ref[0, rows, group], leaving[part]),
                )
        for number in numbers:
            rows = slice(number * CHUNK, (number + 1) * CHUNK)
            for row in range(PARTS * heads):
                part, head = divmod(row, heads)
                lanes = slice(head * head_width, (head + 1) * head_width)
                wide = slice(row * head_width, (row + 1) * head_width)
                from_start = factors[number][:, wide]
                to_end = factors[number][:, (4 + row) * head_width : (5 + row) * head_width]
                across, dq, dk, written = (
                    product[:, lanes] * factor
                    for product, factor in zip(
                        products[number, part], (from_start, from_start, to_end, to_end)
                    )
                )
                results[number, row] = [
                    (partial_refs[part][i, rows, lanes].astype(F32) + added).astype(BF16)
                    for i, added in enumerate((across, dq, dk, written))
                ]
                queried = (across * cot_ref[0, rows, wide].astype(F32)).astype(BF16)
                kept = (written * v_ref[0, rows, wide].astype(F32)).astype(BF16)
                shares = dot_nt(ones, jnp.concatenate([queried, kept], axis=0))
                at = number * 8 + row
                gate_scr[at : at + 1, :] = shares[0:1, :CHUNK]
                gate_scr[at + 4 : at + 5, :] = shares[0:1, CHUNK:]
        for number in numbers:
            rows = slice(number * CHUNK, (number + 1) * CHUNK)
            for row in range(PARTS * heads):
                wide = slice(row * head_width, (row + 1) * head_width)
                for i in range(4):
                    staged[i, rows, wide] = results[number, row][i]
        for i, copy in enumerate(copies(step)):
            copy.start(priority=i % 2)

    shares = gate_scr[...]
    lane_a, lane_b = iota((CHUNK, CHUNK), 0), iota((CHUNK, CHUNK), 1)
    from_here = dot_nn(shares, (lane_a >= lane_b).astype(F32), PRECISE)
    up_to_here = dot_nn(shares, (lane_a < lane_b).astype(F32), PRECISE)
    all_rows = shares.shape[0]
    totals = jnp.broadcast_to(from_here[:, 0:1], shares.shape)
    row_a, row_b = iota((all_rows, all_rows), 0), iota((all_rows, all_rows), 1)
    outside = ((row_a % 8 < 4) & (row_b // 8 > row_a // 8)) | (
        (row_a % 8 >= 4) & (row_b // 8 < row_a // 8)
    )
    outside = (outside & (row_a % 8 == row_b % 8)).astype(F32)
    sums = dot_nn(outside, totals, PRECISE) + jnp.where(
        iota(shares.shape, 0) % 8 < 4, from_here, up_to_here
    )
    for number in range(num_chunks):
        lanes = slice(number * CHUNK, (number + 1) * CHUNK)
        for row in range(PARTS * heads):
            part, head = divmod(row, heads)
            at = number * 8 + row
            dgate_ref[0, row : row + 1, lanes] = (
                gate_refs[part][0, head : head + 1, lanes]
                + sums[at : at + 1, :]
                + sums[at + 4 : at + 5, :]
                + constants[row]
            )
    for step in range(steps):
        for copy in copies(step):
            copy.wait()


def summed(own, others):
    if not others:
        return own
    if len(others) == 1:
        return own + others[0]
    return (own + others[0]) + (others[1] + others[2])


def shards(queries, keys_raw, values, gates, lengths, key_gain, cotangent):
    tokens, width = queries.shape[1:]
    all_heads, head_width = key_gain.shape
    heads = all_heads // PARTS
    part_width = width // PARTS
    num_chunks = tokens // CHUNK
    rows = num_chunks * 8
    block = min(512, tokens)
    steps = tokens // block
    count = lax.axis_size("ctx")
    middle = count // 2 - 1
    docs = lengths.shape[1]
    after = head_width + CHUNK
    small = (
        jnp.pad(gates[0], ((0, 0), (0, after)))
        + jnp.pad(key_gain, ((0, 0), (tokens, CHUNK)))
        + jnp.pad(lengths, ((0, all_heads - 1), (tokens + head_width, CHUNK - docs))).astype(F32)
    )

    def shape_of(*shape, dtype=F32):
        return jax.ShapeDtypeStruct(shape, dtype)

    hbm = pl.BlockSpec(memory_space=pltpu.HBM)
    vmem = pl.BlockSpec(memory_space=pltpu.VMEM)
    table = shape_of(rows, CHUNK)
    states = shape_of(heads, head_width, head_width)
    decays = shape_of(heads, 1, head_width)
    part_gates = shape_of(1, heads, tokens)
    partials = shape_of(4, tokens, part_width, dtype=BF16)
    streams = (queries, keys_raw, values, cotangent)
    product = 2 * tokens * part_width * head_width

    def ends():
        outs = [states] * (2 * PARTS) + [decays] * PARTS + [table] * 3
        outs += [shape_of(all_heads, head_width), shape_of(4, head_width)]
        outs += [shape_of(1, tokens, width, dtype=BF16)] * 4
        return pl.pallas_call(
            functools.partial(ends_kernel, head_width, lengths.shape[1], count // 2),
            in_specs=[vmem] + [hbm] * 4,
            out_specs=[vmem] * len(outs),
            out_shape=outs,
            scratch_shapes=[
                pltpu.VMEM((rows, CHUNK), F32),
                pltpu.SemaphoreType.DMA((steps, 4)),
            ],
            compiler_params=pltpu.CompilerParams(vmem_limit_bytes=49 << 20),
            cost_estimate=pl.CostEstimate(
                flops=2 * product * PARTS, bytes_accessed=8 * tokens * width, transcendentals=0
            ),
            name="shard_ends",
        )(small, *streams)

    def local(part, gain, cum, fac):
        return pl.pallas_call(
            functools.partial(local_kernel, head_width, part),
            in_specs=[vmem] * 7,
            out_specs=[vmem] * 3,
            out_shape=[partials, part_gates, shape_of(heads, head_width)],
            scratch_shapes=[
                pltpu.VMEM((num_chunks, heads, head_width, head_width), BF16),
                pltpu.VMEM((heads, head_width, head_width), F32),
            ],
            compiler_params=pltpu.CompilerParams(vmem_limit_bytes=24 << 20),
            cost_estimate=pl.CostEstimate(
                flops=12 * product, bytes_accessed=16 * tokens * part_width, transcendentals=0
            ),
            name=f"local_{part}",
        )(*held, gain, cum, fac)

    def merge(*arrays):
        return pl.pallas_call(
            functools.partial(merge_kernel, head_width),
            in_specs=[vmem] * len(arrays),
            out_specs=[hbm] * 4 + [vmem] * 2,
            out_shape=[shape_of(1, tokens, width, dtype=BF16)] * 4
            + [shape_of(*gates.shape), shape_of(*arrays[-1].shape)],
            scratch_shapes=[
                pltpu.VMEM((4, tokens, width), BF16),
                pltpu.VMEM((PARTS, part_width, part_width), BF16),
                pltpu.VMEM((PARTS, part_width, part_width), BF16),
                pltpu.VMEM((16, 8 * head_width), BF16),
                pltpu.VMEM((rows, CHUNK), F32),
                pltpu.SemaphoreType.DMA((steps, 4)),
            ],
            compiler_params=pltpu.CompilerParams(vmem_limit_bytes=24 << 20),
            cost_estimate=pl.CostEstimate(
                flops=4 * product * PARTS, bytes_accessed=24 * tokens * width, transcendentals=0
            ),
            name="merge",
        )(*arrays)

    results = ends()
    near, far, decay = (results[i * PARTS : (i + 1) * PARTS] for i in range(3))
    cum, chunk_fac, shard_fac, gain, flags = results[3 * PARTS : 3 * PARTS + 5]
    held = results[3 * PARTS + 5 :]
    sent = [[] for _ in range(PARTS)]
    arrived = [[] for _ in range(PARTS)]
    local_parts = [None] * PARTS

    def send(part, hop):
        payload = near[part] if hop <= middle else far[part]
        if hop > 0:
            payload = payload + decay[part] * arrived[part][-1]
        sent[part].append(payload)
        arrived[part].append(
            lax.ppermute(
                payload, "ctx", [(hop, hop + 1), (count - 1 - hop, count - 2 - hop)]
            )
        )

    for part in range(PARTS):
        send(part, 0)
    for hop in range(count - 1):
        if hop < PARTS:
            local_cum = cum
            if hop > 0:
                local_cum, _ = lax.optimization_barrier((cum, arrived[0][hop - 1]))
            local_parts[hop] = list(local(hop, gain, local_cum, chunk_fac))
            if hop + 1 < count - 1:
                local_parts[hop][2], arrived[0][-1] = lax.optimization_barrier(
                    (local_parts[hop][2], arrived[0][-1])
                )
        if hop + 1 < count - 1:
            for part in range(PARTS):
                send(part, hop + 1)

    terms = []
    for part in range(PARTS):
        crossed = jnp.sum(sent[part][middle] * arrived[part][middle], axis=2)
        term = local_parts[part][2] + flags[0:1] * crossed
        if middle > 0:
            term = term + jnp.sum(sum(arrived[part][:middle]) * far[part], axis=2)
        terms.append(term)
    gain_term = jnp.concatenate(terms, axis=0)
    half = head_width // lax.axis_size("dp")
    second_half = flags[1:2, :half]
    lower_half, upper_half = gain_term[:, :half], gain_term[:, half:]
    away = (1.0 - second_half) * upper_half + second_half * lower_half
    kept = (1.0 - second_half) * lower_half + second_half * upper_half
    grad_gain = kept + lax.ppermute(away, "dp", [(0, 1), (1, 0)])

    def exchanged(array, reach):
        return lax.ppermute(array, "ctx", [(i, i ^ reach) for i in range(count)])

    pending, reach = [], 1
    while reach < count:
        if pending:
            grad_gain = summed(grad_gain, pending)
        pending = [exchanged(grad_gain, reach)]
        if reach * 2 < count:
            pending += [exchanged(grad_gain, reach * 2), exchanged(grad_gain, reach * 3)]
        reach *= 2 * min(len(pending), 2)

    zeros = jnp.zeros(states.shape, F32)
    if middle == 1:
        firsts, seconds = ([own[i] for own in arrived] for i in range(2))
    else:
        firsts = [sum(own[:middle], zeros) for own in arrived]
        seconds = [sum(own[middle:-1], zeros) for own in arrived]
    done = list(
        merge(
            *held, gain, flags, shard_fac,
            *[local_part[0] for local_part in local_parts],
            *[local_part[1] for local_part in local_parts],
            *firsts, *seconds, *[own[-1] for own in arrived],
            grad_gain, *pending,
        )
    )
    return tuple(done)


def solution(mesh):
    wide = P("dp", "ctx", "head")
    narrow = P("dp", "head", "ctx")
    return jax.shard_map(
        shards,
        mesh=mesh,
        in_specs=(wide, wide, wide, narrow, P("dp", None), P("head", None), wide),
        out_specs=(wide, wide, wide, wide, narrow, P("head", "dp")),
        check_vma=False,
    )
```
